32 devices in a mesh: seq: 8 (over y, x, core), mp: 4 (over z).
Axes of the slice: x: 2, y: 2, z: 4, core: 2. Of those that a mesh axis runs over, the one named last changes fastest.
Arguments:
- x_branch: bfloat16 [2048, 8192], P('seq', 'mp'), may hold values from -6 to 6
- z_branch: bfloat16 [2048, 8192], P('seq', 'mp'), may hold values from -6 to 6
- conv_weight: float32 [4, 8192], P(None, 'mp'), may hold values from -3 to 3
- conv_bias: float32 [8192], P('mp'), may hold values from -0.5 to 0.5
- xproj_weight: bfloat16 [8192, 544], P('mp'), may hold values from -0.0625 to 0.0625
- dt_weight: bfloat16 [512, 8192], P(None, 'mp'), may hold values from -0.25 to 0.25
- dt_bias: float32 [8192], P('mp'), may hold values from -4 to -2
- decay_rate: float32 [16, 8192], P(None, 'mp'), may hold values from 0.0009765625 to 2
- skip_gain: float32 [8192], P('mp'), may hold values from 0.5 to 1.5
- query_rows: bfloat16 [2048, 8192], P('seq', 'mp'), may hold values from -6 to 6
- key_rows: bfloat16 [2048, 1024], P('seq', 'mp'), may hold values from -6 to 6
- value_rows: bfloat16 [2048, 1024], P('seq', 'mp'), may hold values from -6 to 6
- lengths: int32 [4], replicated, may hold values from 1 to 1024, as said below
- destination: int32 [2048], replicated, may hold values from 0 to 2047, as said below
Outputs:
- mamba_out: bfloat16 [2048, 8192], P('seq', 'mp')
- regrouped: bfloat16 [2048, 8192], P('seq', 'mp')
The draws below stay inside these ranges and needn't reach their ends.
Inputs may be any that keep to these rules, and one draw needn't show every extreme that they name: The 4 lengths sum to 2048, and the second of them equals 1024. destination is a permutation of 0 to 2047. Cut each aligned block of 256 positions into 8 runs of 32 consecutive positions: each run goes in order to consecutive rows of one aligned target block, the runs of block i to the rows that start at i * 32 within their target blocks, and the 8 runs of one block go to 8 different target blocks.
All inputs are finite; a program needn't handle non-finite values.
Results may differ from the reference program's by a relative error of at most 0.02.
Values may be sent and summed in bfloat16 or wider, within the bound.
No kernel may reach another device: no remote copies, remote signals or barrier semaphores. Data moves between devices by JAX's collectives and lax.ppermute only.
A program may use at most 128 MiB of HBM per device.

```python
import math
import jax
import jax.numpy as jnp
from jax import lax

DI = 8192
NS = 16
R = 512
KC = 4
QH = 64
KVH = 8
HD = 128
TOK_DEV = 256
TOKENS = 2048
MAXDOC = 1024


def draw_query_rows(key, part):
    drawn_rows = jnp.clip(jax.random.normal(jax.random.fold_in(key, 11), (TOKENS, QH * HD), jnp.float32), -6.0, 6.0)
    return drawn_rows.astype(jnp.bfloat16)


def draw_key_rows(key, part):
    drawn_rows = jnp.clip(jax.random.normal(jax.random.fold_in(key, 12), (TOKENS, KVH * HD), jnp.float32), -6.0, 6.0)
    return drawn_rows.astype(jnp.bfloat16)


def pack_plan(key):
    plan_key = jax.random.fold_in(key, 30)
    first_lo = TOK_DEV + 1
    first_hi = TOKENS // 2 - 2 * TOK_DEV - KC
    first_len = jax.random.randint(jax.random.fold_in(plan_key, 1), (), first_lo, first_hi).astype(jnp.int32)
    after = (TOKENS - MAXDOC - first_len).astype(jnp.int32)
    quarter = after // 4
    third_len = (after // 2 + jax.random.randint(jax.random.fold_in(plan_key, 2), (), -TOK_DEV // 2, TOK_DEV // 2 + 1) * quarter // (TOK_DEV // 2)).astype(jnp.int32)
    lengths = jnp.stack([first_len, jnp.array(MAXDOC, jnp.int32), third_len, (after - third_len).astype(jnp.int32)]).astype(jnp.int32)
    doc_ends = jnp.cumsum(lengths).astype(jnp.int32)
    starts = (doc_ends - lengths).astype(jnp.int32)
    places = jnp.arange(TOKENS, dtype=jnp.int32)
    doc_ids = jnp.sum((places[:, None] >= doc_ends[None, :]).astype(jnp.int32), axis=1)
    depth = places - starts[doc_ids] + 1
    sources = TOKENS // TOK_DEV
    run_rows = TOK_DEV // sources
    block_cost = jnp.sum(depth.reshape(sources, sources, run_rows), axis=2).astype(jnp.int32)

    def place(source, carried):
        load, table = carried
        costs = block_cost[source]
        heavy_first = jnp.argsort(-costs, stable=True).astype(jnp.int32)
        light_first = jnp.argsort(load, stable=True).astype(jnp.int32)
        table = table.at[source, heavy_first].set(light_first)
        load = load.at[light_first].add(costs[heavy_first])
        return (load, table)
    initial = (jnp.zeros((sources,), jnp.int32), jnp.zeros((sources, sources), jnp.int32))
    unused_load, table = lax.fori_loop(0, sources, place, initial)
    source_of = places // TOK_DEV
    run_of = places % TOK_DEV // run_rows
    offset = places % run_rows
    destination = (table[source_of, run_of] * TOK_DEV + source_of * run_rows + offset).astype(jnp.int32)
    return (lengths, destination)


def draw_lengths(key, part):
    return pack_plan(key)[0]


def draw_destination(key, part):
    return pack_plan(key)[1]


def shard_levels(key, extent, cuts, least, top_value):
    def one(axis_at, parts):
        steps = jax.random.uniform(jax.random.fold_in(jax.random.fold_in(key, 6), axis_at), (parts,), jnp.float32, least / len(cuts), top_value / len(cuts))
        return jnp.repeat(jnp.exp(steps), extent[axis_at] // parts).reshape((-1,) + (1,) * (len(extent) - axis_at - 1))

    gain = one(*cuts[0])
    for cut in cuts[1:]:
        gain = gain * one(*cut)
    return gain


def gaussian(stream_key, dims, spread, bound, shards=(), held_as=jnp.bfloat16):
    entries = jax.random.normal(stream_key, dims, jnp.float32) * spread
    if len(shards) > 0:
        entries = shard_levels(stream_key, dims, shards, -0.22, 0.18) * entries
    return jnp.clip(entries, min=-bound, max=bound).astype(held_as)


def setup_inputs(seed: int = 0) -> dict:
    keys = jax.random.split(jax.random.key(seed), 15)
    x_branch = gaussian(keys[0], (TOKENS, DI), 1.0, 6.0, ((0, 8), (1, 4)))
    z_branch = gaussian(keys[1], (TOKENS, DI), 1.0, 6.0, ((0, 8), (1, 4)))
    conv_weight = gaussian(keys[2], (KC, DI), 0.5, 3.0, ((1, 4),), jnp.float32)
    conv_bias = jnp.clip(jax.random.uniform(keys[3], (DI,), jnp.float32, -0.5, 0.5) * shard_levels(keys[3], (DI,), ((0, 4),), -0.4, 0.0), -0.5, 0.5)
    xproj_weight = gaussian(keys[4], (DI, R + 2 * NS), DI ** -0.5, 0.0625, ((0, 4),))
    dt_weight = gaussian(keys[5], (R, DI), R ** -0.5, 0.25, ((1, 4),))
    dt_bias = jnp.clip(-4.0 + 2.0 * jax.random.uniform(keys[6], (DI,), jnp.float32) ** shard_levels(keys[6], (DI,), ((0, 4),), -0.2, 0.2), -4.0, -2.0)
    decay_rate = jnp.clip(jnp.exp(math.log(2.0) - 7.624619 * jax.random.uniform(keys[7], (NS, DI), jnp.float32) ** shard_levels(keys[7], (NS, DI), ((1, 4),), -0.2, 0.2)), 0.0009765625, 2.0)
    skip_gain = jnp.clip(0.5 + 1.0 * jax.random.uniform(keys[8], (DI,), jnp.float32) ** shard_levels(keys[8], (DI,), ((0, 4),), -0.2, 0.2), 0.5, 1.5)
    query_rows = draw_query_rows(jax.random.fold_in(keys[14], 71), 0)
    key_rows = draw_key_rows(jax.random.fold_in(keys[14], 71), 0)
    value_rows = gaussian(keys[11], (TOKENS, KVH * HD), 1.0, 6.0, ((0, 8), (1, 4)))
    lengths = draw_lengths(jax.random.fold_in(keys[14], 71), 0)
    destination = draw_destination(jax.random.fold_in(keys[14], 71), 0)
    return dict(x_branch=x_branch, z_branch=z_branch, conv_weight=conv_weight, conv_bias=conv_bias, xproj_weight=xproj_weight, dt_weight=dt_weight, dt_bias=dt_bias, decay_rate=decay_rate, skip_gain=skip_gain, query_rows=query_rows, key_rows=key_rows, value_rows=value_rows, lengths=lengths, destination=destination)


masked_score = -1.0e30


def doc_lookup(lengths, places):
    doc_ends = jnp.cumsum(lengths).astype(jnp.int32)
    starts = (doc_ends - lengths).astype(jnp.int32)
    doc_ids = jnp.sum((places[:, None] >= doc_ends[None, :]).astype(jnp.int32), axis=1)
    at_start = jnp.any(places[:, None] == starts[None, :], axis=1)
    return doc_ids, at_start


def mamba_mixer(x_branch, z_branch, conv_weight, conv_bias, xproj_weight, dt_weight, dt_bias, decay_rate, skip_gain, lengths):
    places = jnp.arange(TOKENS, dtype=jnp.int32)
    doc_ids, at_start = doc_lookup(lengths, places)
    padded = jnp.concatenate([jnp.zeros((KC - 1, DI), jnp.float32), x_branch.astype(jnp.float32)], axis=0)
    padded_docs, unused = doc_lookup(lengths, jnp.arange(TOKENS + KC - 1, dtype=jnp.int32) - (KC - 1))
    conv_sum = conv_bias[None, :] + jnp.zeros((TOKENS, DI), jnp.float32)
    for lag_step in range(KC):
        window = padded[KC - 1 - lag_step:KC - 1 - lag_step + TOKENS]
        same_doc = padded_docs[KC - 1 - lag_step:KC - 1 - lag_step + TOKENS] == doc_ids
        conv_sum = conv_sum + conv_weight[lag_step][None, :] * jnp.where(same_doc[:, None], window, 0.0)
    inner_act = jax.nn.silu(conv_sum).astype(jnp.bfloat16)
    projected = jnp.dot(inner_act, xproj_weight, preferred_element_type=jnp.float32)
    dt_low = projected[:, :R].astype(jnp.bfloat16)
    step_size = jax.nn.softplus(jnp.dot(dt_low, dt_weight, preferred_element_type=jnp.float32) + dt_bias[None, :])
    b_input = projected[:, R:R + NS]
    c_output = projected[:, R + NS:]
    inner_float = inner_act.astype(jnp.float32)
    drive_term = step_size * inner_float
    keep_mask = jnp.where(at_start, 0.0, 1.0).astype(jnp.float32)

    def advance(carried, inputs):
        step_row, drive_row, keep_row, b_row, c_row = inputs
        decay_now = jnp.exp(-step_row[None, :] * decay_rate) * keep_row
        carried = decay_now * carried + b_row[:, None] * drive_row[None, :]
        return carried, jnp.sum(c_row[:, None] * carried, axis=0)

    initial = jnp.zeros((NS, DI), jnp.float32)
    unused_end, scanned = lax.scan(advance, initial, (step_size, drive_term, keep_mask, b_input, c_output))
    scanned = scanned + skip_gain[None, :] * inner_float
    return (scanned * jax.nn.silu(z_branch.astype(jnp.float32))).astype(jnp.bfloat16), doc_ids


def attend_all(query_rows, key_rows, value_rows, doc_ids):
    group_size = QH // KVH
    span = min(TOKENS, TOK_DEV + MAXDOC)
    factor = HD ** -0.5

    def one_block(block_index):
        query_start = block_index * TOK_DEV
        key_start = jnp.clip(query_start + TOK_DEV - span, 0, TOKENS - span).astype(jnp.int32)
        query_block = lax.dynamic_slice_in_dim(query_rows, query_start, TOK_DEV, 0).astype(jnp.float32).reshape(TOK_DEV, KVH, group_size, HD)
        key_block = lax.dynamic_slice_in_dim(key_rows, key_start, span, 0).astype(jnp.float32).reshape(span, KVH, HD)
        value_block = lax.dynamic_slice_in_dim(value_rows, key_start, span, 0).astype(jnp.float32).reshape(span, KVH, HD)
        query_places = query_start + jnp.arange(TOK_DEV, dtype=jnp.int32)
        key_places = key_start + jnp.arange(span, dtype=jnp.int32)
        query_docs = lax.dynamic_slice_in_dim(doc_ids, query_start, TOK_DEV, 0)
        key_docs = lax.dynamic_slice_in_dim(doc_ids, key_start, span, 0)
        visible = (key_places[None, :] <= query_places[:, None]) & (key_docs[None, :] == query_docs[:, None])
        scores = jnp.einsum("qhgd,khd->hgqk", query_block, key_block) * factor
        scores = jnp.where(visible[None, None], scores, masked_score)
        best_score = jnp.max(scores, axis=3, keepdims=True)
        weights = jnp.where(visible[None, None], jnp.exp(scores - best_score), 0.0)
        weight_sum = jnp.sum(weights, axis=3)
        rounded = lax.optimization_barrier(weights.astype(jnp.bfloat16)).astype(jnp.float32)
        summed = jnp.einsum("hgqk,khd->qhgd", rounded, value_block)
        result = summed / jnp.transpose(weight_sum, (2, 0, 1))[..., None]
        return result.reshape(TOK_DEV, QH * HD).astype(jnp.bfloat16)

    blocks = lax.map(one_block, jnp.arange(TOKENS // TOK_DEV, dtype=jnp.int32))
    return blocks.reshape(TOKENS, QH * HD)


def reference(x_branch, z_branch, conv_weight, conv_bias, xproj_weight, dt_weight, dt_bias, decay_rate, skip_gain, query_rows, key_rows, value_rows, lengths, destination):
    mamba_out, doc_ids = mamba_mixer(x_branch, z_branch, conv_weight, conv_bias, xproj_weight, dt_weight, dt_bias, decay_rate, skip_gain, lengths)
    attended = attend_all(query_rows, key_rows, value_rows, doc_ids)
    regrouped = jnp.zeros((TOKENS, QH * HD), jnp.bfloat16).at[destination].set(attended)
    return (mamba_out, regrouped)
```

```python
import functools

import jax
import jax.numpy as jnp
from jax import lax
from jax.experimental import pallas as pl
from jax.experimental.pallas import tpu as pltpu
from jax.sharding import PartitionSpec as P

HD = 128
LANES = 128
HALO = 16
LOG2E = 1.4426950408889634
RESET = 1e30
APART = 65536.0
VMEM_LIMIT = 48 * 1024 * 1024


def doc_edges(lengths_ref):
    starts, ends, total = [], [], 0
    for i in range(lengths_ref.shape[0]):
        starts.append(total)
        total = total + lengths_ref[i]
        ends.append(total)
    return starts, ends


def doc_start(places, starts):
    found = jnp.zeros_like(places)
    for start in starts[1:]:
        found = jnp.where(places >= start, start, found)
    return found


def channel_chunk(channels):
    return 512 if channels % 512 == 0 else channels


def conv_kernel(lengths_ref, x_ref, halo_ref, w_ref, b_ref, xp_ref, inner_ref, part_ref, ext, acc):
    tok, chunk = x_ref.shape
    starts, _ = doc_edges(lengths_ref)
    anchor = lax.axis_index("seq") * tok
    places = anchor + lax.broadcasted_iota(jnp.int32, (tok, LANES), 0)
    depth = places - doc_start(places, starts)
    ext[0:HALO, :] = halo_ref[...].astype(jnp.float32)
    ext[HALO:, :] = x_ref[...].astype(jnp.float32)
    for lane in range(0, chunk, LANES):
        cols = slice(lane, lane + LANES)
        total = b_ref[:, cols] + w_ref[0:1, cols] * ext[HALO:, cols]
        for lag in range(1, w_ref.shape[0]):
            window = ext[HALO - lag : HALO - lag + tok, cols]
            total += w_ref[lag : lag + 1, cols] * jnp.where(depth >= lag, window, 0.0)
        act = total * (0.5 + 0.5 * jnp.tanh(0.5 * total))
        inner_ref[:, cols] = act.astype(jnp.bfloat16)
    product = jnp.dot(inner_ref[...], xp_ref[...], preferred_element_type=jnp.float32)
    at = pl.program_id(0)

    @pl.when(at == 0)
    def _():
        acc[...] = product

    @pl.when(at > 0)
    def _():
        acc[...] += product

    @pl.when(at == pl.num_programs(0) - 1)
    def _():
        part_ref[...] = acc[...].astype(jnp.bfloat16)


def conv_project(lengths, x_branch, halo, conv_weight, conv_bias, xproj_weight):
    tok, channels = x_branch.shape
    width = xproj_weight.shape[1]
    taps = conv_weight.shape[0]
    chunk = channel_chunk(channels)
    return pl.pallas_call(
        conv_kernel,
        grid=(channels // chunk,),
        in_specs=[
            pl.BlockSpec(memory_space=pltpu.SMEM),
            pl.BlockSpec((tok, chunk), lambda i: (0, i)),
            pl.BlockSpec((HALO, chunk), lambda i: (0, i)),
            pl.BlockSpec((taps, chunk), lambda i: (0, i)),
            pl.BlockSpec((1, chunk), lambda i: (0, i)),
            pl.BlockSpec((chunk, width), lambda i: (i, 0)),
        ],
        out_specs=[
            pl.BlockSpec((tok, chunk), lambda i: (0, i)),
            pl.BlockSpec((tok, width), lambda i: (0, 0)),
        ],
        out_shape=[
            jax.ShapeDtypeStruct((tok, channels), jnp.bfloat16),
            jax.ShapeDtypeStruct((tok, width), jnp.bfloat16),
        ],
        scratch_shapes=[
            pltpu.VMEM((tok + HALO, chunk), jnp.float32),
            pltpu.VMEM((tok, width), jnp.float32),
        ],
        compiler_params=pltpu.CompilerParams(vmem_limit_bytes=VMEM_LIMIT),
        cost_estimate=pl.CostEstimate(
            flops=2 * tok * channels * width, bytes_accessed=8 * tok * channels, transcendentals=tok * channels
        ),
        name="conv_project",
    )(lengths, x_branch, halo, conv_weight, conv_bias.reshape(1, channels), xproj_weight)


def spread(columns):
    tok, k = columns.shape
    rows = jnp.broadcast_to(columns.astype(jnp.float32)[:, None, :], (tok, k, k))
    own = lax.broadcasted_iota(jnp.int32, (tok, k, k), 1) == lax.broadcasted_iota(jnp.int32, (tok, k, k), 2)
    picked = jnp.where(own, rows, 0.0).reshape(tok * k, k).astype(jnp.bfloat16)
    return jnp.dot(picked, jnp.ones((k, LANES), jnp.bfloat16), preferred_element_type=jnp.float32)


def advance(state, tile, row, rate2, step_ref, drive_ref, b_rows):
    out = []
    for i, held in enumerate(state):
        cols = slice(i * LANES, (i + 1) * LANES)
        decay = jnp.exp2(rate2[i] * step_ref[tile, row : row + 1, cols])
        out.append(decay * held + b_rows * drive_ref[tile, row : row + 1, cols])
    return out


def lane_tiles(value):
    return [value[:, i : i + LANES] for i in range(0, value.shape[1], LANES)]


ROWS = 8
UNROLL = 2 * ROWS


def state_kernel(
    low_rank, lengths_ref, proj_ref, dtw_ref, bias_ref, rate_ref, inner_ref, step_ref, drive_ref, state_ref, b_spread
):
    tok, chunk = inner_ref.shape
    states = rate_ref.shape[0]
    starts, _ = doc_edges(lengths_ref)

    @pl.when(pl.program_id(0) == 0)
    def _():
        b_spread[...] = spread(proj_ref[:, low_rank : low_rank + states])

    anchor = lax.axis_index("seq") * tok
    places = anchor + lax.broadcasted_iota(jnp.int32, (tok, LANES), 0)
    at_start = places == doc_start(places, starts)
    raw = jnp.dot(proj_ref[:, :low_rank], dtw_ref[...], preferred_element_type=jnp.float32)
    totals = []
    for lane in range(0, chunk, LANES):
        cols = slice(lane, lane + LANES)
        biased = raw[:, cols] + bias_ref[:, cols]
        step = jnp.maximum(biased, 0.0) + jnp.log1p(jnp.exp(-jnp.abs(biased)))
        drive = step * inner_ref[:, cols].astype(jnp.float32)
        drive_ref[:, :, cols] = drive.reshape(tok // ROWS, ROWS, LANES)
        step = jnp.where(at_start, RESET, step)
        step_ref[:, :, cols] = step.reshape(tok // ROWS, ROWS, LANES)
        totals.append(jnp.sum(step, axis=0, keepdims=True))
    rate2 = lane_tiles(rate_ref[...] * (-LOG2E))

    def body(turn, state):
        for u in range(UNROLL):
            tile = turn * (UNROLL // ROWS) + u // ROWS
            at = pl.multiple_of(turn * UNROLL * states, states) + u * states
            state = advance(state, tile, u % ROWS, rate2, step_ref, drive_ref, b_spread[pl.ds(at, states), :])
        return state

    end = lax.fori_loop(0, tok // UNROLL, body, [jnp.zeros_like(r) for r in rate2])
    total = jnp.concatenate(totals, axis=1)
    high = total.astype(jnp.bfloat16)
    low = (total - high.astype(jnp.float32)).astype(jnp.bfloat16)
    state_ref[0:states, :] = jnp.concatenate(end, axis=1).astype(jnp.bfloat16)
    row = lax.broadcasted_iota(jnp.int32, (16, chunk), 0)
    both = jnp.where(row == 0, high.astype(jnp.float32), jnp.where(row == 1, low.astype(jnp.float32), 0.0))
    state_ref[states : states + 16, :] = both.astype(jnp.bfloat16)


def local_state(lengths, projected, dt_weight, dt_bias, decay_rate, inner_act):
    tok, channels = inner_act.shape
    low_rank = dt_weight.shape[0]
    states = decay_rate.shape[0]
    width = projected.shape[1]
    chunk = channel_chunk(channels)
    by_chunk = lambda rows: pl.BlockSpec((rows, chunk), lambda i: (0, i))
    by_tile = pl.BlockSpec((tok // ROWS, ROWS, chunk), lambda i: (0, 0, i))
    return pl.pallas_call(
        functools.partial(state_kernel, low_rank),
        grid=(channels // chunk,),
        in_specs=[
            pl.BlockSpec(memory_space=pltpu.SMEM),
            pl.BlockSpec((tok, width), lambda i: (0, 0)),
            by_chunk(low_rank),
            by_chunk(1),
            by_chunk(states),
            by_chunk(tok),
        ],
        out_specs=[by_tile, by_tile, by_chunk(states + 16)],
        out_shape=[
            jax.ShapeDtypeStruct((tok // ROWS, ROWS, channels), jnp.float32),
            jax.ShapeDtypeStruct((tok // ROWS, ROWS, channels), jnp.float32),
            jax.ShapeDtypeStruct((states + 16, channels), jnp.bfloat16),
        ],
        scratch_shapes=[pltpu.VMEM((tok * states, LANES), jnp.float32)],
        compiler_params=pltpu.CompilerParams(vmem_limit_bytes=VMEM_LIMIT),
        cost_estimate=pl.CostEstimate(
            flops=8 * tok * channels * states,
            bytes_accessed=12 * tok * channels,
            transcendentals=tok * channels * states,
        ),
        name="local_state",
    )(lengths, projected, dt_weight, dt_bias.reshape(1, channels), decay_rate, inner_act)


def output_kernel(
    low_rank,
    reach,
    proj_ref,
    step_ref,
    drive_ref,
    inner_ref,
    z_ref,
    rate_ref,
    skip_ref,
    mine_ref,
    theirs_ref,
    out_ref,
    bc_spread,
    parts,
    scanned,
):
    tok, chunk = inner_ref.shape
    states = rate_ref.shape[0]
    fold = 8

    @pl.when(pl.program_id(0) == 0)
    def _():
        bc_spread[...] = spread(proj_ref[:, low_rank : low_rank + 2 * states])

    rate2 = lane_tiles(rate_ref[...] * (-LOG2E))
    odd = lax.rem(lax.axis_index("seq"), 2)
    state = [jnp.zeros_like(r) for r in rate2]
    for back in range(reach, 0, -1):
        if back % 2 == 0:
            block = mine_ref[back // 2]
        else:
            block = theirs_ref[(back + 1) // 2 - odd]
        block = block.astype(jnp.float32)
        total = block[states : states + 1] + block[states + 1 : states + 2]
        state = [
            jnp.exp2(r * t) * s + e
            for r, t, s, e in zip(rate2, lane_tiles(total), state, lane_tiles(block[:states]))
        ]

    def body(turn, state):
        base = pl.multiple_of(turn * UNROLL, UNROLL)
        for u in range(UNROLL):
            tile = turn * (UNROLL // ROWS) + u // ROWS
            at = pl.multiple_of(turn * UNROLL * 2 * states, 2 * states) + u * 2 * states
            state = advance(state, tile, u % ROWS, rate2, step_ref, drive_ref, bc_spread[pl.ds(at, states), :])
            c_rows = bc_spread[pl.ds(at + states, states), :]
            for i, held in enumerate(state):
                term = c_rows * held
                part = term[0:fold]
                for more in range(fold, states, fold):
                    part = part + term[more : more + fold]
                parts[i, u * fold : (u + 1) * fold, :] = part
        for group in range(0, UNROLL, 8):
            for i in range(len(state)):
                cols = slice(i * LANES, (i + 1) * LANES)
                row = parts[i, pl.ds(group * fold, 8, stride=fold), :]
                for n in range(1, fold):
                    row = row + parts[i, pl.ds(group * fold + n, 8, stride=fold), :]
                scanned[pl.ds(base + group, 8), cols] = row
        return state

    lax.fori_loop(0, tok // UNROLL, body, state)
    for lane in range(0, chunk, LANES):
        cols = slice(lane, lane + LANES)
        z = z_ref[:, cols].astype(jnp.float32)
        gate = z * (0.5 + 0.5 * jnp.tanh(0.5 * z))
        y = scanned[:, cols] + skip_ref[:, cols] * inner_ref[:, cols].astype(jnp.float32)
        out_ref[:, cols] = (y * gate).astype(jnp.bfloat16)


def scan_output(projected, step, drive, inner_act, z_branch, decay_rate, skip_gain, mine, theirs, low_rank, reach):
    tok, channels = inner_act.shape
    states = decay_rate.shape[0]
    width = projected.shape[1]
    chunk = channel_chunk(channels)
    by_chunk = lambda rows: pl.BlockSpec((rows, chunk), lambda i: (0, i))
    by_tile = pl.BlockSpec((tok // ROWS, ROWS, chunk), lambda i: (0, 0, i))
    stacked = lambda a: pl.BlockSpec((a.shape[0], a.shape[1], chunk), lambda i: (0, 0, i))
    return pl.pallas_call(
        functools.partial(output_kernel, low_rank, reach),
        grid=(channels // chunk,),
        in_specs=[
            pl.BlockSpec((tok, width), lambda i: (0, 0)),
            by_tile,
            by_tile,
            by_chunk(tok),
            by_chunk(tok),
            by_chunk(states),
            by_chunk(1),
            stacked(mine),
            stacked(theirs),
        ],
        out_specs=by_chunk(tok),
        out_shape=jax.ShapeDtypeStruct((tok, channels), jnp.bfloat16),
        scratch_shapes=[
            pltpu.VMEM((tok * 2 * states, LANES), jnp.float32),
            pltpu.VMEM((chunk // LANES, UNROLL * 8, LANES), jnp.float32),
            pltpu.VMEM((tok, chunk), jnp.float32),
        ],
        compiler_params=pltpu.CompilerParams(vmem_limit_bytes=VMEM_LIMIT),
        cost_estimate=pl.CostEstimate(
            flops=12 * tok * channels * states,
            bytes_accessed=14 * tok * channels,
            transcendentals=tok * channels * states,
        ),
        name="scan_output",
    )(projected, step, drive, inner_act, z_branch, decay_rate, skip_gain.reshape(1, channels), mine, theirs)


def attend_kernel(lengths_ref, place_ref, q_ref, mine_ref, theirs_ref, out_ref, tops, sums, acc):
    tok = q_ref.shape[0]
    heads = q_ref.shape[1] // HD
    kv_local = mine_ref.shape[2] // (2 * HD)
    group = pl.program_id(0)
    position = lax.axis_index("seq")
    odd = lax.rem(position, 2)
    anchor = position * tok
    scale = LOG2E * HD**-0.5
    starts, ends = doc_edges(lengths_ref)
    lane = lax.broadcasted_iota(jnp.int32, (1, LANES), 1)
    first = jnp.full((1, LANES), 2**30, jnp.int32)
    last = jnp.zeros((1, LANES), jnp.int32)
    for i, (start, end) in enumerate(zip(starts, ends)):
        first = jnp.where(lane == i, start, first)
        last = jnp.where(lane == i, end, last)
    rows = lax.broadcasted_iota(jnp.int32, (tok, LANES), 0)

    def in_doc(base):
        return (rows + base >= first) & (rows + base < last)

    apart = jnp.where(in_doc(anchor) | (lane >= len(starts)), 0.0, -APART).astype(jnp.bfloat16)
    key_cols = pl.ds(pl.multiple_of(group * HD, HD), HD)
    value_cols = pl.ds(pl.multiple_of((group + kv_local) * HD, HD), HD)
    causal = lax.broadcasted_iota(jnp.int32, (tok, tok), 0) <= lax.broadcasted_iota(jnp.int32, (tok, tok), 1)

    def block_terms(keys, values, base):
        marks = jnp.where(in_doc(base), 1.0, 0.0).astype(jnp.bfloat16)
        return jnp.concatenate([keys, marks], axis=1), values.astype(jnp.float32).T.astype(jnp.bfloat16)

    def scores(keys, head):
        queries = jnp.concatenate([q_ref[:, head * HD : (head + 1) * HD], apart], axis=1)
        return lax.dot_general(keys, queries, (((1,), (1,)), ((), ())), preferred_element_type=jnp.float32)

    keys, values = block_terms(mine_ref[0, :, key_cols], mine_ref[0, :, value_cols], anchor)
    for head in range(heads):
        s = jnp.where(causal, scores(keys, head), -APART)
        top = jnp.max(s, axis=0, keepdims=True)
        weights = jnp.exp2((s - top) * scale)
        tops[head] = top
        sums[head] = jnp.sum(weights, axis=0, keepdims=True)
        acc[head] = jnp.dot(values, weights.astype(jnp.bfloat16), preferred_element_type=jnp.float32)

    def absorb(keys, values):
        for head in range(heads):
            s = scores(keys, head)
            old = tops[head]
            top = jnp.maximum(old, jnp.max(s, axis=0, keepdims=True))
            weights = jnp.exp2((s - top) * scale)
            shrink = jnp.exp2((old - top) * scale)
            tops[head] = top
            sums[head] = sums[head] * shrink + jnp.sum(weights, axis=0, keepdims=True)
            acc[head] = acc[head] * shrink + jnp.dot(
                values, weights.astype(jnp.bfloat16), preferred_element_type=jnp.float32
            )

    begin = jnp.int32(0)
    for start in starts[1:]:
        begin = jnp.where(anchor >= start, start, begin)
    earlier = (anchor - begin + tok - 1) // tok
    far = mine_ref.shape[0]

    def one(back, carry):
        even = lax.rem(back, 2) == 0
        base = anchor - back * tok

        @pl.when(even)
        def _():
            at = back // 2
            absorb(*block_terms(mine_ref[at, :, key_cols], mine_ref[at, :, value_cols], base))

        @pl.when(jnp.logical_not(even))
        def _():
            at = (back + 1) // 2 - odd
            absorb(*block_terms(theirs_ref[at, :, key_cols], theirs_ref[at, :, value_cols], base))

        return carry

    lax.fori_loop(1, earlier + 1, one, 0)
    order = place_ref[pl.ds(position, 1), :]
    move = (lax.broadcasted_iota(jnp.int32, (tok, tok), 0) == order).astype(jnp.float32).astype(jnp.bfloat16)
    for head in range(heads):
        result = (acc[head] / sums[head]).astype(jnp.bfloat16)
        moved = lax.dot_general(move, result, (((1,), (1,)), ((), ())), preferred_element_type=jnp.float32)
        out_ref[:, head * HD : (head + 1) * HD] = moved.astype(jnp.bfloat16)


def attend(lengths, send_place, query_rows, mine, theirs):
    tok, width = query_rows.shape
    kv_local = mine.shape[2] // (2 * HD)
    share = width // kv_local
    heads = share // HD
    whole = lambda a: pl.BlockSpec(a.shape, lambda i: (0,) * a.ndim)
    return pl.pallas_call(
        attend_kernel,
        grid=(kv_local,),
        in_specs=[
            pl.BlockSpec(memory_space=pltpu.SMEM),
            whole(send_place),
            pl.BlockSpec((tok, share), lambda i: (0, i)),
            whole(mine),
            whole(theirs),
        ],
        out_specs=pl.BlockSpec((tok, share), lambda i: (0, i)),
        out_shape=jax.ShapeDtypeStruct((tok, width), jnp.bfloat16),
        scratch_shapes=[
            pltpu.VMEM((heads, 1, tok), jnp.float32),
            pltpu.VMEM((heads, 1, tok), jnp.float32),
            pltpu.VMEM((heads, HD, tok), jnp.float32),
        ],
        compiler_params=pltpu.CompilerParams(vmem_limit_bytes=VMEM_LIMIT),
        cost_estimate=pl.CostEstimate(
            flops=4 * tok * width * tok * 4, bytes_accessed=8 * tok * width, transcendentals=tok * tok * 4 * width // HD
        ),
        name="attend",
    )(lengths, send_place, query_rows, mine, theirs)


def shifted(value, steps):
    count = lax.axis_size("seq")
    return lax.ppermute(value, "seq", [(source, source + steps) for source in range(count - steps)])


def look_back(value, reach):
    count = lax.axis_size("seq")
    mine = jnp.stack([value] + [shifted(value, 2 * k) for k in range(1, (reach + 1) // 2 + 1)])
    theirs = lax.ppermute(mine, "seq", [(source, source ^ 1) for source in range(count)])
    return mine, theirs


def local(
    x_branch,
    z_branch,
    conv_weight,
    conv_bias,
    xproj_weight,
    dt_weight,
    dt_bias,
    decay_rate,
    skip_gain,
    query_rows,
    key_rows,
    value_rows,
    lengths,
    destination,
):
    tok = x_branch.shape[0]
    n_seq = lax.axis_size("seq")
    n_mp = lax.axis_size("mp")
    low_rank = dt_weight.shape[0]
    reach = n_seq // 2
    run_rows = tok // n_seq

    halo = shifted(x_branch[tok - HALO :], 1)
    kv_mine, kv_theirs = look_back(jnp.concatenate([key_rows, value_rows], axis=1), reach)
    send_place = ((destination // tok) * run_rows + destination % run_rows).reshape(n_seq, tok)

    inner_act, partial = conv_project(lengths, x_branch, halo, conv_weight, conv_bias, xproj_weight)
    pieces = lax.all_to_all(partial, "mp", split_axis=0, concat_axis=0, tiled=True)
    summed = jnp.sum(pieces.reshape(n_mp, tok // n_mp, -1).astype(jnp.float32), axis=0).astype(jnp.bfloat16)
    spread_sum = jnp.broadcast_to(summed[None], (n_mp,) + summed.shape).reshape(partial.shape)
    projected = lax.all_to_all(spread_sum, "mp", split_axis=0, concat_axis=0, tiled=True)

    attended = attend(lengths, send_place, query_rows, kv_mine, kv_theirs)
    regrouped = lax.all_to_all(attended, "seq", split_axis=0, concat_axis=0, tiled=True)

    step, drive, state = local_state(lengths, projected, dt_weight, dt_bias, decay_rate, inner_act)
    st_mine, st_theirs = look_back(state, reach)
    mamba_out = scan_output(
        projected, step, drive, inner_act, z_branch, decay_rate, skip_gain, st_mine, st_theirs, low_rank, reach
    )
    return (mamba_out, regrouped)


def solution(mesh):
    placed = (
        P("seq", "mp"),
        P("seq", "mp"),
        P(None, "mp"),
        P("mp"),
        P("mp", None),
        P(None, "mp"),
        P("mp"),
        P(None, "mp"),
        P("mp"),
        P("seq", "mp"),
        P("seq", "mp"),
        P("seq", "mp"),
        P(),
        P(),
    )
    return jax.shard_map(
        local,
        mesh=mesh,
        in_specs=placed,
        out_specs=(P("seq", "mp"), P("seq", "mp")),
        check_vma=False,
    )
```

```python
import functools

import jax
import jax.numpy as jnp
from jax import lax
from jax.experimental import pallas as pl
from jax.experimental.pallas import tpu as pltpu
from jax.sharding import PartitionSpec as P

HD = 128
LANES = 128
HALO = 16
LOG2E = 1.4426950408889634
RESET = 1e30
APART = 65536.0
VMEM_LIMIT = 56 * 1024 * 1024


def doc_edges(lengths_ref):
    starts, ends, total = [], [], 0
    for i in range(lengths_ref.shape[0]):
        starts.append(total)
        total = total + lengths_ref[i]
        ends.append(total)
    return starts, ends


def doc_start(places, starts):
    found = jnp.zeros_like(places)
    for start in starts[1:]:
        found = jnp.where(places >= start, start, found)
    return found


def channel_chunk(channels):
    return 512 if channels % 512 == 0 else channels


def conv_kernel(lengths_ref, x_ref, halo_ref, w_ref, b_ref, xp_ref, inner_ref, part_ref, ext, acc):
    tok, chunk = x_ref.shape
    starts, _ = doc_edges(lengths_ref)
    anchor = lax.axis_index("seq") * tok
    places = anchor + lax.broadcasted_iota(jnp.int32, (tok, LANES), 0)
    depth = places - doc_start(places, starts)
    ext[0:HALO, :] = halo_ref[...].astype(jnp.float32)
    ext[HALO:, :] = x_ref[...].astype(jnp.float32)
    for lane in range(0, chunk, LANES):
        cols = slice(lane, lane + LANES)
        total = b_ref[:, cols] + w_ref[0:1, cols] * ext[HALO:, cols]
        for lag in range(1, w_ref.shape[0]):
            window = ext[HALO - lag : HALO - lag + tok, cols]
            total += w_ref[lag : lag + 1, cols] * jnp.where(depth >= lag, window, 0.0)
        act = total * (0.5 + 0.5 * jnp.tanh(0.5 * total))
        inner_ref[:, cols] = act.astype(jnp.bfloat16)
    product = lax.dot_general(
        inner_ref[...], xp_ref[...], (((1,), (1,)), ((), ())), preferred_element_type=jnp.float32
    )
    at = pl.program_id(0)

    @pl.when(at == 0)
    def _():
        acc[...] = product

    @pl.when(at > 0)
    def _():
        acc[...] += product

    @pl.when(at == pl.num_programs(0) - 1)
    def _():
        part_ref[...] = acc[...].astype(jnp.bfloat16)


def conv_project(lengths, x_branch, halo, conv_weight, conv_bias, xproj_weight):
    tok, channels = x_branch.shape
    width = xproj_weight.shape[1]
    taps = conv_weight.shape[0]
    chunk = channel_chunk(channels)
    return pl.pallas_call(
        conv_kernel,
        grid=(channels // chunk,),
        in_specs=[
            pl.BlockSpec(memory_space=pltpu.SMEM),
            pl.BlockSpec((tok, chunk), lambda i: (0, i)),
            pl.BlockSpec((HALO, chunk), lambda i: (0, i)),
            pl.BlockSpec((taps, chunk), lambda i: (0, i)),
            pl.BlockSpec((1, chunk), lambda i: (0, i)),
            pl.BlockSpec((width, chunk), lambda i: (0, i)),
        ],
        out_specs=[
            pl.BlockSpec((tok, chunk), lambda i: (0, i)),
            pl.BlockSpec((tok, width), lambda i: (0, 0)),
        ],
        out_shape=[
            jax.ShapeDtypeStruct((tok, channels), jnp.bfloat16),
            jax.ShapeDtypeStruct((tok, width), jnp.bfloat16),
        ],
        scratch_shapes=[
            pltpu.VMEM((tok + HALO, chunk), jnp.float32),
            pltpu.VMEM((tok, width), jnp.float32),
        ],
        compiler_params=pltpu.CompilerParams(vmem_limit_bytes=VMEM_LIMIT),
        cost_estimate=pl.CostEstimate(
            flops=2 * tok * channels * width, bytes_accessed=8 * tok * channels, transcendentals=tok * channels
        ),
        name="conv_project",
    )(lengths, x_branch, halo, conv_weight, conv_bias.reshape(1, channels), xproj_weight.T)


def spread(columns):
    tok, k = columns.shape
    rows = jnp.broadcast_to(columns.astype(jnp.float32)[:, None, :], (tok, k, k))
    own = lax.broadcasted_iota(jnp.int32, (tok, k, k), 1) == lax.broadcasted_iota(jnp.int32, (tok, k, k), 2)
    picked = jnp.where(own, rows, 0.0).reshape(tok * k, k).astype(jnp.bfloat16)
    return jnp.dot(picked, jnp.ones((k, LANES), jnp.bfloat16), preferred_element_type=jnp.float32)


def advance(state, tile, row, rate2, step_ref, drive_ref, b_rows):
    out = []
    for i, held in enumerate(state):
        cols = slice(i * LANES, (i + 1) * LANES)
        decay = jnp.exp2(rate2[i] * step_ref[tile, row : row + 1, cols])
        out.append(decay * held + b_rows * drive_ref[tile, row : row + 1, cols])
    return out


def lane_tiles(value):
    return [value[:, i : i + LANES] for i in range(0, value.shape[1], LANES)]


ROWS = 8
UNROLL = 2 * ROWS


def state_kernel(
    low_rank, lengths_ref, proj_ref, dtw_ref, bias_ref, rate_ref, inner_ref, step_ref, drive_ref, state_ref, b_spread
):
    tok, chunk = inner_ref.shape
    states = rate_ref.shape[0]
    starts, _ = doc_edges(lengths_ref)

    @pl.when(pl.program_id(0) == 0)
    def _():
        b_spread[...] = spread(proj_ref[:, low_rank : low_rank + states])

    anchor = lax.axis_index("seq") * tok
    places = anchor + lax.broadcasted_iota(jnp.int32, (tok, LANES), 0)
    at_start = places == doc_start(places, starts)
    raw = jnp.dot(proj_ref[:, :low_rank], dtw_ref[...], preferred_element_type=jnp.float32)
    totals = []
    for lane in range(0, chunk, LANES):
        cols = slice(lane, lane + LANES)
        biased = raw[:, cols] + bias_ref[:, cols]
        step = jnp.maximum(biased, 0.0) + jnp.log1p(jnp.exp(-jnp.abs(biased)))
        drive = step * inner_ref[:, cols].astype(jnp.float32)
        drive_ref[:, :, cols] = drive.reshape(tok // ROWS, ROWS, LANES)
        step = jnp.where(at_start, RESET, step)
        step_ref[:, :, cols] = step.reshape(tok // ROWS, ROWS, LANES)
        totals.append(jnp.sum(step, axis=0, keepdims=True))
    rate2 = lane_tiles(rate_ref[...] * (-LOG2E))

    def body(turn, state):
        for u in range(UNROLL):
            tile = turn * (UNROLL // ROWS) + u // ROWS
            at = pl.multiple_of(turn * UNROLL * states, states) + u * states
            state = advance(state, tile, u % ROWS, rate2, step_ref, drive_ref, b_spread[pl.ds(at, states), :])
        return state

    end = lax.fori_loop(0, tok // UNROLL, body, [jnp.zeros_like(r) for r in rate2])
    total = jnp.concatenate(totals, axis=1)
    high = total.astype(jnp.bfloat16)
    low = (total - high.astype(jnp.float32)).astype(jnp.bfloat16)
    state_ref[0:states, :] = jnp.concatenate(end, axis=1).astype(jnp.bfloat16)
    row = lax.broadcasted_iota(jnp.int32, (16, chunk), 0)
    both = jnp.where(row == 0, high.astype(jnp.float32), jnp.where(row == 1, low.astype(jnp.float32), 0.0))
    state_ref[states : states + 16, :] = both.astype(jnp.bfloat16)


def local_state(lengths, projected, dt_weight, dt_bias, decay_rate, inner_act):
    tok, channels = inner_act.shape
    low_rank = dt_weight.shape[0]
    states = decay_rate.shape[0]
    width = projected.shape[1]
    chunk = channel_chunk(channels)
    by_chunk = lambda rows: pl.BlockSpec((rows, chunk), lambda i: (0, i))
    by_tile = pl.BlockSpec((tok // ROWS, ROWS, chunk), lambda i: (0, 0, i))
    return pl.pallas_call(
        functools.partial(state_kernel, low_rank),
        grid=(channels // chunk,),
        in_specs=[
            pl.BlockSpec(memory_space=pltpu.SMEM),
            pl.BlockSpec((tok, width), lambda i: (0, 0)),
            by_chunk(low_rank),
            by_chunk(1),
            by_chunk(states),
            by_chunk(tok),
        ],
        out_specs=[by_tile, by_tile, by_chunk(states + 16)],
        out_shape=[
            jax.ShapeDtypeStruct((tok // ROWS, ROWS, channels), jnp.float32),
            jax.ShapeDtypeStruct((tok // ROWS, ROWS, channels), jnp.float32),
            jax.ShapeDtypeStruct((states + 16, channels), jnp.bfloat16),
        ],
        scratch_shapes=[pltpu.VMEM((tok * states, LANES), jnp.float32)],
        compiler_params=pltpu.CompilerParams(vmem_limit_bytes=VMEM_LIMIT),
        cost_estimate=pl.CostEstimate(
            flops=8 * tok * channels * states,
            bytes_accessed=12 * tok * channels,
            transcendentals=tok * channels * states,
        ),
        name="local_state",
    )(lengths, projected, dt_weight, dt_bias.reshape(1, channels), decay_rate, inner_act)


def output_kernel(
    low_rank,
    proj_ref,
    step_ref,
    drive_ref,
    inner_ref,
    z_ref,
    rate_ref,
    skip_ref,
    gathered_ref,
    out_ref,
    bc_spread,
    parts,
    scanned,
):
    tok, chunk = inner_ref.shape
    states = rate_ref.shape[0]
    fold = 8

    @pl.when(pl.program_id(0) == 0)
    def _():
        bc_spread[...] = spread(proj_ref[:, low_rank : low_rank + 2 * states])

    rate2 = lane_tiles(rate_ref[...] * (-LOG2E))
    position = lax.axis_index("seq")

    def follow(block_at, state):
        block = gathered_ref[block_at].astype(jnp.float32)
        total = block[states : states + 1] + block[states + 1 : states + 2]
        return [
            jnp.exp2(r * t) * s + e
            for r, t, s, e in zip(rate2, lane_tiles(total), state, lane_tiles(block[:states]))
        ]

    reach = gathered_ref.shape[0] // 2
    state = lax.fori_loop(
        jnp.maximum(position - reach, 0), position, follow, [jnp.zeros_like(r) for r in rate2]
    )

    def body(turn, state):
        base = pl.multiple_of(turn * UNROLL, UNROLL)
        for u in range(UNROLL):
            tile = turn * (UNROLL // ROWS) + u // ROWS
            at = pl.multiple_of(turn * UNROLL * 2 * states, 2 * states) + u * 2 * states
            state = advance(state, tile, u % ROWS, rate2, step_ref, drive_ref, bc_spread[pl.ds(at, states), :])
            c_rows = bc_spread[pl.ds(at + states, states), :]
            for i, held in enumerate(state):
                term = c_rows * held
                part = term[0:fold]
                for more in range(fold, states, fold):
                    part = part + term[more : more + fold]
                parts[i, u * fold : (u + 1) * fold, :] = part
        for group in range(0, UNROLL, 8):
            for i in range(len(state)):
                cols = slice(i * LANES, (i + 1) * LANES)
                row = parts[i, pl.ds(group * fold, 8, stride=fold), :]
                for n in range(1, fold):
                    row = row + parts[i, pl.ds(group * fold + n, 8, stride=fold), :]
                scanned[pl.ds(base + group, 8), cols] = row
        return state

    lax.fori_loop(0, tok // UNROLL, body, state)
    for lane in range(0, chunk, LANES):
        cols = slice(lane, lane + LANES)
        z = z_ref[:, cols].astype(jnp.float32)
        gate = z * (0.5 + 0.5 * jnp.tanh(0.5 * z))
        y = scanned[:, cols] + skip_ref[:, cols] * inner_ref[:, cols].astype(jnp.float32)
        out_ref[:, cols] = (y * gate).astype(jnp.bfloat16)


def scan_output(projected, step, drive, inner_act, z_branch, decay_rate, skip_gain, gathered, low_rank):
    tok, channels = inner_act.shape
    states = decay_rate.shape[0]
    width = projected.shape[1]
    chunk = channel_chunk(channels)
    by_chunk = lambda rows: pl.BlockSpec((rows, chunk), lambda i: (0, i))
    by_tile = pl.BlockSpec((tok // ROWS, ROWS, chunk), lambda i: (0, 0, i))
    return pl.pallas_call(
        functools.partial(output_kernel, low_rank),
        grid=(channels // chunk,),
        in_specs=[
            pl.BlockSpec((tok, width), lambda i: (0, 0)),
            by_tile,
            by_tile,
            by_chunk(tok),
            by_chunk(tok),
            by_chunk(states),
            by_chunk(1),
            pl.BlockSpec(gathered.shape[:2] + (chunk,), lambda i: (0, 0, i)),
        ],
        out_specs=by_chunk(tok),
        out_shape=jax.ShapeDtypeStruct((tok, channels), jnp.bfloat16),
        scratch_shapes=[
            pltpu.VMEM((tok * 2 * states, LANES), jnp.float32),
            pltpu.VMEM((chunk // LANES, UNROLL * 8, LANES), jnp.float32),
            pltpu.VMEM((tok, chunk), jnp.float32),
        ],
        compiler_params=pltpu.CompilerParams(vmem_limit_bytes=VMEM_LIMIT),
        cost_estimate=pl.CostEstimate(
            flops=12 * tok * channels * states,
            bytes_accessed=14 * tok * channels,
            transcendentals=tok * channels * states,
        ),
        name="scan_output",
    )(projected, step, drive, inner_act, z_branch, decay_rate, skip_gain.reshape(1, channels), gathered)


def attend_kernel(lengths_ref, place_ref, q_ref, kv_ref, out_ref, queries, scores, tops, acc):
    tok = q_ref.shape[0]
    heads = q_ref.shape[1] // HD
    kv_local = kv_ref.shape[2] // (2 * HD)
    group = pl.program_id(0)
    position = lax.axis_index("seq")
    anchor = position * tok
    scale = LOG2E * HD**-0.5
    starts, ends = doc_edges(lengths_ref)
    lane = lax.broadcasted_iota(jnp.int32, (1, LANES), 1)
    first = jnp.full((1, LANES), 2**30, jnp.int32)
    last = jnp.zeros((1, LANES), jnp.int32)
    for i, (start, end) in enumerate(zip(starts, ends)):
        first = jnp.where(lane == i, start, first)
        last = jnp.where(lane == i, end, last)
    rows = lax.broadcasted_iota(jnp.int32, (tok, LANES), 0)

    def in_doc(base):
        return (rows + base >= first) & (rows + base < last)

    apart = jnp.where(in_doc(anchor) | (lane >= len(starts)), 0.0, -APART).astype(jnp.bfloat16)
    for head in range(heads):
        queries[head * tok : (head + 1) * tok, :HD] = q_ref[:, head * HD : (head + 1) * HD]
        queries[head * tok : (head + 1) * tok, HD:] = apart
    key_cols = pl.ds(pl.multiple_of(group * HD, HD), HD)
    value_cols = pl.ds(pl.multiple_of((group + kv_local) * HD, HD), HD)

    def score(back):
        marks = jnp.where(in_doc(anchor - back * tok), 1.0, 0.0).astype(jnp.bfloat16)
        keys = jnp.concatenate([kv_ref[position - back, :, key_cols], marks], axis=1)
        return lax.dot_general(queries[...], keys, (((1,), (1,)), ((), ())), preferred_element_type=jnp.float32)

    def widest(s):
        top = s[:, :LANES]
        for at in range(LANES, tok, LANES):
            top = jnp.maximum(top, s[:, at : at + LANES])
        return top

    own = score(0)
    causal = lax.broadcasted_iota(jnp.int32, (tok, tok), 1) <= lax.broadcasted_iota(jnp.int32, (tok, tok), 0)
    for head in range(heads):
        part = slice(head * tok, (head + 1) * tok)
        s = jnp.where(causal, own[part], -APART)
        scores[0, part, :] = s
        tops[part, :] = widest(s)

    begin = jnp.int32(0)
    for start in starts[1:]:
        begin = jnp.where(anchor >= start, start, begin)
    earlier = (anchor - begin + tok - 1) // tok

    def look(back, carry):
        s = score(back)
        scores[back] = s
        tops[...] = jnp.maximum(tops[...], widest(s))
        return carry

    lax.fori_loop(1, earlier + 1, look, 0)
    tops[...] = jnp.broadcast_to(jnp.max(tops[...], axis=1, keepdims=True) * scale, tops.shape)
    acc[...] = jnp.zeros_like(acc)

    def absorb(back, carry):
        values = jnp.concatenate(
            [kv_ref[position - back, :, value_cols], jnp.ones((tok, HD), jnp.bfloat16)], axis=1
        )
        top = tops[...]
        weights = [
            jnp.exp2(scores[back, :, at : at + LANES] * scale - top).astype(jnp.bfloat16)
            for at in range(0, tok, LANES)
        ]
        acc[...] += jnp.dot(jnp.concatenate(weights, axis=1), values, preferred_element_type=jnp.float32)
        return carry

    lax.fori_loop(0, earlier + 1, absorb, 0)
    order = place_ref[pl.ds(position, 1), :]
    move = (lax.broadcasted_iota(jnp.int32, (tok, tok), 0) == order).astype(jnp.float32).astype(jnp.bfloat16)
    for head in range(heads):
        part = slice(head * tok, (head + 1) * tok)
        result = (acc[part, :HD] / acc[part, HD:]).astype(jnp.bfloat16)
        moved = jnp.dot(move, result, preferred_element_type=jnp.float32)
        out_ref[:, head * HD : (head + 1) * HD] = moved.astype(jnp.bfloat16)


def attend(lengths, send_place, query_rows, kv):
    tok, width = query_rows.shape
    kv_local = kv.shape[2] // (2 * HD)
    share = width // kv_local
    heads = share // HD
    reach = kv.shape[0] // 2
    whole = lambda a: pl.BlockSpec(a.shape, lambda i: (0,) * a.ndim)
    return pl.pallas_call(
        attend_kernel,
        grid=(kv_local,),
        in_specs=[
            pl.BlockSpec(memory_space=pltpu.SMEM),
            whole(send_place),
            pl.BlockSpec((tok, share), lambda i: (0, i)),
            whole(kv),
        ],
        out_specs=pl.BlockSpec((tok, share), lambda i: (0, i)),
        out_shape=jax.ShapeDtypeStruct((tok, width), jnp.bfloat16),
        scratch_shapes=[
            pltpu.VMEM((heads * tok, 2 * HD), jnp.bfloat16),
            pltpu.VMEM((reach + 1, heads * tok, tok), jnp.float32),
            pltpu.VMEM((heads * tok, LANES), jnp.float32),
            pltpu.VMEM((heads * tok, 2 * HD), jnp.float32),
        ],
        compiler_params=pltpu.CompilerParams(vmem_limit_bytes=VMEM_LIMIT),
        cost_estimate=pl.CostEstimate(
            flops=4 * tok * width * tok * 4, bytes_accessed=8 * tok * width, transcendentals=tok * tok * 4 * width // HD
        ),
        name="attend",
    )(lengths, send_place, query_rows, kv)


def shifted(value, steps):
    count = lax.axis_size("seq")
    return lax.ppermute(value, "seq", [(source, source + steps) for source in range(count - steps)])


def local(
    x_branch,
    z_branch,
    conv_weight,
    conv_bias,
    xproj_weight,
    dt_weight,
    dt_bias,
    decay_rate,
    skip_gain,
    query_rows,
    key_rows,
    value_rows,
    lengths,
    destination,
):
    tok = x_branch.shape[0]
    n_seq = lax.axis_size("seq")
    n_mp = lax.axis_size("mp")
    low_rank = dt_weight.shape[0]
    run_rows = tok // n_seq

    halo = shifted(x_branch[tok - HALO :], 1)
    kv = lax.all_gather(jnp.concatenate([key_rows, value_rows], axis=1), "seq")
    send_place = ((destination // tok) * run_rows + destination % run_rows).reshape(n_seq, tok)

    inner_act, partial = conv_project(lengths, x_branch, halo, conv_weight, conv_bias, xproj_weight)
    pieces = lax.all_to_all(partial, "mp", split_axis=0, concat_axis=0, tiled=True)
    summed = jnp.sum(pieces.reshape(n_mp, tok // n_mp, -1).astype(jnp.float32), axis=0).astype(jnp.bfloat16)
    spread_sum = jnp.broadcast_to(summed[None], (n_mp,) + summed.shape).reshape(partial.shape)
    projected = lax.all_to_all(spread_sum, "mp", split_axis=0, concat_axis=0, tiled=True)

    attended = attend(lengths, send_place, query_rows, kv)

    projected, attended = lax.optimization_barrier((projected, attended))
    regrouped = lax.all_to_all(attended, "seq", split_axis=0, concat_axis=0, tiled=True)
    step, drive, state = local_state(lengths, projected, dt_weight, dt_bias, decay_rate, inner_act)
    states = lax.all_gather(state, "seq")
    mamba_out = scan_output(projected, step, drive, inner_act, z_branch, decay_rate, skip_gain, states, low_rank)
    return (mamba_out, regrouped)


def solution(mesh):
    placed = (
        P("seq", "mp"),
        P("seq", "mp"),
        P(None, "mp"),
        P("mp"),
        P("mp", None),
        P(None, "mp"),
        P("mp"),
        P(None, "mp"),
        P("mp"),
        P("seq", "mp"),
        P("seq", "mp"),
        P("seq", "mp"),
        P(),
        P(),
    )
    return jax.shard_map(
        local,
        mesh=mesh,
        in_specs=placed,
        out_specs=(P("seq", "mp"), P("seq", "mp")),
        check_vma=False,
    )
```

```python
import functools

import jax
import jax.numpy as jnp
from jax import lax
from jax.experimental import pallas as pl
from jax.experimental.pallas import tpu as pltpu
from jax.sharding import PartitionSpec as P

HD = 128
LANES = 128
HALO = 16
LOG2E = 1.4426950408889634
RESET = 1e30
APART = 65536.0
VMEM_LIMIT = 32 * 1024 * 1024


def doc_edges(lengths_ref):
    starts, ends, total = [], [], 0
    for i in range(lengths_ref.shape[0]):
        starts.append(total)
        total = total + lengths_ref[i]
        ends.append(total)
    return starts, ends


def doc_start(places, starts):
    found = jnp.zeros_like(places)
    for start in starts[1:]:
        found = jnp.where(places >= start, start, found)
    return found


def channel_chunk(channels):
    return 512 if channels % 512 == 0 else channels


def pack_kernel(x_ref, k_ref, v_ref, halo_ref, kv_ref):
    width = k_ref.shape[1]
    halo_ref[...] = x_ref[...]
    kv_ref[:, :width] = k_ref[...]
    kv_ref[:, width:] = v_ref[...]


def pack(x_branch, key_rows, value_rows):
    tok, channels = x_branch.shape
    width = key_rows.shape[1]
    whole = lambda rows, columns: pl.BlockSpec((rows, columns), lambda i: (0, 0))
    return pl.pallas_call(
        pack_kernel,
        grid=(1,),
        in_specs=[
            pl.BlockSpec((HALO, channels), lambda i: (tok // HALO - 1, 0)),
            whole(tok, width),
            whole(tok, width),
        ],
        out_specs=[whole(HALO, channels), whole(tok, 2 * width)],
        out_shape=[
            jax.ShapeDtypeStruct((HALO, channels), x_branch.dtype),
            jax.ShapeDtypeStruct((tok, 2 * width), key_rows.dtype),
        ],
        compiler_params=pltpu.CompilerParams(vmem_limit_bytes=VMEM_LIMIT),
        cost_estimate=pl.CostEstimate(flops=0, bytes_accessed=16 * tok * width, transcendentals=0),
        name="pack",
    )(x_branch, key_rows, value_rows)


def conv_kernel(lengths_ref, x_ref, halo_ref, w_ref, b_ref, xp_ref, inner_ref, part_ref, ext, acc):
    tok, chunk = x_ref.shape
    starts, _ = doc_edges(lengths_ref)
    anchor = lax.axis_index("seq") * tok
    places = anchor + lax.broadcasted_iota(jnp.int32, (tok, LANES), 0)
    depth = places - doc_start(places, starts)
    ext[0:HALO, :] = halo_ref[...].astype(jnp.float32)
    ext[HALO:, :] = x_ref[...].astype(jnp.float32)
    for lane in range(0, chunk, LANES):
        cols = slice(lane, lane + LANES)
        total = b_ref[:, cols] + w_ref[0:1, cols] * ext[HALO:, cols]
        for lag in range(1, w_ref.shape[0]):
            window = ext[HALO - lag : HALO - lag + tok, cols]
            total += w_ref[lag : lag + 1, cols] * jnp.where(depth >= lag, window, 0.0)
        act = total * (0.5 + 0.5 * jnp.tanh(0.5 * total))
        inner_ref[:, cols] = act.astype(jnp.bfloat16)
    product = lax.dot_general(
        xp_ref[...], inner_ref[...], (((1,), (1,)), ((), ())), preferred_element_type=jnp.float32
    )
    at = pl.program_id(0)

    @pl.when(at == 0)
    def _():
        acc[...] = product

    @pl.when(at > 0)
    def _():
        acc[...] += product

    @pl.when(at == pl.num_programs(0) - 1)
    def _():
        part_ref[...] = acc[...].astype(jnp.bfloat16)


def conv_project(lengths, x_branch, halo, conv_weight, conv_bias, xproj_weight):
    tok, channels = x_branch.shape
    width = xproj_weight.shape[1]
    taps = conv_weight.shape[0]
    chunk = channel_chunk(channels)
    return pl.pallas_call(
        conv_kernel,
        grid=(channels // chunk,),
        in_specs=[
            pl.BlockSpec(memory_space=pltpu.SMEM),
            pl.BlockSpec((tok, chunk), lambda i: (0, i)),
            pl.BlockSpec((HALO, chunk), lambda i: (0, i)),
            pl.BlockSpec((taps, chunk), lambda i: (0, i)),
            pl.BlockSpec((1, chunk), lambda i: (0, i)),
            pl.BlockSpec((width, chunk), lambda i: (0, i)),
        ],
        out_specs=[
            pl.BlockSpec((tok, chunk), lambda i: (0, i)),
            pl.BlockSpec((width, tok), lambda i: (0, 0)),
        ],
        out_shape=[
            jax.ShapeDtypeStruct((tok, channels), jnp.bfloat16),
            jax.ShapeDtypeStruct((width, tok), jnp.bfloat16),
        ],
        scratch_shapes=[
            pltpu.VMEM((tok + HALO, chunk), jnp.float32),
            pltpu.VMEM((width, tok), jnp.float32),
        ],
        compiler_params=pltpu.CompilerParams(vmem_limit_bytes=VMEM_LIMIT),
        cost_estimate=pl.CostEstimate(
            flops=2 * tok * channels * width, bytes_accessed=8 * tok * channels, transcendentals=tok * channels
        ),
        name="conv_project",
    )(lengths, x_branch, halo, conv_weight, conv_bias.reshape(1, channels), xproj_weight.T)


def spread(columns):
    tok, k = columns.shape
    rows = jnp.broadcast_to(columns.astype(jnp.float32)[:, None, :], (tok, k, k))
    own = lax.broadcasted_iota(jnp.int32, (tok, k, k), 1) == lax.broadcasted_iota(jnp.int32, (tok, k, k), 2)
    picked = jnp.where(own, rows, 0.0).reshape(tok * k, k).astype(jnp.bfloat16)
    return jnp.dot(picked, jnp.ones((k, LANES), jnp.bfloat16), preferred_element_type=jnp.float32)


def advance(state, tile, row, rate2, step_ref, drive_ref, b_rows):
    out = []
    for i, held in enumerate(state):
        cols = slice(i * LANES, (i + 1) * LANES)
        decay = jnp.exp2(rate2[i] * step_ref[tile, row : row + 1, cols])
        out.append(decay * held + b_rows * drive_ref[tile, row : row + 1, cols])
    return out


def lane_tiles(value):
    return [value[:, i : i + LANES] for i in range(0, value.shape[1], LANES)]


ROWS = 8
UNROLL = 2 * ROWS


def fold_rows(parts, lane, group):
    row = parts[lane, pl.ds(group * ROWS, ROWS, stride=ROWS), :]
    for n in range(1, ROWS):
        row = row + parts[lane, pl.ds(group * ROWS + n, ROWS, stride=ROWS), :]
    return row


def halves(term):
    total = term[0:ROWS]
    for more in range(ROWS, term.shape[0], ROWS):
        total = total + term[more : more + ROWS]
    return total


def local_kernel(
    lengths_ref,
    proj_ref,
    dtw_ref,
    bias_ref,
    rate_ref,
    skip_ref,
    inner_ref,
    y_ref,
    sum_ref,
    state_ref,
    low_cols,
    bc_spread,
    step_ref,
    drive_ref,
    parts,
    totals,
):
    tok, chunk = inner_ref.shape
    states = rate_ref.shape[0]
    low_rank = dtw_ref.shape[0]
    tiles = chunk // LANES
    starts, _ = doc_edges(lengths_ref)
    at = pl.program_id(0)

    @pl.when(at == 0)
    def _():
        low_cols[...] = proj_ref[:low_rank, :].astype(jnp.float32).T.astype(jnp.bfloat16)
        bc_spread[...] = spread(proj_ref[low_rank:, :].astype(jnp.float32).T)

    anchor = lax.axis_index("seq") * tok
    places = anchor + lax.broadcasted_iota(jnp.int32, (tok, LANES), 0)
    at_start = places == doc_start(places, starts)
    upto = lax.broadcasted_iota(jnp.int32, (tok, tok), 0) >= lax.broadcasted_iota(jnp.int32, (tok, tok), 1)
    upto = upto.astype(jnp.float32).astype(jnp.bfloat16)
    raw = jnp.dot(low_cols[...], dtw_ref[...], preferred_element_type=jnp.float32)
    for i in range(tiles):
        cols = slice(i * LANES, (i + 1) * LANES)
        biased = raw[:, cols] + bias_ref[:, cols]
        step = jnp.maximum(biased, 0.0) + jnp.log1p(jnp.exp(-jnp.abs(biased)))
        drive = step * inner_ref[:, cols].astype(jnp.float32)
        drive_ref[:, :, cols] = drive.reshape(tok // ROWS, ROWS, LANES)
        step = jnp.where(at_start, RESET, step)
        step_ref[:, :, cols] = step.reshape(tok // ROWS, ROWS, LANES)
        high = step.astype(jnp.bfloat16)
        low = (step - high.astype(jnp.float32)).astype(jnp.bfloat16)
        summed = jnp.dot(upto, high, preferred_element_type=jnp.float32) + jnp.dot(
            upto, low, preferred_element_type=jnp.float32
        )
        sum_ref[:, :, cols] = summed.reshape(tok // ROWS, ROWS, LANES)
        totals[at * tiles + i] = summed[tok - 1 : tok]
    rate2 = lane_tiles(rate_ref[...] * (-LOG2E))

    def body(turn, state):
        base = pl.multiple_of(turn * UNROLL, UNROLL)
        for u in range(UNROLL):
            tile = turn * (UNROLL // ROWS) + u // ROWS
            row = pl.multiple_of(turn * UNROLL * 2 * states, 2 * states) + u * 2 * states
            state = advance(state, tile, u % ROWS, rate2, step_ref, drive_ref, bc_spread[pl.ds(row, states), :])
            c_rows = bc_spread[pl.ds(row + states, states), :]
            for i, held in enumerate(state):
                parts[i, u * ROWS : (u + 1) * ROWS, :] = halves(c_rows * held)
        for group in range(0, UNROLL, ROWS):
            for i in range(tiles):
                y_ref[pl.ds(base + group, ROWS), i * LANES : (i + 1) * LANES] = fold_rows(parts, i, group)
        return state

    end = lax.fori_loop(0, tok // UNROLL, body, [jnp.zeros_like(r) for r in rate2])
    for i in range(tiles):
        cols = slice(i * LANES, (i + 1) * LANES)
        y_ref[:, cols] += skip_ref[:, cols] * inner_ref[:, cols].astype(jnp.float32)
        state_ref[at * tiles + i] = end[i].astype(jnp.bfloat16)

    @pl.when(at == pl.num_programs(0) - 1)
    def _():
        lanes = totals.shape[0]
        row = lax.broadcasted_iota(jnp.int32, (states, LANES), 0)
        table = jnp.zeros((states, LANES), jnp.float32)
        for i in range(lanes):
            table = jnp.where(row == i, totals[i], table)
        high = table.astype(jnp.bfloat16)
        state_ref[lanes] = high
        state_ref[lanes + 1] = (table - high.astype(jnp.float32)).astype(jnp.bfloat16)


def local_scan(lengths, projected, dt_weight, dt_bias, decay_rate, skip_gain, inner_act):
    tok, channels = inner_act.shape
    low_rank = dt_weight.shape[0]
    states = decay_rate.shape[0]
    width = projected.shape[0]
    chunk = channel_chunk(channels)
    lanes = channels // LANES
    by_chunk = lambda rows: pl.BlockSpec((rows, chunk), lambda i: (0, i))
    return pl.pallas_call(
        local_kernel,
        grid=(channels // chunk,),
        in_specs=[
            pl.BlockSpec(memory_space=pltpu.SMEM),
            pl.BlockSpec((width, tok), lambda i: (0, 0)),
            by_chunk(low_rank),
            by_chunk(1),
            by_chunk(states),
            by_chunk(1),
            by_chunk(tok),
        ],
        out_specs=[
            by_chunk(tok),
            pl.BlockSpec((tok // ROWS, ROWS, chunk), lambda i: (0, 0, i)),
            pl.BlockSpec((lanes + 2, states, LANES), lambda i: (0, 0, 0)),
        ],
        out_shape=[
            jax.ShapeDtypeStruct((tok, channels), jnp.float32),
            jax.ShapeDtypeStruct((tok // ROWS, ROWS, channels), jnp.float32),
            jax.ShapeDtypeStruct((lanes + 2, states, LANES), jnp.bfloat16),
        ],
        scratch_shapes=[
            pltpu.VMEM((tok, low_rank), jnp.bfloat16),
            pltpu.VMEM((tok * 2 * states, LANES), jnp.float32),
            pltpu.VMEM((tok // ROWS, ROWS, chunk), jnp.float32),
            pltpu.VMEM((tok // ROWS, ROWS, chunk), jnp.float32),
            pltpu.VMEM((chunk // LANES, UNROLL * ROWS, LANES), jnp.float32),
            pltpu.VMEM((lanes, 1, LANES), jnp.float32),
        ],
        compiler_params=pltpu.CompilerParams(vmem_limit_bytes=VMEM_LIMIT),
        cost_estimate=pl.CostEstimate(
            flops=12 * tok * channels * states,
            bytes_accessed=12 * tok * channels,
            transcendentals=tok * channels * states,
        ),
        name="local_scan",
    )(
        lengths,
        projected,
        dt_weight,
        dt_bias.reshape(1, channels),
        decay_rate,
        skip_gain.reshape(1, channels),
        inner_act,
    )


def join_kernel(low_rank, reach, proj_ref, y_ref, sum_ref, z_ref, rate_ref, *refs):
    blocks, out_ref, c_spread, parts = refs[:reach], refs[reach], refs[reach + 1], refs[reach + 2]
    tok, chunk = y_ref.shape
    states = rate_ref.shape[0]
    tiles = chunk // LANES
    lanes = blocks[0].shape[0] - 2
    at = pl.program_id(0)

    @pl.when(at == 0)
    def _():
        c_spread[...] = spread(proj_ref[low_rank + states :, :].astype(jnp.float32).T).astype(jnp.bfloat16)

    rate2 = lane_tiles(rate_ref[...] * (-LOG2E))
    row = lax.broadcasted_iota(jnp.int32, (states, LANES), 0)
    entering = [jnp.zeros_like(r) for r in rate2]
    for block in reversed(blocks):
        table = block[lanes].astype(jnp.float32) + block[lanes + 1].astype(jnp.float32)
        for i, held in enumerate(entering):
            total = jnp.sum(jnp.where(row == at * tiles + i, table, 0.0), axis=0, keepdims=True)
            entering[i] = jnp.exp2(rate2[i] * total) * held + block[at * tiles + i].astype(jnp.float32)
    entering = [e.astype(jnp.bfloat16) for e in entering]

    def body(turn, carry):
        base = pl.multiple_of(turn * UNROLL, UNROLL)
        for u in range(UNROLL):
            tile = turn * (UNROLL // ROWS) + u // ROWS
            c_rows = c_spread[pl.ds(pl.multiple_of(turn * UNROLL * states, states) + u * states, states), :]
            for i in range(tiles):
                cols = slice(i * LANES, (i + 1) * LANES)
                power = rate2[i] * sum_ref[tile, u % ROWS : u % ROWS + 1, cols]
                term = jnp.exp2(power.astype(jnp.bfloat16)) * entering[i] * c_rows
                parts[i, u * ROWS : (u + 1) * ROWS, :] = halves(term.astype(jnp.float32))
        for i in range(tiles):
            cols = slice(i * LANES, (i + 1) * LANES)
            rows = pl.ds(base, UNROLL)
            more = jnp.concatenate([fold_rows(parts, i, group) for group in range(0, UNROLL, ROWS)], axis=0)
            z = z_ref[rows, cols].astype(jnp.float32)
            gate = z * (0.5 + 0.5 * jnp.tanh(0.5 * z))
            out_ref[rows, cols] = ((y_ref[rows, cols] + more) * gate).astype(jnp.bfloat16)
        return carry

    lax.fori_loop(0, tok // UNROLL, body, 0)


def join_states(projected, y, sums, z_branch, decay_rate, blocks, low_rank):
    tok, channels = z_branch.shape
    states = decay_rate.shape[0]
    width = projected.shape[0]
    chunk = channel_chunk(channels)
    by_chunk = lambda rows: pl.BlockSpec((rows, chunk), lambda i: (0, i))
    return pl.pallas_call(
        functools.partial(join_kernel, low_rank, len(blocks)),
        grid=(channels // chunk,),
        in_specs=[
            pl.BlockSpec((width, tok), lambda i: (0, 0)),
            by_chunk(tok),
            pl.BlockSpec((tok // ROWS, ROWS, chunk), lambda i: (0, 0, i)),
            by_chunk(tok),
            by_chunk(states),
        ]
        + [pl.BlockSpec(block.shape, lambda i: (0, 0, 0)) for block in blocks],
        out_specs=by_chunk(tok),
        out_shape=jax.ShapeDtypeStruct((tok, channels), jnp.bfloat16),
        scratch_shapes=[
            pltpu.VMEM((tok * states, LANES), jnp.bfloat16),
            pltpu.VMEM((chunk // LANES, UNROLL * ROWS, LANES), jnp.float32),
        ],
        compiler_params=pltpu.CompilerParams(vmem_limit_bytes=VMEM_LIMIT),
        cost_estimate=pl.CostEstimate(
            flops=8 * tok * channels * states,
            bytes_accessed=14 * tok * channels,
            transcendentals=tok * channels * states,
        ),
        name="join_states",
    )(projected, y, sums, z_branch, decay_rate, *blocks)


def attend_kernel(kv_local, first_group, lengths_ref, place_ref, q_ref, mine_ref, theirs_ref, *refs):
    out_ref, queries, scores, tops, acc = refs[-5:]
    tok = q_ref.shape[0]
    heads = q_ref.shape[1] // HD
    group = pl.program_id(0) + first_group
    position = lax.axis_index("seq")
    odd = lax.rem(position, 2)
    anchor = position * tok
    scale = LOG2E * HD**-0.5
    starts, ends = doc_edges(lengths_ref)
    lane = lax.broadcasted_iota(jnp.int32, (1, LANES), 1)
    first = jnp.full((1, LANES), 2**30, jnp.int32)
    last = jnp.zeros((1, LANES), jnp.int32)
    for i, (start, end) in enumerate(zip(starts, ends)):
        first = jnp.where(lane == i, start, first)
        last = jnp.where(lane == i, end, last)
    rows = lax.broadcasted_iota(jnp.int32, (tok, LANES), 0)

    def in_doc(base):
        return (rows + base >= first) & (rows + base < last)

    apart = jnp.where(in_doc(anchor) | (lane >= len(starts)), 0.0, -APART).astype(jnp.bfloat16)
    for head in range(heads):
        queries[head * tok : (head + 1) * tok, :HD] = q_ref[:, head * HD : (head + 1) * HD]
        queries[head * tok : (head + 1) * tok, HD:] = apart
    key_cols = pl.ds(pl.multiple_of(group * HD, HD), HD)
    value_cols = pl.ds(pl.multiple_of((group + kv_local) * HD, HD), HD)

    def rows_of(back, cols):
        if isinstance(back, int) and back == 0:
            return mine_ref[0, :, cols]
        ours = mine_ref[back // 2, :, cols]
        other = theirs_ref[(back + 1) // 2 - odd, :, cols]
        return jnp.where(lax.rem(back, 2) == 0, ours, other)

    def score(back):
        marks = jnp.where(in_doc(anchor - back * tok), 1.0, 0.0).astype(jnp.bfloat16)
        keys = jnp.concatenate([rows_of(back, key_cols), marks], axis=1)
        return lax.dot_general(queries[...], keys, (((1,), (1,)), ((), ())), preferred_element_type=jnp.float32)

    def widest(s):
        top = s[:, :LANES]
        for at in range(LANES, tok, LANES):
            top = jnp.maximum(top, s[:, at : at + LANES])
        return top

    own = score(0)
    causal = lax.broadcasted_iota(jnp.int32, (tok, tok), 1) <= lax.broadcasted_iota(jnp.int32, (tok, tok), 0)
    for head in range(heads):
        part = slice(head * tok, (head + 1) * tok)
        s = jnp.where(causal, own[part], -APART)
        scores[0, part, :] = s
        tops[part, :] = widest(s)

    begin = jnp.int32(0)
    for start in starts[1:]:
        begin = jnp.where(anchor >= start, start, begin)
    earlier = (anchor - begin + tok - 1) // tok

    def look(back, carry):
        s = score(back)
        scores[back] = s
        tops[...] = jnp.maximum(tops[...], widest(s))
        return carry

    lax.fori_loop(1, earlier + 1, look, 0)
    tops[...] = jnp.broadcast_to(jnp.max(tops[...], axis=1, keepdims=True) * scale, tops.shape)

    def weighted(back):
        values = jnp.concatenate([rows_of(back, value_cols), jnp.ones((tok, HD), jnp.bfloat16)], axis=1)
        top = tops[...]
        weights = [
            jnp.exp2((scores[back, :, at : at + LANES] * scale - top).astype(jnp.bfloat16))
            for at in range(0, tok, LANES)
        ]
        return jnp.dot(jnp.concatenate(weights, axis=1), values, preferred_element_type=jnp.float32)

    acc[...] = weighted(0)

    def absorb(back, carry):
        acc[...] += weighted(back)
        return carry

    lax.fori_loop(1, earlier + 1, absorb, 0)
    order = place_ref[pl.ds(position, 1), :]
    move = (lax.broadcasted_iota(jnp.int32, (tok, tok), 0) == order).astype(jnp.float32).astype(jnp.bfloat16)
    for head in range(heads):
        part = slice(head * tok, (head + 1) * tok)
        result = (acc[part, :HD] / acc[part, HD:]).astype(jnp.bfloat16)
        moved = jnp.dot(move, result, preferred_element_type=jnp.float32)
        out_ref[:, head * HD : (head + 1) * HD] = moved.astype(jnp.bfloat16)


def attend(lengths, send_place, query_rows, mine, theirs, groups, so_far):
    tok, width = query_rows.shape
    kv_local = mine.shape[2] // (2 * HD)
    share = width // kv_local
    heads = share // HD
    reach = 2 * (mine.shape[0] - 1)
    count = groups[1] - groups[0]
    whole = lambda a: pl.BlockSpec(a.shape, lambda i: (0,) * a.ndim)
    in_specs = [
        pl.BlockSpec(memory_space=pltpu.SMEM),
        whole(send_place),
        pl.BlockSpec((tok, share), lambda i: (0, i + groups[0])),
        whole(mine),
        whole(theirs),
    ]
    operands = [lengths, send_place, query_rows, mine, theirs]
    aliases = {}
    if so_far is not None:
        aliases = {len(operands): 0}
        in_specs.append(pl.BlockSpec(memory_space=pl.ANY))
        operands.append(so_far)
    return pl.pallas_call(
        functools.partial(attend_kernel, kv_local, groups[0]),
        grid=(count,),
        in_specs=in_specs,
        out_specs=pl.BlockSpec((tok, share), lambda i: (0, i + groups[0])),
        out_shape=jax.ShapeDtypeStruct((tok, width), jnp.bfloat16),
        scratch_shapes=[
            pltpu.VMEM((heads * tok, 2 * HD), jnp.bfloat16),
            pltpu.VMEM((reach + 1, heads * tok, tok), jnp.float32),
            pltpu.VMEM((heads * tok, LANES), jnp.float32),
            pltpu.VMEM((heads * tok, 2 * HD), jnp.float32),
        ],
        input_output_aliases=aliases,
        compiler_params=pltpu.CompilerParams(vmem_limit_bytes=VMEM_LIMIT // 2 + 4 * (reach + 1) * heads * tok * tok),
        cost_estimate=pl.CostEstimate(
            flops=4 * tok * share * count * tok * 4,
            bytes_accessed=8 * tok * share * count,
            transcendentals=tok * tok * 4 * heads * count,
        ),
        name="attend",
    )(*operands)


def shifted(value, steps):
    count = lax.axis_size("seq")
    return lax.ppermute(value, "seq", [(source, source + steps) for source in range(count - steps)])


def local(
    x_branch,
    z_branch,
    conv_weight,
    conv_bias,
    xproj_weight,
    dt_weight,
    dt_bias,
    decay_rate,
    skip_gain,
    query_rows,
    key_rows,
    value_rows,
    lengths,
    destination,
):
    tok = x_branch.shape[0]
    n_seq = lax.axis_size("seq")
    n_mp = lax.axis_size("mp")
    low_rank = dt_weight.shape[0]
    reach = n_seq // 2
    run_rows = tok // n_seq
    kv_local = key_rows.shape[1] // HD
    fence = lax.optimization_barrier

    halo, kv = pack(x_branch, key_rows, value_rows)
    earlier_rows = shifted(halo, 1)
    held = [kv] + [shifted(kv, 2 * k) for k in range(1, (reach + 1) // 2 + 1)]
    send_place = ((destination // tok) * run_rows + destination % run_rows).reshape(n_seq, tok)

    inner_act, partial = conv_project(lengths, x_branch, earlier_rows, conv_weight, conv_bias, xproj_weight)
    partial, *held = fence((partial, *held))
    pieces = lax.all_to_all(partial, "mp", split_axis=0, concat_axis=0, tiled=True)
    mine = jnp.stack(held)
    theirs = lax.ppermute(mine, "seq", [(source, source ^ 1) for source in range(n_seq)])
    early = max(kv_local // 2, 1)
    attended = attend(lengths, send_place, query_rows, mine, theirs, (0, early), None)
    pieces, attended = fence((pieces, attended))
    summed = jnp.sum(pieces.reshape(n_mp, -1, tok).astype(jnp.float32), axis=0).astype(jnp.bfloat16)
    copies = jnp.broadcast_to(summed[None], (n_mp,) + summed.shape).reshape(partial.shape)
    copies, attended = fence((copies, attended))
    projected = lax.all_to_all(copies, "mp", split_axis=0, concat_axis=0, tiled=True)
    if early < kv_local:
        attended = attend(lengths, send_place, query_rows, mine, theirs, (early, kv_local), attended)
    projected, attended = fence((projected, attended))
    regrouped = lax.all_to_all(attended, "seq", split_axis=0, concat_axis=0, tiled=True)

    y, sums, state = local_scan(lengths, projected, dt_weight, dt_bias, decay_rate, skip_gain, inner_act)
    blocks = [shifted(state, back) for back in range(1, reach + 1)]
    mamba_out = join_states(projected, y, sums, z_branch, decay_rate, blocks, low_rank)
    return (mamba_out, regrouped)


def solution(mesh):
    placed = (
        P("seq", "mp"),
        P("seq", "mp"),
        P(None, "mp"),
        P("mp"),
        P("mp", None),
        P(None, "mp"),
        P("mp"),
        P(None, "mp"),
        P("mp"),
        P("seq", "mp"),
        P("seq", "mp"),
        P("seq", "mp"),
        P(),
        P(),
    )
    return jax.shard_map(
        local,
        mesh=mesh,
        in_specs=placed,
        out_specs=(P("seq", "mp"), P("seq", "mp")),
        check_vma=False,
    )
```

```python
import functools

import jax
import jax.numpy as jnp
from jax import lax
from jax.experimental import pallas as pl
from jax.experimental.pallas import tpu as pltpu
from jax.sharding import PartitionSpec as P

HD = 128
LANES = 128
HALO = 16
LOG2E = 1.4426950408889634
RESET = 1e30
APART = 65536.0
VMEM_LIMIT = 32 * 1024 * 1024
VMEM_MOST = 56 * 1024 * 1024


def doc_edges(lengths_ref):
    starts, ends, total = [], [], 0
    for i in range(lengths_ref.shape[0]):
        starts.append(total)
        total = total + lengths_ref[i]
        ends.append(total)
    return starts, ends


def doc_start(places, starts):
    found = jnp.zeros_like(places)
    for start in starts[1:]:
        found = jnp.where(places >= start, start, found)
    return found


def channel_chunk(channels):
    return 512 if channels % 512 == 0 else channels


def pack_kernel(x_ref, k_ref, v_ref, halo_ref, kv_ref):
    width = k_ref.shape[1]
    halo_ref[...] = x_ref[...]
    kv_ref[:, :width] = k_ref[...]
    kv_ref[:, width:] = v_ref[...]


def pack(x_branch, key_rows, value_rows):
    tok, channels = x_branch.shape
    width = key_rows.shape[1]
    whole = lambda rows, columns: pl.BlockSpec((rows, columns), lambda i: (0, 0))
    return pl.pallas_call(
        pack_kernel,
        grid=(1,),
        in_specs=[
            pl.BlockSpec((HALO, channels), lambda i: (tok // HALO - 1, 0)),
            whole(tok, width),
            whole(tok, width),
        ],
        out_specs=[whole(HALO, channels), whole(tok, 2 * width)],
        out_shape=[
            jax.ShapeDtypeStruct((HALO, channels), x_branch.dtype),
            jax.ShapeDtypeStruct((tok, 2 * width), key_rows.dtype),
        ],
        compiler_params=pltpu.CompilerParams(vmem_limit_bytes=VMEM_MOST),
        cost_estimate=pl.CostEstimate(flops=0, bytes_accessed=16 * tok * width, transcendentals=0),
        name="pack",
    )(x_branch, key_rows, value_rows)


def conv_kernel(lengths_ref, x_ref, halo_ref, w_ref, b_ref, xp_ref, inner_ref, part_ref, ext, acc):
    tok, chunk = x_ref.shape
    starts, _ = doc_edges(lengths_ref)
    anchor = lax.axis_index("seq") * tok
    places = anchor + lax.broadcasted_iota(jnp.int32, (tok, LANES), 0)
    depth = places - doc_start(places, starts)
    ext[0:HALO, :] = halo_ref[...].astype(jnp.float32)
    ext[HALO:, :] = x_ref[...].astype(jnp.float32)
    for lane in range(0, chunk, LANES):
        cols = slice(lane, lane + LANES)
        total = b_ref[:, cols] + w_ref[0:1, cols] * ext[HALO:, cols]
        for lag in range(1, w_ref.shape[0]):
            window = ext[HALO - lag : HALO - lag + tok, cols]
            total += w_ref[lag : lag + 1, cols] * jnp.where(depth >= lag, window, 0.0)
        act = total * (0.5 + 0.5 * jnp.tanh(0.5 * total))
        inner_ref[:, cols] = act.astype(jnp.bfloat16)
    product = lax.dot_general(
        xp_ref[...], inner_ref[...], (((1,), (1,)), ((), ())), preferred_element_type=jnp.float32
    )
    at = pl.program_id(0)

    @pl.when(at == 0)
    def _():
        acc[...] = product

    @pl.when(at > 0)
    def _():
        acc[...] += product

    @pl.when(at == pl.num_programs(0) - 1)
    def _():
        part_ref[...] = acc[...].astype(jnp.bfloat16)


def conv_project(lengths, x_branch, halo, conv_weight, conv_bias, xproj_weight):
    tok, channels = x_branch.shape
    width = xproj_weight.shape[1]
    taps = conv_weight.shape[0]
    chunk = channel_chunk(channels)
    return pl.pallas_call(
        conv_kernel,
        grid=(channels // chunk,),
        in_specs=[
            pl.BlockSpec(memory_space=pltpu.SMEM),
            pl.BlockSpec((tok, chunk), lambda i: (0, i)),
            pl.BlockSpec((HALO, chunk), lambda i: (0, i)),
            pl.BlockSpec((taps, chunk), lambda i: (0, i)),
            pl.BlockSpec((1, chunk), lambda i: (0, i)),
            pl.BlockSpec((width, chunk), lambda i: (0, i)),
        ],
        out_specs=[
            pl.BlockSpec((tok, chunk), lambda i: (0, i)),
            pl.BlockSpec((width, tok), lambda i: (0, 0)),
        ],
        out_shape=[
            jax.ShapeDtypeStruct((tok, channels), jnp.bfloat16),
            jax.ShapeDtypeStruct((width, tok), jnp.bfloat16),
        ],
        scratch_shapes=[
            pltpu.VMEM((tok + HALO, chunk), jnp.float32),
            pltpu.VMEM((width, tok), jnp.float32),
        ],
        compiler_params=pltpu.CompilerParams(vmem_limit_bytes=VMEM_MOST),
        cost_estimate=pl.CostEstimate(
            flops=2 * tok * channels * width, bytes_accessed=8 * tok * channels, transcendentals=tok * channels
        ),
        name="conv_project",
    )(lengths, x_branch, halo, conv_weight, conv_bias.reshape(1, channels), xproj_weight.T)


def spread(columns):
    tok, k = columns.shape
    rows = jnp.broadcast_to(columns.astype(jnp.float32)[:, None, :], (tok, k, k))
    own = lax.broadcasted_iota(jnp.int32, (tok, k, k), 1) == lax.broadcasted_iota(jnp.int32, (tok, k, k), 2)
    picked = jnp.where(own, rows, 0.0).reshape(tok * k, k).astype(jnp.bfloat16)
    return jnp.dot(picked, jnp.ones((k, LANES), jnp.bfloat16), preferred_element_type=jnp.float32)


def advance(state, tile, row, rate2, step_ref, drive_ref, b_rows):
    out = []
    for i, held in enumerate(state):
        cols = slice(i * LANES, (i + 1) * LANES)
        decay = jnp.exp2(rate2[i] * step_ref[tile, row : row + 1, cols])
        out.append(decay * held + b_rows * drive_ref[tile, row : row + 1, cols])
    return out


def lane_tiles(value):
    return [value[:, i : i + LANES] for i in range(0, value.shape[1], LANES)]


ROWS = 8
UNROLL = 2 * ROWS


def state_rows(columns):
    tok, k = columns.shape
    lane = lambda shape, axis: lax.broadcasted_iota(jnp.int32, shape, axis)
    copies = (lane((k, UNROLL * k), 1) % k == lane((k, UNROLL * k), 0)).astype(jnp.float32).astype(jnp.bfloat16)
    tiled = jnp.dot(columns.astype(jnp.bfloat16), copies, preferred_element_type=jnp.float32)
    own = lane(tiled.shape, 1) // k == lane(tiled.shape, 0) % UNROLL
    return jnp.where(own, tiled, 0.0).astype(jnp.bfloat16)


def paired(tok, held, c_rows, scan, finish, state):
    def total(group, buffer):
        rows = pl.ds(pl.multiple_of(group * UNROLL, UNROLL), UNROLL)
        finish(rows, jnp.dot(c_rows[rows, :], held[buffer], preferred_element_type=jnp.float32))

    def body(turn, state):
        total(jnp.maximum(2 * turn - 1, 0), 1)
        state = scan(2 * turn, 0, state)
        total(2 * turn, 0)
        return scan(2 * turn + 1, 1, state)

    groups = tok // UNROLL
    state = lax.fori_loop(0, groups // 2, body, state)
    total(groups - 1, 1)
    return state


def local_kernel(
    lengths_ref,
    proj_ref,
    dtw_ref,
    bias_ref,
    rate_ref,
    skip_ref,
    inner_ref,
    y_ref,
    sum_ref,
    state_ref,
    low_cols,
    b_spread,
    c_rows,
    step_ref,
    drive_ref,
    held,
    totals,
):
    tok, chunk = inner_ref.shape
    states = rate_ref.shape[0]
    low_rank = dtw_ref.shape[0]
    tiles = chunk // LANES
    starts, _ = doc_edges(lengths_ref)
    at = pl.program_id(0)

    @pl.when(at == 0)
    def _():
        low_cols[...] = proj_ref[:low_rank, :].astype(jnp.float32).T.astype(jnp.bfloat16)
        both = proj_ref[low_rank:, :].astype(jnp.float32).T
        b_spread[...] = spread(both[:, :states])
        c_rows[...] = state_rows(both[:, states:])

    anchor = lax.axis_index("seq") * tok
    places = anchor + lax.broadcasted_iota(jnp.int32, (tok, LANES), 0)
    at_start = places == doc_start(places, starts)
    upto = lax.broadcasted_iota(jnp.int32, (tok, tok), 0) >= lax.broadcasted_iota(jnp.int32, (tok, tok), 1)
    upto = upto.astype(jnp.float32).astype(jnp.bfloat16)
    raw = jnp.dot(low_cols[...], dtw_ref[...], preferred_element_type=jnp.float32)
    for i in range(tiles):
        cols = slice(i * LANES, (i + 1) * LANES)
        biased = raw[:, cols] + bias_ref[:, cols]
        step = jnp.maximum(biased, 0.0) + jnp.log1p(jnp.exp(-jnp.abs(biased)))
        drive = step * inner_ref[:, cols].astype(jnp.float32)
        drive_ref[:, :, cols] = drive.reshape(tok // ROWS, ROWS, LANES)
        step = jnp.where(at_start, RESET, step)
        step_ref[:, :, cols] = step.reshape(tok // ROWS, ROWS, LANES)
        high = step.astype(jnp.bfloat16)
        low = (step - high.astype(jnp.float32)).astype(jnp.bfloat16)
        summed = jnp.dot(upto, high, preferred_element_type=jnp.float32) + jnp.dot(
            upto, low, preferred_element_type=jnp.float32
        )
        sum_ref[:, :, cols] = summed.reshape(tok // ROWS, ROWS, LANES)
        totals[at * tiles + i] = summed[tok - 1 : tok]
    rate2 = lane_tiles(rate_ref[...] * (-LOG2E))

    def scan(group, buffer, state):
        for u in range(UNROLL):
            tile = group * (UNROLL // ROWS) + u // ROWS
            row = pl.multiple_of(group * UNROLL * states, UNROLL * states) + u * states
            state = advance(state, tile, u % ROWS, rate2, step_ref, drive_ref, b_spread[pl.ds(row, states), :])
            for i, now in enumerate(state):
                cols = slice(i * LANES, (i + 1) * LANES)
                held[buffer, u * states : (u + 1) * states, cols] = now.astype(jnp.bfloat16)
        return state

    def finish(rows, total):
        y_ref[rows, :] = total + skip_ref[...] * inner_ref[rows, :].astype(jnp.float32)

    held[1] = jnp.zeros(held.shape[1:], held.dtype)
    end = paired(tok, held, c_rows, scan, finish, [jnp.zeros_like(r) for r in rate2])
    for i in range(tiles):
        state_ref[at * tiles + i] = end[i].astype(jnp.bfloat16)

    @pl.when(at == pl.num_programs(0) - 1)
    def _():
        lanes = totals.shape[0]
        row = lax.broadcasted_iota(jnp.int32, (states, LANES), 0)
        table = jnp.zeros((states, LANES), jnp.float32)
        for i in range(lanes):
            table = jnp.where(row == i, totals[i], table)
        high = table.astype(jnp.bfloat16)
        state_ref[lanes] = high
        state_ref[lanes + 1] = (table - high.astype(jnp.float32)).astype(jnp.bfloat16)


def local_scan(lengths, projected, dt_weight, dt_bias, decay_rate, skip_gain, inner_act):
    tok, channels = inner_act.shape
    low_rank = dt_weight.shape[0]
    states = decay_rate.shape[0]
    width = projected.shape[0]
    chunk = channel_chunk(channels)
    lanes = channels // LANES
    by_chunk = lambda rows: pl.BlockSpec((rows, chunk), lambda i: (0, i))
    return pl.pallas_call(
        local_kernel,
        grid=(channels // chunk,),
        in_specs=[
            pl.BlockSpec(memory_space=pltpu.SMEM),
            pl.BlockSpec((width, tok), lambda i: (0, 0)),
            by_chunk(low_rank),
            by_chunk(1),
            by_chunk(states),
            by_chunk(1),
            by_chunk(tok),
        ],
        out_specs=[
            by_chunk(tok),
            pl.BlockSpec((tok // ROWS, ROWS, chunk), lambda i: (0, 0, i)),
            pl.BlockSpec((lanes + 2, states, LANES), lambda i: (0, 0, 0)),
        ],
        out_shape=[
            jax.ShapeDtypeStruct((tok, channels), jnp.float32),
            jax.ShapeDtypeStruct((tok // ROWS, ROWS, channels), jnp.float32),
            jax.ShapeDtypeStruct((lanes + 2, states, LANES), jnp.bfloat16),
        ],
        scratch_shapes=[
            pltpu.VMEM((tok, low_rank), jnp.bfloat16),
            pltpu.VMEM((tok * states, LANES), jnp.float32),
            pltpu.VMEM((tok, UNROLL * states), jnp.bfloat16),
            pltpu.VMEM((tok // ROWS, ROWS, chunk), jnp.float32),
            pltpu.VMEM((tok // ROWS, ROWS, chunk), jnp.float32),
            pltpu.VMEM((2, UNROLL * states, chunk), jnp.bfloat16),
            pltpu.VMEM((lanes, 1, LANES), jnp.float32),
        ],
        compiler_params=pltpu.CompilerParams(vmem_limit_bytes=VMEM_MOST),
        cost_estimate=pl.CostEstimate(
            flops=12 * tok * channels * states,
            bytes_accessed=12 * tok * channels,
            transcendentals=tok * channels * states,
        ),
        name="local_scan",
    )(
        lengths,
        projected,
        dt_weight,
        dt_bias.reshape(1, channels),
        decay_rate,
        skip_gain.reshape(1, channels),
        inner_act,
    )


def join_kernel(low_rank, reach, proj_ref, y_ref, sum_ref, z_ref, rate_ref, moved_ref, *refs):
    blocks, (out_ref, regrouped_ref, c_rows, held) = refs[:reach], refs[reach:]
    tok, chunk = y_ref.shape
    states = rate_ref.shape[0]
    tiles = chunk // LANES
    lanes = blocks[0].shape[0] - 2
    at = pl.program_id(0)

    @pl.when(at == 0)
    def _():
        c_rows[...] = state_rows(proj_ref[low_rank + states :, :].astype(jnp.float32).T)

    regrouped_ref[...] = moved_ref[...]

    rate2 = lane_tiles(rate_ref[...] * (-LOG2E))
    row = lax.broadcasted_iota(jnp.int32, (states, LANES), 0)
    entering = [jnp.zeros_like(r) for r in rate2]
    for block in reversed(blocks):
        table = block[lanes].astype(jnp.float32) + block[lanes + 1].astype(jnp.float32)
        for i, before in enumerate(entering):
            total = jnp.sum(jnp.where(row == at * tiles + i, table, 0.0), axis=0, keepdims=True)
            entering[i] = jnp.exp2(rate2[i] * total) * before + block[at * tiles + i].astype(jnp.float32)
    entering = [e.astype(jnp.bfloat16) for e in entering]

    def scan(group, buffer, carry):
        for u in range(UNROLL):
            tile = group * (UNROLL // ROWS) + u // ROWS
            for i in range(tiles):
                cols = slice(i * LANES, (i + 1) * LANES)
                power = rate2[i] * sum_ref[tile, u % ROWS : u % ROWS + 1, cols]
                held[buffer, u * states : (u + 1) * states, cols] = (
                    jnp.exp2(power.astype(jnp.bfloat16)) * entering[i]
                )
        return carry

    def finish(rows, total):
        z = z_ref[rows, :].astype(jnp.float32)
        gate = z * (0.5 + 0.5 * jnp.tanh(0.5 * z))
        out_ref[rows, :] = ((y_ref[rows, :] + total) * gate).astype(jnp.bfloat16)

    held[1] = jnp.zeros(held.shape[1:], held.dtype)
    paired(tok, held, c_rows, scan, finish, 0)


def join_states(projected, y, sums, z_branch, decay_rate, moved, blocks, low_rank):
    tok, channels = z_branch.shape
    states = decay_rate.shape[0]
    width = projected.shape[0]
    chunk = channel_chunk(channels)
    by_chunk = lambda rows: pl.BlockSpec((rows, chunk), lambda i: (0, i))
    return pl.pallas_call(
        functools.partial(join_kernel, low_rank, len(blocks)),
        grid=(channels // chunk,),
        in_specs=[
            pl.BlockSpec((width, tok), lambda i: (0, 0)),
            by_chunk(tok),
            pl.BlockSpec((tok // ROWS, ROWS, chunk), lambda i: (0, 0, i)),
            by_chunk(tok),
            by_chunk(states),
            by_chunk(tok),
        ]
        + [pl.BlockSpec(block.shape, lambda i: (0, 0, 0)) for block in blocks],
        out_specs=[by_chunk(tok), by_chunk(tok)],
        out_shape=[jax.ShapeDtypeStruct((tok, channels), jnp.bfloat16)] * 2,
        scratch_shapes=[
            pltpu.VMEM((tok, UNROLL * states), jnp.bfloat16),
            pltpu.VMEM((2, UNROLL * states, chunk), jnp.bfloat16),
        ],
        compiler_params=pltpu.CompilerParams(vmem_limit_bytes=VMEM_LIMIT),
        cost_estimate=pl.CostEstimate(
            flops=8 * tok * channels * states,
            bytes_accessed=14 * tok * channels,
            transcendentals=tok * channels * states,
        ),
        name="join_states",
    )(projected, y, sums, z_branch, decay_rate, moved, *blocks)


def attend_kernel(kv_local, first_group, lengths_ref, place_ref, q_ref, mine_ref, theirs_ref, *refs):
    out_ref, queries, scores, tops, acc = refs[-5:]
    tok = q_ref.shape[0]
    heads = q_ref.shape[1] // HD
    group = pl.program_id(0) + first_group
    position = lax.axis_index("seq")
    odd = lax.rem(position, 2)
    anchor = position * tok
    scale = LOG2E * HD**-0.5
    starts, ends = doc_edges(lengths_ref)
    lane = lax.broadcasted_iota(jnp.int32, (1, LANES), 1)
    first = jnp.full((1, LANES), 2**30, jnp.int32)
    last = jnp.zeros((1, LANES), jnp.int32)
    for i, (start, end) in enumerate(zip(starts, ends)):
        first = jnp.where(lane == i, start, first)
        last = jnp.where(lane == i, end, last)
    rows = lax.broadcasted_iota(jnp.int32, (tok, LANES), 0)

    def in_doc(base):
        return (rows + base >= first) & (rows + base < last)

    apart = jnp.where(in_doc(anchor) | (lane >= len(starts)), 0.0, -APART).astype(jnp.bfloat16)
    for head in range(heads):
        queries[head * tok : (head + 1) * tok, :HD] = q_ref[:, head * HD : (head + 1) * HD]
        queries[head * tok : (head + 1) * tok, HD:] = apart
    key_cols = pl.ds(pl.multiple_of(group * HD, HD), HD)
    value_cols = pl.ds(pl.multiple_of((group + kv_local) * HD, HD), HD)

    def rows_of(back, cols):
        if isinstance(back, int) and back == 0:
            return mine_ref[0, :, cols]
        ours = mine_ref[back // 2, :, cols]
        other = theirs_ref[(back + 1) // 2 - odd, :, cols]
        return jnp.where(lax.rem(back, 2) == 0, ours, other)

    def score(back):
        marks = jnp.where(in_doc(anchor - back * tok), 1.0, 0.0).astype(jnp.bfloat16)
        keys = jnp.concatenate([rows_of(back, key_cols), marks], axis=1)
        return lax.dot_general(queries[...], keys, (((1,), (1,)), ((), ())), preferred_element_type=jnp.float32)

    def widest(s):
        top = s[:, :LANES]
        for at in range(LANES, tok, LANES):
            top = jnp.maximum(top, s[:, at : at + LANES])
        return top

    own = score(0)
    causal = lax.broadcasted_iota(jnp.int32, (tok, tok), 1) <= lax.broadcasted_iota(jnp.int32, (tok, tok), 0)
    for head in range(heads):
        part = slice(head * tok, (head + 1) * tok)
        s = jnp.where(causal, own[part], -APART)
        scores[0, part, :] = s
        tops[part, :] = widest(s)

    begin = jnp.int32(0)
    for start in starts[1:]:
        begin = jnp.where(anchor >= start, start, begin)
    earlier = (anchor - begin + tok - 1) // tok

    def look(back, carry):
        s = score(back)
        scores[back] = s
        tops[...] = jnp.maximum(tops[...], widest(s))
        return carry

    lax.fori_loop(1, earlier + 1, look, 0)
    tops[...] = jnp.broadcast_to(jnp.max(tops[...], axis=1, keepdims=True) * scale, tops.shape)

    def weighted(back):
        values = jnp.concatenate([rows_of(back, value_cols), jnp.ones((tok, HD), jnp.bfloat16)], axis=1)
        top = tops[...]
        weights = [
            jnp.exp2((scores[back, :, at : at + LANES] * scale - top).astype(jnp.bfloat16))
            for at in range(0, tok, LANES)
        ]
        return jnp.dot(jnp.concatenate(weights, axis=1), values, preferred_element_type=jnp.float32)

    acc[...] = weighted(0)

    def absorb(back, carry):
        acc[...] += weighted(back)
        return carry

    lax.fori_loop(1, earlier + 1, absorb, 0)
    order = place_ref[pl.ds(position, 1), :]
    move = (lax.broadcasted_iota(jnp.int32, (tok, tok), 0) == order).astype(jnp.float32).astype(jnp.bfloat16)
    for head in range(heads):
        part = slice(head * tok, (head + 1) * tok)
        result = (acc[part, :HD] / acc[part, HD:]).astype(jnp.bfloat16)
        moved = jnp.dot(move, result, preferred_element_type=jnp.float32)
        out_ref[:, head * HD : (head + 1) * HD] = moved.astype(jnp.bfloat16)


def attend(lengths, send_place, query_rows, mine, theirs, groups, so_far):
    tok, width = query_rows.shape
    kv_local = mine.shape[2] // (2 * HD)
    share = width // kv_local
    heads = share // HD
    reach = 2 * (mine.shape[0] - 1)
    count = groups[1] - groups[0]
    whole = lambda a: pl.BlockSpec(a.shape, lambda i: (0,) * a.ndim)
    in_specs = [
        pl.BlockSpec(memory_space=pltpu.SMEM),
        whole(send_place),
        pl.BlockSpec((tok, share), lambda i: (0, i + groups[0])),
        whole(mine),
        whole(theirs),
    ]
    operands = [lengths, send_place, query_rows, mine, theirs]
    aliases = {}
    if so_far is not None:
        aliases = {len(operands): 0}
        in_specs.append(pl.BlockSpec(memory_space=pl.ANY))
        operands.append(so_far)
    return pl.pallas_call(
        functools.partial(attend_kernel, kv_local, groups[0]),
        grid=(count,),
        in_specs=in_specs,
        out_specs=pl.BlockSpec((tok, share), lambda i: (0, i + groups[0])),
        out_shape=jax.ShapeDtypeStruct((tok, width), jnp.bfloat16),
        scratch_shapes=[
            pltpu.VMEM((heads * tok, 2 * HD), jnp.bfloat16),
            pltpu.VMEM((reach + 1, heads * tok, tok), jnp.float32),
            pltpu.VMEM((heads * tok, LANES), jnp.float32),
            pltpu.VMEM((heads * tok, 2 * HD), jnp.float32),
        ],
        input_output_aliases=aliases,
        compiler_params=pltpu.CompilerParams(vmem_limit_bytes=VMEM_LIMIT // 2 + 4 * (reach + 1) * heads * tok * tok),
        cost_estimate=pl.CostEstimate(
            flops=4 * tok * share * count * tok * 4,
            bytes_accessed=8 * tok * share * count,
            transcendentals=tok * tok * 4 * heads * count,
        ),
        name="attend",
    )(*operands)


def shifted(value, steps):
    count = lax.axis_size("seq")
    return lax.ppermute(value, "seq", [(source, source + steps) for source in range(count - steps)])


def local(
    x_branch,
    z_branch,
    conv_weight,
    conv_bias,
    xproj_weight,
    dt_weight,
    dt_bias,
    decay_rate,
    skip_gain,
    query_rows,
    key_rows,
    value_rows,
    lengths,
    destination,
):
    tok = x_branch.shape[0]
    n_seq = lax.axis_size("seq")
    n_mp = lax.axis_size("mp")
    low_rank = dt_weight.shape[0]
    reach = n_seq // 2
    run_rows = tok // n_seq
    kv_local = key_rows.shape[1] // HD
    fence = lax.optimization_barrier

    halo, kv = pack(x_branch, key_rows, value_rows)
    earlier_rows, kv = fence((shifted(halo, 1), kv))
    held = [kv] + [shifted(kv, 2 * k) for k in range(1, (reach + 1) // 2 + 1)]
    send_place = ((destination // tok) * run_rows + destination % run_rows).reshape(n_seq, tok)

    inner_act, partial = conv_project(lengths, x_branch, earlier_rows, conv_weight, conv_bias, xproj_weight)
    partial, *held = fence((partial, *held))
    pieces = lax.all_to_all(partial, "mp", split_axis=0, concat_axis=0, tiled=True)
    mine = jnp.stack(held)
    theirs = lax.ppermute(mine, "seq", [(source, source ^ 1) for source in range(n_seq)])
    early = max(kv_local // 2, 1)
    attended = attend(lengths, send_place, query_rows, mine, theirs, (0, early), None)
    pieces, attended = fence((pieces, attended))
    summed = jnp.sum(pieces.reshape(n_mp, -1, tok).astype(jnp.float32), axis=0).astype(jnp.bfloat16)
    copies = jnp.broadcast_to(summed[None], (n_mp,) + summed.shape).reshape(partial.shape)
    copies, attended = fence((copies, attended))
    projected = lax.all_to_all(copies, "mp", split_axis=0, concat_axis=0, tiled=True)
    if early < kv_local:
        attended = attend(lengths, send_place, query_rows, mine, theirs, (early, kv_local), attended)
    projected, attended = fence((projected, attended))
    regrouped = lax.all_to_all(attended, "seq", split_axis=0, concat_axis=0, tiled=True)

    y, sums, state = local_scan(lengths, projected, dt_weight, dt_bias, decay_rate, skip_gain, inner_act)
    blocks = [shifted(state, back) for back in range(1, reach + 1)]
    return tuple(join_states(projected, y, sums, z_branch, decay_rate, regrouped, blocks, low_rank))


def solution(mesh):
    placed = (
        P("seq", "mp"),
        P("seq", "mp"),
        P(None, "mp"),
        P("mp"),
        P("mp", None),
        P(None, "mp"),
        P("mp"),
        P(None, "mp"),
        P("mp"),
        P("seq", "mp"),
        P("seq", "mp"),
        P("seq", "mp"),
        P(),
        P(),
    )
    return jax.shard_map(
        local,
        mesh=mesh,
        in_specs=placed,
        out_specs=(P("seq", "mp"), P("seq", "mp")),
        check_vma=False,
    )
```

```python
import functools

import jax
import jax.numpy as jnp
from jax import lax
from jax.experimental import pallas as pl
from jax.experimental.pallas import tpu as pltpu
from jax.sharding import PartitionSpec as P

HD = 128
LANES = 128
HALO = 16
LOG2E = 1.4426950408889634
RESET = 1e30
APART = 65536.0
VMEM_LIMIT = 32 * 1024 * 1024
VMEM_MOST = 56 * 1024 * 1024


def doc_edges(lengths_ref):
    starts, ends, total = [], [], 0
    for i in range(lengths_ref.shape[0]):
        starts.append(total)
        total = total + lengths_ref[i]
        ends.append(total)
    return starts, ends


def doc_start(places, starts):
    found = jnp.zeros_like(places)
    for start in starts[1:]:
        found = jnp.where(places >= start, start, found)
    return found


def channel_chunk(channels):
    return 512 if channels % 512 == 0 else channels


def pack_kernel(x_ref, k_ref, v_ref, halo_ref, kv_ref):
    width = k_ref.shape[1]
    halo_ref[...] = x_ref[...]
    kv_ref[:, :width] = k_ref[...]
    kv_ref[:, width:] = v_ref[...]


def pack(x_branch, key_rows, value_rows):
    tok, channels = x_branch.shape
    width = key_rows.shape[1]
    whole = lambda rows, columns: pl.BlockSpec((rows, columns), lambda i: (0, 0))
    return pl.pallas_call(
        pack_kernel,
        grid=(1,),
        in_specs=[
            pl.BlockSpec((HALO, channels), lambda i: (tok // HALO - 1, 0)),
            whole(tok, width),
            whole(tok, width),
        ],
        out_specs=[whole(HALO, channels), whole(tok, 2 * width)],
        out_shape=[
            jax.ShapeDtypeStruct((HALO, channels), x_branch.dtype),
            jax.ShapeDtypeStruct((tok, 2 * width), key_rows.dtype),
        ],
        compiler_params=pltpu.CompilerParams(vmem_limit_bytes=VMEM_MOST),
        cost_estimate=pl.CostEstimate(flops=0, bytes_accessed=16 * tok * width, transcendentals=0),
        name="pack",
    )(x_branch, key_rows, value_rows)


def conv_kernel(lengths_ref, x_ref, halo_ref, w_ref, b_ref, xp_ref, inner_ref, part_ref, ext, acc):
    tok, chunk = x_ref.shape
    starts, _ = doc_edges(lengths_ref)
    anchor = lax.axis_index("seq") * tok
    places = anchor + lax.broadcasted_iota(jnp.int32, (tok, LANES), 0)
    depth = places - doc_start(places, starts)
    ext[0:HALO, :] = halo_ref[...].astype(jnp.float32)
    ext[HALO:, :] = x_ref[...].astype(jnp.float32)
    for lane in range(0, chunk, LANES):
        cols = slice(lane, lane + LANES)
        total = b_ref[:, cols] + w_ref[0:1, cols] * ext[HALO:, cols]
        for lag in range(1, w_ref.shape[0]):
            window = ext[HALO - lag : HALO - lag + tok, cols]
            total += w_ref[lag : lag + 1, cols] * jnp.where(depth >= lag, window, 0.0)
        act = total * (0.5 + 0.5 * jnp.tanh(0.5 * total))
        inner_ref[:, cols] = act.astype(jnp.bfloat16)
    product = lax.dot_general(
        xp_ref[...], inner_ref[...], (((1,), (1,)), ((), ())), preferred_element_type=jnp.float32
    )
    at = pl.program_id(0)

    @pl.when(at == 0)
    def _():
        acc[...] = product

    @pl.when(at > 0)
    def _():
        acc[...] += product

    @pl.when(at == pl.num_programs(0) - 1)
    def _():
        part_ref[...] = acc[...].astype(jnp.bfloat16)


def conv_project(lengths, x_branch, halo, conv_weight, conv_bias, xproj_weight):
    tok, channels = x_branch.shape
    width = xproj_weight.shape[1]
    taps = conv_weight.shape[0]
    chunk = channel_chunk(channels)
    return pl.pallas_call(
        conv_kernel,
        grid=(channels // chunk,),
        in_specs=[
            pl.BlockSpec(memory_space=pltpu.SMEM),
            pl.BlockSpec((tok, chunk), lambda i: (0, i)),
            pl.BlockSpec((HALO, chunk), lambda i: (0, i)),
            pl.BlockSpec((taps, chunk), lambda i: (0, i)),
            pl.BlockSpec((1, chunk), lambda i: (0, i)),
            pl.BlockSpec((width, chunk), lambda i: (0, i)),
        ],
        out_specs=[
            pl.BlockSpec((tok, chunk), lambda i: (0, i)),
            pl.BlockSpec((width, tok), lambda i: (0, 0)),
        ],
        out_shape=[
            jax.ShapeDtypeStruct((tok, channels), jnp.bfloat16),
            jax.ShapeDtypeStruct((width, tok), jnp.bfloat16),
        ],
        scratch_shapes=[
            pltpu.VMEM((tok + HALO, chunk), jnp.float32),
            pltpu.VMEM((width, tok), jnp.float32),
        ],
        compiler_params=pltpu.CompilerParams(vmem_limit_bytes=VMEM_MOST),
        cost_estimate=pl.CostEstimate(
            flops=80 * tok * channels * width, bytes_accessed=8 * tok * channels, transcendentals=tok * channels
        ),
        name="conv_project",
    )(lengths, x_branch, halo, conv_weight, conv_bias.reshape(1, channels), xproj_weight.T)


def spread(columns):
    tok, k = columns.shape
    own = lax.broadcasted_iota(jnp.int32, (k, k), 0) == lax.broadcasted_iota(jnp.int32, (k, k), 1)
    picked = jnp.where(own[None], columns.astype(jnp.float32)[:, None, :], 0.0).reshape(tok * k, k)
    ones = jnp.ones((k, LANES), jnp.bfloat16)
    return jnp.dot(picked.astype(jnp.bfloat16), ones, preferred_element_type=jnp.float32)


def lane_tiles(value):
    return [value[:, i : i + LANES] for i in range(0, value.shape[1], LANES)]


ROWS = 8
UNROLL = 2 * ROWS


def fold_rows(parts, lane, group):
    row = parts[lane, pl.ds(group * ROWS, ROWS, stride=ROWS), :]
    for n in range(1, ROWS):
        row = row + parts[lane, pl.ds(group * ROWS + n, ROWS, stride=ROWS), :]
    return row


def halves(term):
    total = term[0:ROWS]
    for more in range(ROWS, term.shape[0], ROWS):
        total = total + term[more : more + ROWS]
    return total


def keep_terms(parts, terms):
    for i, of_lane in enumerate(terms):
        for u, term in enumerate(of_lane):
            parts[i, u * ROWS : (u + 1) * ROWS, :] = term


def local_kernel(
    lengths_ref,
    proj_ref,
    dtw_ref,
    bias_ref,
    rate_ref,
    skip_ref,
    inner_ref,
    y_ref,
    sum_ref,
    state_ref,
    low_cols,
    bc_spread,
    step_ref,
    drive_ref,
    parts,
    totals,
):
    tok, chunk = inner_ref.shape
    states = rate_ref.shape[0]
    low_rank = dtw_ref.shape[0]
    tiles = chunk // LANES
    starts, _ = doc_edges(lengths_ref)
    at = pl.program_id(0)

    @pl.when(at == 0)
    def _():
        low_cols[...] = proj_ref[:low_rank, :].astype(jnp.float32).T.astype(jnp.bfloat16)
        bc_spread[...] = spread(proj_ref[low_rank:, :].astype(jnp.float32).T)

    anchor = lax.axis_index("seq") * tok
    places = anchor + lax.broadcasted_iota(jnp.int32, (tok, LANES), 0)
    at_start = places == doc_start(places, starts)
    upto = lax.broadcasted_iota(jnp.int32, (tok, tok), 0) >= lax.broadcasted_iota(jnp.int32, (tok, tok), 1)
    upto = upto.astype(jnp.float32).astype(jnp.bfloat16)
    raw = jnp.dot(low_cols[...], dtw_ref[...], preferred_element_type=jnp.float32)
    for i in range(tiles):
        cols = slice(i * LANES, (i + 1) * LANES)
        biased = raw[:, cols] + bias_ref[:, cols]
        step = jnp.maximum(biased, 0.0) + jnp.log(1.0 + jnp.exp(-jnp.abs(biased)))
        drive = step * inner_ref[:, cols].astype(jnp.float32)
        drive_ref[:, :, cols] = drive.reshape(tok // ROWS, ROWS, LANES)
        step = jnp.where(at_start, RESET, step)
        step_ref[:, :, cols] = step.reshape(tok // ROWS, ROWS, LANES)
        summed = jnp.dot(upto, step.astype(jnp.bfloat16), preferred_element_type=jnp.float32)
        sum_ref[:, :, cols] = summed.reshape(tok // ROWS, ROWS, LANES)
        totals[at * tiles + i] = summed[tok - 1 : tok]
    rate2 = lane_tiles(rate_ref[...] * (-LOG2E))

    def body(turn, state):
        base = pl.multiple_of(turn * UNROLL, UNROLL)
        spread_at = pl.multiple_of(turn * UNROLL * 2 * states, UNROLL * 2 * states)
        state, terms = list(state), [[] for _ in range(tiles)]
        for first in range(0, tiles, 2):
            for u in range(UNROLL):
                tile = turn * (UNROLL // ROWS) + u // ROWS
                row = slice(u % ROWS, u % ROWS + 1)
                b_rows = bc_spread[pl.ds(spread_at + u * 2 * states, states), :]
                c_rows = bc_spread[pl.ds(spread_at + u * 2 * states + states, states), :]
                for i in range(first, min(first + 2, tiles)):
                    cols = slice(i * LANES, (i + 1) * LANES)
                    decay = jnp.exp2(rate2[i] * step_ref[tile, row, cols])
                    state[i] = decay * state[i] + b_rows * drive_ref[tile, row, cols]
                    terms[i].append(halves(c_rows * state[i]))
        keep_terms(parts, terms)
        for group in range(0, UNROLL, ROWS):
            for i in range(tiles):
                y_ref[pl.ds(base + group, ROWS), i * LANES : (i + 1) * LANES] = fold_rows(parts, i, group)
        return state

    end = lax.fori_loop(0, tok // UNROLL, body, [jnp.zeros_like(r) for r in rate2])
    y_ref[...] += skip_ref[...] * inner_ref[...].astype(jnp.float32)
    for i in range(tiles):
        state_ref[at * tiles + i] = end[i].astype(jnp.bfloat16)

    @pl.when(at == pl.num_programs(0) - 1)
    def _():
        lanes = totals.shape[0]
        row = lax.broadcasted_iota(jnp.int32, (states, LANES), 0)
        table = jnp.zeros((states, LANES), jnp.float32)
        for i in range(lanes):
            table = jnp.where(row == i, totals[i], table)
        high = table.astype(jnp.bfloat16)
        state_ref[lanes] = high
        state_ref[lanes + 1] = (table - high.astype(jnp.float32)).astype(jnp.bfloat16)


def local_scan(lengths, projected, dt_weight, dt_bias, decay_rate, skip_gain, inner_act):
    tok, channels = inner_act.shape
    low_rank = dt_weight.shape[0]
    states = decay_rate.shape[0]
    width = projected.shape[0]
    chunk = channel_chunk(channels)
    lanes = channels // LANES
    by_chunk = lambda rows: pl.BlockSpec((rows, chunk), lambda i: (0, i))
    return pl.pallas_call(
        local_kernel,
        grid=(channels // chunk,),
        in_specs=[
            pl.BlockSpec(memory_space=pltpu.SMEM),
            pl.BlockSpec((width, tok), lambda i: (0, 0)),
            by_chunk(low_rank),
            by_chunk(1),
            by_chunk(states),
            by_chunk(1),
            by_chunk(tok),
        ],
        out_specs=[
            by_chunk(tok),
            pl.BlockSpec((tok // ROWS, ROWS, chunk), lambda i: (0, 0, i)),
            pl.BlockSpec((lanes + 2, states, LANES), lambda i: (0, 0, 0)),
        ],
        out_shape=[
            jax.ShapeDtypeStruct((tok, channels), jnp.float32),
            jax.ShapeDtypeStruct((tok // ROWS, ROWS, channels), jnp.float32),
            jax.ShapeDtypeStruct((lanes + 2, states, LANES), jnp.bfloat16),
        ],
        scratch_shapes=[
            pltpu.VMEM((tok, low_rank), jnp.bfloat16),
            pltpu.VMEM((tok * 2 * states, LANES), jnp.float32),
            pltpu.VMEM((tok // ROWS, ROWS, chunk), jnp.float32),
            pltpu.VMEM((tok // ROWS, ROWS, chunk), jnp.float32),
            pltpu.VMEM((chunk // LANES, UNROLL * ROWS, LANES), jnp.float32),
            pltpu.VMEM((lanes, 1, LANES), jnp.float32),
        ],
        compiler_params=pltpu.CompilerParams(vmem_limit_bytes=VMEM_LIMIT),
        cost_estimate=pl.CostEstimate(
            flops=12 * tok * channels * states,
            bytes_accessed=12 * tok * channels,
            transcendentals=tok * channels * states,
        ),
        name="local_scan",
    )(
        lengths,
        projected,
        dt_weight,
        dt_bias.reshape(1, channels),
        decay_rate,
        skip_gain.reshape(1, channels),
        inner_act,
    )


def join_kernel(
    low_rank,
    reach,
    proj_ref,
    y_ref,
    sum_ref,
    z_ref,
    rate_ref,
    moved_ref,
    mine_ref,
    theirs_ref,
    out_ref,
    regrouped_ref,
    c_spread,
    parts,
):
    tok, chunk = y_ref.shape
    states = rate_ref.shape[0]
    tiles = chunk // LANES
    lanes = mine_ref.shape[1] - 2
    at = pl.program_id(0)

    @pl.when(at == 0)
    def _():
        c_spread[...] = spread(proj_ref[low_rank + states :, :].astype(jnp.float32).T).astype(jnp.bfloat16)

    regrouped_ref[...] = moved_ref[...]

    rate2 = lane_tiles(rate_ref[...] * (-LOG2E))
    row = lax.broadcasted_iota(jnp.int32, (states, LANES), 0)
    entering = [jnp.zeros_like(r) for r in rate2]
    odd = lax.rem(lax.axis_index("seq"), 2)
    for back in range(reach, 0, -1):
        ref, which = (mine_ref, back // 2) if back % 2 == 0 else (theirs_ref, (back + 1) // 2 - odd)
        table = ref[which, lanes].astype(jnp.float32) + ref[which, lanes + 1].astype(jnp.float32)
        for i, before in enumerate(entering):
            total = jnp.sum(jnp.where(row == at * tiles + i, table, 0.0), axis=0, keepdims=True)
            entering[i] = jnp.exp2(rate2[i] * total) * before + ref[which, at * tiles + i].astype(jnp.float32)
    entering = [e.astype(jnp.bfloat16) for e in entering]

    def body(turn, carry):
        rows = pl.ds(pl.multiple_of(turn * UNROLL, UNROLL), UNROLL)
        spread_at = pl.multiple_of(turn * UNROLL * states, UNROLL * states)
        terms = [[] for _ in range(tiles)]
        for first in range(0, tiles, 2):
            for u in range(UNROLL):
                tile = turn * (UNROLL // ROWS) + u // ROWS
                c_rows = c_spread[pl.ds(spread_at + u * states, states), :]
                for i in range(first, min(first + 2, tiles)):
                    power = rate2[i] * sum_ref[tile, u % ROWS : u % ROWS + 1, i * LANES : (i + 1) * LANES]
                    term = jnp.exp2(power.astype(jnp.bfloat16)) * entering[i] * c_rows
                    terms[i].append(halves(term.astype(jnp.float32)))
        keep_terms(parts, terms)
        for i in range(tiles):
            cols = slice(i * LANES, (i + 1) * LANES)
            more = jnp.concatenate([fold_rows(parts, i, group) for group in range(0, UNROLL, ROWS)], axis=0)
            z = z_ref[rows, cols].astype(jnp.float32)
            gate = z * (0.5 + 0.5 * jnp.tanh(0.5 * z))
            out_ref[rows, cols] = ((y_ref[rows, cols] + more) * gate).astype(jnp.bfloat16)
        return carry

    lax.fori_loop(0, tok // UNROLL, body, 0)


def join_states(projected, y, sums, z_branch, decay_rate, moved, mine, theirs, low_rank, reach):
    tok, channels = z_branch.shape
    states = decay_rate.shape[0]
    width = projected.shape[0]
    chunk = channel_chunk(channels)
    by_chunk = lambda rows: pl.BlockSpec((rows, chunk), lambda i: (0, i))
    return pl.pallas_call(
        functools.partial(join_kernel, low_rank, reach),
        grid=(channels // chunk,),
        in_specs=[
            pl.BlockSpec((width, tok), lambda i: (0, 0)),
            by_chunk(tok),
            pl.BlockSpec((tok // ROWS, ROWS, chunk), lambda i: (0, 0, i)),
            by_chunk(tok),
            by_chunk(states),
            by_chunk(tok),
            pl.BlockSpec(mine.shape, lambda i: (0, 0, 0, 0)),
            pl.BlockSpec(theirs.shape, lambda i: (0, 0, 0, 0)),
        ],
        out_specs=[by_chunk(tok), by_chunk(tok)],
        out_shape=[jax.ShapeDtypeStruct((tok, channels), jnp.bfloat16)] * 2,
        scratch_shapes=[
            pltpu.VMEM((tok * states, LANES), jnp.bfloat16),
            pltpu.VMEM((chunk // LANES, UNROLL * ROWS, LANES), jnp.float32),
        ],
        compiler_params=pltpu.CompilerParams(vmem_limit_bytes=VMEM_LIMIT),
        cost_estimate=pl.CostEstimate(
            flops=8 * tok * channels * states,
            bytes_accessed=14 * tok * channels,
            transcendentals=tok * channels * states,
        ),
        name="join_states",
    )(projected, y, sums, z_branch, decay_rate, moved, mine, theirs)


def attend_kernel(kv_local, first_group, lengths_ref, place_ref, q_ref, mine_ref, theirs_ref, *refs):
    out_ref, queries, scores, tops, acc = refs[-5:]
    tok = q_ref.shape[0]
    heads = q_ref.shape[1] // HD
    group = pl.program_id(0) + first_group
    position = lax.axis_index("seq")
    odd = lax.rem(position, 2)
    anchor = position * tok
    scale = LOG2E * HD**-0.5
    starts, ends = doc_edges(lengths_ref)
    lane = lax.broadcasted_iota(jnp.int32, (1, LANES), 1)
    first = jnp.full((1, LANES), 2**30, jnp.int32)
    last = jnp.zeros((1, LANES), jnp.int32)
    for i, (start, end) in enumerate(zip(starts, ends)):
        first = jnp.where(lane == i, start, first)
        last = jnp.where(lane == i, end, last)
    rows = lax.broadcasted_iota(jnp.int32, (tok, LANES), 0)

    def in_doc(base):
        return (rows + base >= first) & (rows + base < last)

    apart = jnp.where(in_doc(anchor) | (lane >= len(starts)), 0.0, -APART).astype(jnp.bfloat16)
    for head in range(heads):
        queries[head * tok : (head + 1) * tok, :HD] = q_ref[:, head * HD : (head + 1) * HD]
        queries[head * tok : (head + 1) * tok, HD:] = apart
    key_cols = pl.ds(pl.multiple_of(group * HD, HD), HD)
    value_cols = pl.ds(pl.multiple_of((group + kv_local) * HD, HD), HD)

    def rows_of(back, cols):
        if isinstance(back, int) and back == 0:
            return mine_ref[0, :, cols]
        ours = mine_ref[back // 2, :, cols]
        other = theirs_ref[(back + 1) // 2 - odd, :, cols]
        return jnp.where(lax.rem(back, 2) == 0, ours, other)

    def score(back):
        marks = jnp.where(in_doc(anchor - back * tok), 1.0, 0.0).astype(jnp.bfloat16)
        keys = jnp.concatenate([rows_of(back, key_cols), marks], axis=1)
        return lax.dot_general(queries[...], keys, (((1,), (1,)), ((), ())), preferred_element_type=jnp.float32)

    def widest(s):
        top = s[:, :LANES]
        for at in range(LANES, tok, LANES):
            top = jnp.maximum(top, s[:, at : at + LANES])
        return top

    own = score(0)
    causal = lax.broadcasted_iota(jnp.int32, (tok, tok), 1) <= lax.broadcasted_iota(jnp.int32, (tok, tok), 0)
    for head in range(heads):
        part = slice(head * tok, (head + 1) * tok)
        s = jnp.where(causal, own[part], -APART)
        scores[0, part, :] = s
        tops[part, :] = widest(s)

    begin = jnp.int32(0)
    for start in starts[1:]:
        begin = jnp.where(anchor >= start, start, begin)
    earlier = (anchor - begin + tok - 1) // tok

    def look(back, carry):
        s = score(back)
        scores[back] = s
        tops[...] = jnp.maximum(tops[...], widest(s))
        return carry

    lax.fori_loop(1, earlier + 1, look, 0)
    tops[...] = jnp.broadcast_to(jnp.max(tops[...], axis=1, keepdims=True) * scale, tops.shape)

    def weighted(back):
        values = jnp.concatenate([rows_of(back, value_cols), jnp.ones((tok, HD), jnp.bfloat16)], axis=1)
        top = tops[...]
        weights = [
            jnp.exp2((scores[back, :, at : at + LANES] * scale - top).astype(jnp.bfloat16))
            for at in range(0, tok, LANES)
        ]
        return jnp.dot(jnp.concatenate(weights, axis=1), values, preferred_element_type=jnp.float32)

    acc[...] = weighted(0)

    def absorb(back, carry):
        acc[...] += weighted(back)
        return carry

    lax.fori_loop(1, earlier + 1, absorb, 0)
    order = place_ref[pl.ds(position, 1), :]
    move = (lax.broadcasted_iota(jnp.int32, (tok, tok), 0) == order).astype(jnp.float32).astype(jnp.bfloat16)
    for head in range(heads):
        part = slice(head * tok, (head + 1) * tok)
        result = (acc[part, :HD] / acc[part, HD:]).astype(jnp.bfloat16)
        moved = jnp.dot(move, result, preferred_element_type=jnp.float32)
        out_ref[:, head * HD : (head + 1) * HD] = moved.astype(jnp.bfloat16)


def attend(lengths, send_place, query_rows, mine, theirs, groups, so_far):
    tok, width = query_rows.shape
    kv_local = mine.shape[2] // (2 * HD)
    share = width // kv_local
    heads = share // HD
    reach = 2 * (mine.shape[0] - 1)
    count = groups[1] - groups[0]
    whole = lambda a: pl.BlockSpec(a.shape, lambda i: (0,) * a.ndim)
    in_specs = [
        pl.BlockSpec(memory_space=pltpu.SMEM),
        whole(send_place),
        pl.BlockSpec((tok, share), lambda i: (0, i + groups[0])),
        whole(mine),
        whole(theirs),
    ]
    operands = [lengths, send_place, query_rows, mine, theirs]
    aliases = {}
    if so_far is not None:
        aliases = {len(operands): 0}
        in_specs.append(pl.BlockSpec(memory_space=pl.ANY))
        operands.append(so_far)
    return pl.pallas_call(
        functools.partial(attend_kernel, kv_local, groups[0]),
        grid=(count,),
        in_specs=in_specs,
        out_specs=pl.BlockSpec((tok, share), lambda i: (0, i + groups[0])),
        out_shape=jax.ShapeDtypeStruct((tok, width), jnp.bfloat16),
        scratch_shapes=[
            pltpu.VMEM((heads * tok, 2 * HD), jnp.bfloat16),
            pltpu.VMEM((reach + 1, heads * tok, tok), jnp.float32),
            pltpu.VMEM((heads * tok, LANES), jnp.float32),
            pltpu.VMEM((heads * tok, 2 * HD), jnp.float32),
        ],
        input_output_aliases=aliases,
        compiler_params=pltpu.CompilerParams(vmem_limit_bytes=VMEM_LIMIT // 2 + 4 * (reach + 1) * heads * tok * tok),
        cost_estimate=pl.CostEstimate(
            flops=4 * tok * share * count * tok * 4,
            bytes_accessed=8 * tok * share * count,
            transcendentals=tok * tok * 4 * heads * count,
        ),
        name="attend",
    )(*operands)


def shifted(value, steps):
    count = lax.axis_size("seq")
    return lax.ppermute(value, "seq", [(source, source + steps) for source in range(count - steps)])


def with_partner(held):
    mine = jnp.stack(held)
    count = lax.axis_size("seq")
    return mine, lax.ppermute(mine, "seq", [(source, source ^ 1) for source in range(count)])


def even_back(value, reach):
    return [value] + [shifted(value, 2 * k) for k in range(1, (reach + 1) // 2 + 1)]


def local(
    x_branch,
    z_branch,
    conv_weight,
    conv_bias,
    xproj_weight,
    dt_weight,
    dt_bias,
    decay_rate,
    skip_gain,
    query_rows,
    key_rows,
    value_rows,
    lengths,
    destination,
):
    tok = x_branch.shape[0]
    n_seq = lax.axis_size("seq")
    n_mp = lax.axis_size("mp")
    low_rank = dt_weight.shape[0]
    reach = n_seq // 2
    run_rows = tok // n_seq
    kv_local = key_rows.shape[1] // HD
    fence = lax.optimization_barrier

    halo, kv = pack(x_branch, key_rows, value_rows)
    earlier_rows = shifted(halo, 1)
    held = even_back(kv, reach)
    send_place = ((destination // tok) * run_rows + destination % run_rows).reshape(n_seq, tok)

    inner_act, partial = conv_project(lengths, x_branch, earlier_rows, conv_weight, conv_bias, xproj_weight)
    _, *held = fence((partial, *held))
    pieces = lax.all_to_all(partial, "mp", split_axis=0, concat_axis=0, tiled=True)
    mine, theirs = with_partner(held)
    early = max(kv_local // 2, 1)
    attended = attend(lengths, send_place, query_rows, mine, theirs, (0, early), None)
    pieces, attended = fence((pieces, attended))
    summed = jnp.sum(pieces.reshape(n_mp, -1, tok).astype(jnp.float32), axis=0).astype(jnp.bfloat16)
    copies = jnp.broadcast_to(summed[None], (n_mp,) + summed.shape).reshape(partial.shape)
    copies, attended = fence((copies, attended))
    projected = lax.all_to_all(copies, "mp", split_axis=0, concat_axis=0, tiled=True)
    if early < kv_local:
        attended = attend(lengths, send_place, query_rows, mine, theirs, (early, kv_local), attended)
    projected, attended = fence((projected, attended))
    regrouped = lax.all_to_all(attended, "seq", split_axis=0, concat_axis=0, tiled=True)

    y, sums, state = local_scan(lengths, projected, dt_weight, dt_bias, decay_rate, skip_gain, inner_act)
    own, other = with_partner(even_back(state, reach))
    return tuple(join_states(projected, y, sums, z_branch, decay_rate, regrouped, own, other, low_rank, reach))


def solution(mesh):
    placed = (
        P("seq", "mp"),
        P("seq", "mp"),
        P(None, "mp"),
        P("mp"),
        P("mp", None),
        P(None, "mp"),
        P("mp"),
        P(None, "mp"),
        P("mp"),
        P("seq", "mp"),
        P("seq", "mp"),
        P("seq", "mp"),
        P(),
        P(),
    )
    return jax.shard_map(
        local,
        mesh=mesh,
        in_specs=placed,
        out_specs=(P("seq", "mp"), P("seq", "mp")),
        check_vma=False,
    )
```

```python
import functools

import jax
import jax.numpy as jnp
from jax import lax
from jax.experimental import pallas as pl
from jax.experimental.pallas import tpu as pltpu
from jax.sharding import PartitionSpec as P

HD = 128
LANES = 128
HALO = 16
LOG2E = 1.4426950408889634
RESET = 1e30
APART = 65536.0
VMEM_LIMIT = 32 * 1024 * 1024
VMEM_MOST = 56 * 1024 * 1024


def doc_edges(lengths_ref):
    starts, ends, total = [], [], 0
    for i in range(lengths_ref.shape[0]):
        starts.append(total)
        total = total + lengths_ref[i]
        ends.append(total)
    return starts, ends


def doc_start(places, starts):
    found = jnp.zeros_like(places)
    for start in starts[1:]:
        found = jnp.where(places >= start, start, found)
    return found


def channel_chunk(channels):
    return 512 if channels % 512 == 0 else channels


def pack_kernel(x_ref, k_ref, v_ref, halo_ref, kv_ref):
    width = k_ref.shape[1]
    halo_ref[...] = x_ref[...]
    kv_ref[:, :width] = k_ref[...]
    kv_ref[:, width:] = v_ref[...]


def pack(x_branch, key_rows, value_rows):
    tok, channels = x_branch.shape
    width = key_rows.shape[1]
    whole = lambda rows, columns: pl.BlockSpec((rows, columns), lambda i: (0, 0))
    return pl.pallas_call(
        pack_kernel,
        grid=(1,),
        in_specs=[
            pl.BlockSpec((HALO, channels), lambda i: (tok // HALO - 1, 0)),
            whole(tok, width),
            whole(tok, width),
        ],
        out_specs=[whole(HALO, channels), whole(tok, 2 * width)],
        out_shape=[
            jax.ShapeDtypeStruct((HALO, channels), x_branch.dtype),
            jax.ShapeDtypeStruct((tok, 2 * width), key_rows.dtype),
        ],
        compiler_params=pltpu.CompilerParams(vmem_limit_bytes=VMEM_MOST),
        cost_estimate=pl.CostEstimate(flops=0, bytes_accessed=16 * tok * width, transcendentals=0),
        name="pack",
    )(x_branch, key_rows, value_rows)


def conv_kernel(lengths_ref, x_ref, halo_ref, w_ref, b_ref, xp_ref, inner_ref, part_ref, ext, acc):
    tok, chunk = x_ref.shape
    starts, _ = doc_edges(lengths_ref)
    anchor = lax.axis_index("seq") * tok
    places = anchor + lax.broadcasted_iota(jnp.int32, (tok, LANES), 0)
    depth = places - doc_start(places, starts)
    ext[0:HALO, :] = halo_ref[...].astype(jnp.float32)
    ext[HALO:, :] = x_ref[...].astype(jnp.float32)
    for lane in range(0, chunk, LANES):
        cols = slice(lane, lane + LANES)
        total = b_ref[:, cols] + w_ref[0:1, cols] * ext[HALO:, cols]
        for lag in range(1, w_ref.shape[0]):
            window = ext[HALO - lag : HALO - lag + tok, cols]
            total += w_ref[lag : lag + 1, cols] * jnp.where(depth >= lag, window, 0.0)
        act = total * (0.5 + 0.5 * jnp.tanh(0.5 * total))
        inner_ref[:, cols] = act.astype(jnp.bfloat16)
    product = lax.dot_general(
        xp_ref[...], inner_ref[...], (((1,), (1,)), ((), ())), preferred_element_type=jnp.float32
    )
    at = pl.program_id(0)

    @pl.when(at == 0)
    def _():
        acc[...] = product

    @pl.when(at > 0)
    def _():
        acc[...] += product

    @pl.when(at == pl.num_programs(0) - 1)
    def _():
        part_ref[...] = acc[...].astype(jnp.bfloat16)


def conv_project(lengths, x_branch, halo, conv_weight, conv_bias, xproj_weight):
    tok, channels = x_branch.shape
    width = xproj_weight.shape[1]
    taps = conv_weight.shape[0]
    chunk = channel_chunk(channels)
    return pl.pallas_call(
        conv_kernel,
        grid=(channels // chunk,),
        in_specs=[
            pl.BlockSpec(memory_space=pltpu.SMEM),
            pl.BlockSpec((tok, chunk), lambda i: (0, i)),
            pl.BlockSpec((HALO, chunk), lambda i: (0, i)),
            pl.BlockSpec((taps, chunk), lambda i: (0, i)),
            pl.BlockSpec((1, chunk), lambda i: (0, i)),
            pl.BlockSpec((width, chunk), lambda i: (0, i)),
        ],
        out_specs=[
            pl.BlockSpec((tok, chunk), lambda i: (0, i)),
            pl.BlockSpec((width, tok), lambda i: (0, 0)),
        ],
        out_shape=[
            jax.ShapeDtypeStruct((tok, channels), jnp.bfloat16),
            jax.ShapeDtypeStruct((width, tok), jnp.bfloat16),
        ],
        scratch_shapes=[
            pltpu.VMEM((tok + HALO, chunk), jnp.float32),
            pltpu.VMEM((width, tok), jnp.float32),
        ],
        compiler_params=pltpu.CompilerParams(vmem_limit_bytes=VMEM_MOST),
        cost_estimate=pl.CostEstimate(
            flops=80 * tok * channels * width, bytes_accessed=8 * tok * channels, transcendentals=tok * channels
        ),
        name="conv_project",
    )(lengths, x_branch, halo, conv_weight, conv_bias.reshape(1, channels), xproj_weight.T)


def spread(columns):
    tok, k = columns.shape
    own = lax.broadcasted_iota(jnp.int32, (k, k), 0) == lax.broadcasted_iota(jnp.int32, (k, k), 1)
    picked = jnp.where(own[None], columns.astype(jnp.float32)[:, None, :], 0.0).reshape(tok * k, k)
    ones = jnp.ones((k, LANES), jnp.bfloat16)
    return jnp.dot(picked.astype(jnp.bfloat16), ones, preferred_element_type=jnp.float32)


def lane_tiles(value):
    return [value[:, i : i + LANES] for i in range(0, value.shape[1], LANES)]


ROWS = 8
UNROLL = 2 * ROWS


def fold_rows(parts, lane, group):
    row = parts[lane, pl.ds(group * ROWS, ROWS, stride=ROWS), :]
    for n in range(1, ROWS):
        row = row + parts[lane, pl.ds(group * ROWS + n, ROWS, stride=ROWS), :]
    return row


def halves(term):
    total = term[0:ROWS]
    for more in range(ROWS, term.shape[0], ROWS):
        total = total + term[more : more + ROWS]
    return total


def keep_terms(parts, terms):
    for i, of_lane in enumerate(terms):
        for u, term in enumerate(of_lane):
            parts[i, u * ROWS : (u + 1) * ROWS, :] = term


def local_kernel(
    lengths_ref,
    proj_ref,
    dtw_ref,
    bias_ref,
    rate_ref,
    skip_ref,
    inner_ref,
    y_ref,
    sum_ref,
    state_ref,
    low_cols,
    bc_spread,
    step_ref,
    drive_ref,
    parts,
    totals,
):
    tok, chunk = inner_ref.shape
    states = rate_ref.shape[0]
    low_rank = dtw_ref.shape[0]
    tiles = chunk // LANES
    starts, _ = doc_edges(lengths_ref)
    at = pl.program_id(0)

    @pl.when(at == 0)
    def _():
        low_cols[...] = proj_ref[:low_rank, :].astype(jnp.float32).T.astype(jnp.bfloat16)
        bc_spread[...] = spread(proj_ref[low_rank:, :].astype(jnp.float32).T)

    anchor = lax.axis_index("seq") * tok
    places = anchor + lax.broadcasted_iota(jnp.int32, (tok, LANES), 0)
    at_start = places == doc_start(places, starts)
    upto = lax.broadcasted_iota(jnp.int32, (tok, tok), 0) >= lax.broadcasted_iota(jnp.int32, (tok, tok), 1)
    upto = upto.astype(jnp.float32).astype(jnp.bfloat16)
    raw = jnp.dot(low_cols[...], dtw_ref[...], preferred_element_type=jnp.float32)
    for i in range(tiles):
        cols = slice(i * LANES, (i + 1) * LANES)
        biased = raw[:, cols] + bias_ref[:, cols]
        step = jnp.maximum(biased, 0.0) + jnp.log(1.0 + jnp.exp(-jnp.abs(biased)))
        drive = step * inner_ref[:, cols].astype(jnp.float32)
        drive_ref[:, :, cols] = drive.reshape(tok // ROWS, ROWS, LANES)
        step = jnp.where(at_start, RESET, step)
        step_ref[:, :, cols] = step.reshape(tok // ROWS, ROWS, LANES)
        summed = jnp.dot(upto, step.astype(jnp.bfloat16), preferred_element_type=jnp.float32)
        sum_ref[:, :, cols] = summed.reshape(tok // ROWS, ROWS, LANES)
        totals[at * tiles + i] = summed[tok - 1 : tok]
    rate2 = lane_tiles(rate_ref[...] * (-LOG2E))

    def body(turn, state):
        base = pl.multiple_of(turn * UNROLL, UNROLL)
        spread_at = pl.multiple_of(turn * UNROLL * 2 * states, UNROLL * 2 * states)
        state, terms = list(state), [[] for _ in range(tiles)]
        for first in range(0, tiles, 2):
            for u in range(UNROLL):
                tile = turn * (UNROLL // ROWS) + u // ROWS
                row = slice(u % ROWS, u % ROWS + 1)
                b_rows = bc_spread[pl.ds(spread_at + u * 2 * states, states), :]
                c_rows = bc_spread[pl.ds(spread_at + u * 2 * states + states, states), :]
                for i in range(first, min(first + 2, tiles)):
                    cols = slice(i * LANES, (i + 1) * LANES)
                    decay = jnp.exp2(rate2[i] * step_ref[tile, row, cols])
                    state[i] = decay * state[i] + b_rows * drive_ref[tile, row, cols]
                    terms[i].append(halves(c_rows * state[i]))
        keep_terms(parts, terms)
        for group in range(0, UNROLL, ROWS):
            for i in range(tiles):
                y_ref[pl.ds(base + group, ROWS), i * LANES : (i + 1) * LANES] = fold_rows(parts, i, group)
        return state

    end = lax.fori_loop(0, tok // UNROLL, body, [jnp.zeros_like(r) for r in rate2])
    y_ref[...] += skip_ref[...] * inner_ref[...].astype(jnp.float32)
    for i in range(tiles):
        state_ref[at * tiles + i] = end[i].astype(jnp.bfloat16)

    @pl.when(at == pl.num_programs(0) - 1)
    def _():
        lanes = totals.shape[0]
        row = lax.broadcasted_iota(jnp.int32, (states, LANES), 0)
        table = jnp.zeros((states, LANES), jnp.float32)
        for i in range(lanes):
            table = jnp.where(row == i, totals[i], table)
        high = table.astype(jnp.bfloat16)
        state_ref[lanes] = high
        state_ref[lanes + 1] = (table - high.astype(jnp.float32)).astype(jnp.bfloat16)


def local_scan(lengths, projected, dt_weight, dt_bias, decay_rate, skip_gain, inner_act):
    tok, channels = inner_act.shape
    low_rank = dt_weight.shape[0]
    states = decay_rate.shape[0]
    width = projected.shape[0]
    chunk = channel_chunk(channels)
    lanes = channels // LANES
    by_chunk = lambda rows: pl.BlockSpec((rows, chunk), lambda i: (0, i))
    return pl.pallas_call(
        local_kernel,
        grid=(channels // chunk,),
        in_specs=[
            pl.BlockSpec(memory_space=pltpu.SMEM),
            pl.BlockSpec((width, tok), lambda i: (0, 0)),
            by_chunk(low_rank),
            by_chunk(1),
            by_chunk(states),
            by_chunk(1),
            by_chunk(tok),
        ],
        out_specs=[
            by_chunk(tok),
            pl.BlockSpec((tok // ROWS, ROWS, chunk), lambda i: (0, 0, i)),
            pl.BlockSpec((lanes + 2, states, LANES), lambda i: (0, 0, 0)),
        ],
        out_shape=[
            jax.ShapeDtypeStruct((tok, channels), jnp.float32),
            jax.ShapeDtypeStruct((tok // ROWS, ROWS, channels), jnp.float32),
            jax.ShapeDtypeStruct((lanes + 2, states, LANES), jnp.bfloat16),
        ],
        scratch_shapes=[
            pltpu.VMEM((tok, low_rank), jnp.bfloat16),
            pltpu.VMEM((tok * 2 * states, LANES), jnp.float32),
            pltpu.VMEM((tok // ROWS, ROWS, chunk), jnp.float32),
            pltpu.VMEM((tok // ROWS, ROWS, chunk), jnp.float32),
            pltpu.VMEM((chunk // LANES, UNROLL * ROWS, LANES), jnp.float32),
            pltpu.VMEM((lanes, 1, LANES), jnp.float32),
        ],
        compiler_params=pltpu.CompilerParams(vmem_limit_bytes=VMEM_MOST),
        cost_estimate=pl.CostEstimate(
            flops=12 * tok * channels * states,
            bytes_accessed=12 * tok * channels,
            transcendentals=tok * channels * states,
        ),
        name="local_scan",
    )(
        lengths,
        projected,
        dt_weight,
        dt_bias.reshape(1, channels),
        decay_rate,
        skip_gain.reshape(1, channels),
        inner_act,
    )


def join_kernel(
    low_rank,
    reach,
    proj_ref,
    y_ref,
    sum_ref,
    z_ref,
    rate_ref,
    moved_ref,
    mine_ref,
    theirs_ref,
    out_ref,
    regrouped_ref,
    c_spread,
    parts,
):
    tok, chunk = y_ref.shape
    states = rate_ref.shape[0]
    tiles = chunk // LANES
    lanes = mine_ref.shape[1] - 2
    at = pl.program_id(0)

    @pl.when(at == 0)
    def _():
        c_spread[...] = spread(proj_ref[low_rank + states :, :].astype(jnp.float32).T).astype(jnp.bfloat16)

    regrouped_ref[...] = moved_ref[...]

    rate = lane_tiles(-rate_ref[...])
    row = lax.broadcasted_iota(jnp.int32, (states, LANES), 0)
    entering = [jnp.zeros_like(r) for r in rate]
    odd = lax.rem(lax.axis_index("seq"), 2)
    for back in range(reach, 0, -1):
        ref, which = (mine_ref, back // 2) if back % 2 == 0 else (theirs_ref, (back + 1) // 2 - odd)
        table = ref[which, lanes].astype(jnp.float32) + ref[which, lanes + 1].astype(jnp.float32)
        for i, before in enumerate(entering):
            total = jnp.sum(jnp.where(row == at * tiles + i, table, 0.0), axis=0, keepdims=True)
            entering[i] = jnp.exp(rate[i] * total) * before + ref[which, at * tiles + i].astype(jnp.float32)
    entering = [e.astype(jnp.bfloat16) for e in entering]

    def body(turn, carry):
        rows = pl.ds(pl.multiple_of(turn * UNROLL, UNROLL), UNROLL)
        spread_at = pl.multiple_of(turn * UNROLL * states, UNROLL * states)
        terms = [[] for _ in range(tiles)]
        for first in range(0, tiles, 2):
            for u in range(UNROLL):
                tile = turn * (UNROLL // ROWS) + u // ROWS
                c_rows = c_spread[pl.ds(spread_at + u * states, states), :]
                for i in range(first, min(first + 2, tiles)):
                    power = rate[i] * sum_ref[tile, u % ROWS : u % ROWS + 1, i * LANES : (i + 1) * LANES]
                    term = jnp.exp(power.astype(jnp.bfloat16)) * entering[i] * c_rows
                    terms[i].append(halves(term.astype(jnp.float32)))
        keep_terms(parts, terms)
        for i in range(tiles):
            cols = slice(i * LANES, (i + 1) * LANES)
            more = jnp.concatenate([fold_rows(parts, i, group) for group in range(0, UNROLL, ROWS)], axis=0)
            z = z_ref[rows, cols].astype(jnp.float32)
            gate = z * (0.5 + 0.5 * jnp.tanh(0.5 * z))
            out_ref[rows, cols] = ((y_ref[rows, cols] + more) * gate).astype(jnp.bfloat16)
        return carry

    lax.fori_loop(0, tok // UNROLL, body, 0)


def join_states(projected, y, sums, z_branch, decay_rate, moved, mine, theirs, low_rank, reach):
    tok, channels = z_branch.shape
    states = decay_rate.shape[0]
    width = projected.shape[0]
    chunk = channel_chunk(channels)
    by_chunk = lambda rows: pl.BlockSpec((rows, chunk), lambda i: (0, i))
    return pl.pallas_call(
        functools.partial(join_kernel, low_rank, reach),
        grid=(channels // chunk,),
        in_specs=[
            pl.BlockSpec((width, tok), lambda i: (0, 0)),
            by_chunk(tok),
            pl.BlockSpec((tok // ROWS, ROWS, chunk), lambda i: (0, 0, i)),
            by_chunk(tok),
            by_chunk(states),
            by_chunk(tok),
            pl.BlockSpec(mine.shape, lambda i: (0, 0, 0, 0)),
            pl.BlockSpec(theirs.shape, lambda i: (0, 0, 0, 0)),
        ],
        out_specs=[by_chunk(tok), by_chunk(tok)],
        out_shape=[jax.ShapeDtypeStruct((tok, channels), jnp.bfloat16)] * 2,
        scratch_shapes=[
            pltpu.VMEM((tok * states, LANES), jnp.bfloat16),
            pltpu.VMEM((chunk // LANES, UNROLL * ROWS, LANES), jnp.float32),
        ],
        compiler_params=pltpu.CompilerParams(vmem_limit_bytes=VMEM_MOST),
        cost_estimate=pl.CostEstimate(
            flops=8 * tok * channels * states,
            bytes_accessed=14 * tok * channels,
            transcendentals=tok * channels * states,
        ),
        name="join_states",
    )(projected, y, sums, z_branch, decay_rate, moved, mine, theirs)


def attend_kernel(kv_local, first_group, lengths_ref, place_ref, q_ref, mine_ref, theirs_ref, *refs):
    out_ref, queries, scores, tops, acc = refs[-5:]
    tok = q_ref.shape[0]
    heads = q_ref.shape[1] // HD
    group = pl.program_id(0) + first_group
    position = lax.axis_index("seq")
    odd = lax.rem(position, 2)
    anchor = position * tok
    scale = HD**-0.5
    starts, ends = doc_edges(lengths_ref)
    lane = lax.broadcasted_iota(jnp.int32, (1, LANES), 1)
    first = jnp.full((1, LANES), 2**30, jnp.int32)
    last = jnp.zeros((1, LANES), jnp.int32)
    for i, (start, end) in enumerate(zip(starts, ends)):
        first = jnp.where(lane == i, start, first)
        last = jnp.where(lane == i, end, last)
    rows = lax.broadcasted_iota(jnp.int32, (tok, LANES), 0)

    def in_doc(base):
        return (rows + base >= first) & (rows + base < last)

    apart = jnp.where(in_doc(anchor) | (lane >= len(starts)), 0.0, -APART).astype(jnp.bfloat16)
    for head in range(heads):
        queries[head * tok : (head + 1) * tok, :HD] = q_ref[:, head * HD : (head + 1) * HD]
        queries[head * tok : (head + 1) * tok, HD:] = apart
    key_cols = pl.ds(pl.multiple_of(group * HD, HD), HD)
    value_cols = pl.ds(pl.multiple_of((group + kv_local) * HD, HD), HD)

    def rows_of(back, cols):
        if isinstance(back, int) and back == 0:
            return mine_ref[0, :, cols]
        ours = mine_ref[back // 2, :, cols]
        other = theirs_ref[(back + 1) // 2 - odd, :, cols]
        return jnp.where(lax.rem(back, 2) == 0, ours, other)

    def score(back):
        marks = jnp.where(in_doc(anchor - back * tok), 1.0, 0.0).astype(jnp.bfloat16)
        keys = jnp.concatenate([rows_of(back, key_cols), marks], axis=1)
        return lax.dot_general(queries[...], keys, (((1,), (1,)), ((), ())), preferred_element_type=jnp.float32)

    def widest(s):
        top = s[:, :LANES]
        for at in range(LANES, tok, LANES):
            top = jnp.maximum(top, s[:, at : at + LANES])
        return top

    own = score(0)
    causal = lax.broadcasted_iota(jnp.int32, (tok, tok), 1) <= lax.broadcasted_iota(jnp.int32, (tok, tok), 0)
    for head in range(heads):
        part = slice(head * tok, (head + 1) * tok)
        s = jnp.where(causal, own[part], -APART)
        scores[0, part, :] = s
        tops[part, :] = widest(s)

    begin = jnp.int32(0)
    for start in starts[1:]:
        begin = jnp.where(anchor >= start, start, begin)
    earlier = (anchor - begin + tok - 1) // tok

    def look(back, carry):
        s = score(back)
        scores[back] = s
        tops[...] = jnp.maximum(tops[...], widest(s))
        return carry

    lax.fori_loop(1, earlier + 1, look, 0)
    tops[...] = jnp.broadcast_to(jnp.max(tops[...], axis=1, keepdims=True) * scale, tops.shape)

    def weighted(back):
        values = jnp.concatenate([rows_of(back, value_cols), jnp.ones((tok, HD), jnp.bfloat16)], axis=1)
        top = tops[...]
        weights = [
            jnp.exp((scores[back, :, at : at + LANES] * scale - top).astype(jnp.bfloat16))
            for at in range(0, tok, LANES)
        ]
        return jnp.dot(jnp.concatenate(weights, axis=1), values, preferred_element_type=jnp.float32)

    acc[...] = weighted(0)

    def absorb(back, carry):
        acc[...] += weighted(back)
        return carry

    lax.fori_loop(1, earlier + 1, absorb, 0)
    order = place_ref[pl.ds(position, 1), :]
    move = (lax.broadcasted_iota(jnp.int32, (tok, tok), 0) == order).astype(jnp.float32).astype(jnp.bfloat16)
    for head in range(heads):
        part = slice(head * tok, (head + 1) * tok)
        result = (acc[part, :HD] / acc[part, HD:]).astype(jnp.bfloat16)
        moved = jnp.dot(move, result, preferred_element_type=jnp.float32)
        out_ref[:, head * HD : (head + 1) * HD] = moved.astype(jnp.bfloat16)


def attend(lengths, send_place, query_rows, mine, theirs, groups, so_far):
    tok, width = query_rows.shape
    kv_local = mine.shape[2] // (2 * HD)
    share = width // kv_local
    heads = share // HD
    reach = 2 * (mine.shape[0] - 1)
    count = groups[1] - groups[0]
    whole = lambda a: pl.BlockSpec(a.shape, lambda i: (0,) * a.ndim)
    in_specs = [
        pl.BlockSpec(memory_space=pltpu.SMEM),
        whole(send_place),
        pl.BlockSpec((tok, share), lambda i: (0, i + groups[0])),
        whole(mine),
        whole(theirs),
    ]
    operands = [lengths, send_place, query_rows, mine, theirs]
    aliases = {}
    if so_far is not None:
        aliases = {len(operands): 0}
        in_specs.append(pl.BlockSpec(memory_space=pl.ANY))
        operands.append(so_far)
    return pl.pallas_call(
        functools.partial(attend_kernel, kv_local, groups[0]),
        grid=(count,),
        in_specs=in_specs,
        out_specs=pl.BlockSpec((tok, share), lambda i: (0, i + groups[0])),
        out_shape=jax.ShapeDtypeStruct((tok, width), jnp.bfloat16),
        scratch_shapes=[
            pltpu.VMEM((heads * tok, 2 * HD), jnp.bfloat16),
            pltpu.VMEM((reach + 1, heads * tok, tok), jnp.float32),
            pltpu.VMEM((heads * tok, LANES), jnp.float32),
            pltpu.VMEM((heads * tok, 2 * HD), jnp.float32),
        ],
        input_output_aliases=aliases,
        compiler_params=pltpu.CompilerParams(vmem_limit_bytes=VMEM_LIMIT // 2 + 4 * (reach + 1) * heads * tok * tok),
        cost_estimate=pl.CostEstimate(
            flops=tok * share * count, bytes_accessed=tok * share * count, transcendentals=0
        ),
        name="attend",
    )(*operands)


def shifted(value, steps):
    count = lax.axis_size("seq")
    return lax.ppermute(value, "seq", [(source, source + steps) for source in range(count - steps)])


def with_partner(held):
    mine = jnp.stack(held)
    count = lax.axis_size("seq")
    return mine, lax.ppermute(mine, "seq", [(source, source ^ 1) for source in range(count)])


def even_back(value, reach):
    return [value] + [shifted(value, 2 * k) for k in range(1, (reach + 1) // 2 + 1)]


def local(
    x_branch,
    z_branch,
    conv_weight,
    conv_bias,
    xproj_weight,
    dt_weight,
    dt_bias,
    decay_rate,
    skip_gain,
    query_rows,
    key_rows,
    value_rows,
    lengths,
    destination,
):
    tok = x_branch.shape[0]
    n_seq = lax.axis_size("seq")
    n_mp = lax.axis_size("mp")
    low_rank = dt_weight.shape[0]
    reach = n_seq // 2
    run_rows = tok // n_seq
    kv_local = key_rows.shape[1] // HD
    fence = lax.optimization_barrier

    halo, kv = pack(x_branch, key_rows, value_rows)
    earlier_rows = shifted(halo, 1)
    held = even_back(kv, reach)
    send_place = ((destination // tok) * run_rows + destination % run_rows).reshape(n_seq, tok)

    inner_act, partial = conv_project(lengths, x_branch, earlier_rows, conv_weight, conv_bias, xproj_weight)
    _, *held = fence((partial, *held))
    pieces = lax.all_to_all(partial, "mp", split_axis=0, concat_axis=0, tiled=True)
    mine, theirs = with_partner(held)
    early = max(kv_local // 2, 1)
    attended = attend(lengths, send_place, query_rows, mine, theirs, (0, early), None)
    pieces, attended = fence((pieces, attended))
    summed = jnp.sum(pieces.reshape(n_mp, -1, tok).astype(jnp.float32), axis=0).astype(jnp.bfloat16)
    copies = jnp.broadcast_to(summed[None], (n_mp,) + summed.shape).reshape(partial.shape)
    copies, attended = fence((copies, attended))
    projected = lax.all_to_all(copies, "mp", split_axis=0, concat_axis=0, tiled=True)
    if early < kv_local:
        attended = attend(lengths, send_place, query_rows, mine, theirs, (early, kv_local), attended)
    projected, attended = fence((projected, attended))
    regrouped = lax.all_to_all(attended, "seq", split_axis=0, concat_axis=0, tiled=True)

    y, sums, state = local_scan(lengths, projected, dt_weight, dt_bias, decay_rate, skip_gain, inner_act)
    own, other = with_partner(even_back(state, reach))
    return tuple(join_states(projected, y, sums, z_branch, decay_rate, regrouped, own, other, low_rank, reach))


def solution(mesh):
    placed = (
        P("seq", "mp"),
        P("seq", "mp"),
        P(None, "mp"),
        P("mp"),
        P("mp", None),
        P(None, "mp"),
        P("mp"),
        P(None, "mp"),
        P("mp"),
        P("seq", "mp"),
        P("seq", "mp"),
        P("seq", "mp"),
        P(),
        P(),
    )
    return jax.shard_map(
        local,
        mesh=mesh,
        in_specs=placed,
        out_specs=(P("seq", "mp"), P("seq", "mp")),
        check_vma=False,
    )
```

```python
import functools

import jax
import jax.numpy as jnp
from jax import lax
from jax.experimental import pallas as pl
from jax.experimental.pallas import tpu as pltpu
from jax.sharding import PartitionSpec as P

HD = 128
LANES = 128
HALO = 16
LOG2E = 1.4426950408889634
RESET = 1e30
APART = 65536.0
VMEM_LIMIT = 32 * 1024 * 1024
VMEM_MOST = 56 * 1024 * 1024


def doc_edges(lengths_ref):
    starts, ends, total = [], [], 0
    for i in range(lengths_ref.shape[0]):
        starts.append(total)
        total = total + lengths_ref[i]
        ends.append(total)
    return starts, ends


def doc_start(places, starts):
    found = jnp.zeros_like(places)
    for start in starts[1:]:
        found = jnp.where(places >= start, start, found)
    return found


def channel_chunk(channels):
    return 512 if channels % 512 == 0 else channels


def pack_kernel(x_ref, k_ref, v_ref, halo_ref, kv_ref):
    width = k_ref.shape[1]
    halo_ref[...] = x_ref[...]
    kv_ref[:, :width] = k_ref[...]
    kv_ref[:, width:] = v_ref[...]


def pack(x_branch, key_rows, value_rows):
    tok, channels = x_branch.shape
    width = key_rows.shape[1]
    whole = lambda rows, columns: pl.BlockSpec((rows, columns), lambda i: (0, 0))
    return pl.pallas_call(
        pack_kernel,
        grid=(1,),
        in_specs=[
            pl.BlockSpec((HALO, channels), lambda i: (tok // HALO - 1, 0)),
            whole(tok, width),
            whole(tok, width),
        ],
        out_specs=[whole(HALO, channels), whole(tok, 2 * width)],
        out_shape=[
            jax.ShapeDtypeStruct((HALO, channels), x_branch.dtype),
            jax.ShapeDtypeStruct((tok, 2 * width), key_rows.dtype),
        ],
        compiler_params=pltpu.CompilerParams(vmem_limit_bytes=VMEM_MOST),
        cost_estimate=pl.CostEstimate(flops=0, bytes_accessed=16 * tok * width, transcendentals=0),
        name="pack",
    )(x_branch, key_rows, value_rows)


def conv_kernel(lengths_ref, x_ref, halo_ref, w_ref, b_ref, xp_ref, inner_ref, part_ref, ext, acc):
    tok, chunk = x_ref.shape
    starts, _ = doc_edges(lengths_ref)
    anchor = lax.axis_index("seq") * tok
    places = anchor + lax.broadcasted_iota(jnp.int32, (tok, LANES), 0)
    depth = places - doc_start(places, starts)
    ext[0:HALO, :] = halo_ref[...].astype(jnp.float32)
    ext[HALO:, :] = x_ref[...].astype(jnp.float32)
    for lane in range(0, chunk, LANES):
        cols = slice(lane, lane + LANES)
        total = b_ref[:, cols] + w_ref[0:1, cols] * ext[HALO:, cols]
        for lag in range(1, w_ref.shape[0]):
            window = ext[HALO - lag : HALO - lag + tok, cols]
            total += w_ref[lag : lag + 1, cols] * jnp.where(depth >= lag, window, 0.0)
        act = total * (0.5 + 0.5 * jnp.tanh(0.5 * total))
        inner_ref[:, cols] = act.astype(jnp.bfloat16)
    product = lax.dot_general(
        xp_ref[...], inner_ref[...], (((1,), (1,)), ((), ())), preferred_element_type=jnp.float32
    )
    at = pl.program_id(0)

    @pl.when(at == 0)
    def _():
        acc[...] = product

    @pl.when(at > 0)
    def _():
        acc[...] += product

    @pl.when(at == pl.num_programs(0) - 1)
    def _():
        part_ref[...] = acc[...].astype(jnp.bfloat16)


def conv_project(lengths, x_branch, halo, conv_weight, conv_bias, xproj_weight):
    tok, channels = x_branch.shape
    width = xproj_weight.shape[1]
    taps = conv_weight.shape[0]
    chunk = channel_chunk(channels)
    return pl.pallas_call(
        conv_kernel,
        grid=(channels // chunk,),
        in_specs=[
            pl.BlockSpec(memory_space=pltpu.SMEM),
            pl.BlockSpec((tok, chunk), lambda i: (0, i)),
            pl.BlockSpec((HALO, chunk), lambda i: (0, i)),
            pl.BlockSpec((taps, chunk), lambda i: (0, i)),
            pl.BlockSpec((1, chunk), lambda i: (0, i)),
            pl.BlockSpec((width, chunk), lambda i: (0, i)),
        ],
        out_specs=[
            pl.BlockSpec((tok, chunk), lambda i: (0, i)),
            pl.BlockSpec((width, tok), lambda i: (0, 0)),
        ],
        out_shape=[
            jax.ShapeDtypeStruct((tok, channels), jnp.bfloat16),
            jax.ShapeDtypeStruct((width, tok), jnp.bfloat16),
        ],
        scratch_shapes=[
            pltpu.VMEM((tok + HALO, chunk), jnp.float32),
            pltpu.VMEM((width, tok), jnp.float32),
        ],
        compiler_params=pltpu.CompilerParams(vmem_limit_bytes=VMEM_MOST),
        cost_estimate=pl.CostEstimate(
            flops=80 * tok * channels * width, bytes_accessed=8 * tok * channels, transcendentals=tok * channels
        ),
        name="conv_project",
    )(lengths, x_branch, halo, conv_weight, conv_bias.reshape(1, channels), xproj_weight.T)


ROWS = 8
PAIR = 2 * ROWS
BLOCK = 64


def spread(columns):
    tok, k = columns.shape
    own = lax.broadcasted_iota(jnp.int32, (k, k), 0) == lax.broadcasted_iota(jnp.int32, (k, k), 1)
    picked = jnp.where(own[None], columns.astype(jnp.float32)[:, None, :], 0.0).reshape(tok * k, k)
    ones = jnp.ones((k, LANES), jnp.bfloat16)
    return jnp.dot(picked.astype(jnp.bfloat16), ones, preferred_element_type=jnp.float32).reshape(tok, k, LANES)


def lane(tile):
    return slice(tile * LANES, (tile + 1) * LANES)


def sublanes(tile):
    return slice(tile * ROWS, (tile + 1) * ROWS)


def by_register(rate_ref, rates):
    states = rate_ref.shape[0]
    count = rates.shape[0] // states
    for n in range(states):
        for h in range(count):
            tiles = [rate_ref[n : n + 1, lane(h * ROWS + j)] for j in range(ROWS)]
            rates[n * count + h] = jnp.concatenate(tiles, axis=0) * (-LOG2E)


def local_kernel(
    lengths_ref,
    proj_ref,
    dtw_ref,
    bias_ref,
    rate_ref,
    inner_ref,
    y_ref,
    sum_ref,
    state_ref,
    low_cols,
    bc_spread,
    raw,
    rates,
    step_tiles,
    drive_tiles,
    carry,
):
    tok = proj_ref.shape[1]
    block, channels = inner_ref.shape
    states = rate_ref.shape[0]
    low_rank = dtw_ref.shape[0]
    tiles = channels // LANES
    count = tiles // ROWS
    starts, _ = doc_edges(lengths_ref)
    at = pl.program_id(0)

    @pl.when(at == 0)
    def _():
        low_cols[...] = proj_ref[:low_rank, :].astype(jnp.float32).T.astype(jnp.bfloat16)
        bc_spread[...] = spread(proj_ref[low_rank:, :].astype(jnp.float32).T)
        by_register(rate_ref, rates)
        carry[...] = jnp.zeros_like(carry)
        for first in range(0, tiles, 4):
            cols = slice(first * LANES, (first + 4) * LANES)
            part = jnp.dot(low_cols[...], dtw_ref[:, cols], preferred_element_type=jnp.float32)
            for i in range(4):
                raw[:, sublanes(first + i), :] = part[:, lane(i)].reshape(tok // ROWS, ROWS, LANES)

    def steps(pair, unused):
        rows = pl.ds(pl.multiple_of(pair * PAIR, PAIR), PAIR)
        places = lax.axis_index("seq") * tok + at * block + pair * PAIR
        places = places + lax.broadcasted_iota(jnp.int32, (PAIR, LANES), 0)
        at_start = places == doc_start(places, starts)
        for tile in range(tiles):
            inner = inner_ref[rows, lane(tile)].astype(jnp.float32)
            bias = bias_ref[:, lane(tile)]
            for k in range(2):
                biased = raw[at * (block // ROWS) + 2 * pair + k, sublanes(tile), :] + bias
                step = jnp.maximum(biased, 0.0) + jnp.log(1.0 + jnp.exp(-jnp.abs(biased)))
                drive_tiles[2 * pair + k, sublanes(tile), :] = step * inner[sublanes(k)]
                step_tiles[2 * pair + k, sublanes(tile), :] = jnp.where(at_start[sublanes(k)], RESET, step)
        return unused

    lax.fori_loop(0, block // PAIR, steps, 0)

    def scan(t8, held):
        held, total = list(held[0]), list(held[1])
        for first in range(0, ROWS, 4):
            done = []
            for r in range(first, first + 4):
                token = at * block + t8 * ROWS + r
                picked = [pl.ds(r + h * ROWS * ROWS, ROWS, stride=ROWS) for h in range(count)]
                step = [step_tiles[t8, rows, :] for rows in picked]
                drive = [drive_tiles[t8, rows, :] for rows in picked]
                out = [None] * count
                for n in range(states):
                    b_row = bc_spread[token, n : n + 1, :]
                    c_row = bc_spread[token, states + n : states + n + 1, :]
                    for h in range(count):
                        i = n * count + h
                        held[i] = jnp.exp2(rates[i] * step[h]) * held[i] + b_row * drive[h]
                        term = c_row * held[i]
                        out[h] = term if out[h] is None else out[h] + term
                total = [so_far + more for so_far, more in zip(total, step)]
                done.append((out, total))
            for k, (out, so_far) in enumerate(done):
                for h in range(count):
                    y_ref[t8 * ROWS + first + k, sublanes(h), :] = out[h]
                    sum_ref[t8 * ROWS + first + k, sublanes(h), :] = so_far[h]
        return held, total

    kept = states * count
    held = ([carry[i] for i in range(kept)], [carry[kept + h] for h in range(count)])
    held, total = lax.fori_loop(0, block // ROWS, scan, held)
    for i, value in enumerate(held + total):
        carry[i] = value

    @pl.when(at == pl.num_programs(0) - 1)
    def _():
        state_ref[: states * tiles, :] = jnp.concatenate(held, axis=0).astype(jnp.bfloat16)
        whole = jnp.concatenate(total, axis=0)
        high = whole.astype(jnp.bfloat16).astype(jnp.float32)
        state_ref[states * tiles :, :] = jnp.concatenate([high, whole - high], axis=0).astype(jnp.bfloat16)


def local_scan(lengths, projected, dt_weight, dt_bias, decay_rate, inner_act):
    tok, channels = inner_act.shape
    low_rank = dt_weight.shape[0]
    states = decay_rate.shape[0]
    tiles = channels // LANES
    count = tiles // ROWS
    whole = lambda a: pl.BlockSpec(a.shape, lambda i: (0,) * a.ndim)
    bias = dt_bias.reshape(1, channels)
    by_token = pl.BlockSpec((BLOCK, tiles, LANES), lambda i: (i, 0, 0))
    state_rows = (states + 2) * tiles
    return pl.pallas_call(
        local_kernel,
        grid=(tok // BLOCK,),
        in_specs=[
            pl.BlockSpec(memory_space=pltpu.SMEM),
            whole(projected),
            whole(dt_weight),
            whole(bias),
            whole(decay_rate),
            pl.BlockSpec((BLOCK, channels), lambda i: (i, 0)),
        ],
        out_specs=[by_token, by_token, pl.BlockSpec((state_rows, LANES), lambda i: (0, 0))],
        out_shape=[
            jax.ShapeDtypeStruct((tok, tiles, LANES), jnp.float32),
            jax.ShapeDtypeStruct((tok, tiles, LANES), jnp.float32),
            jax.ShapeDtypeStruct((state_rows, LANES), jnp.bfloat16),
        ],
        scratch_shapes=[
            pltpu.VMEM((tok, low_rank), jnp.bfloat16),
            pltpu.VMEM((tok, 2 * states, LANES), jnp.float32),
            pltpu.VMEM((tok // ROWS, tiles * ROWS, LANES), jnp.float32),
            pltpu.VMEM((states * count, ROWS, LANES), jnp.float32),
            pltpu.VMEM((BLOCK // ROWS, tiles * ROWS, LANES), jnp.float32),
            pltpu.VMEM((BLOCK // ROWS, tiles * ROWS, LANES), jnp.float32),
            pltpu.VMEM(((states + 1) * count, ROWS, LANES), jnp.float32),
        ],
        compiler_params=pltpu.CompilerParams(vmem_limit_bytes=VMEM_MOST),
        cost_estimate=pl.CostEstimate(
            flops=12 * tok * channels * states,
            bytes_accessed=12 * tok * channels,
            transcendentals=tok * channels * states,
        ),
        name="local_scan",
    )(lengths, projected, dt_weight, bias, decay_rate, inner_act)


def join_kernel(
    low_rank,
    reach,
    proj_ref,
    y_ref,
    sum_ref,
    inner_ref,
    z_ref,
    rate_ref,
    skip_ref,
    moved_ref,
    mine_ref,
    theirs_ref,
    out_ref,
    regrouped_ref,
    c_spread,
    rates,
    entering,
    rows_tiles,
):
    block, channels = z_ref.shape
    states = rate_ref.shape[0]
    tiles = channels // LANES
    count = tiles // ROWS
    kept = states * count
    at = pl.program_id(0)

    @pl.when(at == 0)
    def _():
        c_spread[...] = spread(proj_ref[low_rank + states :, :].astype(jnp.float32).T)
        by_register(rate_ref, rates)
        odd = lax.rem(lax.axis_index("seq"), 2)
        state = [jnp.zeros((ROWS, LANES), jnp.float32)] * kept
        for back in range(reach, 0, -1):
            ref, which = (mine_ref, back // 2) if back % 2 == 0 else (theirs_ref, (back + 1) // 2 - odd)
            sent = ref[which].astype(jnp.float32)
            totals = sent[states * tiles : (states + 1) * tiles] + sent[(states + 1) * tiles :]
            state = [
                jnp.exp2(rates[i] * totals[sublanes(i % count)]) * state[i] + sent[sublanes(i)] for i in range(kept)
            ]
        for i in range(kept):
            entering[i] = state[i]

    regrouped_ref[...] = moved_ref[...]

    def body(pair, unused):
        rows = pl.ds(pl.multiple_of(pair * PAIR, PAIR), PAIR)
        for k in range(2):
            first = pair * PAIR + k * ROWS
            total = [[sum_ref[first + r, sublanes(h), :] for h in range(count)] for r in range(ROWS)]
            out = [[y_ref[first + r, sublanes(h), :] for h in range(count)] for r in range(ROWS)]
            for n in range(states):
                for r in range(ROWS):
                    c_row = c_spread[at * block + first + r, n : n + 1, :]
                    for h in range(count):
                        i = n * count + h
                        out[r][h] += jnp.exp2(rates[i] * total[r][h]) * entering[i] * c_row
            for r in range(ROWS):
                for h in range(count):
                    rows_tiles[k, pl.ds(r + h * ROWS * ROWS, ROWS, stride=ROWS), :] = out[r][h]
        for tile in range(tiles):
            cols = lane(tile)
            z = z_ref[rows, cols].astype(jnp.float32)
            gate = z * (0.5 + 0.5 * jnp.tanh(0.5 * z))
            scanned = jnp.concatenate([rows_tiles[k, sublanes(tile), :] for k in range(2)], axis=0)
            scanned = scanned + skip_ref[:, cols] * inner_ref[rows, cols].astype(jnp.float32)
            out_ref[rows, cols] = (scanned * gate).astype(jnp.bfloat16)
        return unused

    lax.fori_loop(0, block // PAIR, body, 0)


def join_states(projected, y, sums, inner_act, z_branch, decay_rate, skip_gain, moved, mine, theirs, low_rank, reach):
    tok, channels = z_branch.shape
    states = decay_rate.shape[0]
    tiles = channels // LANES
    count = tiles // ROWS
    whole = lambda a: pl.BlockSpec(a.shape, lambda i: (0,) * a.ndim)
    by_token = pl.BlockSpec((BLOCK, tiles, LANES), lambda i: (i, 0, 0))
    by_row = pl.BlockSpec((BLOCK, channels), lambda i: (i, 0))
    skip = skip_gain.reshape(1, channels)
    return pl.pallas_call(
        functools.partial(join_kernel, low_rank, reach),
        grid=(tok // BLOCK,),
        in_specs=[
            whole(projected),
            by_token,
            by_token,
            by_row,
            by_row,
            whole(decay_rate),
            whole(skip),
            by_row,
            whole(mine),
            whole(theirs),
        ],
        out_specs=[by_row, by_row],
        out_shape=[jax.ShapeDtypeStruct((tok, channels), jnp.bfloat16)] * 2,
        scratch_shapes=[
            pltpu.VMEM((tok, states, LANES), jnp.float32),
            pltpu.VMEM((states * count, ROWS, LANES), jnp.float32),
            pltpu.VMEM((states * count, ROWS, LANES), jnp.float32),
            pltpu.VMEM((2, tiles * ROWS, LANES), jnp.float32),
        ],
        compiler_params=pltpu.CompilerParams(vmem_limit_bytes=VMEM_MOST),
        cost_estimate=pl.CostEstimate(
            flops=8 * tok * channels * states,
            bytes_accessed=14 * tok * channels,
            transcendentals=tok * channels * states,
        ),
        name="join_states",
    )(projected, y, sums, inner_act, z_branch, decay_rate, skip, moved, mine, theirs)


def attend_kernel(kv_local, first_group, lengths_ref, place_ref, q_ref, mine_ref, theirs_ref, *refs):
    out_ref, queries, scores, tops, acc = refs[-5:]
    tok = q_ref.shape[0]
    heads = q_ref.shape[1] // HD
    group = pl.program_id(0) + first_group
    position = lax.axis_index("seq")
    odd = lax.rem(position, 2)
    anchor = position * tok
    scale = HD**-0.5
    starts, ends = doc_edges(lengths_ref)
    lane = lax.broadcasted_iota(jnp.int32, (1, LANES), 1)
    first = jnp.full((1, LANES), 2**30, jnp.int32)
    last = jnp.zeros((1, LANES), jnp.int32)
    for i, (start, end) in enumerate(zip(starts, ends)):
        first = jnp.where(lane == i, start, first)
        last = jnp.where(lane == i, end, last)
    rows = lax.broadcasted_iota(jnp.int32, (tok, LANES), 0)

    def in_doc(base):
        return (rows + base >= first) & (rows + base < last)

    apart = jnp.where(in_doc(anchor) | (lane >= len(starts)), 0.0, -APART).astype(jnp.bfloat16)
    for head in range(heads):
        queries[head * tok : (head + 1) * tok, :HD] = q_ref[:, head * HD : (head + 1) * HD]
        queries[head * tok : (head + 1) * tok, HD:] = apart
    key_cols = pl.ds(pl.multiple_of(group * HD, HD), HD)
    value_cols = pl.ds(pl.multiple_of((group + kv_local) * HD, HD), HD)

    def rows_of(back, cols):
        if isinstance(back, int) and back == 0:
            return mine_ref[0, :, cols]
        ours = mine_ref[back // 2, :, cols]
        other = theirs_ref[(back + 1) // 2 - odd, :, cols]
        return jnp.where(lax.rem(back, 2) == 0, ours, other)

    def score(back):
        marks = jnp.where(in_doc(anchor - back * tok), 1.0, 0.0).astype(jnp.bfloat16)
        keys = jnp.concatenate([rows_of(back, key_cols), marks], axis=1)
        return lax.dot_general(queries[...], keys, (((1,), (1,)), ((), ())), preferred_element_type=jnp.float32)

    def widest(s):
        top = s[:, :LANES]
        for at in range(LANES, tok, LANES):
            top = jnp.maximum(top, s[:, at : at + LANES])
        return top

    own = score(0)
    causal = lax.broadcasted_iota(jnp.int32, (tok, tok), 1) <= lax.broadcasted_iota(jnp.int32, (tok, tok), 0)
    for head in range(heads):
        part = slice(head * tok, (head + 1) * tok)
        s = jnp.where(causal, own[part], -APART)
        scores[0, part, :] = s
        tops[part, :] = widest(s)

    begin = jnp.int32(0)
    for start in starts[1:]:
        begin = jnp.where(anchor >= start, start, begin)
    earlier = (anchor - begin + tok - 1) // tok

    def look(back, carry):
        s = score(back)
        scores[back] = s
        tops[...] = jnp.maximum(tops[...], widest(s))
        return carry

    lax.fori_loop(1, earlier + 1, look, 0)
    tops[...] = jnp.broadcast_to(jnp.max(tops[...], axis=1, keepdims=True) * scale, tops.shape)

    def weighted(back):
        values = jnp.concatenate([rows_of(back, value_cols), jnp.ones((tok, HD), jnp.bfloat16)], axis=1)
        top = tops[...]
        weights = [
            jnp.exp((scores[back, :, at : at + LANES] * scale - top).astype(jnp.bfloat16))
            for at in range(0, tok, LANES)
        ]
        return jnp.dot(jnp.concatenate(weights, axis=1), values, preferred_element_type=jnp.float32)

    acc[...] = weighted(0)

    def absorb(back, carry):
        acc[...] += weighted(back)
        return carry

    lax.fori_loop(1, earlier + 1, absorb, 0)
    order = place_ref[pl.ds(position, 1), :]
    move = (lax.broadcasted_iota(jnp.int32, (tok, tok), 0) == order).astype(jnp.float32).astype(jnp.bfloat16)
    for head in range(heads):
        part = slice(head * tok, (head + 1) * tok)
        result = (acc[part, :HD] / acc[part, HD:]).astype(jnp.bfloat16)
        moved = jnp.dot(move, result, preferred_element_type=jnp.float32)
        out_ref[:, head * HD : (head + 1) * HD] = moved.astype(jnp.bfloat16)


def attend(lengths, send_place, query_rows, mine, theirs, groups, so_far):
    tok, width = query_rows.shape
    kv_local = mine.shape[2] // (2 * HD)
    share = width // kv_local
    heads = share // HD
    reach = 2 * (mine.shape[0] - 1)
    count = groups[1] - groups[0]
    whole = lambda a: pl.BlockSpec(a.shape, lambda i: (0,) * a.ndim)
    in_specs = [
        pl.BlockSpec(memory_space=pltpu.SMEM),
        whole(send_place),
        pl.BlockSpec((tok, share), lambda i: (0, i + groups[0])),
        whole(mine),
        whole(theirs),
    ]
    operands = [lengths, send_place, query_rows, mine, theirs]
    aliases = {}
    if so_far is not None:
        aliases = {len(operands): 0}
        in_specs.append(pl.BlockSpec(memory_space=pl.ANY))
        operands.append(so_far)
    return pl.pallas_call(
        functools.partial(attend_kernel, kv_local, groups[0]),
        grid=(count,),
        in_specs=in_specs,
        out_specs=pl.BlockSpec((tok, share), lambda i: (0, i + groups[0])),
        out_shape=jax.ShapeDtypeStruct((tok, width), jnp.bfloat16),
        scratch_shapes=[
            pltpu.VMEM((heads * tok, 2 * HD), jnp.bfloat16),
            pltpu.VMEM((reach + 1, heads * tok, tok), jnp.float32),
            pltpu.VMEM((heads * tok, LANES), jnp.float32),
            pltpu.VMEM((heads * tok, 2 * HD), jnp.float32),
        ],
        input_output_aliases=aliases,
        compiler_params=pltpu.CompilerParams(vmem_limit_bytes=VMEM_LIMIT // 2 + 4 * (reach + 1) * heads * tok * tok),
        cost_estimate=pl.CostEstimate(
            flops=tok * share * count, bytes_accessed=tok * share * count, transcendentals=0
        ),
        name="attend",
    )(*operands)


def shifted(value, steps):
    count = lax.axis_size("seq")
    return lax.ppermute(value, "seq", [(source, source + steps) for source in range(count - steps)])


def with_partner(held):
    mine = jnp.stack(held)
    count = lax.axis_size("seq")
    return mine, lax.ppermute(mine, "seq", [(source, source ^ 1) for source in range(count)])


def even_back(value, reach):
    return [value] + [shifted(value, 2 * k) for k in range(1, (reach + 1) // 2 + 1)]


def local(
    x_branch,
    z_branch,
    conv_weight,
    conv_bias,
    xproj_weight,
    dt_weight,
    dt_bias,
    decay_rate,
    skip_gain,
    query_rows,
    key_rows,
    value_rows,
    lengths,
    destination,
):
    tok = x_branch.shape[0]
    n_seq = lax.axis_size("seq")
    n_mp = lax.axis_size("mp")
    low_rank = dt_weight.shape[0]
    reach = n_seq // 2
    run_rows = tok // n_seq
    kv_local = key_rows.shape[1] // HD
    fence = lax.optimization_barrier

    halo, kv = pack(x_branch, key_rows, value_rows)
    earlier_rows = shifted(halo, 1)
    held = even_back(kv, reach)
    send_place = ((destination // tok) * run_rows + destination % run_rows).reshape(n_seq, tok)

    inner_act, partial = conv_project(lengths, x_branch, earlier_rows, conv_weight, conv_bias, xproj_weight)
    _, *held = fence((partial, *held))
    pieces = lax.all_to_all(partial, "mp", split_axis=0, concat_axis=0, tiled=True)
    mine, theirs = with_partner(held)
    early = max(kv_local // 2, 1)
    attended = attend(lengths, send_place, query_rows, mine, theirs, (0, early), None)
    pieces, attended = fence((pieces, attended))
    summed = jnp.sum(pieces.reshape(n_mp, -1, tok).astype(jnp.float32), axis=0).astype(jnp.bfloat16)
    copies = jnp.broadcast_to(summed[None], (n_mp,) + summed.shape).reshape(partial.shape)
    copies, attended = fence((copies, attended))
    projected = lax.all_to_all(copies, "mp", split_axis=0, concat_axis=0, tiled=True)
    if early < kv_local:
        attended = attend(lengths, send_place, query_rows, mine, theirs, (early, kv_local), attended)
    projected, attended = fence((projected, attended))
    regrouped = lax.all_to_all(attended, "seq", split_axis=0, concat_axis=0, tiled=True)

    y, sums, state = local_scan(lengths, projected, dt_weight, dt_bias, decay_rate, inner_act)
    own, other = with_partner(even_back(state, reach))
    return tuple(
        join_states(
            projected, y, sums, inner_act, z_branch, decay_rate, skip_gain, regrouped, own, other, low_rank, reach
        )
    )


def solution(mesh):
    placed = (
        P("seq", "mp"),
        P("seq", "mp"),
        P(None, "mp"),
        P("mp"),
        P("mp", None),
        P(None, "mp"),
        P("mp"),
        P(None, "mp"),
        P("mp"),
        P("seq", "mp"),
        P("seq", "mp"),
        P("seq", "mp"),
        P(),
        P(),
    )
    return jax.shard_map(
        local,
        mesh=mesh,
        in_specs=placed,
        out_specs=(P("seq", "mp"), P("seq", "mp")),
        check_vma=False,
    )
```

```python
import functools

import jax
import jax.numpy as jnp
from jax import lax
from jax.experimental import pallas as pl
from jax.experimental.pallas import tpu as pltpu
from jax.sharding import PartitionSpec as P

HD = 128
LANES = 128
HALO = 16
LOG2E = 1.4426950408889634
RESET = 1e30
APART = 65536.0
VMEM_LIMIT = 32 * 1024 * 1024
VMEM_MOST = 56 * 1024 * 1024


def doc_edges(lengths_ref):
    starts, ends, total = [], [], 0
    for i in range(lengths_ref.shape[0]):
        starts.append(total)
        total = total + lengths_ref[i]
        ends.append(total)
    return starts, ends


def doc_start(places, starts):
    found = jnp.zeros_like(places)
    for start in starts[1:]:
        found = jnp.where(places >= start, start, found)
    return found


def channel_chunk(channels):
    return 512 if channels % 512 == 0 else channels


def pack_kernel(x_ref, k_ref, v_ref, halo_ref, kv_ref):
    width = k_ref.shape[1]
    halo_ref[...] = x_ref[...]
    kv_ref[:, :width] = k_ref[...]
    kv_ref[:, width:] = v_ref[...]


def pack(x_branch, key_rows, value_rows):
    tok, channels = x_branch.shape
    width = key_rows.shape[1]
    whole = lambda rows, columns: pl.BlockSpec((rows, columns), lambda i: (0, 0))
    return pl.pallas_call(
        pack_kernel,
        grid=(1,),
        in_specs=[
            pl.BlockSpec((HALO, channels), lambda i: (tok // HALO - 1, 0)),
            whole(tok, width),
            whole(tok, width),
        ],
        out_specs=[whole(HALO, channels), whole(tok, 2 * width)],
        out_shape=[
            jax.ShapeDtypeStruct((HALO, channels), x_branch.dtype),
            jax.ShapeDtypeStruct((tok, 2 * width), key_rows.dtype),
        ],
        compiler_params=pltpu.CompilerParams(vmem_limit_bytes=VMEM_MOST),
        cost_estimate=pl.CostEstimate(flops=0, bytes_accessed=16 * tok * width, transcendentals=0),
        name="pack",
    )(x_branch, key_rows, value_rows)


def conv_kernel(lengths_ref, x_ref, halo_ref, w_ref, b_ref, xp_ref, inner_ref, part_ref, ext, acc):
    tok, chunk = x_ref.shape
    starts, _ = doc_edges(lengths_ref)
    anchor = lax.axis_index("seq") * tok
    places = anchor + lax.broadcasted_iota(jnp.int32, (tok, LANES), 0)
    depth = places - doc_start(places, starts)
    ext[0:HALO, :] = halo_ref[...].astype(jnp.float32)
    ext[HALO:, :] = x_ref[...].astype(jnp.float32)
    for lane in range(0, chunk, LANES):
        cols = slice(lane, lane + LANES)
        total = b_ref[:, cols] + w_ref[0:1, cols] * ext[HALO:, cols]
        for lag in range(1, w_ref.shape[0]):
            window = ext[HALO - lag : HALO - lag + tok, cols]
            total += w_ref[lag : lag + 1, cols] * jnp.where(depth >= lag, window, 0.0)
        act = total * (0.5 + 0.5 * jnp.tanh(0.5 * total))
        inner_ref[:, cols] = act.astype(jnp.bfloat16)
    product = lax.dot_general(
        xp_ref[...], inner_ref[...], (((1,), (1,)), ((), ())), preferred_element_type=jnp.float32
    )
    at = pl.program_id(0)

    @pl.when(at == 0)
    def _():
        acc[...] = product

    @pl.when(at > 0)
    def _():
        acc[...] += product

    @pl.when(at == pl.num_programs(0) - 1)
    def _():
        part_ref[...] = acc[...].astype(jnp.bfloat16)


def conv_project(lengths, x_branch, halo, conv_weight, conv_bias, xproj_weight):
    tok, channels = x_branch.shape
    width = xproj_weight.shape[1]
    taps = conv_weight.shape[0]
    chunk = channel_chunk(channels)
    return pl.pallas_call(
        conv_kernel,
        grid=(channels // chunk,),
        in_specs=[
            pl.BlockSpec(memory_space=pltpu.SMEM),
            pl.BlockSpec((tok, chunk), lambda i: (0, i)),
            pl.BlockSpec((HALO, chunk), lambda i: (0, i)),
            pl.BlockSpec((taps, chunk), lambda i: (0, i)),
            pl.BlockSpec((1, chunk), lambda i: (0, i)),
            pl.BlockSpec((width, chunk), lambda i: (0, i)),
        ],
        out_specs=[
            pl.BlockSpec((tok, chunk), lambda i: (0, i)),
            pl.BlockSpec((width, tok), lambda i: (0, 0)),
        ],
        out_shape=[
            jax.ShapeDtypeStruct((tok, channels), jnp.bfloat16),
            jax.ShapeDtypeStruct((width, tok), jnp.bfloat16),
        ],
        scratch_shapes=[
            pltpu.VMEM((tok + HALO, chunk), jnp.float32),
            pltpu.VMEM((width, tok), jnp.float32),
        ],
        compiler_params=pltpu.CompilerParams(vmem_limit_bytes=VMEM_MOST),
        cost_estimate=pl.CostEstimate(
            flops=80 * tok * channels * width, bytes_accessed=8 * tok * channels, transcendentals=tok * channels
        ),
        name="conv_project",
    )(lengths, x_branch, halo, conv_weight, conv_bias.reshape(1, channels), xproj_weight.T)


ROWS = 8
PAIR = 2 * ROWS
BLOCK = 128
SHARE = ROWS * LANES


def spread(columns):
    tok, k = columns.shape
    own = lax.broadcasted_iota(jnp.int32, (k, k), 0) == lax.broadcasted_iota(jnp.int32, (k, k), 1)
    picked = jnp.where(own[None], columns.astype(jnp.float32)[:, None, :], 0.0).reshape(tok * k, k)
    ones = jnp.ones((k, LANES), jnp.bfloat16)
    return jnp.dot(picked.astype(jnp.bfloat16), ones, preferred_element_type=jnp.float32).reshape(tok, k, LANES)


def lane(tile):
    return slice(tile * LANES, (tile + 1) * LANES)


def sublanes(tile):
    return slice(tile * ROWS, (tile + 1) * ROWS)


def by_register(rate_ref, n):
    return jnp.concatenate([rate_ref[n : n + 1, lane(j)] for j in range(ROWS)], axis=0) * (-LOG2E)


def local_kernel(
    lengths_ref,
    proj_ref,
    dtw_ref,
    bias_ref,
    rate_ref,
    inner_ref,
    y_ref,
    sum_ref,
    product_ref,
    state_ref,
    low_cols,
    bc_spread,
    raw,
    rates,
    step_tiles,
    drive_tiles,
    carry,
):
    tok = proj_ref.shape[1]
    block = inner_ref.shape[0]
    states = rate_ref.shape[0]
    stored = product_ref.shape[2] // ROWS
    low_rank = dtw_ref.shape[0]
    starts, _ = doc_edges(lengths_ref)
    at = pl.program_id(1)

    @pl.when((pl.program_id(0) == 0) & (at == 0))
    def _():
        low_cols[...] = proj_ref[:low_rank, :].astype(jnp.float32).T.astype(jnp.bfloat16)
        bc_spread[...] = spread(proj_ref[low_rank:, :].astype(jnp.float32).T)

    @pl.when(at == 0)
    def _():
        for n in range(states):
            rates[n] = by_register(rate_ref, n)
        for i in range(states + stored + 1):
            carry[i] = jnp.full((ROWS, LANES), 1.0 if states <= i < states + stored else 0.0, jnp.float32)
        half = ROWS // 2
        for first in range(0, ROWS, half):
            cols = slice(first * LANES, (first + half) * LANES)
            part = jnp.dot(low_cols[...], dtw_ref[:, cols], preferred_element_type=jnp.float32)
            for i in range(half):
                raw[:, sublanes(first + i), :] = part[:, lane(i)].reshape(tok // ROWS, ROWS, LANES)

    def steps(pair, unused):
        rows = pl.ds(pl.multiple_of(pair * PAIR, PAIR), PAIR)
        places = lax.axis_index("seq") * tok + at * block + pair * PAIR
        places = places + lax.broadcasted_iota(jnp.int32, (PAIR, LANES), 0)
        at_start = places == doc_start(places, starts)
        for tile in range(ROWS):
            inner = inner_ref[rows, lane(tile)].astype(jnp.float32)
            bias = bias_ref[:, lane(tile)]
            for k in range(2):
                biased = raw[at * (block // ROWS) + 2 * pair + k, sublanes(tile), :] + bias
                step = jnp.maximum(biased, 0.0) + jnp.log(1.0 + jnp.exp(-jnp.abs(biased)))
                drive_tiles[2 * pair + k, sublanes(tile), :] = step * inner[sublanes(k)]
                step_tiles[2 * pair + k, sublanes(tile), :] = jnp.where(at_start[sublanes(k)], RESET, step)
        return unused

    lax.fori_loop(0, block // PAIR, steps, 0)

    def scan(t8, held):
        held, product, total = list(held[0]), list(held[1]), held[2]
        for first in range(0, ROWS, 2):
            done = []
            for r in range(first, first + 2):
                token = at * block + t8 * ROWS + r
                picked = pl.ds(r, ROWS, stride=ROWS)
                step = step_tiles[t8, picked, :]
                drive = drive_tiles[t8, picked, :]
                out = None
                for n in range(states):
                    decay = jnp.exp2(rates[n] * step)
                    held[n] = decay * held[n] + bc_spread[token, n : n + 1, :] * drive
                    if n < stored:
                        product[n] = decay * product[n]
                    term = bc_spread[token, states + n : states + n + 1, :] * held[n]
                    out = term if out is None else out + term
                total = total + step
                done.append((out, total, list(product)))
            for k, (out, so_far, products) in enumerate(done):
                row = t8 * ROWS + first + k
                y_ref[row] = out
                sum_ref[row] = so_far
                for n in range(0, stored, 2):
                    both = jnp.concatenate(products[n : n + 2], axis=0).astype(jnp.bfloat16)
                    product_ref[0, row, n * ROWS : (n + 2) * ROWS, :] = both
        return held, product, total

    held = (
        [carry[n] for n in range(states)],
        [carry[states + n] for n in range(stored)],
        carry[states + stored],
    )
    held, product, total = lax.fori_loop(0, block // ROWS, scan, held)
    for i, value in enumerate(held + product + [total]):
        carry[i] = value

    @pl.when(at == pl.num_programs(1) - 1)
    def _():
        state_ref[0, : states * ROWS, :] = jnp.concatenate(held, axis=0).astype(jnp.bfloat16)
        high = total.astype(jnp.bfloat16).astype(jnp.float32)
        state_ref[0, states * ROWS :, :] = jnp.concatenate([high, total - high], axis=0).astype(jnp.bfloat16)


def local_scan(lengths, projected, dt_weight, dt_bias, decay_rate, inner_act):
    tok, channels = inner_act.shape
    low_rank = dt_weight.shape[0]
    states = decay_rate.shape[0]
    shares = channels // SHARE
    stored = states // 2
    whole = lambda a: pl.BlockSpec(a.shape, lambda s, t: (0,) * a.ndim)
    by_share = lambda rows: pl.BlockSpec((rows, SHARE), lambda s, t: (0, s))
    by_token = pl.BlockSpec((BLOCK, ROWS, LANES), lambda s, t: (t, s, 0))
    state_rows = (states + 2) * ROWS
    return pl.pallas_call(
        local_kernel,
        grid=(shares, tok // BLOCK),
        in_specs=[
            pl.BlockSpec(memory_space=pltpu.SMEM),
            whole(projected),
            by_share(low_rank),
            by_share(1),
            by_share(states),
            pl.BlockSpec((BLOCK, SHARE), lambda s, t: (t, s)),
        ],
        out_specs=[
            by_token,
            by_token,
            pl.BlockSpec((1, BLOCK, stored * ROWS, LANES), lambda s, t: (s, t, 0, 0)),
            pl.BlockSpec((1, state_rows, LANES), lambda s, t: (s, 0, 0)),
        ],
        out_shape=[
            jax.ShapeDtypeStruct((tok, shares * ROWS, LANES), jnp.float32),
            jax.ShapeDtypeStruct((tok, shares * ROWS, LANES), jnp.float32),
            jax.ShapeDtypeStruct((shares, tok, stored * ROWS, LANES), jnp.bfloat16),
            jax.ShapeDtypeStruct((shares, state_rows, LANES), jnp.bfloat16),
        ],
        scratch_shapes=[
            pltpu.VMEM((tok, low_rank), jnp.bfloat16),
            pltpu.VMEM((tok, 2 * states, LANES), jnp.float32),
            pltpu.VMEM((tok // ROWS, ROWS * ROWS, LANES), jnp.float32),
            pltpu.VMEM((states, ROWS, LANES), jnp.float32),
            pltpu.VMEM((BLOCK // ROWS, ROWS * ROWS, LANES), jnp.float32),
            pltpu.VMEM((BLOCK // ROWS, ROWS * ROWS, LANES), jnp.float32),
            pltpu.VMEM((states + stored + 1, ROWS, LANES), jnp.float32),
        ],
        compiler_params=pltpu.CompilerParams(vmem_limit_bytes=VMEM_MOST),
        cost_estimate=pl.CostEstimate(
            flops=12 * tok * channels * states,
            bytes_accessed=12 * tok * channels,
            transcendentals=tok * channels * states,
        ),
        name="local_scan",
    )(lengths, projected, dt_weight, dt_bias.reshape(1, channels), decay_rate, inner_act)


def join_kernel(
    low_rank,
    reach,
    proj_ref,
    y_ref,
    sum_ref,
    product_ref,
    inner_ref,
    z_ref,
    rate_ref,
    skip_ref,
    moved_ref,
    mine_ref,
    theirs_ref,
    out_ref,
    regrouped_ref,
    c_spread,
    rates,
    entering,
    rows_tiles,
):
    block = z_ref.shape[0]
    states = rate_ref.shape[0]
    stored = product_ref.shape[2] // ROWS
    at = pl.program_id(1)

    @pl.when((pl.program_id(0) == 0) & (at == 0))
    def _():
        c_spread[...] = spread(proj_ref[low_rank + states :, :].astype(jnp.float32).T)

    @pl.when(at == 0)
    def _():
        rate = [by_register(rate_ref, n) for n in range(states)]
        odd = lax.rem(lax.axis_index("seq"), 2)
        state = [jnp.zeros((ROWS, LANES), jnp.float32)] * states
        for back in range(reach, 0, -1):
            ref, which = (mine_ref, back // 2) if back % 2 == 0 else (theirs_ref, (back + 1) // 2 - odd)
            sent = ref[which, 0].astype(jnp.float32)
            total = sent[sublanes(states)] + sent[sublanes(states + 1)]
            state = [jnp.exp2(rate[n] * total) * state[n] + sent[sublanes(n)] for n in range(states)]
        for n in range(states):
            rates[n] = rate[n]
            entering[n] = state[n]

    regrouped_ref[...] = moved_ref[...]

    def body(pair, unused):
        rows = pl.ds(pl.multiple_of(pair * PAIR, PAIR), PAIR)
        for k in range(2):
            first = pair * PAIR + k * ROWS
            total = [sum_ref[first + r] for r in range(ROWS)]
            out = [y_ref[first + r] for r in range(ROWS)]
            for n in range(states // 2):
                for r in range(ROWS):
                    c_row = lambda m: c_spread[at * block + first + r, m : m + 1, :]
                    if n % 2 == 0 and n < stored:
                        both = product_ref[0, first + r, n * ROWS : (n + 2) * ROWS, :].astype(jnp.float32)
                        for m in range(2):
                            out[r] += both[sublanes(m)] * entering[n + m] * c_row(n + m)
                    m = states // 2 + n
                    out[r] += jnp.exp2(rates[m] * total[r]) * entering[m] * c_row(m)
            for r in range(ROWS):
                rows_tiles[k, pl.ds(r, ROWS, stride=ROWS), :] = out[r]
        for tile in range(ROWS):
            cols = lane(tile)
            z = z_ref[rows, cols].astype(jnp.float32)
            gate = z * (0.5 + 0.5 * jnp.tanh(0.5 * z))
            scanned = jnp.concatenate([rows_tiles[k, sublanes(tile), :] for k in range(2)], axis=0)
            scanned = scanned + skip_ref[:, cols] * inner_ref[rows, cols].astype(jnp.float32)
            out_ref[rows, cols] = (scanned * gate).astype(jnp.bfloat16)
        return unused

    lax.fori_loop(0, block // PAIR, body, 0)


def join_states(
    projected, y, sums, products, inner_act, z_branch, decay_rate, skip_gain, moved, mine, theirs, low_rank, reach
):
    tok, channels = z_branch.shape
    states = decay_rate.shape[0]
    whole = lambda a: pl.BlockSpec(a.shape, lambda s, t: (0,) * a.ndim)
    by_share = lambda rows: pl.BlockSpec((rows, SHARE), lambda s, t: (0, s))
    by_token = pl.BlockSpec((BLOCK, ROWS, LANES), lambda s, t: (t, s, 0))
    by_row = pl.BlockSpec((BLOCK, SHARE), lambda s, t: (t, s))
    sent = pl.BlockSpec((mine.shape[0], 1) + mine.shape[2:], lambda s, t: (0, s, 0, 0))
    return pl.pallas_call(
        functools.partial(join_kernel, low_rank, reach),
        grid=(channels // SHARE, tok // BLOCK),
        in_specs=[
            whole(projected),
            by_token,
            by_token,
            pl.BlockSpec((1, BLOCK) + products.shape[2:], lambda s, t: (s, t, 0, 0)),
            by_row,
            by_row,
            by_share(states),
            by_share(1),
            by_row,
            sent,
            sent,
        ],
        out_specs=[by_row, by_row],
        out_shape=[jax.ShapeDtypeStruct((tok, channels), jnp.bfloat16)] * 2,
        scratch_shapes=[
            pltpu.VMEM((tok, states, LANES), jnp.float32),
            pltpu.VMEM((states, ROWS, LANES), jnp.float32),
            pltpu.VMEM((states, ROWS, LANES), jnp.float32),
            pltpu.VMEM((2, ROWS * ROWS, LANES), jnp.float32),
        ],
        compiler_params=pltpu.CompilerParams(vmem_limit_bytes=VMEM_MOST),
        cost_estimate=pl.CostEstimate(
            flops=8 * tok * channels * states,
            bytes_accessed=14 * tok * channels,
            transcendentals=tok * channels * states,
        ),
        name="join_states",
    )(
        projected,
        y,
        sums,
        products,
        inner_act,
        z_branch,
        decay_rate,
        skip_gain.reshape(1, channels),
        moved,
        mine,
        theirs,
    )


def attend_kernel(kv_local, first_group, lengths_ref, place_ref, q_ref, mine_ref, theirs_ref, *refs):
    out_ref, queries, scores, tops, acc = refs[-5:]
    tok = q_ref.shape[0]
    heads = q_ref.shape[1] // HD
    group = pl.program_id(0) + first_group
    position = lax.axis_index("seq")
    odd = lax.rem(position, 2)
    anchor = position * tok
    scale = HD**-0.5
    starts, ends = doc_edges(lengths_ref)
    lane = lax.broadcasted_iota(jnp.int32, (1, LANES), 1)
    first = jnp.full((1, LANES), 2**30, jnp.int32)
    last = jnp.zeros((1, LANES), jnp.int32)
    for i, (start, end) in enumerate(zip(starts, ends)):
        first = jnp.where(lane == i, start, first)
        last = jnp.where(lane == i, end, last)
    rows = lax.broadcasted_iota(jnp.int32, (tok, LANES), 0)

    def in_doc(base):
        return (rows + base >= first) & (rows + base < last)

    apart = jnp.where(in_doc(anchor) | (lane >= len(starts)), 0.0, -APART).astype(jnp.bfloat16)
    for head in range(heads):
        queries[head * tok : (head + 1) * tok, :HD] = q_ref[:, head * HD : (head + 1) * HD]
        queries[head * tok : (head + 1) * tok, HD:] = apart
    key_cols = pl.ds(pl.multiple_of(group * HD, HD), HD)
    value_cols = pl.ds(pl.multiple_of((group + kv_local) * HD, HD), HD)

    def rows_of(back, cols):
        if isinstance(back, int) and back == 0:
            return mine_ref[0, :, cols]
        ours = mine_ref[back // 2, :, cols]
        other = theirs_ref[(back + 1) // 2 - odd, :, cols]
        return jnp.where(lax.rem(back, 2) == 0, ours, other)

    def score(back):
        marks = jnp.where(in_doc(anchor - back * tok), 1.0, 0.0).astype(jnp.bfloat16)
        keys = jnp.concatenate([rows_of(back, key_cols), marks], axis=1)
        return lax.dot_general(queries[...], keys, (((1,), (1,)), ((), ())), preferred_element_type=jnp.float32)

    def widest(s):
        top = s[:, :LANES]
        for at in range(LANES, tok, LANES):
            top = jnp.maximum(top, s[:, at : at + LANES])
        return top

    own = score(0)
    causal = lax.broadcasted_iota(jnp.int32, (tok, tok), 1) <= lax.broadcasted_iota(jnp.int32, (tok, tok), 0)
    for head in range(heads):
        part = slice(head * tok, (head + 1) * tok)
        s = jnp.where(causal, own[part], -APART)
        scores[0, part, :] = s
        tops[part, :] = widest(s)

    begin = jnp.int32(0)
    for start in starts[1:]:
        begin = jnp.where(anchor >= start, start, begin)
    earlier = (anchor - begin + tok - 1) // tok

    def look(back, carry):
        s = score(back)
        scores[back] = s
        tops[...] = jnp.maximum(tops[...], widest(s))
        return carry

    lax.fori_loop(1, earlier + 1, look, 0)
    tops[...] = jnp.broadcast_to(jnp.max(tops[...], axis=1, keepdims=True) * scale, tops.shape)

    def weighted(back):
        values = jnp.concatenate([rows_of(back, value_cols), jnp.ones((tok, HD), jnp.bfloat16)], axis=1)
        top = tops[...]
        weights = [
            jnp.exp((scores[back, :, at : at + LANES] * scale - top).astype(jnp.bfloat16))
            for at in range(0, tok, LANES)
        ]
        return jnp.dot(jnp.concatenate(weights, axis=1), values, preferred_element_type=jnp.float32)

    acc[...] = weighted(0)

    def absorb(back, carry):
        acc[...] += weighted(back)
        return carry

    lax.fori_loop(1, earlier + 1, absorb, 0)
    order = place_ref[pl.ds(position, 1), :]
    move = (lax.broadcasted_iota(jnp.int32, (tok, tok), 0) == order).astype(jnp.float32).astype(jnp.bfloat16)
    for head in range(heads):
        part = slice(head * tok, (head + 1) * tok)
        result = (acc[part, :HD] / acc[part, HD:]).astype(jnp.bfloat16)
        moved = jnp.dot(move, result, preferred_element_type=jnp.float32)
        out_ref[:, head * HD : (head + 1) * HD] = moved.astype(jnp.bfloat16)


def attend(lengths, send_place, query_rows, mine, theirs, groups, so_far):
    tok, width = query_rows.shape
    kv_local = mine.shape[2] // (2 * HD)
    share = width // kv_local
    heads = share // HD
    reach = 2 * (mine.shape[0] - 1)
    count = groups[1] - groups[0]
    whole = lambda a: pl.BlockSpec(a.shape, lambda i: (0,) * a.ndim)
    in_specs = [
        pl.BlockSpec(memory_space=pltpu.SMEM),
        whole(send_place),
        pl.BlockSpec((tok, share), lambda i: (0, i + groups[0])),
        whole(mine),
        whole(theirs),
    ]
    operands = [lengths, send_place, query_rows, mine, theirs]
    aliases = {}
    if so_far is not None:
        aliases = {len(operands): 0}
        in_specs.append(pl.BlockSpec(memory_space=pl.ANY))
        operands.append(so_far)
    return pl.pallas_call(
        functools.partial(attend_kernel, kv_local, groups[0]),
        grid=(count,),
        in_specs=in_specs,
        out_specs=pl.BlockSpec((tok, share), lambda i: (0, i + groups[0])),
        out_shape=jax.ShapeDtypeStruct((tok, width), jnp.bfloat16),
        scratch_shapes=[
            pltpu.VMEM((heads * tok, 2 * HD), jnp.bfloat16),
            pltpu.VMEM((reach + 1, heads * tok, tok), jnp.float32),
            pltpu.VMEM((heads * tok, LANES), jnp.float32),
            pltpu.VMEM((heads * tok, 2 * HD), jnp.float32),
        ],
        input_output_aliases=aliases,
        compiler_params=pltpu.CompilerParams(vmem_limit_bytes=VMEM_LIMIT // 2 + 4 * (reach + 1) * heads * tok * tok),
        cost_estimate=pl.CostEstimate(
            flops=tok * share * count, bytes_accessed=tok * share * count, transcendentals=0
        ),
        name="attend",
    )(*operands)


def shifted(value, steps):
    count = lax.axis_size("seq")
    return lax.ppermute(value, "seq", [(source, source + steps) for source in range(count - steps)])


def with_partner(held):
    mine = jnp.stack(held)
    count = lax.axis_size("seq")
    return mine, lax.ppermute(mine, "seq", [(source, source ^ 1) for source in range(count)])


def even_back(value, reach):
    return [value] + [shifted(value, 2 * k) for k in range(1, (reach + 1) // 2 + 1)]


def local(
    x_branch,
    z_branch,
    conv_weight,
    conv_bias,
    xproj_weight,
    dt_weight,
    dt_bias,
    decay_rate,
    skip_gain,
    query_rows,
    key_rows,
    value_rows,
    lengths,
    destination,
):
    tok = x_branch.shape[0]
    n_seq = lax.axis_size("seq")
    n_mp = lax.axis_size("mp")
    low_rank = dt_weight.shape[0]
    reach = n_seq // 2
    run_rows = tok // n_seq
    kv_local = key_rows.shape[1] // HD
    fence = lax.optimization_barrier

    halo, kv = pack(x_branch, key_rows, value_rows)
    earlier_rows = shifted(halo, 1)
    held = even_back(kv, reach)
    send_place = ((destination // tok) * run_rows + destination % run_rows).reshape(n_seq, tok)

    inner_act, partial = conv_project(lengths, x_branch, earlier_rows, conv_weight, conv_bias, xproj_weight)
    _, *held = fence((partial, *held))
    pieces = lax.all_to_all(partial, "mp", split_axis=0, concat_axis=0, tiled=True)
    mine, theirs = with_partner(held)
    early = max(kv_local // 2, 1)
    attended = attend(lengths, send_place, query_rows, mine, theirs, (0, early), None)
    pieces, attended = fence((pieces, attended))
    summed = jnp.sum(pieces.reshape(n_mp, -1, tok).astype(jnp.float32), axis=0).astype(jnp.bfloat16)
    copies = jnp.broadcast_to(summed[None], (n_mp,) + summed.shape).reshape(partial.shape)
    copies, attended = fence((copies, attended))
    projected = lax.all_to_all(copies, "mp", split_axis=0, concat_axis=0, tiled=True)
    if early < kv_local:
        attended = attend(lengths, send_place, query_rows, mine, theirs, (early, kv_local), attended)
    projected, attended = fence((projected, attended))
    regrouped = lax.all_to_all(attended, "seq", split_axis=0, concat_axis=0, tiled=True)

    y, sums, products, state = local_scan(lengths, projected, dt_weight, dt_bias, decay_rate, inner_act)
    own, other = with_partner(even_back(state, reach))
    return tuple(
        join_states(
            projected,
            y,
            sums,
            products,
            inner_act,
            z_branch,
            decay_rate,
            skip_gain,
            regrouped,
            own,
            other,
            low_rank,
            reach,
        )
    )


def solution(mesh):
    placed = (
        P("seq", "mp"),
        P("seq", "mp"),
        P(None, "mp"),
        P("mp"),
        P("mp", None),
        P(None, "mp"),
        P("mp"),
        P(None, "mp"),
        P("mp"),
        P("seq", "mp"),
        P("seq", "mp"),
        P("seq", "mp"),
        P(),
        P(),
    )
    return jax.shard_map(
        local,
        mesh=mesh,
        in_specs=placed,
        out_specs=(P("seq", "mp"), P("seq", "mp")),
        check_vma=False,
    )
```

```python
import functools

import jax
import jax.numpy as jnp
from jax import lax
from jax.experimental import pallas as pl
from jax.experimental.pallas import tpu as pltpu
from jax.sharding import PartitionSpec as P

HD = 128
LANES = 128
HALO = 16
LOG2E = 1.4426950408889634
RESET = 1e30
APART = 65536.0
VMEM_LIMIT = 32 * 1024 * 1024
VMEM_MOST = 56 * 1024 * 1024
VMEM_NEARLY = 53 * 1024 * 1024 + 512 * 1024


def doc_edges(lengths_ref):
    starts, ends, total = [], [], 0
    for i in range(lengths_ref.shape[0]):
        starts.append(total)
        total = total + lengths_ref[i]
        ends.append(total)
    return starts, ends


def doc_start(places, starts):
    found = jnp.zeros_like(places)
    for start in starts[1:]:
        found = jnp.where(places >= start, start, found)
    return found


def channel_chunk(channels):
    return 512 if channels % 512 == 0 else channels


def pack_kernel(x_ref, k_ref, v_ref, halo_ref, kv_ref):
    width = k_ref.shape[1]
    halo_ref[...] = x_ref[...]
    kv_ref[:, :width] = k_ref[...]
    kv_ref[:, width:] = v_ref[...]


def pack(x_branch, key_rows, value_rows):
    tok, channels = x_branch.shape
    width = key_rows.shape[1]
    whole = lambda rows, columns: pl.BlockSpec((rows, columns), lambda i: (0, 0))
    return pl.pallas_call(
        pack_kernel,
        grid=(1,),
        in_specs=[
            pl.BlockSpec((HALO, channels), lambda i: (tok // HALO - 1, 0)),
            whole(tok, width),
            whole(tok, width),
        ],
        out_specs=[whole(HALO, channels), whole(tok, 2 * width)],
        out_shape=[
            jax.ShapeDtypeStruct((HALO, channels), x_branch.dtype),
            jax.ShapeDtypeStruct((tok, 2 * width), key_rows.dtype),
        ],
        compiler_params=pltpu.CompilerParams(vmem_limit_bytes=VMEM_MOST),
        cost_estimate=pl.CostEstimate(flops=0, bytes_accessed=16 * tok * width, transcendentals=0),
        name="pack",
    )(x_branch, key_rows, value_rows)


def conv_kernel(lengths_ref, x_ref, halo_ref, w_ref, b_ref, xp_ref, inner_ref, part_ref, ext, acc):
    tok, chunk = x_ref.shape
    starts, _ = doc_edges(lengths_ref)
    anchor = lax.axis_index("seq") * tok
    places = anchor + lax.broadcasted_iota(jnp.int32, (tok, LANES), 0)
    depth = places - doc_start(places, starts)
    ext[0:HALO, :] = halo_ref[...].astype(jnp.float32)
    ext[HALO:, :] = x_ref[...].astype(jnp.float32)
    for lane in range(0, chunk, LANES):
        cols = slice(lane, lane + LANES)
        total = b_ref[:, cols] + w_ref[0:1, cols] * ext[HALO:, cols]
        for lag in range(1, w_ref.shape[0]):
            window = ext[HALO - lag : HALO - lag + tok, cols]
            total += w_ref[lag : lag + 1, cols] * jnp.where(depth >= lag, window, 0.0)
        act = total * (0.5 + 0.5 * jnp.tanh(0.5 * total))
        inner_ref[:, cols] = act.astype(jnp.bfloat16)
    product = lax.dot_general(
        xp_ref[...], inner_ref[...], (((1,), (1,)), ((), ())), preferred_element_type=jnp.float32
    )
    at = pl.program_id(0)

    @pl.when(at == 0)
    def _():
        acc[...] = product

    @pl.when(at > 0)
    def _():
        acc[...] += product

    @pl.when(at == pl.num_programs(0) - 1)
    def _():
        part_ref[...] = acc[...].astype(jnp.bfloat16)


def conv_project(lengths, x_branch, halo, conv_weight, conv_bias, xproj_weight):
    tok, channels = x_branch.shape
    width = xproj_weight.shape[1]
    taps = conv_weight.shape[0]
    chunk = channel_chunk(channels)
    return pl.pallas_call(
        conv_kernel,
        grid=(channels // chunk,),
        in_specs=[
            pl.BlockSpec(memory_space=pltpu.SMEM),
            pl.BlockSpec((tok, chunk), lambda i: (0, i)),
            pl.BlockSpec((HALO, chunk), lambda i: (0, i)),
            pl.BlockSpec((taps, chunk), lambda i: (0, i)),
            pl.BlockSpec((1, chunk), lambda i: (0, i)),
            pl.BlockSpec((width, chunk), lambda i: (0, i)),
        ],
        out_specs=[
            pl.BlockSpec((tok, chunk), lambda i: (0, i)),
            pl.BlockSpec((width, tok), lambda i: (0, 0)),
        ],
        out_shape=[
            jax.ShapeDtypeStruct((tok, channels), jnp.bfloat16),
            jax.ShapeDtypeStruct((width, tok), jnp.bfloat16),
        ],
        scratch_shapes=[
            pltpu.VMEM((tok + HALO, chunk), jnp.float32),
            pltpu.VMEM((width, tok), jnp.float32),
        ],
        compiler_params=pltpu.CompilerParams(vmem_limit_bytes=VMEM_NEARLY),
        cost_estimate=pl.CostEstimate(
            flops=80 * tok * channels * width, bytes_accessed=8 * tok * channels, transcendentals=tok * channels
        ),
        name="conv_project",
    )(lengths, x_branch, halo, conv_weight, conv_bias.reshape(1, channels), xproj_weight.T)


ROWS = 8
PAIR = 2 * ROWS
BLOCK = 64
GROUP = 8


def spread(columns):
    tok, k = columns.shape
    own = lax.broadcasted_iota(jnp.int32, (k, k), 0) == lax.broadcasted_iota(jnp.int32, (k, k), 1)
    picked = jnp.where(own[None], columns.astype(jnp.float32)[:, None, :], 0.0).reshape(tok * k, k)
    ones = jnp.ones((k, LANES), jnp.bfloat16)
    return jnp.dot(picked.astype(jnp.bfloat16), ones, preferred_element_type=jnp.float32).reshape(tok, k, LANES)


def lane(tile):
    return slice(tile * LANES, (tile + 1) * LANES)


def sublanes(tile):
    return slice(tile * ROWS, (tile + 1) * ROWS)


def by_register(rate_ref, rates):
    states = rate_ref.shape[0]
    count = rates.shape[0] // states
    for n in range(states):
        for h in range(count):
            tiles = [rate_ref[n : n + 1, lane(h * ROWS + j)] for j in range(ROWS)]
            rates[n * count + h] = jnp.concatenate(tiles, axis=0) * (-LOG2E)


def local_kernel(
    lengths_ref,
    proj_ref,
    dtw_ref,
    bias_ref,
    rate_ref,
    inner_ref,
    y_ref,
    sum_ref,
    state_ref,
    low_cols,
    bc_spread,
    raw,
    rates,
    step_tiles,
    drive_tiles,
    carry,
):
    tok = proj_ref.shape[1]
    block, channels = inner_ref.shape
    states = rate_ref.shape[0]
    low_rank = dtw_ref.shape[0]
    tiles = channels // LANES
    count = tiles // ROWS
    starts, _ = doc_edges(lengths_ref)
    at = pl.program_id(0)

    @pl.when(at == 0)
    def _():
        low_cols[...] = proj_ref[:low_rank, :].astype(jnp.float32).T.astype(jnp.bfloat16)
        bc_spread[...] = spread(proj_ref[low_rank:, :].astype(jnp.float32).T)
        by_register(rate_ref, rates)
        carry[...] = jnp.zeros_like(carry)
        for first in range(0, tiles, 4):
            cols = slice(first * LANES, (first + 4) * LANES)
            part = jnp.dot(low_cols[...], dtw_ref[:, cols], preferred_element_type=jnp.float32)
            for i in range(4):
                raw[:, sublanes(first + i), :] = part[:, lane(i)].reshape(tok // ROWS, ROWS, LANES)

    def steps(pair, unused):
        rows = pl.ds(pl.multiple_of(pair * PAIR, PAIR), PAIR)
        places = lax.axis_index("seq") * tok + at * block + pair * PAIR
        places = places + lax.broadcasted_iota(jnp.int32, (PAIR, LANES), 0)
        at_start = places == doc_start(places, starts)
        for tile in range(tiles):
            inner = inner_ref[rows, lane(tile)].astype(jnp.float32)
            bias = bias_ref[:, lane(tile)]
            for k in range(2):
                biased = raw[at * (block // ROWS) + 2 * pair + k, sublanes(tile), :] + bias
                step = jnp.maximum(biased, 0.0) + jnp.log(1.0 + jnp.exp(-jnp.abs(biased)))
                drive_tiles[2 * pair + k, sublanes(tile), :] = step * inner[sublanes(k)]
                step_tiles[2 * pair + k, sublanes(tile), :] = jnp.where(at_start[sublanes(k)], RESET, step)
        return unused

    lax.fori_loop(0, block // PAIR, steps, 0)

    def scan(t8, held):
        held, total = list(held[0]), list(held[1])
        for first in range(0, ROWS, 4):
            done = []
            for r in range(first, first + 4):
                token = at * block + t8 * ROWS + r
                picked = [pl.ds(r + h * ROWS * ROWS, ROWS, stride=ROWS) for h in range(count)]
                step = [step_tiles[t8, rows, :] for rows in picked]
                drive = [drive_tiles[t8, rows, :] for rows in picked]
                out = [None] * count
                for n in range(states):
                    b_row = bc_spread[token, n : n + 1, :]
                    c_row = bc_spread[token, states + n : states + n + 1, :]
                    for h in range(count):
                        i = n * count + h
                        held[i] = jnp.exp2(rates[i] * step[h]) * held[i] + b_row * drive[h]
                        term = c_row * held[i]
                        out[h] = term if out[h] is None else out[h] + term
                total = [so_far + more for so_far, more in zip(total, step)]
                done.append((out, total))
            for k, (out, so_far) in enumerate(done):
                for h in range(count):
                    y_ref[t8 * ROWS + first + k, sublanes(h), :] = out[h]
                    sum_ref[t8 * ROWS + first + k, sublanes(h), :] = so_far[h]
        return held, total

    kept = states * count
    held = ([carry[i] for i in range(kept)], [carry[kept + h] for h in range(count)])
    held, total = lax.fori_loop(0, block // ROWS, scan, held)
    for i, value in enumerate(held + total):
        carry[i] = value

    @pl.when(at == pl.num_programs(0) - 1)
    def _():
        state_ref[: states * tiles, :] = jnp.concatenate(held, axis=0).astype(jnp.bfloat16)
        whole = jnp.concatenate(total, axis=0)
        high = whole.astype(jnp.bfloat16).astype(jnp.float32)
        state_ref[states * tiles :, :] = jnp.concatenate([high, whole - high], axis=0).astype(jnp.bfloat16)


def local_scan(lengths, projected, dt_weight, dt_bias, decay_rate, inner_act):
    tok, channels = inner_act.shape
    low_rank = dt_weight.shape[0]
    states = decay_rate.shape[0]
    tiles = channels // LANES
    count = tiles // ROWS
    whole = lambda a: pl.BlockSpec(a.shape, lambda i: (0,) * a.ndim)
    bias = dt_bias.reshape(1, channels)
    by_token = pl.BlockSpec((BLOCK, tiles, LANES), lambda i: (i, 0, 0))
    state_rows = (states + 2) * tiles
    return pl.pallas_call(
        local_kernel,
        grid=(tok // BLOCK,),
        in_specs=[
            pl.BlockSpec(memory_space=pltpu.SMEM),
            whole(projected),
            whole(dt_weight),
            whole(bias),
            whole(decay_rate),
            pl.BlockSpec((BLOCK, channels), lambda i: (i, 0)),
        ],
        out_specs=[by_token, by_token, pl.BlockSpec((state_rows, LANES), lambda i: (0, 0))],
        out_shape=[
            jax.ShapeDtypeStruct((tok, tiles, LANES), jnp.float32),
            jax.ShapeDtypeStruct((tok, tiles, LANES), jnp.float32),
            jax.ShapeDtypeStruct((state_rows, LANES), jnp.bfloat16),
        ],
        scratch_shapes=[
            pltpu.VMEM((tok, low_rank), jnp.bfloat16),
            pltpu.VMEM((tok, 2 * states, LANES), jnp.float32),
            pltpu.VMEM((tok // ROWS, tiles * ROWS, LANES), jnp.float32),
            pltpu.VMEM((states * count, ROWS, LANES), jnp.float32),
            pltpu.VMEM((BLOCK // ROWS, tiles * ROWS, LANES), jnp.float32),
            pltpu.VMEM((BLOCK // ROWS, tiles * ROWS, LANES), jnp.float32),
            pltpu.VMEM(((states + 1) * count, ROWS, LANES), jnp.float32),
        ],
        compiler_params=pltpu.CompilerParams(vmem_limit_bytes=VMEM_MOST),
        cost_estimate=pl.CostEstimate(
            flops=12 * tok * channels * states,
            bytes_accessed=12 * tok * channels,
            transcendentals=tok * channels * states,
        ),
        name="local_scan",
    )(lengths, projected, dt_weight, bias, decay_rate, inner_act)


def join_kernel(
    low_rank,
    reach,
    proj_ref,
    y_ref,
    sum_ref,
    inner_ref,
    z_ref,
    rate_ref,
    skip_ref,
    moved_ref,
    mine_ref,
    theirs_ref,
    out_ref,
    regrouped_ref,
    c_spread,
    rates,
    rates_twice,
    entering,
    rows_tiles,
):
    block, channels = z_ref.shape
    states = rate_ref.shape[0]
    tiles = channels // LANES
    count = tiles // ROWS
    kept = states * count
    at = pl.program_id(0)

    @pl.when(at == 0)
    def _():
        c_spread[...] = spread(proj_ref[low_rank + states :, :].astype(jnp.float32).T)
        by_register(rate_ref, rates)
        odd = lax.rem(lax.axis_index("seq"), 2)
        state = [jnp.zeros((ROWS, LANES), jnp.float32)] * kept
        for back in range(reach, 0, -1):
            ref, which = (mine_ref, back // 2) if back % 2 == 0 else (theirs_ref, (back + 1) // 2 - odd)
            sent = ref[which].astype(jnp.float32)
            totals = sent[states * tiles : (states + 1) * tiles] + sent[(states + 1) * tiles :]
            state = [
                jnp.exp2(rates[i] * totals[sublanes(i % count)]) * state[i] + sent[sublanes(i)] for i in range(kept)
            ]
        for i in range(kept):
            rates_twice[i] = jnp.concatenate([rates[i]] * 2, axis=0).astype(jnp.bfloat16)
            entering[i] = jnp.concatenate([state[i]] * 2, axis=0).astype(jnp.bfloat16)

    regrouped_ref[...] = moved_ref[...]

    def body(pair, unused):
        rows = pl.ds(pl.multiple_of(pair * PAIR, PAIR), PAIR)
        for k in range(2):
            first = pair * PAIR + k * ROWS
            twos = [(first + r, first + r + 1) for r in range(0, ROWS, 2)]
            shares = [(p, h) for p in range(len(twos)) for h in range(count)]
            total = {
                (p, h): jnp.concatenate([sum_ref[t, sublanes(h), :] for t in twos[p]], axis=0).astype(jnp.bfloat16)
                for p, h in shares
            }
            out = {(p, h): jnp.concatenate([y_ref[t, sublanes(h), :] for t in twos[p]], axis=0) for p, h in shares}
            for begin in range(0, states, GROUP):
                part = {}
                for n in range(begin, begin + GROUP):
                    for p, two in enumerate(twos):
                        c_rows = [
                            jnp.broadcast_to(c_spread[at * block + t, n : n + 1, :], (ROWS, LANES)) for t in two
                        ]
                        c_both = jnp.concatenate(c_rows, axis=0).astype(jnp.bfloat16)
                        for h in range(count):
                            i = n * count + h
                            term = jnp.exp2(rates_twice[i] * total[p, h]) * entering[i] * c_both
                            part[p, h] = part[p, h] + term if (p, h) in part else term
                for key in shares:
                    out[key] = out[key] + part[key].astype(jnp.float32)
            for p, h in shares:
                for which in range(2):
                    place = pl.ds(2 * p + which + h * ROWS * ROWS, ROWS, stride=ROWS)
                    rows_tiles[k, place, :] = out[p, h][sublanes(which)]
        for tile in range(tiles):
            cols = lane(tile)
            z = z_ref[rows, cols].astype(jnp.float32)
            gate = z * (0.5 + 0.5 * jnp.tanh(0.5 * z))
            scanned = jnp.concatenate([rows_tiles[k, sublanes(tile), :] for k in range(2)], axis=0)
            scanned = scanned + skip_ref[:, cols] * inner_ref[rows, cols].astype(jnp.float32)
            out_ref[rows, cols] = (scanned * gate).astype(jnp.bfloat16)
        return unused

    lax.fori_loop(0, block // PAIR, body, 0)


def join_states(projected, y, sums, inner_act, z_branch, decay_rate, skip_gain, moved, mine, theirs, low_rank, reach):
    tok, channels = z_branch.shape
    states = decay_rate.shape[0]
    tiles = channels // LANES
    count = tiles // ROWS
    whole = lambda a: pl.BlockSpec(a.shape, lambda i: (0,) * a.ndim)
    by_token = pl.BlockSpec((BLOCK, tiles, LANES), lambda i: (i, 0, 0))
    by_row = pl.BlockSpec((BLOCK, channels), lambda i: (i, 0))
    skip = skip_gain.reshape(1, channels)
    return pl.pallas_call(
        functools.partial(join_kernel, low_rank, reach),
        grid=(tok // BLOCK,),
        in_specs=[
            whole(projected),
            by_token,
            by_token,
            by_row,
            by_row,
            whole(decay_rate),
            whole(skip),
            by_row,
            whole(mine),
            whole(theirs),
        ],
        out_specs=[by_row, by_row],
        out_shape=[jax.ShapeDtypeStruct((tok, channels), jnp.bfloat16)] * 2,
        scratch_shapes=[
            pltpu.VMEM((tok, states, LANES), jnp.float32),
            pltpu.VMEM((states * count, ROWS, LANES), jnp.float32),
            pltpu.VMEM((states * count, PAIR, LANES), jnp.bfloat16),
            pltpu.VMEM((states * count, PAIR, LANES), jnp.bfloat16),
            pltpu.VMEM((2, tiles * ROWS, LANES), jnp.float32),
        ],
        compiler_params=pltpu.CompilerParams(vmem_limit_bytes=VMEM_NEARLY),
        cost_estimate=pl.CostEstimate(
            flops=8 * tok * channels * states,
            bytes_accessed=14 * tok * channels,
            transcendentals=tok * channels * states,
        ),
        name="join_states",
    )(projected, y, sums, inner_act, z_branch, decay_rate, skip, moved, mine, theirs)


def attend_kernel(kv_local, first_group, lengths_ref, place_ref, q_ref, mine_ref, theirs_ref, *refs):
    out_ref, queries, scores, tops, acc = refs[-5:]
    tok = q_ref.shape[0]
    heads = q_ref.shape[1] // HD
    group = pl.program_id(0) + first_group
    position = lax.axis_index("seq")
    odd = lax.rem(position, 2)
    anchor = position * tok
    scale = jnp.bfloat16(LOG2E * HD**-0.5)
    starts, ends = doc_edges(lengths_ref)
    lane = lax.broadcasted_iota(jnp.int32, (1, LANES), 1)
    first = jnp.full((1, LANES), 2**30, jnp.int32)
    last = jnp.zeros((1, LANES), jnp.int32)
    for i, (start, end) in enumerate(zip(starts, ends)):
        first = jnp.where(lane == i, start, first)
        last = jnp.where(lane == i, end, last)
    rows = lax.broadcasted_iota(jnp.int32, (tok, LANES), 0)

    def in_doc(base):
        return (rows + base >= first) & (rows + base < last)

    apart = jnp.where(in_doc(anchor) | (lane >= len(starts)), 0.0, -APART).astype(jnp.bfloat16)
    for head in range(heads):
        queries[head * tok : (head + 1) * tok, :HD] = q_ref[:, head * HD : (head + 1) * HD]
        queries[head * tok : (head + 1) * tok, HD:] = apart
    key_cols = pl.ds(pl.multiple_of(group * HD, HD), HD)
    value_cols = pl.ds(pl.multiple_of((group + kv_local) * HD, HD), HD)

    def rows_of(back, cols):
        if isinstance(back, int) and back == 0:
            return mine_ref[0, :, cols]
        ours = mine_ref[back // 2, :, cols]
        other = theirs_ref[(back + 1) // 2 - odd, :, cols]
        return jnp.where(lax.rem(back, 2) == 0, ours, other)

    def score(back):
        marks = jnp.where(in_doc(anchor - back * tok), 1.0, 0.0).astype(jnp.bfloat16)
        keys = jnp.concatenate([rows_of(back, key_cols), marks], axis=1)
        return lax.dot_general(queries[...], keys, (((1,), (1,)), ((), ())), preferred_element_type=jnp.float32)

    def widest(s):
        top = s[:, :LANES]
        for at in range(LANES, tok, LANES):
            top = jnp.maximum(top, s[:, at : at + LANES])
        return top

    own = score(0)
    causal = lax.broadcasted_iota(jnp.int32, (tok, tok), 1) <= lax.broadcasted_iota(jnp.int32, (tok, tok), 0)
    for head in range(heads):
        part = slice(head * tok, (head + 1) * tok)
        s = jnp.where(causal, own[part], -APART)
        scores[0, part, :] = s
        tops[part, :] = widest(s)

    begin = jnp.int32(0)
    for start in starts[1:]:
        begin = jnp.where(anchor >= start, start, begin)
    earlier = (anchor - begin + tok - 1) // tok

    def look(back, carry):
        s = score(back)
        scores[back] = s
        tops[...] = jnp.maximum(tops[...], widest(s))
        return carry

    lax.fori_loop(1, earlier + 1, look, 0)
    tops[...] = jnp.broadcast_to(jnp.max(tops[...], axis=1, keepdims=True), tops.shape)

    def weighted(back):
        values = jnp.concatenate([rows_of(back, value_cols), jnp.ones((tok, HD), jnp.bfloat16)], axis=1)
        top = tops[...]
        weights = [
            jnp.exp2((scores[back, :, at : at + LANES] - top).astype(jnp.bfloat16) * scale)
            for at in range(0, tok, LANES)
        ]
        return jnp.dot(jnp.concatenate(weights, axis=1), values, preferred_element_type=jnp.float32)

    acc[...] = weighted(0)

    def absorb(back, carry):
        acc[...] += weighted(back)
        return carry

    lax.fori_loop(1, earlier + 1, absorb, 0)
    order = place_ref[pl.ds(position, 1), :]
    move = (lax.broadcasted_iota(jnp.int32, (tok, tok), 0) == order).astype(jnp.float32).astype(jnp.bfloat16)
    for head in range(heads):
        part = slice(head * tok, (head + 1) * tok)
        result = (acc[part, :HD] / acc[part, HD:]).astype(jnp.bfloat16)
        moved = jnp.dot(move, result, preferred_element_type=jnp.float32)
        out_ref[:, head * HD : (head + 1) * HD] = moved.astype(jnp.bfloat16)


def attend(lengths, send_place, query_rows, mine, theirs, groups, so_far):
    tok, width = query_rows.shape
    kv_local = mine.shape[2] // (2 * HD)
    share = width // kv_local
    heads = share // HD
    reach = 2 * (mine.shape[0] - 1)
    count = groups[1] - groups[0]
    whole = lambda a: pl.BlockSpec(a.shape, lambda i: (0,) * a.ndim)
    in_specs = [
        pl.BlockSpec(memory_space=pltpu.SMEM),
        whole(send_place),
        pl.BlockSpec((tok, share), lambda i: (0, i + groups[0])),
        whole(mine),
        whole(theirs),
    ]
    operands = [lengths, send_place, query_rows, mine, theirs]
    aliases = {}
    if so_far is not None:
        aliases = {len(operands): 0}
        in_specs.append(pl.BlockSpec(memory_space=pl.ANY))
        operands.append(so_far)
    return pl.pallas_call(
        functools.partial(attend_kernel, kv_local, groups[0]),
        grid=(count,),
        in_specs=in_specs,
        out_specs=pl.BlockSpec((tok, share), lambda i: (0, i + groups[0])),
        out_shape=jax.ShapeDtypeStruct((tok, width), jnp.bfloat16),
        scratch_shapes=[
            pltpu.VMEM((heads * tok, 2 * HD), jnp.bfloat16),
            pltpu.VMEM((reach + 1, heads * tok, tok), jnp.float32),
            pltpu.VMEM((heads * tok, LANES), jnp.float32),
            pltpu.VMEM((heads * tok, 2 * HD), jnp.float32),
        ],
        input_output_aliases=aliases,
        compiler_params=pltpu.CompilerParams(vmem_limit_bytes=VMEM_LIMIT // 2 + 4 * (reach + 1) * heads * tok * tok),
        cost_estimate=pl.CostEstimate(
            flops=tok * share * count, bytes_accessed=tok * share * count, transcendentals=0
        ),
        name="attend",
    )(*operands)


def shifted(value, steps):
    count = lax.axis_size("seq")
    return lax.ppermute(value, "seq", [(source, source + steps) for source in range(count - steps)])


def with_partner(held):
    mine = jnp.stack(held)
    count = lax.axis_size("seq")
    return mine, lax.ppermute(mine, "seq", [(source, source ^ 1) for source in range(count)])


def even_back(value, reach):
    return [value] + [shifted(value, 2 * k) for k in range(1, (reach + 1) // 2 + 1)]


def local(
    x_branch,
    z_branch,
    conv_weight,
    conv_bias,
    xproj_weight,
    dt_weight,
    dt_bias,
    decay_rate,
    skip_gain,
    query_rows,
    key_rows,
    value_rows,
    lengths,
    destination,
):
    tok = x_branch.shape[0]
    n_seq = lax.axis_size("seq")
    n_mp = lax.axis_size("mp")
    low_rank = dt_weight.shape[0]
    reach = n_seq // 2
    run_rows = tok // n_seq
    kv_local = key_rows.shape[1] // HD
    fence = lax.optimization_barrier

    halo, kv = pack(x_branch, key_rows, value_rows)
    earlier_rows = shifted(halo, 1)
    held = even_back(kv, reach)
    send_place = ((destination // tok) * run_rows + destination % run_rows).reshape(n_seq, tok)

    inner_act, partial = conv_project(lengths, x_branch, earlier_rows, conv_weight, conv_bias, xproj_weight)
    _, *held = fence((partial, *held))
    mine, theirs = with_partner(held)
    middle = max(kv_local // 2, 1)
    parts = [groups for groups in ((0, middle), (middle, kv_local)) if groups[0] < groups[1]]
    projected, attended = partial, None

    def attend_next():
        return attend(lengths, send_place, query_rows, mine, theirs, parts.pop(0), attended)

    steps = [1 << k for k in range((n_mp - 1).bit_length())]
    for step in steps:
        other = lax.ppermute(projected, "mp", [(source, source ^ step) for source in range(n_mp)])
        if parts:
            attended = attend_next()
            other, attended = fence((other, attended))
        projected = (projected.astype(jnp.float32) + other.astype(jnp.float32)).astype(jnp.bfloat16)
        if attended is not None:
            projected, attended = fence((projected, attended))
    while parts:
        attended = attend_next()
    projected, attended = fence((projected, attended))
    regrouped = lax.all_to_all(attended, "seq", split_axis=0, concat_axis=0, tiled=True)

    y, sums, state = local_scan(lengths, projected, dt_weight, dt_bias, decay_rate, inner_act)
    own, other = with_partner(even_back(state, reach))
    return tuple(
        join_states(
            projected, y, sums, inner_act, z_branch, decay_rate, skip_gain, regrouped, own, other, low_rank, reach
        )
    )


def solution(mesh):
    placed = (
        P("seq", "mp"),
        P("seq", "mp"),
        P(None, "mp"),
        P("mp"),
        P("mp", None),
        P(None, "mp"),
        P("mp"),
        P(None, "mp"),
        P("mp"),
        P("seq", "mp"),
        P("seq", "mp"),
        P("seq", "mp"),
        P(),
        P(),
    )
    return jax.shard_map(
        local,
        mesh=mesh,
        in_specs=placed,
        out_specs=(P("seq", "mp"), P("seq", "mp")),
        check_vma=False,
    )
```

```python
import functools

import jax
import jax.numpy as jnp
from jax import lax
from jax.experimental import pallas as pl
from jax.experimental.pallas import tpu as pltpu
from jax.sharding import PartitionSpec as P

HD = 128
LANES = 128
HALO = 16
LOG2E = 1.4426950408889634
RESET = 1e30
APART = 65536.0
VMEM_LIMIT = 32 * 1024 * 1024
VMEM_MOST = 56 * 1024 * 1024


def doc_edges(lengths_ref):
    starts, ends, total = [], [], 0
    for i in range(lengths_ref.shape[0]):
        starts.append(total)
        total = total + lengths_ref[i]
        ends.append(total)
    return starts, ends


def doc_start(places, starts):
    found = jnp.zeros_like(places)
    for start in starts[1:]:
        found = jnp.where(places >= start, start, found)
    return found


def channel_chunk(channels):
    return 512 if channels % 512 == 0 else channels


def pack_kernel(x_ref, k_ref, v_ref, halo_ref, kv_ref, sems):
    tok, width = k_ref.shape
    copies = [
        pltpu.make_async_copy(x_ref.at[pl.ds(tok - HALO, HALO), :], halo_ref, sems.at[0]),
        pltpu.make_async_copy(k_ref, kv_ref.at[:, pl.ds(0, width)], sems.at[1]),
        pltpu.make_async_copy(v_ref, kv_ref.at[:, pl.ds(width, width)], sems.at[2]),
    ]
    for copy in copies:
        copy.start()
    for copy in copies:
        copy.wait()


def pack(x_branch, key_rows, value_rows):
    tok, channels = x_branch.shape
    width = key_rows.shape[1]
    return pl.pallas_call(
        pack_kernel,
        in_specs=[pl.BlockSpec(memory_space=pl.ANY)] * 3,
        out_specs=[pl.BlockSpec(memory_space=pl.ANY)] * 2,
        out_shape=[
            jax.ShapeDtypeStruct((HALO, channels), x_branch.dtype),
            jax.ShapeDtypeStruct((tok, 2 * width), key_rows.dtype),
        ],
        scratch_shapes=[pltpu.SemaphoreType.DMA((3,))],
        compiler_params=pltpu.CompilerParams(vmem_limit_bytes=VMEM_MOST),
        cost_estimate=pl.CostEstimate(flops=0, bytes_accessed=16 * tok * width, transcendentals=0),
        name="pack",
    )(x_branch, key_rows, value_rows)


def conv_kernel(lengths_ref, x_ref, halo_ref, w_ref, b_ref, xp_ref, inner_ref, part_ref, ext, acc):
    tok, chunk = x_ref.shape
    starts, _ = doc_edges(lengths_ref)
    anchor = lax.axis_index("seq") * tok
    places = anchor + lax.broadcasted_iota(jnp.int32, (tok, LANES), 0)
    depth = places - doc_start(places, starts)
    ext[0:HALO, :] = halo_ref[...].astype(jnp.float32)
    ext[HALO:, :] = x_ref[...].astype(jnp.float32)
    for lane in range(0, chunk, LANES):
        cols = slice(lane, lane + LANES)
        total = b_ref[:, cols] + w_ref[0:1, cols] * ext[HALO:, cols]
        for lag in range(1, w_ref.shape[0]):
            window = ext[HALO - lag : HALO - lag + tok, cols]
            total += w_ref[lag : lag + 1, cols] * jnp.where(depth >= lag, window, 0.0)
        act = total * (0.5 + 0.5 * jnp.tanh(0.5 * total))
        inner_ref[:, cols] = act.astype(jnp.bfloat16)
    product = lax.dot_general(
        xp_ref[...], inner_ref[...], (((1,), (1,)), ((), ())), preferred_element_type=jnp.float32
    )
    at = pl.program_id(0)

    @pl.when(at == 0)
    def _():
        acc[...] = product

    @pl.when(at > 0)
    def _():
        acc[...] += product

    @pl.when(at == pl.num_programs(0) - 1)
    def _():
        part_ref[...] = acc[...].astype(jnp.bfloat16)


def conv_project(lengths, x_branch, halo, conv_weight, conv_bias, xproj_weight):
    tok, channels = x_branch.shape
    width = xproj_weight.shape[1]
    taps = conv_weight.shape[0]
    chunk = channel_chunk(channels)
    return pl.pallas_call(
        conv_kernel,
        grid=(channels // chunk,),
        in_specs=[
            pl.BlockSpec(memory_space=pltpu.SMEM),
            pl.BlockSpec((tok, chunk), lambda i: (0, i)),
            pl.BlockSpec((HALO, chunk), lambda i: (0, i)),
            pl.BlockSpec((taps, chunk), lambda i: (0, i)),
            pl.BlockSpec((1, chunk), lambda i: (0, i)),
            pl.BlockSpec((width, chunk), lambda i: (0, i)),
        ],
        out_specs=[
            pl.BlockSpec((tok, chunk), lambda i: (0, i)),
            pl.BlockSpec((width, tok), lambda i: (0, 0)),
        ],
        out_shape=[
            jax.ShapeDtypeStruct((tok, channels), jnp.bfloat16),
            jax.ShapeDtypeStruct((width, tok), jnp.bfloat16),
        ],
        scratch_shapes=[
            pltpu.VMEM((tok + HALO, chunk), jnp.float32),
            pltpu.VMEM((width, tok), jnp.float32),
        ],
        compiler_params=pltpu.CompilerParams(vmem_limit_bytes=VMEM_MOST),
        cost_estimate=pl.CostEstimate(
            flops=80 * tok * channels * width, bytes_accessed=8 * tok * channels, transcendentals=tok * channels
        ),
        name="conv_project",
    )(lengths, x_branch, halo, conv_weight, conv_bias.reshape(1, channels), xproj_weight.T)


ROWS = 8
PAIR = 2 * ROWS
BLOCK = 64


def spread(columns):
    tok, k = columns.shape
    own = lax.broadcasted_iota(jnp.int32, (k, k), 0) == lax.broadcasted_iota(jnp.int32, (k, k), 1)
    picked = jnp.where(own[None], columns.astype(jnp.float32)[:, None, :], 0.0).reshape(tok * k, k)
    ones = jnp.ones((k, LANES), jnp.bfloat16)
    return jnp.dot(picked.astype(jnp.bfloat16), ones, preferred_element_type=jnp.float32).reshape(tok, k, LANES)


def lane(tile):
    return slice(tile * LANES, (tile + 1) * LANES)


def sublanes(tile):
    return slice(tile * ROWS, (tile + 1) * ROWS)


def by_register(rate_ref, rates):
    states = rate_ref.shape[0]
    count = rates.shape[0] // states
    for n in range(states):
        for h in range(count):
            tiles = [rate_ref[n : n + 1, lane(h * ROWS + j)] for j in range(ROWS)]
            rates[n * count + h] = jnp.concatenate(tiles, axis=0) * (-LOG2E)


def local_kernel(
    lengths_ref,
    proj_ref,
    dtw_ref,
    bias_ref,
    rate_ref,
    inner_ref,
    y_ref,
    sum_ref,
    state_ref,
    low_cols,
    bc_spread,
    raw,
    rates,
    step_tiles,
    drive_tiles,
    carry,
):
    tok = proj_ref.shape[1]
    block, channels = inner_ref.shape
    states = rate_ref.shape[0]
    low_rank = dtw_ref.shape[0]
    tiles = channels // LANES
    count = tiles // ROWS
    starts, _ = doc_edges(lengths_ref)
    at = pl.program_id(0)

    @pl.when(at == 0)
    def _():
        low_cols[...] = proj_ref[:low_rank, :].astype(jnp.float32).T.astype(jnp.bfloat16)
        bc_spread[...] = spread(proj_ref[low_rank:, :].astype(jnp.float32).T)
        by_register(rate_ref, rates)
        carry[...] = jnp.zeros_like(carry)
        for first in range(0, tiles, 4):
            cols = slice(first * LANES, (first + 4) * LANES)
            part = jnp.dot(low_cols[...], dtw_ref[:, cols], preferred_element_type=jnp.float32)
            for i in range(4):
                raw[:, sublanes(first + i), :] = part[:, lane(i)].reshape(tok // ROWS, ROWS, LANES)

    def steps(pair, unused):
        rows = pl.ds(pl.multiple_of(pair * PAIR, PAIR), PAIR)
        places = lax.axis_index("seq") * tok + at * block + pair * PAIR
        places = places + lax.broadcasted_iota(jnp.int32, (PAIR, LANES), 0)
        at_start = places == doc_start(places, starts)
        for tile in range(tiles):
            inner = inner_ref[rows, lane(tile)].astype(jnp.float32)
            bias = bias_ref[:, lane(tile)]
            for k in range(2):
                biased = raw[at * (block // ROWS) + 2 * pair + k, sublanes(tile), :] + bias
                step = jnp.maximum(biased, 0.0) + jnp.log(1.0 + jnp.exp(-jnp.abs(biased)))
                drive_tiles[2 * pair + k, sublanes(tile), :] = step * inner[sublanes(k)]
                step_tiles[2 * pair + k, sublanes(tile), :] = jnp.where(at_start[sublanes(k)], RESET, step)
        return unused

    lax.fori_loop(0, block // PAIR, steps, 0)

    def scan(t8, held):
        held, total = list(held[0]), list(held[1])
        for first in range(0, ROWS, 2):
            tokens = range(first, first + 2)
            picked = [[pl.ds(r + h * ROWS * ROWS, ROWS, stride=ROWS) for h in range(count)] for r in tokens]
            step = [[step_tiles[t8, rows, :] for rows in of_token] for of_token in picked]
            drive = [[drive_tiles[t8, rows, :] for rows in of_token] for of_token in picked]
            out = [[None] * count for _ in tokens]
            for n in range(states):
                where = [at * block + t8 * ROWS + r for r in tokens]
                b_row = [bc_spread[token, n : n + 1, :] for token in where]
                c_row = [bc_spread[token, states + n : states + n + 1, :] for token in where]
                for h in range(count):
                    i = n * count + h
                    rate = rates[i]
                    decay = [jnp.exp2(rate * step[k][h]) for k in range(2)]
                    for k in range(2):
                        held[i] = decay[k] * held[i] + b_row[k] * drive[k][h]
                        term = c_row[k] * held[i]
                        out[k][h] = term if out[k][h] is None else out[k][h] + term
            for k, r in enumerate(tokens):
                for h in range(count):
                    total[h] = total[h] + step[k][h]
                    y_ref[t8 * ROWS + r, sublanes(h), :] = out[k][h]
                    sum_ref[t8 * ROWS + r, sublanes(h), :] = total[h]
        return held, total

    kept = states * count
    held = ([carry[i] for i in range(kept)], [carry[kept + h] for h in range(count)])
    held, total = lax.fori_loop(0, block // ROWS, scan, held)
    for i, value in enumerate(held + total):
        carry[i] = value

    @pl.when(at == pl.num_programs(0) - 1)
    def _():
        state_ref[: states * tiles, :] = jnp.concatenate(held, axis=0).astype(jnp.bfloat16)
        whole = jnp.concatenate(total, axis=0)
        high = whole.astype(jnp.bfloat16).astype(jnp.float32)
        state_ref[states * tiles :, :] = jnp.concatenate([high, whole - high], axis=0).astype(jnp.bfloat16)


def local_scan(lengths, projected, dt_weight, dt_bias, decay_rate, inner_act):
    tok, channels = inner_act.shape
    low_rank = dt_weight.shape[0]
    states = decay_rate.shape[0]
    tiles = channels // LANES
    count = tiles // ROWS
    whole = lambda a: pl.BlockSpec(a.shape, lambda i: (0,) * a.ndim)
    bias = dt_bias.reshape(1, channels)
    by_token = pl.BlockSpec((BLOCK, tiles, LANES), lambda i: (i, 0, 0))
    state_rows = (states + 2) * tiles
    return pl.pallas_call(
        local_kernel,
        grid=(tok // BLOCK,),
        in_specs=[
            pl.BlockSpec(memory_space=pltpu.SMEM),
            whole(projected),
            whole(dt_weight),
            whole(bias),
            whole(decay_rate),
            pl.BlockSpec((BLOCK, channels), lambda i: (i, 0)),
        ],
        out_specs=[by_token, by_token, pl.BlockSpec((state_rows, LANES), lambda i: (0, 0))],
        out_shape=[
            jax.ShapeDtypeStruct((tok, tiles, LANES), jnp.float32),
            jax.ShapeDtypeStruct((tok, tiles, LANES), jnp.float32),
            jax.ShapeDtypeStruct((state_rows, LANES), jnp.bfloat16),
        ],
        scratch_shapes=[
            pltpu.VMEM((tok, low_rank), jnp.bfloat16),
            pltpu.VMEM((tok, 2 * states, LANES), jnp.float32),
            pltpu.VMEM((tok // ROWS, tiles * ROWS, LANES), jnp.float32),
            pltpu.VMEM((states * count, ROWS, LANES), jnp.float32),
            pltpu.VMEM((BLOCK // ROWS, tiles * ROWS, LANES), jnp.float32),
            pltpu.VMEM((BLOCK // ROWS, tiles * ROWS, LANES), jnp.float32),
            pltpu.VMEM(((states + 1) * count, ROWS, LANES), jnp.float32),
        ],
        compiler_params=pltpu.CompilerParams(vmem_limit_bytes=VMEM_MOST),
        cost_estimate=pl.CostEstimate(
            flops=12 * tok * channels * states,
            bytes_accessed=12 * tok * channels,
            transcendentals=tok * channels * states,
        ),
        name="local_scan",
    )(lengths, projected, dt_weight, bias, decay_rate, inner_act)


def join_kernel(
    low_rank,
    reach,
    proj_ref,
    y_ref,
    sum_ref,
    inner_ref,
    z_ref,
    rate_ref,
    skip_ref,
    moved_ref,
    mine_ref,
    theirs_ref,
    out_ref,
    regrouped_ref,
    c_spread,
    rates,
    entering,
    rows_tiles,
):
    block, channels = z_ref.shape
    states = rate_ref.shape[0]
    tiles = channels // LANES
    count = tiles // ROWS
    kept = states * count
    at = pl.program_id(0)

    @pl.when(at == 0)
    def _():
        c_spread[...] = spread(proj_ref[low_rank + states :, :].astype(jnp.float32).T)
        by_register(rate_ref, rates)
        odd = lax.rem(lax.axis_index("seq"), 2)
        state = [jnp.zeros((ROWS, LANES), jnp.float32)] * kept
        for back in range(reach, 0, -1):
            ref, which = (mine_ref, back // 2) if back % 2 == 0 else (theirs_ref, (back + 1) // 2 - odd)
            sent = ref[which].astype(jnp.float32)
            totals = sent[states * tiles : (states + 1) * tiles] + sent[(states + 1) * tiles :]
            state = [
                jnp.exp2(rates[i] * totals[sublanes(i % count)]) * state[i] + sent[sublanes(i)] for i in range(kept)
            ]
        for i in range(kept):
            entering[i] = state[i]

    regrouped_ref[...] = moved_ref[...]

    def body(pair, unused):
        rows = pl.ds(pl.multiple_of(pair * PAIR, PAIR), PAIR)
        for k in range(2):
            first = pair * PAIR + k * ROWS
            total = [[sum_ref[first + r, sublanes(h), :] for h in range(count)] for r in range(ROWS)]
            out = [[y_ref[first + r, sublanes(h), :] for h in range(count)] for r in range(ROWS)]
            for n in range(states):
                c_row = [c_spread[at * block + first + r, n : n + 1, :] for r in range(ROWS)]
                for h in range(count):
                    rate, state = rates[n * count + h], entering[n * count + h]
                    for r in range(ROWS):
                        out[r][h] += jnp.exp2(rate * total[r][h]) * state * c_row[r]
            for r in range(ROWS):
                for h in range(count):
                    rows_tiles[k, pl.ds(r + h * ROWS * ROWS, ROWS, stride=ROWS), :] = out[r][h]
        for tile in range(tiles):
            cols = lane(tile)
            z = z_ref[rows, cols].astype(jnp.float32)
            gate = z * (0.5 + 0.5 * jnp.tanh(0.5 * z))
            scanned = jnp.concatenate([rows_tiles[k, sublanes(tile), :] for k in range(2)], axis=0)
            scanned = scanned + skip_ref[:, cols] * inner_ref[rows, cols].astype(jnp.float32)
            out_ref[rows, cols] = (scanned * gate).astype(jnp.bfloat16)
        return unused

    lax.fori_loop(0, block // PAIR, body, 0)


def join_states(projected, y, sums, inner_act, z_branch, decay_rate, skip_gain, moved, mine, theirs, low_rank, reach):
    tok, channels = z_branch.shape
    states = decay_rate.shape[0]
    tiles = channels // LANES
    count = tiles // ROWS
    whole = lambda a: pl.BlockSpec(a.shape, lambda i: (0,) * a.ndim)
    by_token = pl.BlockSpec((BLOCK, tiles, LANES), lambda i: (i, 0, 0))
    by_row = pl.BlockSpec((BLOCK, channels), lambda i: (i, 0))
    skip = skip_gain.reshape(1, channels)
    return pl.pallas_call(
        functools.partial(join_kernel, low_rank, reach),
        grid=(tok // BLOCK,),
        in_specs=[
            whole(projected),
            by_token,
            by_token,
            by_row,
            by_row,
            whole(decay_rate),
            whole(skip),
            by_row,
            whole(mine),
            whole(theirs),
        ],
        out_specs=[by_row, by_row],
        out_shape=[jax.ShapeDtypeStruct((tok, channels), jnp.bfloat16)] * 2,
        scratch_shapes=[
            pltpu.VMEM((tok, states, LANES), jnp.float32),
            pltpu.VMEM((states * count, ROWS, LANES), jnp.float32),
            pltpu.VMEM((states * count, ROWS, LANES), jnp.float32),
            pltpu.VMEM((2, tiles * ROWS, LANES), jnp.float32),
        ],
        compiler_params=pltpu.CompilerParams(vmem_limit_bytes=VMEM_MOST),
        cost_estimate=pl.CostEstimate(
            flops=8 * tok * channels * states,
            bytes_accessed=14 * tok * channels,
            transcendentals=tok * channels * states,
        ),
        name="join_states",
    )(projected, y, sums, inner_act, z_branch, decay_rate, skip, moved, mine, theirs)


def attend_kernel(kv_local, first_group, lengths_ref, place_ref, q_ref, mine_ref, theirs_ref, *refs):
    out_ref, queries, scores, tops, acc = refs[-5:]
    tok = q_ref.shape[0]
    heads = q_ref.shape[1] // HD
    group = pl.program_id(0) + first_group
    position = lax.axis_index("seq")
    odd = lax.rem(position, 2)
    anchor = position * tok
    scale = jnp.bfloat16(LOG2E * HD**-0.5)
    starts, ends = doc_edges(lengths_ref)
    lane = lax.broadcasted_iota(jnp.int32, (1, LANES), 1)
    first = jnp.full((1, LANES), 2**30, jnp.int32)
    last = jnp.zeros((1, LANES), jnp.int32)
    for i, (start, end) in enumerate(zip(starts, ends)):
        first = jnp.where(lane == i, start, first)
        last = jnp.where(lane == i, end, last)
    rows = lax.broadcasted_iota(jnp.int32, (tok, LANES), 0)

    def in_doc(base):
        return (rows + base >= first) & (rows + base < last)

    apart = jnp.where(in_doc(anchor) | (lane >= len(starts)), 0.0, -APART).astype(jnp.bfloat16)
    for head in range(heads):
        queries[head * tok : (head + 1) * tok, :HD] = q_ref[:, head * HD : (head + 1) * HD]
        queries[head * tok : (head + 1) * tok, HD:] = apart
    key_cols = pl.ds(pl.multiple_of(group * HD, HD), HD)
    value_cols = pl.ds(pl.multiple_of((group + kv_local) * HD, HD), HD)

    def rows_of(back, cols):
        if isinstance(back, int) and back == 0:
            return mine_ref[0, :, cols]
        ours = mine_ref[back // 2, :, cols]
        other = theirs_ref[(back + 1) // 2 - odd, :, cols]
        return jnp.where(lax.rem(back, 2) == 0, ours, other)

    def score(back):
        marks = jnp.where(in_doc(anchor - back * tok), 1.0, 0.0).astype(jnp.bfloat16)
        keys = jnp.concatenate([rows_of(back, key_cols), marks], axis=1)
        return lax.dot_general(queries[...], keys, (((1,), (1,)), ((), ())), preferred_element_type=jnp.float32)

    def widest(s):
        top = s[:, :LANES]
        for at in range(LANES, tok, LANES):
            top = jnp.maximum(top, s[:, at : at + LANES])
        return top

    own = score(0)
    causal = lax.broadcasted_iota(jnp.int32, (tok, tok), 1) <= lax.broadcasted_iota(jnp.int32, (tok, tok), 0)
    for head in range(heads):
        part = slice(head * tok, (head + 1) * tok)
        s = jnp.where(causal, own[part], -APART)
        scores[0, part, :] = s
        tops[part, :] = widest(s)

    begin = jnp.int32(0)
    for start in starts[1:]:
        begin = jnp.where(anchor >= start, start, begin)
    earlier = (anchor - begin + tok - 1) // tok

    def look(back, carry):
        s = score(back)
        scores[back] = s
        tops[...] = jnp.maximum(tops[...], widest(s))
        return carry

    lax.fori_loop(1, earlier + 1, look, 0)
    tops[...] = jnp.broadcast_to(jnp.max(tops[...], axis=1, keepdims=True), tops.shape)

    def weighted(back):
        values = jnp.concatenate([rows_of(back, value_cols), jnp.ones((tok, HD), jnp.bfloat16)], axis=1)
        top = tops[...]
        weights = [
            jnp.exp2((scores[back, :, at : at + LANES] - top).astype(jnp.bfloat16) * scale)
            for at in range(0, tok, LANES)
        ]
        return jnp.dot(jnp.concatenate(weights, axis=1), values, preferred_element_type=jnp.float32)

    acc[...] = weighted(0)

    def absorb(back, carry):
        acc[...] += weighted(back)
        return carry

    lax.fori_loop(1, earlier + 1, absorb, 0)
    order = place_ref[pl.ds(position, 1), :]
    move = (lax.broadcasted_iota(jnp.int32, (tok, tok), 0) == order).astype(jnp.float32).astype(jnp.bfloat16)
    for head in range(heads):
        part = slice(head * tok, (head + 1) * tok)
        result = (acc[part, :HD] / acc[part, HD:]).astype(jnp.bfloat16)
        moved = jnp.dot(move, result, preferred_element_type=jnp.float32)
        out_ref[:, head * HD : (head + 1) * HD] = moved.astype(jnp.bfloat16)


def attend(lengths, send_place, query_rows, mine, theirs, groups, so_far):
    tok, width = query_rows.shape
    kv_local = mine.shape[2] // (2 * HD)
    share = width // kv_local
    heads = share // HD
    reach = 2 * (mine.shape[0] - 1)
    count = groups[1] - groups[0]
    whole = lambda a: pl.BlockSpec(a.shape, lambda i: (0,) * a.ndim)
    in_specs = [
        pl.BlockSpec(memory_space=pltpu.SMEM),
        whole(send_place),
        pl.BlockSpec((tok, share), lambda i: (0, i + groups[0])),
        whole(mine),
        whole(theirs),
    ]
    operands = [lengths, send_place, query_rows, mine, theirs]
    aliases = {}
    if so_far is not None:
        aliases = {len(operands): 0}
        in_specs.append(pl.BlockSpec(memory_space=pl.ANY))
        operands.append(so_far)
    return pl.pallas_call(
        functools.partial(attend_kernel, kv_local, groups[0]),
        grid=(count,),
        in_specs=in_specs,
        out_specs=pl.BlockSpec((tok, share), lambda i: (0, i + groups[0])),
        out_shape=jax.ShapeDtypeStruct((tok, width), jnp.bfloat16),
        scratch_shapes=[
            pltpu.VMEM((heads * tok, 2 * HD), jnp.bfloat16),
            pltpu.VMEM((reach + 1, heads * tok, tok), jnp.float32),
            pltpu.VMEM((heads * tok, LANES), jnp.float32),
            pltpu.VMEM((heads * tok, 2 * HD), jnp.float32),
        ],
        input_output_aliases=aliases,
        compiler_params=pltpu.CompilerParams(vmem_limit_bytes=VMEM_LIMIT // 2 + 4 * (reach + 1) * heads * tok * tok),
        cost_estimate=pl.CostEstimate(
            flops=tok * share * count, bytes_accessed=tok * share * count, transcendentals=0
        ),
        name="attend",
    )(*operands)


def shifted(value, steps):
    count = lax.axis_size("seq")
    return lax.ppermute(value, "seq", [(source, source + steps) for source in range(count - steps)])


def with_partner(held):
    mine = jnp.stack(held)
    count = lax.axis_size("seq")
    return mine, lax.ppermute(mine, "seq", [(source, source ^ 1) for source in range(count)])


def even_back(value, reach):
    return [value] + [shifted(value, 2 * k) for k in range(1, (reach + 1) // 2 + 1)]


def local(
    x_branch,
    z_branch,
    conv_weight,
    conv_bias,
    xproj_weight,
    dt_weight,
    dt_bias,
    decay_rate,
    skip_gain,
    query_rows,
    key_rows,
    value_rows,
    lengths,
    destination,
):
    tok = x_branch.shape[0]
    n_seq = lax.axis_size("seq")
    n_mp = lax.axis_size("mp")
    low_rank = dt_weight.shape[0]
    reach = n_seq // 2
    run_rows = tok // n_seq
    kv_local = key_rows.shape[1] // HD
    fence = lax.optimization_barrier

    halo, kv = pack(x_branch, key_rows, value_rows)
    earlier_rows = shifted(halo, 1)
    held = even_back(kv, reach)
    send_place = ((destination // tok) * run_rows + destination % run_rows).reshape(n_seq, tok)

    inner_act, partial = conv_project(lengths, x_branch, earlier_rows, conv_weight, conv_bias, xproj_weight)
    _, *held = fence((partial, *held))
    mine, theirs = with_partner(held)
    middle = max(kv_local // 2, 1)
    parts = [groups for groups in ((0, middle), (middle, kv_local)) if groups[0] < groups[1]]
    projected, attended = partial, None

    def attend_next():
        return attend(lengths, send_place, query_rows, mine, theirs, parts.pop(0), attended)

    steps = [1 << k for k in range((n_mp - 1).bit_length())]
    for step in steps:
        other = lax.ppermute(projected, "mp", [(source, source ^ step) for source in range(n_mp)])
        if parts:
            attended = attend_next()
            other, attended = fence((other, attended))
        projected = (projected.astype(jnp.float32) + other.astype(jnp.float32)).astype(jnp.bfloat16)
        if parts:
            projected, attended = fence((projected, attended))
    while parts:
        attended = attend_next()
    regrouped = lax.all_to_all(attended, "seq", split_axis=0, concat_axis=0, tiled=True)
    projected, _ = fence((projected, attended))

    y, sums, state = local_scan(lengths, projected, dt_weight, dt_bias, decay_rate, inner_act)
    own, other = with_partner(even_back(state, reach))
    return tuple(
        join_states(
            projected, y, sums, inner_act, z_branch, decay_rate, skip_gain, regrouped, own, other, low_rank, reach
        )
    )


def solution(mesh):
    placed = (
        P("seq", "mp"),
        P("seq", "mp"),
        P(None, "mp"),
        P("mp"),
        P("mp", None),
        P(None, "mp"),
        P("mp"),
        P(None, "mp"),
        P("mp"),
        P("seq", "mp"),
        P("seq", "mp"),
        P("seq", "mp"),
        P(),
        P(),
    )
    return jax.shard_map(
        local,
        mesh=mesh,
        in_specs=placed,
        out_specs=(P("seq", "mp"), P("seq", "mp")),
        check_vma=False,
    )
```

```python
import functools

import jax
import jax.numpy as jnp
from jax import lax
from jax.experimental import pallas as pl
from jax.experimental.pallas import tpu as pltpu
from jax.sharding import PartitionSpec as P

HD = 128
LANES = 128
HALO = 16
LOG2E = 1.4426950408889634
RESET = 1e30
APART = 65536.0
VMEM_LIMIT = 32 * 1024 * 1024
VMEM_MOST = 56 * 1024 * 1024


def doc_edges(lengths_ref):
    starts, ends, total = [], [], 0
    for i in range(lengths_ref.shape[0]):
        starts.append(total)
        total = total + lengths_ref[i]
        ends.append(total)
    return starts, ends


def doc_start(places, starts):
    found = jnp.zeros_like(places)
    for start in starts[1:]:
        found = jnp.where(places >= start, start, found)
    return found


def channel_chunk(channels):
    return 512 if channels % 512 == 0 else channels


def pack_kernel(x_ref, k_ref, v_ref, halo_ref, kv_ref):
    width = k_ref.shape[1]
    halo_ref[...] = x_ref[...]
    kv_ref[:, :width] = k_ref[...]
    kv_ref[:, width:] = v_ref[...]


def pack(x_branch, key_rows, value_rows):
    tok, channels = x_branch.shape
    width = key_rows.shape[1]
    whole = lambda rows, columns: pl.BlockSpec((rows, columns), lambda i: (0, 0))
    return pl.pallas_call(
        pack_kernel,
        grid=(1,),
        in_specs=[
            pl.BlockSpec((HALO, channels), lambda i: (tok // HALO - 1, 0)),
            whole(tok, width),
            whole(tok, width),
        ],
        out_specs=[whole(HALO, channels), whole(tok, 2 * width)],
        out_shape=[
            jax.ShapeDtypeStruct((HALO, channels), x_branch.dtype),
            jax.ShapeDtypeStruct((tok, 2 * width), key_rows.dtype),
        ],
        compiler_params=pltpu.CompilerParams(vmem_limit_bytes=VMEM_MOST),
        cost_estimate=pl.CostEstimate(flops=0, bytes_accessed=16 * tok * width, transcendentals=0),
        name="pack",
    )(x_branch, key_rows, value_rows)


def conv_kernel(lengths_ref, x_ref, halo_ref, w_ref, b_ref, xp_ref, inner_ref, part_ref, ext, acc):
    tok, chunk = x_ref.shape
    starts, _ = doc_edges(lengths_ref)
    anchor = lax.axis_index("seq") * tok
    places = anchor + lax.broadcasted_iota(jnp.int32, (tok, LANES), 0)
    depth = places - doc_start(places, starts)
    ext[0:HALO, :] = halo_ref[...].astype(jnp.float32)
    ext[HALO:, :] = x_ref[...].astype(jnp.float32)
    for lane in range(0, chunk, LANES):
        cols = slice(lane, lane + LANES)
        total = b_ref[:, cols] + w_ref[0:1, cols] * ext[HALO:, cols]
        for lag in range(1, w_ref.shape[0]):
            window = ext[HALO - lag : HALO - lag + tok, cols]
            total += w_ref[lag : lag + 1, cols] * jnp.where(depth >= lag, window, 0.0)
        act = total * (0.5 + 0.5 * jnp.tanh(0.5 * total))
        inner_ref[:, cols] = act.astype(jnp.bfloat16)
    product = lax.dot_general(
        xp_ref[...], inner_ref[...], (((1,), (1,)), ((), ())), preferred_element_type=jnp.float32
    )
    at = pl.program_id(0)

    @pl.when(at == 0)
    def _():
        acc[...] = product

    @pl.when(at > 0)
    def _():
        acc[...] += product

    @pl.when(at == pl.num_programs(0) - 1)
    def _():
        part_ref[...] = acc[...].astype(jnp.bfloat16)


def conv_project(lengths, x_branch, halo, conv_weight, conv_bias, xproj_weight):
    tok, channels = x_branch.shape
    width = xproj_weight.shape[1]
    taps = conv_weight.shape[0]
    chunk = channel_chunk(channels)
    return pl.pallas_call(
        conv_kernel,
        grid=(channels // chunk,),
        in_specs=[
            pl.BlockSpec(memory_space=pltpu.SMEM),
            pl.BlockSpec((tok, chunk), lambda i: (0, i)),
            pl.BlockSpec((HALO, chunk), lambda i: (0, i)),
            pl.BlockSpec((taps, chunk), lambda i: (0, i)),
            pl.BlockSpec((1, chunk), lambda i: (0, i)),
            pl.BlockSpec((width, chunk), lambda i: (0, i)),
        ],
        out_specs=[
            pl.BlockSpec((tok, chunk), lambda i: (0, i)),
            pl.BlockSpec((width, tok), lambda i: (0, 0)),
        ],
        out_shape=[
            jax.ShapeDtypeStruct((tok, channels), jnp.bfloat16),
            jax.ShapeDtypeStruct((width, tok), jnp.bfloat16),
        ],
        scratch_shapes=[
            pltpu.VMEM((tok + HALO, chunk), jnp.float32),
            pltpu.VMEM((width, tok), jnp.float32),
        ],
        compiler_params=pltpu.CompilerParams(vmem_limit_bytes=VMEM_MOST),
        cost_estimate=pl.CostEstimate(
            flops=80 * tok * channels * width, bytes_accessed=8 * tok * channels, transcendentals=tok * channels
        ),
        name="conv_project",
    )(lengths, x_branch, halo, conv_weight, conv_bias.reshape(1, channels), xproj_weight.T)


ROWS = 8
PAIR = 2 * ROWS
BLOCK = 64


def spread(columns):
    tok, k = columns.shape
    own = lax.broadcasted_iota(jnp.int32, (k, k), 0) == lax.broadcasted_iota(jnp.int32, (k, k), 1)
    picked = jnp.where(own[None], columns.astype(jnp.float32)[:, None, :], 0.0).reshape(tok * k, k)
    ones = jnp.ones((k, LANES), jnp.bfloat16)
    return jnp.dot(picked.astype(jnp.bfloat16), ones, preferred_element_type=jnp.float32).reshape(tok, k, LANES)


def lane(tile):
    return slice(tile * LANES, (tile + 1) * LANES)


def sublanes(tile):
    return slice(tile * ROWS, (tile + 1) * ROWS)


def added(one_ref, other_ref, rows):
    total = one_ref[rows, :].astype(jnp.float32) + other_ref[rows, :].astype(jnp.float32)
    return total.astype(jnp.bfloat16).astype(jnp.float32)


def by_register(rate_ref, rates):
    states = rate_ref.shape[0]
    count = rates.shape[0] // states
    for n in range(states):
        for h in range(count):
            tiles = [rate_ref[n : n + 1, lane(h * ROWS + j)] for j in range(ROWS)]
            rates[n * count + h] = -jnp.concatenate(tiles, axis=0)


def local_kernel(
    lengths_ref,
    proj_ref,
    other_ref,
    dtw_ref,
    bias_ref,
    rate_ref,
    inner_ref,
    y_ref,
    sum_ref,
    state_ref,
    low_cols,
    bc_spread,
    raw,
    rates,
    step_tiles,
    drive_tiles,
    carry,
):
    tok = proj_ref.shape[1]
    block, channels = inner_ref.shape
    states = rate_ref.shape[0]
    low_rank = dtw_ref.shape[0]
    tiles = channels // LANES
    count = tiles // ROWS
    starts, _ = doc_edges(lengths_ref)
    at = pl.program_id(0)

    @pl.when(at == 0)
    def _():
        low_cols[...] = added(proj_ref, other_ref, slice(0, low_rank)).T.astype(jnp.bfloat16)
        bc_spread[...] = spread(added(proj_ref, other_ref, slice(low_rank, None)).T)
        by_register(rate_ref, rates)
        carry[...] = jnp.zeros_like(carry)
        for first in range(0, tiles, 4):
            cols = slice(first * LANES, (first + 4) * LANES)
            part = jnp.dot(low_cols[...], dtw_ref[:, cols], preferred_element_type=jnp.float32)
            for i in range(4):
                raw[:, sublanes(first + i), :] = part[:, lane(i)].reshape(tok // ROWS, ROWS, LANES)

    def steps(pair, unused):
        rows = pl.ds(pl.multiple_of(pair * PAIR, PAIR), PAIR)
        places = lax.axis_index("seq") * tok + at * block + pair * PAIR
        places = places + lax.broadcasted_iota(jnp.int32, (PAIR, LANES), 0)
        at_start = places == doc_start(places, starts)
        for tile in range(tiles):
            inner = inner_ref[rows, lane(tile)].astype(jnp.float32)
            bias = bias_ref[:, lane(tile)]
            for k in range(2):
                biased = raw[at * (block // ROWS) + 2 * pair + k, sublanes(tile), :] + bias
                step = jnp.maximum(biased, 0.0) + jnp.log(1.0 + jnp.exp(-jnp.abs(biased)))
                drive_tiles[2 * pair + k, sublanes(tile), :] = step * inner[sublanes(k)]
                step_tiles[2 * pair + k, sublanes(tile), :] = jnp.where(at_start[sublanes(k)], RESET, step)
        return unused

    lax.fori_loop(0, block // PAIR, steps, 0)

    def scan(t8, held):
        held, total = list(held[0]), list(held[1])
        for first in range(0, ROWS, 2):
            tokens = range(first, first + 2)
            picked = [[pl.ds(r + h * ROWS * ROWS, ROWS, stride=ROWS) for h in range(count)] for r in tokens]
            step = [[step_tiles[t8, rows, :] for rows in of_token] for of_token in picked]
            drive = [[drive_tiles[t8, rows, :] for rows in of_token] for of_token in picked]
            out = [[None] * count for _ in tokens]
            for n in range(states):
                where = [at * block + t8 * ROWS + r for r in tokens]
                b_row = [bc_spread[token, n : n + 1, :] for token in where]
                c_row = [bc_spread[token, states + n : states + n + 1, :] for token in where]
                for h in range(count):
                    i = n * count + h
                    rate = rates[i]
                    decay = [jnp.exp(rate * step[k][h]) for k in range(2)]
                    for k in range(2):
                        held[i] = decay[k] * held[i] + b_row[k] * drive[k][h]
                        term = c_row[k] * held[i]
                        out[k][h] = term if out[k][h] is None else out[k][h] + term
            for k, r in enumerate(tokens):
                for h in range(count):
                    total[h] = total[h] + step[k][h]
                    y_ref[t8 * ROWS + r, sublanes(h), :] = out[k][h]
                    sum_ref[t8 * ROWS + r, sublanes(h), :] = total[h]
        return held, total

    kept = states * count
    held = ([carry[i] for i in range(kept)], [carry[kept + h] for h in range(count)])
    held, total = lax.fori_loop(0, block // ROWS, scan, held)
    for i, value in enumerate(held + total):
        carry[i] = value

    @pl.when(at == pl.num_programs(0) - 1)
    def _():
        state_ref[: states * tiles, :] = jnp.concatenate(held, axis=0).astype(jnp.bfloat16)
        whole = jnp.concatenate(total, axis=0)
        high = whole.astype(jnp.bfloat16).astype(jnp.float32)
        state_ref[states * tiles :, :] = jnp.concatenate([high, whole - high], axis=0).astype(jnp.bfloat16)


def local_scan(lengths, projected, other, dt_weight, dt_bias, decay_rate, inner_act):
    tok, channels = inner_act.shape
    low_rank = dt_weight.shape[0]
    states = decay_rate.shape[0]
    tiles = channels // LANES
    count = tiles // ROWS
    whole = lambda a: pl.BlockSpec(a.shape, lambda i: (0,) * a.ndim)
    bias = dt_bias.reshape(1, channels)
    by_token = pl.BlockSpec((BLOCK, tiles, LANES), lambda i: (i, 0, 0))
    state_rows = (states + 2) * tiles
    return pl.pallas_call(
        local_kernel,
        grid=(tok // BLOCK,),
        in_specs=[
            pl.BlockSpec(memory_space=pltpu.SMEM),
            whole(projected),
            whole(other),
            whole(dt_weight),
            whole(bias),
            whole(decay_rate),
            pl.BlockSpec((BLOCK, channels), lambda i: (i, 0)),
        ],
        out_specs=[by_token, by_token, pl.BlockSpec((state_rows, LANES), lambda i: (0, 0))],
        out_shape=[
            jax.ShapeDtypeStruct((tok, tiles, LANES), jnp.float32),
            jax.ShapeDtypeStruct((tok, tiles, LANES), jnp.float32),
            jax.ShapeDtypeStruct((state_rows, LANES), jnp.bfloat16),
        ],
        scratch_shapes=[
            pltpu.VMEM((tok, low_rank), jnp.bfloat16),
            pltpu.VMEM((tok, 2 * states, LANES), jnp.float32),
            pltpu.VMEM((tok // ROWS, tiles * ROWS, LANES), jnp.float32),
            pltpu.VMEM((states * count, ROWS, LANES), jnp.float32),
            pltpu.VMEM((BLOCK // ROWS, tiles * ROWS, LANES), jnp.float32),
            pltpu.VMEM((BLOCK // ROWS, tiles * ROWS, LANES), jnp.float32),
            pltpu.VMEM(((states + 1) * count, ROWS, LANES), jnp.float32),
        ],
        compiler_params=pltpu.CompilerParams(vmem_limit_bytes=VMEM_MOST),
        cost_estimate=pl.CostEstimate(
            flops=12 * tok * channels * states,
            bytes_accessed=12 * tok * channels,
            transcendentals=tok * channels * states,
        ),
        name="local_scan",
    )(lengths, projected, other, dt_weight, bias, decay_rate, inner_act)


def join_kernel(
    low_rank,
    reach,
    proj_ref,
    other_ref,
    y_ref,
    sum_ref,
    inner_ref,
    z_ref,
    rate_ref,
    skip_ref,
    moved_ref,
    mine_ref,
    theirs_ref,
    out_ref,
    regrouped_ref,
    c_spread,
    rates,
    entering,
    rows_tiles,
):
    block, channels = z_ref.shape
    states = rate_ref.shape[0]
    tiles = channels // LANES
    count = tiles // ROWS
    kept = states * count
    at = pl.program_id(0)

    @pl.when(at == 0)
    def _():
        c_spread[...] = spread(added(proj_ref, other_ref, slice(low_rank + states, None)).T)
        by_register(rate_ref, rates)
        odd = lax.rem(lax.axis_index("seq"), 2)
        state = [jnp.zeros((ROWS, LANES), jnp.float32)] * kept
        for back in range(reach, 0, -1):
            ref, which = (mine_ref, back // 2) if back % 2 == 0 else (theirs_ref, (back + 1) // 2 - odd)
            sent = ref[which].astype(jnp.float32)
            totals = sent[states * tiles : (states + 1) * tiles] + sent[(states + 1) * tiles :]
            state = [
                jnp.exp(rates[i] * totals[sublanes(i % count)]) * state[i] + sent[sublanes(i)] for i in range(kept)
            ]
        for i in range(kept):
            entering[i] = state[i]

    regrouped_ref[...] = moved_ref[...]

    def body(pair, unused):
        rows = pl.ds(pl.multiple_of(pair * PAIR, PAIR), PAIR)
        for k in range(2):
            first = pair * PAIR + k * ROWS
            total = [[sum_ref[first + r, sublanes(h), :] for h in range(count)] for r in range(ROWS)]
            out = [[y_ref[first + r, sublanes(h), :] for h in range(count)] for r in range(ROWS)]
            for n in range(states):
                c_row = [c_spread[at * block + first + r, n : n + 1, :] for r in range(ROWS)]
                for h in range(count):
                    rate, state = rates[n * count + h], entering[n * count + h]
                    for r in range(ROWS):
                        out[r][h] += jnp.exp(rate * total[r][h]) * state * c_row[r]
            for r in range(ROWS):
                for h in range(count):
                    rows_tiles[k, pl.ds(r + h * ROWS * ROWS, ROWS, stride=ROWS), :] = out[r][h]
        for tile in range(tiles):
            cols = lane(tile)
            z = z_ref[rows, cols].astype(jnp.float32)
            gate = z * (0.5 + 0.5 * jnp.tanh(0.5 * z))
            scanned = jnp.concatenate([rows_tiles[k, sublanes(tile), :] for k in range(2)], axis=0)
            scanned = scanned + skip_ref[:, cols] * inner_ref[rows, cols].astype(jnp.float32)
            out_ref[rows, cols] = (scanned * gate).astype(jnp.bfloat16)
        return unused

    lax.fori_loop(0, block // PAIR, body, 0)


def join_states(projected, other, y, sums, inner_act, z_branch, decay_rate, skip_gain, moved, mine, theirs, low_rank, reach):
    tok, channels = z_branch.shape
    states = decay_rate.shape[0]
    tiles = channels // LANES
    count = tiles // ROWS
    whole = lambda a: pl.BlockSpec(a.shape, lambda i: (0,) * a.ndim)
    by_token = pl.BlockSpec((BLOCK, tiles, LANES), lambda i: (i, 0, 0))
    by_row = pl.BlockSpec((BLOCK, channels), lambda i: (i, 0))
    skip = skip_gain.reshape(1, channels)
    return pl.pallas_call(
        functools.partial(join_kernel, low_rank, reach),
        grid=(tok // BLOCK,),
        in_specs=[
            whole(projected),
            whole(other),
            by_token,
            by_token,
            by_row,
            by_row,
            whole(decay_rate),
            whole(skip),
            by_row,
            whole(mine),
            whole(theirs),
        ],
        out_specs=[by_row, by_row],
        out_shape=[jax.ShapeDtypeStruct((tok, channels), jnp.bfloat16)] * 2,
        scratch_shapes=[
            pltpu.VMEM((tok, states, LANES), jnp.float32),
            pltpu.VMEM((states * count, ROWS, LANES), jnp.float32),
            pltpu.VMEM((states * count, ROWS, LANES), jnp.float32),
            pltpu.VMEM((2, tiles * ROWS, LANES), jnp.float32),
        ],
        compiler_params=pltpu.CompilerParams(vmem_limit_bytes=VMEM_MOST),
        cost_estimate=pl.CostEstimate(
            flops=8 * tok * channels * states,
            bytes_accessed=14 * tok * channels,
            transcendentals=tok * channels * states,
        ),
        name="join_states",
    )(projected, other, y, sums, inner_act, z_branch, decay_rate, skip, moved, mine, theirs)


def attend_kernel(kv_local, first_group, lengths_ref, place_ref, q_ref, mine_ref, theirs_ref, *refs):
    out_ref, queries, scores, tops, acc = refs[-5:]
    tok = q_ref.shape[0]
    heads = q_ref.shape[1] // HD
    group = pl.program_id(0) + first_group
    position = lax.axis_index("seq")
    odd = lax.rem(position, 2)
    anchor = position * tok
    scale = jnp.bfloat16(LOG2E * HD**-0.5)
    starts, ends = doc_edges(lengths_ref)
    lane = lax.broadcasted_iota(jnp.int32, (1, LANES), 1)
    first = jnp.full((1, LANES), 2**30, jnp.int32)
    last = jnp.zeros((1, LANES), jnp.int32)
    for i, (start, end) in enumerate(zip(starts, ends)):
        first = jnp.where(lane == i, start, first)
        last = jnp.where(lane == i, end, last)
    rows = lax.broadcasted_iota(jnp.int32, (tok, LANES), 0)

    def in_doc(base):
        return (rows + base >= first) & (rows + base < last)

    apart = jnp.where(in_doc(anchor) | (lane >= len(starts)), 0.0, -APART).astype(jnp.bfloat16)
    for head in range(heads):
        queries[head * tok : (head + 1) * tok, :HD] = q_ref[:, head * HD : (head + 1) * HD]
        queries[head * tok : (head + 1) * tok, HD:] = apart
    key_cols = pl.ds(pl.multiple_of(group * HD, HD), HD)
    value_cols = pl.ds(pl.multiple_of((group + kv_local) * HD, HD), HD)

    def rows_of(back, cols):
        if isinstance(back, int) and back == 0:
            return mine_ref[0, :, cols]
        ours = mine_ref[back // 2, :, cols]
        other = theirs_ref[(back + 1) // 2 - odd, :, cols]
        return jnp.where(lax.rem(back, 2) == 0, ours, other)

    def score(back):
        marks = jnp.where(in_doc(anchor - back * tok), 1.0, 0.0).astype(jnp.bfloat16)
        keys = jnp.concatenate([rows_of(back, key_cols), marks], axis=1)
        return lax.dot_general(queries[...], keys, (((1,), (1,)), ((), ())), preferred_element_type=jnp.float32)

    def widest(s):
        top = s[:, :LANES]
        for at in range(LANES, tok, LANES):
            top = jnp.maximum(top, s[:, at : at + LANES])
        return top

    own = score(0)
    causal = lax.broadcasted_iota(jnp.int32, (tok, tok), 1) <= lax.broadcasted_iota(jnp.int32, (tok, tok), 0)
    for head in range(heads):
        part = slice(head * tok, (head + 1) * tok)
        s = jnp.where(causal, own[part], -APART)
        scores[0, part, :] = s
        tops[part, :] = widest(s)

    begin = jnp.int32(0)
    for start in starts[1:]:
        begin = jnp.where(anchor >= start, start, begin)
    earlier = (anchor - begin + tok - 1) // tok

    def look(back, carry):
        s = score(back)
        scores[back] = s
        tops[...] = jnp.maximum(tops[...], widest(s))
        return carry

    lax.fori_loop(1, earlier + 1, look, 0)
    tops[...] = jnp.broadcast_to(jnp.max(tops[...], axis=1, keepdims=True), tops.shape)

    def weighted(back):
        values = jnp.concatenate([rows_of(back, value_cols), jnp.ones((tok, HD), jnp.bfloat16)], axis=1)
        top = tops[...]
        weights = [
            jnp.exp2((scores[back, :, at : at + LANES] - top).astype(jnp.bfloat16) * scale)
            for at in range(0, tok, LANES)
        ]
        return jnp.dot(jnp.concatenate(weights, axis=1), values, preferred_element_type=jnp.float32)

    acc[...] = weighted(0)

    def absorb(back, carry):
        acc[...] += weighted(back)
        return carry

    lax.fori_loop(1, earlier + 1, absorb, 0)
    order = place_ref[pl.ds(position, 1), :]
    move = (lax.broadcasted_iota(jnp.int32, (tok, tok), 0) == order).astype(jnp.float32).astype(jnp.bfloat16)
    for head in range(heads):
        part = slice(head * tok, (head + 1) * tok)
        result = (acc[part, :HD] / acc[part, HD:]).astype(jnp.bfloat16)
        moved = jnp.dot(move, result, preferred_element_type=jnp.float32)
        out_ref[:, head * HD : (head + 1) * HD] = moved.astype(jnp.bfloat16)


def attend(lengths, send_place, query_rows, mine, theirs, groups, so_far):
    tok, width = query_rows.shape
    kv_local = mine.shape[2] // (2 * HD)
    share = width // kv_local
    heads = share // HD
    reach = 2 * (mine.shape[0] - 1)
    count = groups[1] - groups[0]
    whole = lambda a: pl.BlockSpec(a.shape, lambda i: (0,) * a.ndim)
    in_specs = [
        pl.BlockSpec(memory_space=pltpu.SMEM),
        whole(send_place),
        pl.BlockSpec((tok, share), lambda i: (0, i + groups[0])),
        whole(mine),
        whole(theirs),
    ]
    operands = [lengths, send_place, query_rows, mine, theirs]
    aliases = {}
    if so_far is not None:
        aliases = {len(operands): 0}
        in_specs.append(pl.BlockSpec(memory_space=pl.ANY))
        operands.append(so_far)
    return pl.pallas_call(
        functools.partial(attend_kernel, kv_local, groups[0]),
        grid=(count,),
        in_specs=in_specs,
        out_specs=pl.BlockSpec((tok, share), lambda i: (0, i + groups[0])),
        out_shape=jax.ShapeDtypeStruct((tok, width), jnp.bfloat16),
        scratch_shapes=[
            pltpu.VMEM((heads * tok, 2 * HD), jnp.bfloat16),
            pltpu.VMEM((reach + 1, heads * tok, tok), jnp.float32),
            pltpu.VMEM((heads * tok, LANES), jnp.float32),
            pltpu.VMEM((heads * tok, 2 * HD), jnp.float32),
        ],
        input_output_aliases=aliases,
        compiler_params=pltpu.CompilerParams(vmem_limit_bytes=VMEM_LIMIT // 2 + 4 * (reach + 1) * heads * tok * tok),
        cost_estimate=pl.CostEstimate(
            flops=tok * share * count, bytes_accessed=tok * share * count, transcendentals=0
        ),
        name="attend",
    )(*operands)


def shifted(value, steps):
    count = lax.axis_size("seq")
    return lax.ppermute(value, "seq", [(source, source + steps) for source in range(count - steps)])


def with_partner(held):
    mine = jnp.stack(held)
    count = lax.axis_size("seq")
    return mine, lax.ppermute(mine, "seq", [(source, source ^ 1) for source in range(count)])


def even_back(value, reach):
    return [value] + [shifted(value, 2 * k) for k in range(1, (reach + 1) // 2 + 1)]


def local(
    x_branch,
    z_branch,
    conv_weight,
    conv_bias,
    xproj_weight,
    dt_weight,
    dt_bias,
    decay_rate,
    skip_gain,
    query_rows,
    key_rows,
    value_rows,
    lengths,
    destination,
):
    tok = x_branch.shape[0]
    n_seq = lax.axis_size("seq")
    n_mp = lax.axis_size("mp")
    low_rank = dt_weight.shape[0]
    reach = n_seq // 2
    run_rows = tok // n_seq
    kv_local = key_rows.shape[1] // HD
    fence = lax.optimization_barrier

    halo, kv = pack(x_branch, key_rows, value_rows)
    earlier_rows = shifted(halo, 1)
    held = even_back(kv, reach)
    send_place = ((destination // tok) * run_rows + destination % run_rows).reshape(n_seq, tok)

    inner_act, partial = conv_project(lengths, x_branch, earlier_rows, conv_weight, conv_bias, xproj_weight)
    _, *held = fence((partial, *held))
    mine, theirs = with_partner(held)
    middle = max(kv_local // 2, 1)
    parts = [groups for groups in ((0, middle), (middle, kv_local)) if groups[0] < groups[1]]
    projected, attended = partial, None

    def attend_next():
        return attend(lengths, send_place, query_rows, mine, theirs, parts.pop(0), attended)

    steps = [1 << k for k in range((n_mp - 1).bit_length())]
    other = jnp.zeros_like(projected)
    for step in steps:
        if step > 1:
            projected = (projected.astype(jnp.float32) + other.astype(jnp.float32)).astype(jnp.bfloat16)
            if parts:
                projected, attended = fence((projected, attended))
        other = lax.ppermute(projected, "mp", [(source, source ^ step) for source in range(n_mp)])
        if parts:
            attended = attend_next()
            if step < steps[-1]:
                other, attended = fence((other, attended))
    while parts:
        attended = attend_next()
    regrouped = lax.all_to_all(attended, "seq", split_axis=0, concat_axis=0, tiled=True)
    projected, other, _ = fence((projected, other, attended))

    y, sums, state = local_scan(lengths, projected, other, dt_weight, dt_bias, decay_rate, inner_act)
    states = with_partner(even_back(state, reach))
    return tuple(
        join_states(
            projected,
            other,
            y,
            sums,
            inner_act,
            z_branch,
            decay_rate,
            skip_gain,
            regrouped,
            *states,
            low_rank,
            reach,
        )
    )


def solution(mesh):
    placed = (
        P("seq", "mp"),
        P("seq", "mp"),
        P(None, "mp"),
        P("mp"),
        P("mp", None),
        P(None, "mp"),
        P("mp"),
        P(None, "mp"),
        P("mp"),
        P("seq", "mp"),
        P("seq", "mp"),
        P("seq", "mp"),
        P(),
        P(),
    )
    return jax.shard_map(
        local,
        mesh=mesh,
        in_specs=placed,
        out_specs=(P("seq", "mp"), P("seq", "mp")),
        check_vma=False,
    )
```

```python
import functools

import jax
import jax.numpy as jnp
from jax import lax
from jax.experimental import pallas as pl
from jax.experimental.pallas import tpu as pltpu
from jax.sharding import PartitionSpec as P

HD = 128
LANES = 128
HALO = 16
LOG2E = 1.4426950408889634
RESET = 1e30
APART = 65536.0
VMEM_LIMIT = 32 * 1024 * 1024
VMEM_MOST = 56 * 1024 * 1024


def doc_edges(lengths_ref):
    starts, ends, total = [], [], 0
    for i in range(lengths_ref.shape[0]):
        starts.append(total)
        total = total + lengths_ref[i]
        ends.append(total)
    return starts, ends


def doc_start(places, starts):
    found = jnp.zeros_like(places)
    for start in starts[1:]:
        found = jnp.where(places >= start, start, found)
    return found


def channel_chunk(channels):
    return 512 if channels % 512 == 0 else channels


def pack_kernel(x_ref, k_ref, v_ref, halo_ref, kv_ref):
    width = k_ref.shape[1]
    halo_ref[...] = x_ref[...]
    kv_ref[:, :width] = k_ref[...]
    kv_ref[:, width:] = v_ref[...]


def pack(x_branch, key_rows, value_rows):
    tok, channels = x_branch.shape
    width = key_rows.shape[1]
    whole = lambda rows, columns: pl.BlockSpec((rows, columns), lambda i: (0, 0))
    return pl.pallas_call(
        pack_kernel,
        grid=(1,),
        in_specs=[
            pl.BlockSpec((HALO, channels), lambda i: (tok // HALO - 1, 0)),
            whole(tok, width),
            whole(tok, width),
        ],
        out_specs=[whole(HALO, channels), whole(tok, 2 * width)],
        out_shape=[
            jax.ShapeDtypeStruct((HALO, channels), x_branch.dtype),
            jax.ShapeDtypeStruct((tok, 2 * width), key_rows.dtype),
        ],
        compiler_params=pltpu.CompilerParams(vmem_limit_bytes=VMEM_MOST),
        cost_estimate=pl.CostEstimate(flops=0, bytes_accessed=16 * tok * width, transcendentals=0),
        name="pack",
    )(x_branch, key_rows, value_rows)


def conv_kernel(lengths_ref, x_ref, halo_ref, w_ref, b_ref, xp_ref, inner_ref, part_ref, ext, acc):
    tok, chunk = x_ref.shape
    starts, _ = doc_edges(lengths_ref)
    anchor = lax.axis_index("seq") * tok
    places = anchor + lax.broadcasted_iota(jnp.int32, (tok, LANES), 0)
    depth = places - doc_start(places, starts)
    ext[0:HALO, :] = halo_ref[...].astype(jnp.float32)
    ext[HALO:, :] = x_ref[...].astype(jnp.float32)
    for lane in range(0, chunk, LANES):
        cols = slice(lane, lane + LANES)
        total = b_ref[:, cols] + w_ref[0:1, cols] * ext[HALO:, cols]
        for lag in range(1, w_ref.shape[0]):
            window = ext[HALO - lag : HALO - lag + tok, cols]
            total += w_ref[lag : lag + 1, cols] * jnp.where(depth >= lag, window, 0.0)
        act = total * (0.5 + 0.5 * jnp.tanh(0.5 * total))
        inner_ref[:, cols] = act.astype(jnp.bfloat16)
    product = lax.dot_general(
        xp_ref[...], inner_ref[...], (((1,), (1,)), ((), ())), preferred_element_type=jnp.float32
    )
    at = pl.program_id(0)

    @pl.when(at == 0)
    def _():
        acc[...] = product

    @pl.when(at > 0)
    def _():
        acc[...] += product

    @pl.when(at == pl.num_programs(0) - 1)
    def _():
        part_ref[...] = acc[...].astype(jnp.bfloat16)


def conv_project(lengths, x_branch, halo, conv_weight, conv_bias, xproj_weight):
    tok, channels = x_branch.shape
    width = xproj_weight.shape[1]
    taps = conv_weight.shape[0]
    chunk = channel_chunk(channels)
    return pl.pallas_call(
        conv_kernel,
        grid=(channels // chunk,),
        in_specs=[
            pl.BlockSpec(memory_space=pltpu.SMEM),
            pl.BlockSpec((tok, chunk), lambda i: (0, i)),
            pl.BlockSpec((HALO, chunk), lambda i: (0, i)),
            pl.BlockSpec((taps, chunk), lambda i: (0, i)),
            pl.BlockSpec((1, chunk), lambda i: (0, i)),
            pl.BlockSpec((width, chunk), lambda i: (0, i)),
        ],
        out_specs=[
            pl.BlockSpec((tok, chunk), lambda i: (0, i)),
            pl.BlockSpec((width, tok), lambda i: (0, 0)),
        ],
        out_shape=[
            jax.ShapeDtypeStruct((tok, channels), jnp.bfloat16),
            jax.ShapeDtypeStruct((width, tok), jnp.bfloat16),
        ],
        scratch_shapes=[
            pltpu.VMEM((tok + HALO, chunk), jnp.float32),
            pltpu.VMEM((width, tok), jnp.float32),
        ],
        compiler_params=pltpu.CompilerParams(vmem_limit_bytes=VMEM_MOST),
        cost_estimate=pl.CostEstimate(
            flops=80 * tok * channels * width, bytes_accessed=8 * tok * channels, transcendentals=tok * channels
        ),
        name="conv_project",
    )(lengths, x_branch, halo, conv_weight, conv_bias.reshape(1, channels), xproj_weight.T)


ROWS = 8
PAIR = 2 * ROWS
BLOCK = 64


def spread(columns):
    tok, k = columns.shape
    own = lax.broadcasted_iota(jnp.int32, (k, k), 0) == lax.broadcasted_iota(jnp.int32, (k, k), 1)
    picked = jnp.where(own[None], columns.astype(jnp.float32)[:, None, :], 0.0).reshape(tok * k, k)
    ones = jnp.ones((k, LANES), jnp.bfloat16)
    return jnp.dot(picked.astype(jnp.bfloat16), ones, preferred_element_type=jnp.float32).reshape(tok, k, LANES)


def lane(tile):
    return slice(tile * LANES, (tile + 1) * LANES)


def sublanes(tile):
    return slice(tile * ROWS, (tile + 1) * ROWS)


def added(one_ref, other_ref, rows):
    total = one_ref[rows, :].astype(jnp.float32) + other_ref[rows, :].astype(jnp.float32)
    return total.astype(jnp.bfloat16).astype(jnp.float32)


def by_register(rate_ref, rates):
    states = rate_ref.shape[0]
    count = rates.shape[0] // states
    for n in range(states):
        for h in range(count):
            tiles = [rate_ref[n : n + 1, lane(h * ROWS + j)] for j in range(ROWS)]
            rates[n * count + h] = jnp.concatenate(tiles, axis=0) * (-LOG2E)


def local_kernel(
    lengths_ref,
    proj_ref,
    other_ref,
    dtw_ref,
    bias_ref,
    rate_ref,
    inner_ref,
    y_ref,
    sum_ref,
    state_ref,
    low_cols,
    bc_spread,
    raw,
    rates,
    step_tiles,
    drive_tiles,
    carry,
):
    tok = proj_ref.shape[1]
    block, channels = inner_ref.shape
    states = rate_ref.shape[0]
    low_rank = dtw_ref.shape[0]
    tiles = channels // LANES
    count = tiles // ROWS
    starts, _ = doc_edges(lengths_ref)
    at = pl.program_id(0)

    @pl.when(at == 0)
    def _():
        low_cols[...] = added(proj_ref, other_ref, slice(0, low_rank)).T.astype(jnp.bfloat16)
        bc_spread[...] = spread(added(proj_ref, other_ref, slice(low_rank, None)).T)
        by_register(rate_ref, rates)
        carry[...] = jnp.zeros_like(carry)
        for first in range(0, tiles, 4):
            cols = slice(first * LANES, (first + 4) * LANES)
            part = jnp.dot(low_cols[...], dtw_ref[:, cols], preferred_element_type=jnp.float32)
            for i in range(4):
                raw[:, sublanes(first + i), :] = part[:, lane(i)].reshape(tok // ROWS, ROWS, LANES)

    def steps(pair, unused):
        rows = pl.ds(pl.multiple_of(pair * PAIR, PAIR), PAIR)
        places = lax.axis_index("seq") * tok + at * block + pair * PAIR
        places = places + lax.broadcasted_iota(jnp.int32, (PAIR, LANES), 0)
        at_start = places == doc_start(places, starts)
        for tile in range(tiles):
            inner = inner_ref[rows, lane(tile)].astype(jnp.float32)
            bias = bias_ref[:, lane(tile)]
            for k in range(2):
                biased = raw[at * (block // ROWS) + 2 * pair + k, sublanes(tile), :] + bias
                step = jnp.maximum(biased, 0.0) + jnp.log(1.0 + jnp.exp(-jnp.abs(biased)))
                drive_tiles[2 * pair + k, sublanes(tile), :] = step * inner[sublanes(k)]
                step_tiles[2 * pair + k, sublanes(tile), :] = jnp.where(at_start[sublanes(k)], RESET, step)
        return unused

    lax.fori_loop(0, block // PAIR, steps, 0)

    def scan(t8, held):
        held, total = list(held[0]), list(held[1])
        for first in range(0, ROWS, 2):
            tokens = range(first, first + 2)
            picked = [[pl.ds(r + h * ROWS * ROWS, ROWS, stride=ROWS) for h in range(count)] for r in tokens]
            step = [[step_tiles[t8, rows, :] for rows in of_token] for of_token in picked]
            drive = [[drive_tiles[t8, rows, :] for rows in of_token] for of_token in picked]
            out = [[None] * count for _ in tokens]
            for n in range(states):
                where = [at * block + t8 * ROWS + r for r in tokens]
                b_row = [bc_spread[token, n : n + 1, :] for token in where]
                c_row = [bc_spread[token, states + n : states + n + 1, :] for token in where]
                for h in range(count):
                    i = n * count + h
                    rate = rates[i]
                    decay = [jnp.exp2(rate * step[k][h]) for k in range(2)]
                    for k in range(2):
                        held[i] = decay[k] * held[i] + b_row[k] * drive[k][h]
                        term = c_row[k] * held[i]
                        out[k][h] = term if out[k][h] is None else out[k][h] + term
            for k, r in enumerate(tokens):
                for h in range(count):
                    total[h] = total[h] + step[k][h]
                    y_ref[t8 * ROWS + r, sublanes(h), :] = out[k][h]
                    sum_ref[t8 * ROWS + r, sublanes(h), :] = total[h]
        return held, total

    kept = states * count
    held = ([carry[i] for i in range(kept)], [carry[kept + h] for h in range(count)])
    held, total = lax.fori_loop(0, block // ROWS, scan, held)
    for i, value in enumerate(held + total):
        carry[i] = value

    @pl.when(at == pl.num_programs(0) - 1)
    def _():
        state_ref[: states * tiles, :] = jnp.concatenate(held, axis=0).astype(jnp.bfloat16)
        whole = jnp.concatenate(total, axis=0)
        high = whole.astype(jnp.bfloat16).astype(jnp.float32)
        state_ref[states * tiles :, :] = jnp.concatenate([high, whole - high], axis=0).astype(jnp.bfloat16)


def local_scan(lengths, projected, other, dt_weight, dt_bias, decay_rate, inner_act):
    tok, channels = inner_act.shape
    low_rank = dt_weight.shape[0]
    states = decay_rate.shape[0]
    tiles = channels // LANES
    count = tiles // ROWS
    whole = lambda a: pl.BlockSpec(a.shape, lambda i: (0,) * a.ndim)
    bias = dt_bias.reshape(1, channels)
    by_token = pl.BlockSpec((BLOCK, tiles, LANES), lambda i: (i, 0, 0))
    state_rows = (states + 2) * tiles
    return pl.pallas_call(
        local_kernel,
        grid=(tok // BLOCK,),
        in_specs=[
            pl.BlockSpec(memory_space=pltpu.SMEM),
            whole(projected),
            whole(other),
            whole(dt_weight),
            whole(bias),
            whole(decay_rate),
            pl.BlockSpec((BLOCK, channels), lambda i: (i, 0)),
        ],
        out_specs=[by_token, by_token, pl.BlockSpec((state_rows, LANES), lambda i: (0, 0))],
        out_shape=[
            jax.ShapeDtypeStruct((tok, tiles, LANES), jnp.float32),
            jax.ShapeDtypeStruct((tok, tiles, LANES), jnp.float32),
            jax.ShapeDtypeStruct((state_rows, LANES), jnp.bfloat16),
        ],
        scratch_shapes=[
            pltpu.VMEM((tok, low_rank), jnp.bfloat16),
            pltpu.VMEM((tok, 2 * states, LANES), jnp.float32),
            pltpu.VMEM((tok // ROWS, tiles * ROWS, LANES), jnp.float32),
            pltpu.VMEM((states * count, ROWS, LANES), jnp.float32),
            pltpu.VMEM((BLOCK // ROWS, tiles * ROWS, LANES), jnp.float32),
            pltpu.VMEM((BLOCK // ROWS, tiles * ROWS, LANES), jnp.float32),
            pltpu.VMEM(((states + 1) * count, ROWS, LANES), jnp.float32),
        ],
        compiler_params=pltpu.CompilerParams(vmem_limit_bytes=VMEM_MOST),
        cost_estimate=pl.CostEstimate(
            flops=12 * tok * channels * states,
            bytes_accessed=12 * tok * channels,
            transcendentals=tok * channels * states,
        ),
        name="local_scan",
    )(lengths, projected, other, dt_weight, bias, decay_rate, inner_act)


def join_kernel(
    low_rank,
    reach,
    proj_ref,
    other_ref,
    y_ref,
    sum_ref,
    inner_ref,
    z_ref,
    rate_ref,
    skip_ref,
    moved_ref,
    mine_ref,
    theirs_ref,
    out_ref,
    regrouped_ref,
    c_spread,
    rates,
    entering,
    rows_tiles,
):
    block, channels = z_ref.shape
    states = rate_ref.shape[0]
    tiles = channels // LANES
    count = tiles // ROWS
    kept = states * count
    at = pl.program_id(0)

    @pl.when(at == 0)
    def _():
        c_spread[...] = spread(added(proj_ref, other_ref, slice(low_rank + states, None)).T)
        by_register(rate_ref, rates)
        odd = lax.rem(lax.axis_index("seq"), 2)
        state = [jnp.zeros((ROWS, LANES), jnp.float32)] * kept
        for back in range(reach, 0, -1):
            ref, which = (mine_ref, back // 2) if back % 2 == 0 else (theirs_ref, (back + 1) // 2 - odd)
            sent = ref[which].astype(jnp.float32)
            totals = sent[states * tiles : (states + 1) * tiles] + sent[(states + 1) * tiles :]
            state = [
                jnp.exp2(rates[i] * totals[sublanes(i % count)]) * state[i] + sent[sublanes(i)] for i in range(kept)
            ]
        for i in range(kept):
            entering[i] = state[i]

    regrouped_ref[...] = moved_ref[...]

    def body(pair, unused):
        rows = pl.ds(pl.multiple_of(pair * PAIR, PAIR), PAIR)
        for k in range(2):
            first = pair * PAIR + k * ROWS
            total = [[sum_ref[first + r, sublanes(h), :] for h in range(count)] for r in range(ROWS)]
            out = [[y_ref[first + r, sublanes(h), :] for h in range(count)] for r in range(ROWS)]
            for n in range(states):
                c_row = [c_spread[at * block + first + r, n : n + 1, :] for r in range(ROWS)]
                for h in range(count):
                    rate, state = rates[n * count + h], entering[n * count + h]
                    for r in range(ROWS):
                        out[r][h] += jnp.exp2(rate * total[r][h]) * state * c_row[r]
            for r in range(ROWS):
                for h in range(count):
                    rows_tiles[k, pl.ds(r + h * ROWS * ROWS, ROWS, stride=ROWS), :] = out[r][h]
        for tile in range(tiles):
            cols = lane(tile)
            z = z_ref[rows, cols].astype(jnp.float32)
            gate = z * (0.5 + 0.5 * jnp.tanh(0.5 * z))
            scanned = jnp.concatenate([rows_tiles[k, sublanes(tile), :] for k in range(2)], axis=0)
            scanned = scanned + skip_ref[:, cols] * inner_ref[rows, cols].astype(jnp.float32)
            out_ref[rows, cols] = (scanned * gate).astype(jnp.bfloat16)
        return unused

    lax.fori_loop(0, block // PAIR, body, 0)


def join_states(projected, other, y, sums, inner_act, z_branch, decay_rate, skip_gain, moved, mine, theirs, low_rank, reach):
    tok, channels = z_branch.shape
    states = decay_rate.shape[0]
    tiles = channels // LANES
    count = tiles // ROWS
    whole = lambda a: pl.BlockSpec(a.shape, lambda i: (0,) * a.ndim)
    by_token = pl.BlockSpec((BLOCK, tiles, LANES), lambda i: (i, 0, 0))
    by_row = pl.BlockSpec((BLOCK, channels), lambda i: (i, 0))
    skip = skip_gain.reshape(1, channels)
    return pl.pallas_call(
        functools.partial(join_kernel, low_rank, reach),
        grid=(tok // BLOCK,),
        in_specs=[
            whole(projected),
            whole(other),
            by_token,
            by_token,
            by_row,
            by_row,
            whole(decay_rate),
            whole(skip),
            by_row,
            whole(mine),
            whole(theirs),
        ],
        out_specs=[by_row, by_row],
        out_shape=[jax.ShapeDtypeStruct((tok, channels), jnp.bfloat16)] * 2,
        scratch_shapes=[
            pltpu.VMEM((tok, states, LANES), jnp.float32),
            pltpu.VMEM((states * count, ROWS, LANES), jnp.float32),
            pltpu.VMEM((states * count, ROWS, LANES), jnp.float32),
            pltpu.VMEM((2, tiles * ROWS, LANES), jnp.float32),
        ],
        compiler_params=pltpu.CompilerParams(vmem_limit_bytes=VMEM_MOST),
        cost_estimate=pl.CostEstimate(
            flops=8 * tok * channels * states,
            bytes_accessed=14 * tok * channels,
            transcendentals=tok * channels * states,
        ),
        name="join_states",
    )(projected, other, y, sums, inner_act, z_branch, decay_rate, skip, moved, mine, theirs)


def attend_kernel(
    lengths_ref,
    place_ref,
    q_ref,
    keys_mine,
    keys_theirs,
    values_mine,
    values_theirs,
    out_ref,
    queries,
    scores,
    tops,
    acc,
):
    tok = q_ref.shape[0]
    heads = q_ref.shape[1] // HD
    position = lax.axis_index("seq")
    odd = lax.rem(position, 2)
    anchor = position * tok
    scale = jnp.bfloat16(LOG2E * HD**-0.5)
    starts, ends = doc_edges(lengths_ref)
    lane = lax.broadcasted_iota(jnp.int32, (1, LANES), 1)
    first = jnp.full((1, LANES), 2**30, jnp.int32)
    last = jnp.zeros((1, LANES), jnp.int32)
    for i, (start, end) in enumerate(zip(starts, ends)):
        first = jnp.where(lane == i, start, first)
        last = jnp.where(lane == i, end, last)
    rows = lax.broadcasted_iota(jnp.int32, (tok, LANES), 0)

    def in_doc(base):
        return (rows + base >= first) & (rows + base < last)

    apart = jnp.where(in_doc(anchor) | (lane >= len(starts)), 0.0, -APART).astype(jnp.bfloat16)
    for head in range(heads):
        queries[head * tok : (head + 1) * tok, :HD] = q_ref[:, head * HD : (head + 1) * HD]
        queries[head * tok : (head + 1) * tok, HD:] = apart

    def rows_of(mine_ref, theirs_ref, back):
        if isinstance(back, int) and back == 0:
            return mine_ref[0]
        return jnp.where(lax.rem(back, 2) == 0, mine_ref[back // 2], theirs_ref[(back + 1) // 2 - odd])

    def score(back):
        marks = jnp.where(in_doc(anchor - back * tok), 1.0, 0.0).astype(jnp.bfloat16)
        keys = jnp.concatenate([rows_of(keys_mine, keys_theirs, back), marks], axis=1)
        return lax.dot_general(queries[...], keys, (((1,), (1,)), ((), ())), preferred_element_type=jnp.float32)

    def widest(s):
        top = s[:, :LANES]
        for at in range(LANES, tok, LANES):
            top = jnp.maximum(top, s[:, at : at + LANES])
        return top

    own = score(0)
    causal = lax.broadcasted_iota(jnp.int32, (tok, tok), 1) <= lax.broadcasted_iota(jnp.int32, (tok, tok), 0)
    for head in range(heads):
        part = slice(head * tok, (head + 1) * tok)
        s = jnp.where(causal, own[part], -APART)
        scores[0, part, :] = s
        tops[part, :] = widest(s)

    begin = jnp.int32(0)
    for start in starts[1:]:
        begin = jnp.where(anchor >= start, start, begin)
    earlier = (anchor - begin + tok - 1) // tok

    def look(back, carry):
        s = score(back)
        scores[back] = s
        tops[...] = jnp.maximum(tops[...], widest(s))
        return carry

    lax.fori_loop(1, earlier + 1, look, 0)
    tops[...] = jnp.broadcast_to(jnp.max(tops[...], axis=1, keepdims=True), tops.shape)

    def weighted(back):
        values = jnp.concatenate([rows_of(values_mine, values_theirs, back), jnp.ones((tok, HD), jnp.bfloat16)], axis=1)
        top = tops[...]
        weights = [
            jnp.exp2((scores[back, :, at : at + LANES] - top).astype(jnp.bfloat16) * scale)
            for at in range(0, tok, LANES)
        ]
        return jnp.dot(jnp.concatenate(weights, axis=1), values, preferred_element_type=jnp.float32)

    acc[...] = weighted(0)

    def absorb(back, carry):
        acc[...] += weighted(back)
        return carry

    lax.fori_loop(1, earlier + 1, absorb, 0)
    order = place_ref[pl.ds(position, 1), :]
    move = (lax.broadcasted_iota(jnp.int32, (tok, tok), 0) == order).astype(jnp.float32).astype(jnp.bfloat16)
    for head in range(heads):
        part = slice(head * tok, (head + 1) * tok)
        result = (acc[part, :HD] / acc[part, HD:]).astype(jnp.bfloat16)
        moved = jnp.dot(move, result, preferred_element_type=jnp.float32)
        out_ref[:, head * HD : (head + 1) * HD] = moved.astype(jnp.bfloat16)


def attend(lengths, send_place, query_rows, mine, theirs):
    tok, width = query_rows.shape
    kv_local = mine.shape[2] // (2 * HD)
    share = width // kv_local
    heads = share // HD
    reach = 2 * (mine.shape[0] - 1)
    by_group = pl.BlockSpec((tok, share), lambda i: (0, i))
    keys = pl.BlockSpec(mine.shape[:2] + (HD,), lambda i: (0, 0, i))
    values = pl.BlockSpec(mine.shape[:2] + (HD,), lambda i: (0, 0, i + kv_local))
    return pl.pallas_call(
        attend_kernel,
        grid=(kv_local,),
        in_specs=[
            pl.BlockSpec(memory_space=pltpu.SMEM),
            pl.BlockSpec(send_place.shape, lambda i: (0, 0)),
            by_group,
            keys,
            keys,
            values,
            values,
        ],
        out_specs=by_group,
        out_shape=jax.ShapeDtypeStruct((tok, width), jnp.bfloat16),
        scratch_shapes=[
            pltpu.VMEM((heads * tok, 2 * HD), jnp.bfloat16),
            pltpu.VMEM((reach + 1, heads * tok, tok), jnp.float32),
            pltpu.VMEM((heads * tok, LANES), jnp.float32),
            pltpu.VMEM((heads * tok, 2 * HD), jnp.float32),
        ],
        compiler_params=pltpu.CompilerParams(vmem_limit_bytes=VMEM_LIMIT // 2 + 4 * (reach + 1) * heads * tok * tok),
        cost_estimate=pl.CostEstimate(flops=tok * width, bytes_accessed=tok * width, transcendentals=0),
        name="attend",
    )(lengths, send_place, query_rows, mine, theirs, mine, theirs)


def shifted(value, steps):
    count = lax.axis_size("seq")
    return lax.ppermute(value, "seq", [(source, source + steps) for source in range(count - steps)])


def with_partner(held):
    mine = jnp.stack(held)
    count = lax.axis_size("seq")
    return mine, lax.ppermute(mine, "seq", [(source, source ^ 1) for source in range(count)])


def even_back(value, reach):
    return [value] + [shifted(value, 2 * k) for k in range(1, (reach + 1) // 2 + 1)]


def local(
    x_branch,
    z_branch,
    conv_weight,
    conv_bias,
    xproj_weight,
    dt_weight,
    dt_bias,
    decay_rate,
    skip_gain,
    query_rows,
    key_rows,
    value_rows,
    lengths,
    destination,
):
    tok = x_branch.shape[0]
    n_seq = lax.axis_size("seq")
    n_mp = lax.axis_size("mp")
    low_rank = dt_weight.shape[0]
    reach = n_seq // 2
    run_rows = tok // n_seq
    fence = lax.optimization_barrier

    halo, kv = pack(x_branch, key_rows, value_rows)
    earlier_rows = shifted(halo, 1)
    held = even_back(kv, reach)
    send_place = ((destination // tok) * run_rows + destination % run_rows).reshape(n_seq, tok)

    inner_act, partial = conv_project(lengths, x_branch, earlier_rows, conv_weight, conv_bias, xproj_weight)
    _, *held = fence((partial, *held))
    mine, theirs = with_partner(held)
    total, other = partial, jnp.zeros_like(partial)
    steps = [1 << k for k in range((n_mp - 1).bit_length())]
    for step in steps:
        if step > 1:
            total = (total.astype(jnp.float32) + other.astype(jnp.float32)).astype(jnp.bfloat16)
        if step == steps[-1]:
            total, send_place = fence((total, send_place))
        other = lax.ppermute(total, "mp", [(source, source ^ step) for source in range(n_mp)])
    attended = attend(lengths, send_place, query_rows, mine, theirs)
    total, other, attended = fence((total, other, attended))
    regrouped = lax.all_to_all(attended, "seq", split_axis=0, concat_axis=0, tiled=True)

    y, sums, state = local_scan(lengths, total, other, dt_weight, dt_bias, decay_rate, inner_act)
    states = with_partner(even_back(state, reach))
    return tuple(
        join_states(
            total,
            other,
            y,
            sums,
            inner_act,
            z_branch,
            decay_rate,
            skip_gain,
            regrouped,
            *states,
            low_rank,
            reach,
        )
    )


def solution(mesh):
    placed = (
        P("seq", "mp"),
        P("seq", "mp"),
        P(None, "mp"),
        P("mp"),
        P("mp", None),
        P(None, "mp"),
        P("mp"),
        P(None, "mp"),
        P("mp"),
        P("seq", "mp"),
        P("seq", "mp"),
        P("seq", "mp"),
        P(),
        P(),
    )
    return jax.shard_map(
        local,
        mesh=mesh,
        in_specs=placed,
        out_specs=(P("seq", "mp"), P("seq", "mp")),
        check_vma=False,
    )
```

```python
import functools

import jax
import jax.numpy as jnp
from jax import lax
from jax.experimental import pallas as pl
from jax.experimental.pallas import tpu as pltpu
from jax.sharding import PartitionSpec as P

HD = 128
LANES = 128
HALO = 16
LOG2E = 1.4426950408889634
RESET = 1e30
APART = 65536.0
VMEM_LIMIT = 32 * 1024 * 1024
VMEM_MOST = 56 * 1024 * 1024


def doc_edges(lengths_ref):
    starts, ends, total = [], [], 0
    for i in range(lengths_ref.shape[0]):
        starts.append(total)
        total = total + lengths_ref[i]
        ends.append(total)
    return starts, ends


def doc_start(places, starts):
    found = jnp.zeros_like(places)
    for start in starts[1:]:
        found = jnp.where(places >= start, start, found)
    return found


def channel_chunk(channels):
    return 1024 if channels % 1024 == 0 else channels


def pack_kernel(x_ref, k_ref, v_ref, halo_ref, kv_ref):
    width = k_ref.shape[1]
    halo_ref[...] = x_ref[...]
    kv_ref[:, :width] = k_ref[...]
    kv_ref[:, width:] = v_ref[...]


def pack(x_branch, key_rows, value_rows):
    tok, channels = x_branch.shape
    width = key_rows.shape[1]
    whole = lambda rows, columns: pl.BlockSpec((rows, columns), lambda i: (0, 0))
    return pl.pallas_call(
        pack_kernel,
        grid=(1,),
        in_specs=[
            pl.BlockSpec((HALO, channels), lambda i: (tok // HALO - 1, 0)),
            whole(tok, width),
            whole(tok, width),
        ],
        out_specs=[whole(HALO, channels), whole(tok, 2 * width)],
        out_shape=[
            jax.ShapeDtypeStruct((HALO, channels), x_branch.dtype),
            jax.ShapeDtypeStruct((tok, 2 * width), key_rows.dtype),
        ],
        compiler_params=pltpu.CompilerParams(vmem_limit_bytes=VMEM_MOST),
        cost_estimate=pl.CostEstimate(flops=0, bytes_accessed=16 * tok * width, transcendentals=0),
        name="pack",
    )(x_branch, key_rows, value_rows)


def conv_kernel(lengths_ref, x_ref, halo_ref, w_ref, b_ref, xp_ref, inner_ref, part_ref, ext, acc):
    tok, chunk = x_ref.shape
    starts, _ = doc_edges(lengths_ref)
    anchor = lax.axis_index("seq") * tok
    places = anchor + lax.broadcasted_iota(jnp.int32, (tok, LANES), 0)
    depth = places - doc_start(places, starts)
    ext[0:HALO, :] = halo_ref[...].astype(jnp.float32)
    ext[HALO:, :] = x_ref[...].astype(jnp.float32)
    for lane in range(0, chunk, LANES):
        cols = slice(lane, lane + LANES)
        total = b_ref[:, cols] + w_ref[0:1, cols] * ext[HALO:, cols]
        for lag in range(1, w_ref.shape[0]):
            window = ext[HALO - lag : HALO - lag + tok, cols]
            total += w_ref[lag : lag + 1, cols] * jnp.where(depth >= lag, window, 0.0)
        act = total * (0.5 + 0.5 * jnp.tanh(0.5 * total))
        inner_ref[:, cols] = act.astype(jnp.bfloat16)
    product = lax.dot_general(
        xp_ref[...], inner_ref[...], (((1,), (1,)), ((), ())), preferred_element_type=jnp.float32
    )
    at = pl.program_id(0)

    @pl.when(at == 0)
    def _():
        acc[...] = product

    @pl.when(at > 0)
    def _():
        acc[...] += product

    @pl.when(at == pl.num_programs(0) - 1)
    def _():
        part_ref[...] = acc[...].astype(jnp.bfloat16)


def conv_project(lengths, x_branch, halo, conv_weight, conv_bias, xproj_weight):
    tok, channels = x_branch.shape
    width = xproj_weight.shape[1]
    taps = conv_weight.shape[0]
    chunk = channel_chunk(channels)
    return pl.pallas_call(
        conv_kernel,
        grid=(channels // chunk,),
        in_specs=[
            pl.BlockSpec(memory_space=pltpu.SMEM),
            pl.BlockSpec((tok, chunk), lambda i: (0, i)),
            pl.BlockSpec((HALO, chunk), lambda i: (0, i)),
            pl.BlockSpec((taps, chunk), lambda i: (0, i)),
            pl.BlockSpec((1, chunk), lambda i: (0, i)),
            pl.BlockSpec((width, chunk), lambda i: (0, i)),
        ],
        out_specs=[
            pl.BlockSpec((tok, chunk), lambda i: (0, i)),
            pl.BlockSpec((width, tok), lambda i: (0, 0)),
        ],
        out_shape=[
            jax.ShapeDtypeStruct((tok, channels), jnp.bfloat16),
            jax.ShapeDtypeStruct((width, tok), jnp.bfloat16),
        ],
        scratch_shapes=[
            pltpu.VMEM((tok + HALO, chunk), jnp.float32),
            pltpu.VMEM((width, tok), jnp.float32),
        ],
        compiler_params=pltpu.CompilerParams(vmem_limit_bytes=VMEM_MOST),
        cost_estimate=pl.CostEstimate(
            flops=80 * tok * channels * width, bytes_accessed=8 * tok * channels, transcendentals=tok * channels
        ),
        name="conv_project",
    )(lengths, x_branch, halo, conv_weight, conv_bias.reshape(1, channels), xproj_weight.T)


ROWS = 8
PAIR = 2 * ROWS
BLOCK = 64


def spread(columns):
    tok, k = columns.shape
    own = lax.broadcasted_iota(jnp.int32, (k, k), 0) == lax.broadcasted_iota(jnp.int32, (k, k), 1)
    picked = jnp.where(own[None], columns.astype(jnp.float32)[:, None, :], 0.0).reshape(tok * k, k)
    ones = jnp.ones((k, LANES), jnp.bfloat16)
    return jnp.dot(picked.astype(jnp.bfloat16), ones, preferred_element_type=jnp.float32).reshape(tok, k, LANES)


def lane(tile):
    return slice(tile * LANES, (tile + 1) * LANES)


def sublanes(tile):
    return slice(tile * ROWS, (tile + 1) * ROWS)


def added(one_ref, other_ref, rows):
    total = one_ref[rows, :].astype(jnp.float32) + other_ref[rows, :].astype(jnp.float32)
    return total.astype(jnp.bfloat16).astype(jnp.float32)


def by_register(rate_ref, rates):
    states = rate_ref.shape[0]
    count = rates.shape[0] // states
    for n in range(states):
        for h in range(count):
            tiles = [rate_ref[n : n + 1, lane(h * ROWS + j)] for j in range(ROWS)]
            rates[n * count + h] = jnp.concatenate(tiles, axis=0) * (-LOG2E)


def local_kernel(
    lengths_ref,
    proj_ref,
    other_ref,
    dtw_hbm,
    bias_ref,
    rate_ref,
    inner_ref,
    y_ref,
    sum_ref,
    state_ref,
    dtw_ref,
    fetched,
    low_cols,
    bc_spread,
    raw,
    rates,
    step_tiles,
    drive_tiles,
    carry,
):
    tok = proj_ref.shape[1]
    block, channels = inner_ref.shape
    states = rate_ref.shape[0]
    low_rank = dtw_ref.shape[0]
    tiles = channels // LANES
    count = tiles // ROWS
    starts, _ = doc_edges(lengths_ref)
    at = pl.program_id(0)

    @pl.when(at == 0)
    def _():
        fetch = pltpu.make_async_copy(dtw_hbm, dtw_ref, fetched)
        fetch.start()
        low_cols[...] = added(proj_ref, other_ref, slice(0, low_rank)).T.astype(jnp.bfloat16)
        bc_spread[...] = spread(added(proj_ref, other_ref, slice(low_rank, None)).T)
        by_register(rate_ref, rates)
        carry[...] = jnp.zeros_like(carry)
        fetch.wait()
        for first in range(0, tiles, 4):
            cols = slice(first * LANES, (first + 4) * LANES)
            part = jnp.dot(low_cols[...], dtw_ref[:, cols], preferred_element_type=jnp.float32)
            for i in range(4):
                raw[:, sublanes(first + i), :] = part[:, lane(i)].reshape(tok // ROWS, ROWS, LANES)

    def steps(pair, unused):
        rows = pl.ds(pl.multiple_of(pair * PAIR, PAIR), PAIR)
        places = lax.axis_index("seq") * tok + at * block + pair * PAIR
        places = places + lax.broadcasted_iota(jnp.int32, (PAIR, LANES), 0)
        at_start = places == doc_start(places, starts)
        for tile in range(tiles):
            inner = inner_ref[rows, lane(tile)].astype(jnp.float32)
            bias = bias_ref[:, lane(tile)]
            for k in range(2):
                biased = raw[at * (block // ROWS) + 2 * pair + k, sublanes(tile), :] + bias
                step = jnp.maximum(biased, 0.0) + jnp.log(1.0 + jnp.exp(-jnp.abs(biased)))
                drive_tiles[2 * pair + k, sublanes(tile), :] = step * inner[sublanes(k)]
                step_tiles[2 * pair + k, sublanes(tile), :] = jnp.where(at_start[sublanes(k)], RESET, step)
        return unused

    lax.fori_loop(0, block // PAIR, steps, 0)

    def scan(t8, held):
        held, total = list(held[0]), list(held[1])
        for first in range(0, ROWS, 2):
            tokens = range(first, first + 2)
            picked = [[pl.ds(r + h * ROWS * ROWS, ROWS, stride=ROWS) for h in range(count)] for r in tokens]
            step = [[step_tiles[t8, rows, :] for rows in of_token] for of_token in picked]
            drive = [[drive_tiles[t8, rows, :] for rows in of_token] for of_token in picked]
            out = [[None] * count for _ in tokens]
            for n in range(states):
                where = [at * block + t8 * ROWS + r for r in tokens]
                b_row = [bc_spread[token, n : n + 1, :] for token in where]
                c_row = [bc_spread[token, states + n : states + n + 1, :] for token in where]
                for h in range(count):
                    i = n * count + h
                    rate = rates[i]
                    decay = [jnp.exp2(rate * step[k][h]) for k in range(2)]
                    for k in range(2):
                        held[i] = decay[k] * held[i] + b_row[k] * drive[k][h]
                        term = c_row[k] * held[i]
                        out[k][h] = term if out[k][h] is None else out[k][h] + term
            for k, r in enumerate(tokens):
                for h in range(count):
                    total[h] = total[h] + step[k][h]
                    y_ref[t8 * ROWS + r, sublanes(h), :] = out[k][h]
                    sum_ref[t8 * ROWS + r, sublanes(h), :] = total[h]
        return held, total

    kept = states * count
    held = ([carry[i] for i in range(kept)], [carry[kept + h] for h in range(count)])
    held, total = lax.fori_loop(0, block // ROWS, scan, held)
    for i, value in enumerate(held + total):
        carry[i] = value

    @pl.when(at == pl.num_programs(0) - 1)
    def _():
        state_ref[: states * tiles, :] = jnp.concatenate(held, axis=0).astype(jnp.bfloat16)
        whole = jnp.concatenate(total, axis=0)
        high = whole.astype(jnp.bfloat16).astype(jnp.float32)
        state_ref[states * tiles :, :] = jnp.concatenate([high, whole - high], axis=0).astype(jnp.bfloat16)


def local_scan(lengths, projected, other, dt_weight, dt_bias, decay_rate, inner_act):
    tok, channels = inner_act.shape
    low_rank = dt_weight.shape[0]
    states = decay_rate.shape[0]
    tiles = channels // LANES
    count = tiles // ROWS
    whole = lambda a: pl.BlockSpec(a.shape, lambda i: (0,) * a.ndim)
    bias = dt_bias.reshape(1, channels)
    by_token = pl.BlockSpec((BLOCK, tiles, LANES), lambda i: (i, 0, 0))
    state_rows = (states + 2) * tiles
    return pl.pallas_call(
        local_kernel,
        grid=(tok // BLOCK,),
        in_specs=[
            pl.BlockSpec(memory_space=pltpu.SMEM),
            whole(projected),
            whole(other),
            pl.BlockSpec(memory_space=pl.ANY),
            whole(bias),
            whole(decay_rate),
            pl.BlockSpec((BLOCK, channels), lambda i: (i, 0)),
        ],
        out_specs=[by_token, by_token, pl.BlockSpec((state_rows, LANES), lambda i: (0, 0))],
        out_shape=[
            jax.ShapeDtypeStruct((tok, tiles, LANES), jnp.float32),
            jax.ShapeDtypeStruct((tok, tiles, LANES), jnp.float32),
            jax.ShapeDtypeStruct((state_rows, LANES), jnp.bfloat16),
        ],
        scratch_shapes=[
            pltpu.VMEM(dt_weight.shape, dt_weight.dtype),
            pltpu.SemaphoreType.DMA,
            pltpu.VMEM((tok, low_rank), jnp.bfloat16),
            pltpu.VMEM((tok, 2 * states, LANES), jnp.float32),
            pltpu.VMEM((tok // ROWS, tiles * ROWS, LANES), jnp.float32),
            pltpu.VMEM((states * count, ROWS, LANES), jnp.float32),
            pltpu.VMEM((BLOCK // ROWS, tiles * ROWS, LANES), jnp.float32),
            pltpu.VMEM((BLOCK // ROWS, tiles * ROWS, LANES), jnp.float32),
            pltpu.VMEM(((states + 1) * count, ROWS, LANES), jnp.float32),
        ],
        compiler_params=pltpu.CompilerParams(vmem_limit_bytes=VMEM_MOST),
        cost_estimate=pl.CostEstimate(
            flops=12 * tok * channels * states,
            bytes_accessed=12 * tok * channels,
            transcendentals=tok * channels * states,
        ),
        name="local_scan",
    )(lengths, projected, other, dt_weight, bias, decay_rate, inner_act)


def join_kernel(
    reach,
    proj_ref,
    other_ref,
    y_ref,
    sum_ref,
    inner_ref,
    z_ref,
    rate_ref,
    skip_ref,
    moved_ref,
    mine_ref,
    theirs_ref,
    out_ref,
    regrouped_ref,
    c_cols,
    rates,
    entering,
    rows_tiles,
):
    block, channels = z_ref.shape
    states = rate_ref.shape[0]
    tiles = channels // LANES
    count = tiles // ROWS
    kept = states * count
    at = pl.program_id(0)

    @pl.when(at == 0)
    def _():
        c_cols[:, :, :states] = added(proj_ref, other_ref, slice(None)).T.reshape(-1, ROWS, states)
        by_register(rate_ref, rates)
        odd = lax.rem(lax.axis_index("seq"), 2)
        state = [jnp.zeros((ROWS, LANES), jnp.float32)] * kept
        for back in range(reach, 0, -1):
            ref, which = (mine_ref, back // 2) if back % 2 == 0 else (theirs_ref, (back + 1) // 2 - odd)
            sent = ref[which].astype(jnp.float32)
            totals = sent[states * tiles : (states + 1) * tiles] + sent[(states + 1) * tiles :]
            state = [
                jnp.exp2(rates[i] * totals[sublanes(i % count)]) * state[i] + sent[sublanes(i)] for i in range(kept)
            ]
        for i in range(kept):
            entering[i] = state[i]

    regrouped_ref[...] = moved_ref[...]

    def body(pair, unused):
        rows = pl.ds(pl.multiple_of(pair * PAIR, PAIR), PAIR)
        for k in range(2):
            first = pair * PAIR + k * ROWS
            t8 = at * (block // ROWS) + 2 * pair + k
            c_rows = [c_cols[t8, r : r + 1, :] for r in range(ROWS)]
            total = [[sum_ref[first + r, sublanes(h), :] for h in range(count)] for r in range(ROWS)]
            out = [[y_ref[first + r, sublanes(h), :] for h in range(count)] for r in range(ROWS)]
            for n in range(states):
                c_row = [jnp.broadcast_to(row[:, n : n + 1], (ROWS, LANES)) for row in c_rows]
                for h in range(count):
                    rate, state = rates[n * count + h], entering[n * count + h]
                    for r in range(ROWS):
                        out[r][h] += jnp.exp2(rate * total[r][h]) * state * c_row[r]
            for r in range(ROWS):
                for h in range(count):
                    rows_tiles[k, pl.ds(r + h * ROWS * ROWS, ROWS, stride=ROWS), :] = out[r][h]
        for tile in range(tiles):
            cols = lane(tile)
            z = z_ref[rows, cols].astype(jnp.float32)
            gate = z * (0.5 + 0.5 * jnp.tanh(0.5 * z))
            scanned = jnp.concatenate([rows_tiles[k, sublanes(tile), :] for k in range(2)], axis=0)
            scanned = scanned + skip_ref[:, cols] * inner_ref[rows, cols].astype(jnp.float32)
            out_ref[rows, cols] = (scanned * gate).astype(jnp.bfloat16)
        return unused

    lax.fori_loop(0, block // PAIR, body, 0)


def join_states(projected, other, y, sums, inner_act, z_branch, decay_rate, skip_gain, moved, mine, theirs, low_rank, reach):
    tok, channels = z_branch.shape
    states = decay_rate.shape[0]
    tiles = channels // LANES
    count = tiles // ROWS
    whole = lambda a: pl.BlockSpec(a.shape, lambda i: (0,) * a.ndim)
    by_token = pl.BlockSpec((BLOCK, tiles, LANES), lambda i: (i, 0, 0))
    by_row = pl.BlockSpec((BLOCK, channels), lambda i: (i, 0))
    skip = skip_gain.reshape(1, channels)
    c_part = pl.BlockSpec((states, tok), lambda i: (low_rank // states + 1, 0))
    return pl.pallas_call(
        functools.partial(join_kernel, reach),
        grid=(tok // BLOCK,),
        in_specs=[
            c_part,
            c_part,
            by_token,
            by_token,
            by_row,
            by_row,
            whole(decay_rate),
            whole(skip),
            by_row,
            whole(mine),
            whole(theirs),
        ],
        out_specs=[by_row, by_row],
        out_shape=[jax.ShapeDtypeStruct((tok, channels), jnp.bfloat16)] * 2,
        scratch_shapes=[
            pltpu.VMEM((tok // ROWS, ROWS, LANES), jnp.float32),
            pltpu.VMEM((states * count, ROWS, LANES), jnp.float32),
            pltpu.VMEM((states * count, ROWS, LANES), jnp.float32),
            pltpu.VMEM((2, tiles * ROWS, LANES), jnp.float32),
        ],
        compiler_params=pltpu.CompilerParams(vmem_limit_bytes=VMEM_MOST),
        cost_estimate=pl.CostEstimate(
            flops=8 * tok * channels * states,
            bytes_accessed=14 * tok * channels,
            transcendentals=tok * channels * states,
        ),
        name="join_states",
    )(projected, other, y, sums, inner_act, z_branch, decay_rate, skip, moved, mine, theirs)


def attend_kernel(
    lengths_ref,
    place_ref,
    q_ref,
    keys_mine,
    keys_theirs,
    values_mine,
    values_theirs,
    out_ref,
    queries,
    scores,
    tops,
    acc,
):
    tok = q_ref.shape[0]
    heads = q_ref.shape[1] // HD
    position = lax.axis_index("seq")
    odd = lax.rem(position, 2)
    anchor = position * tok
    scale = jnp.bfloat16(LOG2E * HD**-0.5)
    starts, ends = doc_edges(lengths_ref)
    lane = lax.broadcasted_iota(jnp.int32, (1, LANES), 1)
    first = jnp.full((1, LANES), 2**30, jnp.int32)
    last = jnp.zeros((1, LANES), jnp.int32)
    for i, (start, end) in enumerate(zip(starts, ends)):
        first = jnp.where(lane == i, start, first)
        last = jnp.where(lane == i, end, last)
    rows = lax.broadcasted_iota(jnp.int32, (tok, LANES), 0)

    def in_doc(base):
        return (rows + base >= first) & (rows + base < last)

    apart = jnp.where(in_doc(anchor) | (lane >= len(starts)), 0.0, -APART).astype(jnp.bfloat16)
    for head in range(heads):
        queries[head * tok : (head + 1) * tok, :HD] = q_ref[:, head * HD : (head + 1) * HD]
        queries[head * tok : (head + 1) * tok, HD:] = apart

    def rows_of(mine_ref, theirs_ref, back):
        if isinstance(back, int) and back == 0:
            return mine_ref[0]
        return jnp.where(lax.rem(back, 2) == 0, mine_ref[back // 2], theirs_ref[(back + 1) // 2 - odd])

    def score(back):
        marks = jnp.where(in_doc(anchor - back * tok), 1.0, 0.0).astype(jnp.bfloat16)
        keys = jnp.concatenate([rows_of(keys_mine, keys_theirs, back), marks], axis=1)
        return lax.dot_general(queries[...], keys, (((1,), (1,)), ((), ())), preferred_element_type=jnp.float32)

    def widest(s):
        top = s[:, :LANES]
        for at in range(LANES, tok, LANES):
            top = jnp.maximum(top, s[:, at : at + LANES])
        return top

    own = score(0)
    causal = lax.broadcasted_iota(jnp.int32, (tok, tok), 1) <= lax.broadcasted_iota(jnp.int32, (tok, tok), 0)
    for head in range(heads):
        part = slice(head * tok, (head + 1) * tok)
        s = jnp.where(causal, own[part], -APART)
        scores[0, part, :] = s
        tops[part, :] = widest(s)

    begin = jnp.int32(0)
    for start in starts[1:]:
        begin = jnp.where(anchor >= start, start, begin)
    earlier = (anchor - begin + tok - 1) // tok

    def look(back, carry):
        s = score(back)
        scores[back] = s
        tops[...] = jnp.maximum(tops[...], widest(s))
        return carry

    lax.fori_loop(1, earlier + 1, look, 0)
    tops[...] = jnp.broadcast_to(jnp.max(tops[...], axis=1, keepdims=True), tops.shape)

    def weighted(back):
        values = jnp.concatenate([rows_of(values_mine, values_theirs, back), jnp.ones((tok, HD), jnp.bfloat16)], axis=1)
        top = tops[...]
        weights = [
            jnp.exp2((scores[back, :, at : at + LANES] - top).astype(jnp.bfloat16) * scale)
            for at in range(0, tok, LANES)
        ]
        return jnp.dot(jnp.concatenate(weights, axis=1), values, preferred_element_type=jnp.float32)

    acc[...] = weighted(0)

    def absorb(back, carry):
        acc[...] += weighted(back)
        return carry

    lax.fori_loop(1, earlier + 1, absorb, 0)
    order = place_ref[pl.ds(position, 1), :]
    move = (lax.broadcasted_iota(jnp.int32, (tok, tok), 0) == order).astype(jnp.float32).astype(jnp.bfloat16)
    for head in range(heads):
        part = slice(head * tok, (head + 1) * tok)
        result = (acc[part, :HD] / acc[part, HD:]).astype(jnp.bfloat16)
        moved = jnp.dot(move, result, preferred_element_type=jnp.float32)
        out_ref[:, head * HD : (head + 1) * HD] = moved.astype(jnp.bfloat16)


def attend(lengths, send_place, query_rows, mine, theirs):
    tok, width = query_rows.shape
    kv_local = mine.shape[2] // (2 * HD)
    share = width // kv_local
    heads = share // HD
    reach = 2 * (mine.shape[0] - 1)
    by_group = pl.BlockSpec((tok, share), lambda i: (0, i))
    keys = pl.BlockSpec(mine.shape[:2] + (HD,), lambda i: (0, 0, i))
    values = pl.BlockSpec(mine.shape[:2] + (HD,), lambda i: (0, 0, i + kv_local))
    return pl.pallas_call(
        attend_kernel,
        grid=(kv_local,),
        in_specs=[
            pl.BlockSpec(memory_space=pltpu.SMEM),
            pl.BlockSpec(send_place.shape, lambda i: (0, 0)),
            by_group,
            keys,
            keys,
            values,
            values,
        ],
        out_specs=by_group,
        out_shape=jax.ShapeDtypeStruct((tok, width), jnp.bfloat16),
        scratch_shapes=[
            pltpu.VMEM((heads * tok, 2 * HD), jnp.bfloat16),
            pltpu.VMEM((reach + 1, heads * tok, tok), jnp.float32),
            pltpu.VMEM((heads * tok, LANES), jnp.float32),
            pltpu.VMEM((heads * tok, 2 * HD), jnp.float32),
        ],
        compiler_params=pltpu.CompilerParams(vmem_limit_bytes=VMEM_LIMIT // 2 + 4 * (reach + 1) * heads * tok * tok),
        cost_estimate=pl.CostEstimate(flops=tok * width, bytes_accessed=tok * width, transcendentals=0),
        name="attend",
    )(lengths, send_place, query_rows, mine, theirs, mine, theirs)


def shifted(value, steps):
    count = lax.axis_size("seq")
    return lax.ppermute(value, "seq", [(source, source + steps) for source in range(count - steps)])


def with_partner(held):
    mine = jnp.stack(held)
    count = lax.axis_size("seq")
    return mine, lax.ppermute(mine, "seq", [(source, source ^ 1) for source in range(count)])


def even_back(value, reach):
    return [value] + [shifted(value, 2 * k) for k in range(1, (reach + 1) // 2 + 1)]


def local(
    x_branch,
    z_branch,
    conv_weight,
    conv_bias,
    xproj_weight,
    dt_weight,
    dt_bias,
    decay_rate,
    skip_gain,
    query_rows,
    key_rows,
    value_rows,
    lengths,
    destination,
):
    tok = x_branch.shape[0]
    n_seq = lax.axis_size("seq")
    n_mp = lax.axis_size("mp")
    low_rank = dt_weight.shape[0]
    reach = n_seq // 2
    run_rows = tok // n_seq
    fence = lax.optimization_barrier

    halo, kv = pack(x_branch, key_rows, value_rows)
    earlier_rows = shifted(halo, 1)
    held = even_back(kv, reach)
    send_place = ((destination // tok) * run_rows + destination % run_rows).reshape(n_seq, tok)

    inner_act, partial = conv_project(lengths, x_branch, earlier_rows, conv_weight, conv_bias, xproj_weight)
    _, *held = fence((partial, *held))
    mine, theirs = with_partner(held)
    total, other = partial, jnp.zeros_like(partial)
    steps = [1 << k for k in range((n_mp - 1).bit_length())]
    for step in steps:
        if step > 1:
            total = (total.astype(jnp.float32) + other.astype(jnp.float32)).astype(jnp.bfloat16)
        if step == steps[-1]:
            total, send_place = fence((total, send_place))
        other = lax.ppermute(total, "mp", [(source, source ^ step) for source in range(n_mp)])
    attended = attend(lengths, send_place, query_rows, mine, theirs)
    total, other, attended = fence((total, other, attended))
    regrouped = lax.all_to_all(attended, "seq", split_axis=0, concat_axis=0, tiled=True)

    y, sums, state = local_scan(lengths, total, other, dt_weight, dt_bias, decay_rate, inner_act)
    states = with_partner(even_back(state, reach))
    return tuple(
        join_states(
            total,
            other,
            y,
            sums,
            inner_act,
            z_branch,
            decay_rate,
            skip_gain,
            regrouped,
            *states,
            low_rank,
            reach,
        )
    )


def solution(mesh):
    placed = (
        P("seq", "mp"),
        P("seq", "mp"),
        P(None, "mp"),
        P("mp"),
        P("mp", None),
        P(None, "mp"),
        P("mp"),
        P(None, "mp"),
        P("mp"),
        P("seq", "mp"),
        P("seq", "mp"),
        P("seq", "mp"),
        P(),
        P(),
    )
    return jax.shard_map(
        local,
        mesh=mesh,
        in_specs=placed,
        out_specs=(P("seq", "mp"), P("seq", "mp")),
        check_vma=False,
    )
```

```python
import functools

import jax
import jax.numpy as jnp
from jax import lax
from jax.experimental import pallas as pl
from jax.experimental.pallas import tpu as pltpu
from jax.sharding import PartitionSpec as P

HD = 128
LANES = 128
HALO = 16
LOG2E = 1.4426950408889634
RESET = 1e30
APART = 65536.0
MARKS = 16
VMEM_LIMIT = 32 * 1024 * 1024
VMEM_MOST = 56 * 1024 * 1024


def doc_edges(lengths_ref):
    starts, ends, total = [], [], 0
    for i in range(lengths_ref.shape[0]):
        starts.append(total)
        total = total + lengths_ref[i]
        ends.append(total)
    return starts, ends


def doc_start(places, starts):
    found = jnp.zeros_like(places)
    for start in starts[1:]:
        found = jnp.where(places >= start, start, found)
    return found


def channel_chunk(channels):
    return 1024 if channels % 1024 == 0 else channels


def pack_kernel(x_ref, k_ref, v_ref, halo_ref, kv_ref):
    width = k_ref.shape[1]
    halo_ref[...] = x_ref[...]
    kv_ref[:, :width] = k_ref[...]
    kv_ref[:, width:] = v_ref[...]


def pack(x_branch, key_rows, value_rows):
    tok, channels = x_branch.shape
    width = key_rows.shape[1]
    whole = lambda rows, columns: pl.BlockSpec((rows, columns), lambda i: (0, 0))
    return pl.pallas_call(
        pack_kernel,
        grid=(1,),
        in_specs=[
            pl.BlockSpec((HALO, channels), lambda i: (tok // HALO - 1, 0)),
            whole(tok, width),
            whole(tok, width),
        ],
        out_specs=[whole(HALO, channels), whole(tok, 2 * width)],
        out_shape=[
            jax.ShapeDtypeStruct((HALO, channels), x_branch.dtype),
            jax.ShapeDtypeStruct((tok, 2 * width), key_rows.dtype),
        ],
        compiler_params=pltpu.CompilerParams(vmem_limit_bytes=VMEM_MOST),
        cost_estimate=pl.CostEstimate(flops=0, bytes_accessed=16 * tok * width, transcendentals=0),
        name="pack",
    )(x_branch, key_rows, value_rows)


def conv_kernel(lengths_ref, x_ref, halo_ref, w_ref, b_ref, xp_ref, inner_ref, part_ref, ext, acc):
    tok, chunk = x_ref.shape
    starts, _ = doc_edges(lengths_ref)
    anchor = lax.axis_index("seq") * tok
    places = anchor + lax.broadcasted_iota(jnp.int32, (tok, LANES), 0)
    depth = places - doc_start(places, starts)
    ext[0:HALO, :] = halo_ref[...].astype(jnp.float32)
    ext[HALO:, :] = x_ref[...].astype(jnp.float32)
    for lane in range(0, chunk, LANES):
        cols = slice(lane, lane + LANES)
        total = b_ref[:, cols] + w_ref[0:1, cols] * ext[HALO:, cols]
        for lag in range(1, w_ref.shape[0]):
            window = ext[HALO - lag : HALO - lag + tok, cols]
            total += w_ref[lag : lag + 1, cols] * jnp.where(depth >= lag, window, 0.0)
        act = total * (0.5 + 0.5 * jnp.tanh(0.5 * total))
        inner_ref[:, cols] = act.astype(jnp.bfloat16)
    product = lax.dot_general(
        xp_ref[...], inner_ref[...], (((1,), (1,)), ((), ())), preferred_element_type=jnp.float32
    )
    at = pl.program_id(0)

    @pl.when(at == 0)
    def _():
        acc[...] = product

    @pl.when(at > 0)
    def _():
        acc[...] += product

    @pl.when(at == pl.num_programs(0) - 1)
    def _():
        part_ref[...] = acc[...].astype(jnp.bfloat16)


def conv_project(lengths, x_branch, halo, conv_weight, conv_bias, xproj_weight):
    tok, channels = x_branch.shape
    width = xproj_weight.shape[1]
    taps = conv_weight.shape[0]
    chunk = channel_chunk(channels)
    return pl.pallas_call(
        conv_kernel,
        grid=(channels // chunk,),
        in_specs=[
            pl.BlockSpec(memory_space=pltpu.SMEM),
            pl.BlockSpec((tok, chunk), lambda i: (0, i)),
            pl.BlockSpec((HALO, chunk), lambda i: (0, i)),
            pl.BlockSpec((taps, chunk), lambda i: (0, i)),
            pl.BlockSpec((1, chunk), lambda i: (0, i)),
            pl.BlockSpec((width, chunk), lambda i: (0, i)),
        ],
        out_specs=[
            pl.BlockSpec((tok, chunk), lambda i: (0, i)),
            pl.BlockSpec((width, tok), lambda i: (0, 0)),
        ],
        out_shape=[
            jax.ShapeDtypeStruct((tok, channels), jnp.bfloat16),
            jax.ShapeDtypeStruct((width, tok), jnp.bfloat16),
        ],
        scratch_shapes=[
            pltpu.VMEM((tok + HALO, chunk), jnp.float32),
            pltpu.VMEM((width, tok), jnp.float32),
        ],
        compiler_params=pltpu.CompilerParams(vmem_limit_bytes=VMEM_MOST),
        cost_estimate=pl.CostEstimate(
            flops=80 * tok * channels * width, bytes_accessed=8 * tok * channels, transcendentals=tok * channels
        ),
        name="conv_project",
    )(lengths, x_branch, halo, conv_weight, conv_bias.reshape(1, channels), xproj_weight.T)


ROWS = 8
PAIR = 2 * ROWS
BLOCK = 64


def spread(columns):
    tok, k = columns.shape
    own = lax.broadcasted_iota(jnp.int32, (k, k), 0) == lax.broadcasted_iota(jnp.int32, (k, k), 1)
    picked = jnp.where(own[None], columns.astype(jnp.float32)[:, None, :], 0.0).reshape(tok * k, k)
    ones = jnp.ones((k, LANES), jnp.bfloat16)
    return jnp.dot(picked.astype(jnp.bfloat16), ones, preferred_element_type=jnp.float32).reshape(tok, k, LANES)


def lane(tile):
    return slice(tile * LANES, (tile + 1) * LANES)


def sublanes(tile):
    return slice(tile * ROWS, (tile + 1) * ROWS)


def added(one_ref, other_ref, rows):
    total = one_ref[rows, :].astype(jnp.float32) + other_ref[rows, :].astype(jnp.float32)
    return total.astype(jnp.bfloat16).astype(jnp.float32)


def by_register(rate_ref, rates):
    states = rate_ref.shape[0]
    count = rates.shape[0] // states
    for n in range(states):
        for h in range(count):
            tiles = [rate_ref[n : n + 1, lane(h * ROWS + j)] for j in range(ROWS)]
            rates[n * count + h] = jnp.concatenate(tiles, axis=0) * (-LOG2E)


def local_kernel(
    lengths_ref,
    proj_ref,
    other_ref,
    dtw_ref,
    bias_ref,
    rate_ref,
    inner_ref,
    y_ref,
    sum_ref,
    state_ref,
    low_cols,
    bc_spread,
    raw,
    rates,
    step_tiles,
    drive_tiles,
    carry,
):
    tok = proj_ref.shape[1]
    block, channels = inner_ref.shape
    states = rate_ref.shape[0]
    low_rank = dtw_ref.shape[0]
    tiles = channels // LANES
    count = tiles // ROWS
    starts, _ = doc_edges(lengths_ref)
    at = pl.program_id(0)

    @pl.when(at == 0)
    def _():
        low_cols[...] = added(proj_ref, other_ref, slice(0, low_rank)).T.astype(jnp.bfloat16)
        bc_spread[...] = spread(added(proj_ref, other_ref, slice(low_rank, None)).T)
        by_register(rate_ref, rates)
        carry[...] = jnp.zeros_like(carry)
        for first in range(0, tiles, 4):
            cols = slice(first * LANES, (first + 4) * LANES)
            part = jnp.dot(low_cols[...], dtw_ref[:, cols], preferred_element_type=jnp.float32)
            for i in range(4):
                raw[:, sublanes(first + i), :] = part[:, lane(i)].reshape(tok // ROWS, ROWS, LANES)

    def steps(pair, unused):
        rows = pl.ds(pl.multiple_of(pair * PAIR, PAIR), PAIR)
        places = lax.axis_index("seq") * tok + at * block + pair * PAIR
        places = places + lax.broadcasted_iota(jnp.int32, (PAIR, LANES), 0)
        at_start = places == doc_start(places, starts)
        for tile in range(tiles):
            inner = inner_ref[rows, lane(tile)].astype(jnp.float32)
            bias = bias_ref[:, lane(tile)]
            for k in range(2):
                biased = raw[at * (block // ROWS) + 2 * pair + k, sublanes(tile), :] + bias
                step = jnp.maximum(biased, 0.0) + jnp.log(1.0 + jnp.exp(-jnp.abs(biased)))
                drive_tiles[2 * pair + k, sublanes(tile), :] = step * inner[sublanes(k)]
                step_tiles[2 * pair + k, sublanes(tile), :] = jnp.where(at_start[sublanes(k)], RESET, step)
        return unused

    lax.fori_loop(0, block // PAIR, steps, 0)

    def scan(t8, held):
        held, total = list(held[0]), list(held[1])
        for first in range(0, ROWS, 2):
            tokens = range(first, first + 2)
            picked = [[pl.ds(r + h * ROWS * ROWS, ROWS, stride=ROWS) for h in range(count)] for r in tokens]
            step = [[step_tiles[t8, rows, :] for rows in of_token] for of_token in picked]
            drive = [[drive_tiles[t8, rows, :] for rows in of_token] for of_token in picked]
            out = [[None] * count for _ in tokens]
            for n in range(states):
                where = [at * block + t8 * ROWS + r for r in tokens]
                b_row = [bc_spread[token, n : n + 1, :] for token in where]
                c_row = [bc_spread[token, states + n : states + n + 1, :] for token in where]
                for h in range(count):
                    i = n * count + h
                    rate = rates[i]
                    decay = [jnp.exp2(rate * step[k][h]) for k in range(2)]
                    for k in range(2):
                        held[i] = decay[k] * held[i] + b_row[k] * drive[k][h]
                        term = c_row[k] * held[i]
                        out[k][h] = term if out[k][h] is None else out[k][h] + term
            for k, r in enumerate(tokens):
                for h in range(count):
                    total[h] = total[h] + step[k][h]
                    y_ref[t8 * ROWS + r, sublanes(h), :] = out[k][h]
                    sum_ref[t8 * ROWS + r, sublanes(h), :] = total[h]
        return held, total

    kept = states * count
    held = ([carry[i] for i in range(kept)], [carry[kept + h] for h in range(count)])
    held, total = lax.fori_loop(0, block // ROWS, scan, held)
    for i, value in enumerate(held + total):
        carry[i] = value

    @pl.when(at == pl.num_programs(0) - 1)
    def _():
        state_ref[: states * tiles, :] = jnp.concatenate(held, axis=0).astype(jnp.bfloat16)
        whole = jnp.concatenate(total, axis=0)
        high = whole.astype(jnp.bfloat16).astype(jnp.float32)
        state_ref[states * tiles :, :] = jnp.concatenate([high, whole - high], axis=0).astype(jnp.bfloat16)


def local_scan(lengths, projected, other, dt_weight, dt_bias, decay_rate, inner_act):
    tok, channels = inner_act.shape
    low_rank = dt_weight.shape[0]
    states = decay_rate.shape[0]
    tiles = channels // LANES
    count = tiles // ROWS
    whole = lambda a: pl.BlockSpec(a.shape, lambda i: (0,) * a.ndim)
    bias = dt_bias.reshape(1, channels)
    by_token = pl.BlockSpec((BLOCK, tiles, LANES), lambda i: (i, 0, 0))
    state_rows = (states + 2) * tiles
    return pl.pallas_call(
        local_kernel,
        grid=(tok // BLOCK,),
        in_specs=[
            pl.BlockSpec(memory_space=pltpu.SMEM),
            whole(projected),
            whole(other),
            whole(dt_weight),
            whole(bias),
            whole(decay_rate),
            pl.BlockSpec((BLOCK, channels), lambda i: (i, 0)),
        ],
        out_specs=[by_token, by_token, pl.BlockSpec((state_rows, LANES), lambda i: (0, 0))],
        out_shape=[
            jax.ShapeDtypeStruct((tok, tiles, LANES), jnp.float32),
            jax.ShapeDtypeStruct((tok, tiles, LANES), jnp.float32),
            jax.ShapeDtypeStruct((state_rows, LANES), jnp.bfloat16),
        ],
        scratch_shapes=[
            pltpu.VMEM((tok, low_rank), jnp.bfloat16),
            pltpu.VMEM((tok, 2 * states, LANES), jnp.float32),
            pltpu.VMEM((tok // ROWS, tiles * ROWS, LANES), jnp.float32),
            pltpu.VMEM((states * count, ROWS, LANES), jnp.float32),
            pltpu.VMEM((BLOCK // ROWS, tiles * ROWS, LANES), jnp.float32),
            pltpu.VMEM((BLOCK // ROWS, tiles * ROWS, LANES), jnp.float32),
            pltpu.VMEM(((states + 1) * count, ROWS, LANES), jnp.float32),
        ],
        compiler_params=pltpu.CompilerParams(vmem_limit_bytes=VMEM_MOST),
        cost_estimate=pl.CostEstimate(
            flops=12 * tok * channels * states,
            bytes_accessed=12 * tok * channels,
            transcendentals=tok * channels * states,
        ),
        name="local_scan",
    )(lengths, projected, other, dt_weight, bias, decay_rate, inner_act)


def join_kernel(
    reach,
    proj_ref,
    other_ref,
    y_ref,
    sum_ref,
    inner_ref,
    z_ref,
    rate_ref,
    skip_ref,
    moved_ref,
    mine_ref,
    theirs_ref,
    out_ref,
    regrouped_ref,
    c_spread,
    rates,
    entering,
    rows_tiles,
):
    block, channels = z_ref.shape
    states = rate_ref.shape[0]
    tiles = channels // LANES
    count = tiles // ROWS
    kept = states * count
    at = pl.program_id(0)

    @pl.when(at == 0)
    def _():
        c_spread[...] = spread(added(proj_ref, other_ref, slice(None)).T)
        by_register(rate_ref, rates)
        odd = lax.rem(lax.axis_index("seq"), 2)
        state = [jnp.zeros((ROWS, LANES), jnp.float32)] * kept
        for back in range(reach, 0, -1):
            ref, which = (mine_ref, back // 2) if back % 2 == 0 else (theirs_ref, (back + 1) // 2 - odd)
            sent = ref[which].astype(jnp.float32)
            totals = sent[states * tiles : (states + 1) * tiles] + sent[(states + 1) * tiles :]
            state = [
                jnp.exp2(rates[i] * totals[sublanes(i % count)]) * state[i] + sent[sublanes(i)] for i in range(kept)
            ]
        for i in range(kept):
            entering[i] = state[i]

    regrouped_ref[...] = moved_ref[...]

    def body(pair, unused):
        rows = pl.ds(pl.multiple_of(pair * PAIR, PAIR), PAIR)
        for k in range(2):
            first = pair * PAIR + k * ROWS
            total = [[sum_ref[first + r, sublanes(h), :] for h in range(count)] for r in range(ROWS)]
            out = [[y_ref[first + r, sublanes(h), :] for h in range(count)] for r in range(ROWS)]
            for n in range(states):
                c_row = [c_spread[at * block + first + r, n : n + 1, :] for r in range(ROWS)]
                for h in range(count):
                    rate, state = rates[n * count + h], entering[n * count + h]
                    for r in range(ROWS):
                        out[r][h] += jnp.exp2(rate * total[r][h]) * state * c_row[r]
            for r in range(ROWS):
                for h in range(count):
                    rows_tiles[k, pl.ds(r + h * ROWS * ROWS, ROWS, stride=ROWS), :] = out[r][h]
        for tile in range(tiles):
            cols = lane(tile)
            z = z_ref[rows, cols].astype(jnp.float32)
            gate = z * (0.5 + 0.5 * jnp.tanh(0.5 * z))
            scanned = jnp.concatenate([rows_tiles[k, sublanes(tile), :] for k in range(2)], axis=0)
            scanned = scanned + skip_ref[:, cols] * inner_ref[rows, cols].astype(jnp.float32)
            out_ref[rows, cols] = (scanned * gate).astype(jnp.bfloat16)
        return unused

    lax.fori_loop(0, block // PAIR, body, 0)


def join_states(projected, other, y, sums, inner_act, z_branch, decay_rate, skip_gain, moved, mine, theirs, low_rank, reach):
    tok, channels = z_branch.shape
    states = decay_rate.shape[0]
    tiles = channels // LANES
    count = tiles // ROWS
    whole = lambda a: pl.BlockSpec(a.shape, lambda i: (0,) * a.ndim)
    by_token = pl.BlockSpec((BLOCK, tiles, LANES), lambda i: (i, 0, 0))
    by_row = pl.BlockSpec((BLOCK, channels), lambda i: (i, 0))
    skip = skip_gain.reshape(1, channels)
    c_part = pl.BlockSpec((states, tok), lambda i: (low_rank // states + 1, 0))
    return pl.pallas_call(
        functools.partial(join_kernel, reach),
        grid=(tok // BLOCK,),
        in_specs=[
            c_part,
            c_part,
            by_token,
            by_token,
            by_row,
            by_row,
            whole(decay_rate),
            whole(skip),
            by_row,
            whole(mine),
            whole(theirs),
        ],
        out_specs=[by_row, by_row],
        out_shape=[jax.ShapeDtypeStruct((tok, channels), jnp.bfloat16)] * 2,
        scratch_shapes=[
            pltpu.VMEM((tok, states, LANES), jnp.float32),
            pltpu.VMEM((states * count, ROWS, LANES), jnp.float32),
            pltpu.VMEM((states * count, ROWS, LANES), jnp.float32),
            pltpu.VMEM((2, tiles * ROWS, LANES), jnp.float32),
        ],
        compiler_params=pltpu.CompilerParams(vmem_limit_bytes=VMEM_MOST),
        cost_estimate=pl.CostEstimate(
            flops=8 * tok * channels * states,
            bytes_accessed=14 * tok * channels,
            transcendentals=tok * channels * states,
        ),
        name="join_states",
    )(projected, other, y, sums, inner_act, z_branch, decay_rate, skip, moved, mine, theirs)


def attend_kernel(
    turn_heads,
    lengths_ref,
    place_ref,
    q_ref,
    keys_mine,
    keys_theirs,
    values_mine,
    values_theirs,
    out_ref,
    keys_across,
    values_wide,
):
    tok = q_ref.shape[0]
    heads = q_ref.shape[1] // HD
    reach = values_wide.shape[0] // tok - 1
    position = lax.axis_index("seq")
    odd = lax.rem(position, 2)
    anchor = position * tok
    scale = jnp.bfloat16(LOG2E * HD**-0.5)
    starts, ends = doc_edges(lengths_ref)
    edges = list(zip(starts, ends)) + [(jnp.int32(-(2**30)), jnp.int32(0))]
    lane_at = lax.broadcasted_iota(jnp.int32, (1, LANES), 1)
    places = anchor + lax.broadcasted_iota(jnp.int32, (tok, LANES), 0)
    apart = jnp.where(lane_at < len(edges), -APART, 0.0) + jnp.zeros((tok, LANES), jnp.float32)
    for i, (start, end) in enumerate(edges):
        apart = jnp.where((lane_at == i) & (places >= start) & (places < end), 0.0, apart)
    apart = apart.astype(jnp.bfloat16)

    def stage(back, keys, values):
        at = pl.ds(pl.multiple_of(back * tok, tok), tok)
        place = anchor - back * tok + lax.broadcasted_iota(jnp.int32, (MARKS, tok), 1)
        row = lax.broadcasted_iota(jnp.int32, (MARKS, tok), 0)
        marks = jnp.zeros((MARKS, tok), jnp.float32)
        for i, (start, end) in enumerate(edges):
            marks = jnp.where((row == i) & (place >= start) & (place < end), 1.0, marks)
        keys_across[:HD, at] = keys.astype(jnp.float32).T.astype(jnp.bfloat16)
        keys_across[HD : HD + MARKS, at] = marks.astype(jnp.bfloat16)
        values_wide[at, :HD] = values

    keys_across[HD + MARKS :, :] = jnp.zeros((HD - MARKS, keys_across.shape[1]), jnp.bfloat16)
    values_wide[:, HD:] = jnp.ones((values_wide.shape[0], HD), jnp.bfloat16)
    stage(0, keys_mine[0], values_mine[0])

    def stage_earlier(back, unused):
        even = lax.rem(back, 2) == 0
        ours, other = back // 2, (back + 1) // 2 - odd
        stage(
            back,
            jnp.where(even, keys_mine[ours], keys_theirs[other]),
            jnp.where(even, values_mine[ours], values_theirs[other]),
        )
        return unused

    begin = jnp.int32(0)
    for start in starts[1:]:
        begin = jnp.where(anchor >= start, start, begin)
    pairs = ((anchor - begin + tok - 1) // tok + 1) // 2
    lax.fori_loop(1, 2 * pairs + 1, stage_earlier, 0)

    order = place_ref[pl.ds(position, 1), :]
    move = (lax.broadcasted_iota(jnp.int32, (tok, tok), 0) == order).astype(jnp.float32).astype(jnp.bfloat16)
    causal = lax.broadcasted_iota(jnp.int32, (tok, tok), 1) <= lax.broadcasted_iota(jnp.int32, (tok, tok), 0)

    def one_head(head, blocks):
        cols = pl.ds(pl.multiple_of(head * HD, HD), HD)
        query = jnp.concatenate([q_ref[:, cols], apart], axis=1)
        s = jnp.dot(query, keys_across[:, : blocks * tok], preferred_element_type=jnp.float32)
        parts = [jnp.where(causal, s[:, :tok], -APART)] + ([s[:, tok:]] if blocks > 1 else [])
        pieces = [part[:, at : at + LANES] for part in parts for at in range(0, part.shape[1], LANES)]
        top = functools.reduce(jnp.maximum, pieces)
        top = jnp.broadcast_to(jnp.max(top, axis=1, keepdims=True), top.shape)
        weights = [jnp.exp2((piece - top).astype(jnp.bfloat16) * scale) for piece in pieces]
        both = jnp.dot(
            jnp.concatenate(weights, axis=1), values_wide[: blocks * tok, :], preferred_element_type=jnp.float32
        )
        result = (both[:, :HD] / both[:, HD:]).astype(jnp.bfloat16)
        out_ref[:, cols] = jnp.dot(move, result, preferred_element_type=jnp.float32).astype(jnp.bfloat16)

    def all_heads(blocks):
        def some(turn, unused):
            for k in range(turn_heads):
                one_head(turn * turn_heads + k, blocks)
            return unused

        lax.fori_loop(0, heads // turn_heads, some, 0)

    for case in range(reach // 2 + 1):
        pl.when(pairs == case)(functools.partial(all_heads, 1 + 2 * case))


def attend(lengths, send_place, query_rows, mine, theirs):
    tok, width = query_rows.shape
    kv_local = mine.shape[2] // (2 * HD)
    share = width // kv_local
    heads = share // HD
    reach = 2 * (mine.shape[0] - 1)
    by_group = pl.BlockSpec((tok, share), lambda i: (0, i))
    keys = pl.BlockSpec(mine.shape[:2] + (HD,), lambda i: (0, 0, i))
    values = pl.BlockSpec(mine.shape[:2] + (HD,), lambda i: (0, 0, i + kv_local))
    turn_heads = next(n for n in (4, 2, 1) if heads % n == 0 and n * (reach + 1) <= 24)
    return pl.pallas_call(
        functools.partial(attend_kernel, turn_heads),
        grid=(kv_local,),
        in_specs=[
            pl.BlockSpec(memory_space=pltpu.SMEM),
            pl.BlockSpec(send_place.shape, lambda i: (0, 0)),
            by_group,
            keys,
            keys,
            values,
            values,
        ],
        out_specs=by_group,
        out_shape=jax.ShapeDtypeStruct((tok, width), jnp.bfloat16),
        scratch_shapes=[
            pltpu.VMEM((2 * HD, (reach + 1) * tok), jnp.bfloat16),
            pltpu.VMEM(((reach + 1) * tok, 2 * HD), jnp.bfloat16),
        ],
        compiler_params=pltpu.CompilerParams(vmem_limit_bytes=VMEM_LIMIT),
        cost_estimate=pl.CostEstimate(flops=tok * width, bytes_accessed=tok * width, transcendentals=0),
        name="attend",
    )(lengths, send_place, query_rows, mine, theirs, mine, theirs)


def shifted(value, steps):
    count = lax.axis_size("seq")
    return lax.ppermute(value, "seq", [(source, source + steps) for source in range(count - steps)])


def with_partner(held):
    mine = jnp.stack(held)
    count = lax.axis_size("seq")
    return mine, lax.ppermute(mine, "seq", [(source, source ^ 1) for source in range(count)])


def even_back(value, reach):
    return [value] + [shifted(value, 2 * k) for k in range(1, (reach + 1) // 2 + 1)]


def local(
    x_branch,
    z_branch,
    conv_weight,
    conv_bias,
    xproj_weight,
    dt_weight,
    dt_bias,
    decay_rate,
    skip_gain,
    query_rows,
    key_rows,
    value_rows,
    lengths,
    destination,
):
    tok = x_branch.shape[0]
    n_seq = lax.axis_size("seq")
    n_mp = lax.axis_size("mp")
    low_rank = dt_weight.shape[0]
    reach = n_seq // 2
    run_rows = tok // n_seq
    fence = lax.optimization_barrier

    halo, kv = pack(x_branch, key_rows, value_rows)
    earlier_rows = shifted(halo, 1)
    held = even_back(kv, reach)
    send_place = ((destination // tok) * run_rows + destination % run_rows).reshape(n_seq, tok)

    inner_act, partial = conv_project(lengths, x_branch, earlier_rows, conv_weight, conv_bias, xproj_weight)
    _, *held = fence((partial, *held))
    mine, theirs = with_partner(held)
    total, other = partial, jnp.zeros_like(partial)
    steps = [1 << k for k in range((n_mp - 1).bit_length())]
    for step in steps:
        if step > 1:
            total = (total.astype(jnp.float32) + other.astype(jnp.float32)).astype(jnp.bfloat16)
        if step == steps[-1]:
            total, send_place = fence((total, send_place))
        other = lax.ppermute(total, "mp", [(source, source ^ step) for source in range(n_mp)])
    attended = attend(lengths, send_place, query_rows, mine, theirs)
    total, other, attended = fence((total, other, attended))
    regrouped = lax.all_to_all(attended, "seq", split_axis=0, concat_axis=0, tiled=True)

    y, sums, state = local_scan(lengths, total, other, dt_weight, dt_bias, decay_rate, inner_act)
    states = with_partner(even_back(state, reach))
    return tuple(
        join_states(
            total,
            other,
            y,
            sums,
            inner_act,
            z_branch,
            decay_rate,
            skip_gain,
            regrouped,
            *states,
            low_rank,
            reach,
        )
    )


def solution(mesh):
    placed = (
        P("seq", "mp"),
        P("seq", "mp"),
        P(None, "mp"),
        P("mp"),
        P("mp", None),
        P(None, "mp"),
        P("mp"),
        P(None, "mp"),
        P("mp"),
        P("seq", "mp"),
        P("seq", "mp"),
        P("seq", "mp"),
        P(),
        P(),
    )
    return jax.shard_map(
        local,
        mesh=mesh,
        in_specs=placed,
        out_specs=(P("seq", "mp"), P("seq", "mp")),
        check_vma=False,
    )
```

```python
import functools

import jax
import jax.numpy as jnp
from jax import lax
from jax.experimental import pallas as pl
from jax.experimental.pallas import tpu as pltpu
from jax.sharding import PartitionSpec as P

HD = 128
LANES = 128
HALO = 16
LOG2E = 1.4426950408889634
RESET = 1e30
APART = 65536.0
VMEM_LIMIT = 32 * 1024 * 1024
VMEM_MOST = 56 * 1024 * 1024


def doc_edges(lengths_ref):
    starts, ends, total = [], [], 0
    for i in range(lengths_ref.shape[0]):
        starts.append(total)
        total = total + lengths_ref[i]
        ends.append(total)
    return starts, ends


def doc_start(places, starts):
    found = jnp.zeros_like(places)
    for start in starts[1:]:
        found = jnp.where(places >= start, start, found)
    return found


def channel_chunk(channels):
    return 1024 if channels % 1024 == 0 else channels


def pack_kernel(x_ref, k_ref, v_ref, halo_ref, kv_ref):
    width = k_ref.shape[1]
    halo_ref[...] = x_ref[...]
    kv_ref[:, :width] = k_ref[...]
    kv_ref[:, width:] = v_ref[...]


def pack(x_branch, key_rows, value_rows):
    tok, channels = x_branch.shape
    width = key_rows.shape[1]
    whole = lambda rows, columns: pl.BlockSpec((rows, columns), lambda i: (0, 0))
    return pl.pallas_call(
        pack_kernel,
        grid=(1,),
        in_specs=[
            pl.BlockSpec((HALO, channels), lambda i: (tok // HALO - 1, 0)),
            whole(tok, width),
            whole(tok, width),
        ],
        out_specs=[whole(HALO, channels), whole(tok, 2 * width)],
        out_shape=[
            jax.ShapeDtypeStruct((HALO, channels), x_branch.dtype),
            jax.ShapeDtypeStruct((tok, 2 * width), key_rows.dtype),
        ],
        compiler_params=pltpu.CompilerParams(vmem_limit_bytes=VMEM_MOST),
        cost_estimate=pl.CostEstimate(flops=0, bytes_accessed=16 * tok * width, transcendentals=0),
        name="pack",
    )(x_branch, key_rows, value_rows)


def conv_kernel(lengths_ref, x_ref, halo_ref, w_ref, b_ref, xp_ref, inner_ref, part_ref, ext, acc):
    tok, chunk = x_ref.shape
    starts, _ = doc_edges(lengths_ref)
    anchor = lax.axis_index("seq") * tok
    places = anchor + lax.broadcasted_iota(jnp.int32, (tok, LANES), 0)
    depth = places - doc_start(places, starts)
    ext[0:HALO, :] = halo_ref[...].astype(jnp.float32)
    ext[HALO:, :] = x_ref[...].astype(jnp.float32)
    for lane in range(0, chunk, LANES):
        cols = slice(lane, lane + LANES)
        total = b_ref[:, cols] + w_ref[0:1, cols] * ext[HALO:, cols]
        for lag in range(1, w_ref.shape[0]):
            window = ext[HALO - lag : HALO - lag + tok, cols]
            total += w_ref[lag : lag + 1, cols] * jnp.where(depth >= lag, window, 0.0)
        act = total * (0.5 + 0.5 * jnp.tanh(0.5 * total))
        inner_ref[:, cols] = act.astype(jnp.bfloat16)
    product = lax.dot_general(
        xp_ref[...], inner_ref[...], (((1,), (1,)), ((), ())), preferred_element_type=jnp.float32
    )
    at = pl.program_id(0)

    @pl.when(at == 0)
    def _():
        acc[...] = product

    @pl.when(at > 0)
    def _():
        acc[...] += product

    @pl.when(at == pl.num_programs(0) - 1)
    def _():
        part_ref[...] = acc[...].astype(jnp.bfloat16)


def conv_project(lengths, x_branch, halo, conv_weight, conv_bias, xproj_weight):
    tok, channels = x_branch.shape
    width = xproj_weight.shape[1]
    taps = conv_weight.shape[0]
    chunk = channel_chunk(channels)
    return pl.pallas_call(
        conv_kernel,
        grid=(channels // chunk,),
        in_specs=[
            pl.BlockSpec(memory_space=pltpu.SMEM),
            pl.BlockSpec((tok, chunk), lambda i: (0, i)),
            pl.BlockSpec((HALO, chunk), lambda i: (0, i)),
            pl.BlockSpec((taps, chunk), lambda i: (0, i)),
            pl.BlockSpec((1, chunk), lambda i: (0, i)),
            pl.BlockSpec((width, chunk), lambda i: (0, i)),
        ],
        out_specs=[
            pl.BlockSpec((tok, chunk), lambda i: (0, i)),
            pl.BlockSpec((width, tok), lambda i: (0, 0)),
        ],
        out_shape=[
            jax.ShapeDtypeStruct((tok, channels), jnp.bfloat16),
            jax.ShapeDtypeStruct((width, tok), jnp.bfloat16),
        ],
        scratch_shapes=[
            pltpu.VMEM((tok + HALO, chunk), jnp.float32),
            pltpu.VMEM((width, tok), jnp.float32),
        ],
        compiler_params=pltpu.CompilerParams(vmem_limit_bytes=VMEM_MOST),
        cost_estimate=pl.CostEstimate(
            flops=80 * tok * channels * width, bytes_accessed=8 * tok * channels, transcendentals=tok * channels
        ),
        name="conv_project",
    )(lengths, x_branch, halo, conv_weight, conv_bias.reshape(1, channels), xproj_weight.T)


ROWS = 8
PAIR = 2 * ROWS
BLOCK = 64


def spread(columns):
    tok, k = columns.shape
    own = lax.broadcasted_iota(jnp.int32, (k, k), 0) == lax.broadcasted_iota(jnp.int32, (k, k), 1)
    picked = jnp.where(own[None], columns.astype(jnp.float32)[:, None, :], 0.0).reshape(tok * k, k)
    ones = jnp.ones((k, LANES), jnp.bfloat16)
    return jnp.dot(picked.astype(jnp.bfloat16), ones, preferred_element_type=jnp.float32).reshape(tok, k, LANES)


def lane(tile):
    return slice(tile * LANES, (tile + 1) * LANES)


def sublanes(tile):
    return slice(tile * ROWS, (tile + 1) * ROWS)


def added(one_ref, other_ref, rows):
    total = one_ref[rows, :].astype(jnp.float32) + other_ref[rows, :].astype(jnp.float32)
    return total.astype(jnp.bfloat16).astype(jnp.float32)


def by_register(rate_ref, rates):
    states = rate_ref.shape[0]
    count = rates.shape[0] // states
    for n in range(states):
        for h in range(count):
            tiles = [rate_ref[n : n + 1, lane(h * ROWS + j)] for j in range(ROWS)]
            rates[n * count + h] = jnp.concatenate(tiles, axis=0) * (-LOG2E)


def local_kernel(
    lengths_ref,
    proj_ref,
    other_ref,
    dtw_ref,
    bias_ref,
    rate_ref,
    inner_ref,
    y_ref,
    sum_ref,
    state_ref,
    low_cols,
    bc_spread,
    raw,
    rates,
    step_tiles,
    drive_tiles,
    carry,
):
    tok = proj_ref.shape[1]
    block, channels = inner_ref.shape
    states = rate_ref.shape[0]
    low_rank = dtw_ref.shape[0]
    tiles = channels // LANES
    count = tiles // ROWS
    starts, _ = doc_edges(lengths_ref)
    at = pl.program_id(0)

    @pl.when(at == 0)
    def _():
        low_cols[...] = added(proj_ref, other_ref, slice(0, low_rank)).T.astype(jnp.bfloat16)
        bc_spread[...] = spread(added(proj_ref, other_ref, slice(low_rank, None)).T)
        by_register(rate_ref, rates)
        carry[...] = jnp.zeros_like(carry)
        for first in range(0, tiles, 4):
            cols = slice(first * LANES, (first + 4) * LANES)
            part = jnp.dot(low_cols[...], dtw_ref[:, cols], preferred_element_type=jnp.float32)
            for i in range(4):
                raw[:, sublanes(first + i), :] = part[:, lane(i)].reshape(tok // ROWS, ROWS, LANES)

    def steps(pair, unused):
        rows = pl.ds(pl.multiple_of(pair * PAIR, PAIR), PAIR)
        places = lax.axis_index("seq") * tok + at * block + pair * PAIR
        places = places + lax.broadcasted_iota(jnp.int32, (PAIR, LANES), 0)
        at_start = places == doc_start(places, starts)
        for tile in range(tiles):
            inner = inner_ref[rows, lane(tile)].astype(jnp.float32)
            bias = bias_ref[:, lane(tile)]
            for k in range(2):
                biased = raw[at * (block // ROWS) + 2 * pair + k, sublanes(tile), :] + bias
                step = jnp.maximum(biased, 0.0) + jnp.log(1.0 + jnp.exp(-jnp.abs(biased)))
                drive_tiles[2 * pair + k, sublanes(tile), :] = step * inner[sublanes(k)]
                step_tiles[2 * pair + k, sublanes(tile), :] = jnp.where(at_start[sublanes(k)], RESET, step)
        return unused

    lax.fori_loop(0, block // PAIR, steps, 0)

    def scan(t8, held):
        held, total = list(held[0]), list(held[1])
        for first in range(0, ROWS, 2):
            tokens = range(first, first + 2)
            picked = [[pl.ds(r + h * ROWS * ROWS, ROWS, stride=ROWS) for h in range(count)] for r in tokens]
            step = [[step_tiles[t8, rows, :] for rows in of_token] for of_token in picked]
            drive = [[drive_tiles[t8, rows, :] for rows in of_token] for of_token in picked]
            out = [[None] * count for _ in tokens]
            for n in range(states):
                where = [at * block + t8 * ROWS + r for r in tokens]
                b_row = [bc_spread[token, n : n + 1, :] for token in where]
                c_row = [bc_spread[token, states + n : states + n + 1, :] for token in where]
                for h in range(count):
                    i = n * count + h
                    rate = rates[i]
                    decay = [jnp.exp2(rate * step[k][h]) for k in range(2)]
                    for k in range(2):
                        held[i] = decay[k] * held[i] + b_row[k] * drive[k][h]
                        term = c_row[k] * held[i]
                        out[k][h] = term if out[k][h] is None else out[k][h] + term
            for k, r in enumerate(tokens):
                for h in range(count):
                    total[h] = total[h] + step[k][h]
                    y_ref[t8 * ROWS + r, sublanes(h), :] = out[k][h]
                    sum_ref[t8 * ROWS + r, sublanes(h), :] = total[h]
        return held, total

    kept = states * count
    held = ([carry[i] for i in range(kept)], [carry[kept + h] for h in range(count)])
    held, total = lax.fori_loop(0, block // ROWS, scan, held)
    for i, value in enumerate(held + total):
        carry[i] = value

    @pl.when(at == pl.num_programs(0) - 1)
    def _():
        state_ref[: states * tiles, :] = jnp.concatenate(held, axis=0).astype(jnp.bfloat16)
        whole = jnp.concatenate(total, axis=0)
        high = whole.astype(jnp.bfloat16).astype(jnp.float32)
        state_ref[states * tiles :, :] = jnp.concatenate([high, whole - high], axis=0).astype(jnp.bfloat16)


def local_scan(lengths, projected, other, dt_weight, dt_bias, decay_rate, inner_act):
    tok, channels = inner_act.shape
    low_rank = dt_weight.shape[0]
    states = decay_rate.shape[0]
    tiles = channels // LANES
    count = tiles // ROWS
    whole = lambda a: pl.BlockSpec(a.shape, lambda i: (0,) * a.ndim)
    bias = dt_bias.reshape(1, channels)
    by_token = pl.BlockSpec((BLOCK, tiles, LANES), lambda i: (i, 0, 0))
    state_rows = (states + 2) * tiles
    return pl.pallas_call(
        local_kernel,
        grid=(tok // BLOCK,),
        in_specs=[
            pl.BlockSpec(memory_space=pltpu.SMEM),
            whole(projected),
            whole(other),
            whole(dt_weight),
            whole(bias),
            whole(decay_rate),
            pl.BlockSpec((BLOCK, channels), lambda i: (i, 0)),
        ],
        out_specs=[by_token, by_token, pl.BlockSpec((state_rows, LANES), lambda i: (0, 0))],
        out_shape=[
            jax.ShapeDtypeStruct((tok, tiles, LANES), jnp.float32),
            jax.ShapeDtypeStruct((tok, tiles, LANES), jnp.float32),
            jax.ShapeDtypeStruct((state_rows, LANES), jnp.bfloat16),
        ],
        scratch_shapes=[
            pltpu.VMEM((tok, low_rank), jnp.bfloat16),
            pltpu.VMEM((tok, 2 * states, LANES), jnp.float32),
            pltpu.VMEM((tok // ROWS, tiles * ROWS, LANES), jnp.float32),
            pltpu.VMEM((states * count, ROWS, LANES), jnp.float32),
            pltpu.VMEM((BLOCK // ROWS, tiles * ROWS, LANES), jnp.float32),
            pltpu.VMEM((BLOCK // ROWS, tiles * ROWS, LANES), jnp.float32),
            pltpu.VMEM(((states + 1) * count, ROWS, LANES), jnp.float32),
        ],
        compiler_params=pltpu.CompilerParams(vmem_limit_bytes=VMEM_MOST),
        cost_estimate=pl.CostEstimate(
            flops=12 * tok * channels * states,
            bytes_accessed=12 * tok * channels,
            transcendentals=tok * channels * states,
        ),
        name="local_scan",
    )(lengths, projected, other, dt_weight, bias, decay_rate, inner_act)


def join_kernel(
    reach,
    proj_ref,
    other_ref,
    y_ref,
    sum_ref,
    inner_ref,
    z_ref,
    rate_ref,
    skip_ref,
    moved_ref,
    mine_ref,
    theirs_ref,
    out_ref,
    regrouped_ref,
    c_spread,
    rates,
    entering,
    rows_tiles,
):
    block, channels = z_ref.shape
    states = rate_ref.shape[0]
    tiles = channels // LANES
    count = tiles // ROWS
    kept = states * count
    at = pl.program_id(0)

    @pl.when(at == 0)
    def _():
        c_spread[...] = spread(added(proj_ref, other_ref, slice(None)).T)
        by_register(rate_ref, rates)
        odd = lax.rem(lax.axis_index("seq"), 2)
        state = [jnp.zeros((ROWS, LANES), jnp.float32)] * kept
        for back in range(reach, 0, -1):
            ref, which = (mine_ref, back // 2) if back % 2 == 0 else (theirs_ref, (back + 1) // 2 - odd)
            sent = ref[which].astype(jnp.float32)
            totals = sent[states * tiles : (states + 1) * tiles] + sent[(states + 1) * tiles :]
            state = [
                jnp.exp2(rates[i] * totals[sublanes(i % count)]) * state[i] + sent[sublanes(i)] for i in range(kept)
            ]
        for i in range(kept):
            entering[i] = state[i]

    regrouped_ref[...] = moved_ref[...]

    def body(pair, unused):
        rows = pl.ds(pl.multiple_of(pair * PAIR, PAIR), PAIR)
        for k in range(2):
            first = pair * PAIR + k * ROWS
            total = [[sum_ref[first + r, sublanes(h), :] for h in range(count)] for r in range(ROWS)]
            out = [[y_ref[first + r, sublanes(h), :] for h in range(count)] for r in range(ROWS)]
            for n in range(states):
                c_row = [c_spread[at * block + first + r, n : n + 1, :] for r in range(ROWS)]
                for h in range(count):
                    rate, state = rates[n * count + h], entering[n * count + h]
                    for r in range(ROWS):
                        out[r][h] += jnp.exp2(rate * total[r][h]) * state * c_row[r]
            for r in range(ROWS):
                for h in range(count):
                    rows_tiles[k, pl.ds(r + h * ROWS * ROWS, ROWS, stride=ROWS), :] = out[r][h]
        for tile in range(tiles):
            cols = lane(tile)
            z = z_ref[rows, cols].astype(jnp.float32)
            gate = z * (0.5 + 0.5 * jnp.tanh(0.5 * z))
            scanned = jnp.concatenate([rows_tiles[k, sublanes(tile), :] for k in range(2)], axis=0)
            scanned = scanned + skip_ref[:, cols] * inner_ref[rows, cols].astype(jnp.float32)
            out_ref[rows, cols] = (scanned * gate).astype(jnp.bfloat16)
        return unused

    lax.fori_loop(0, block // PAIR, body, 0)


def join_states(projected, other, y, sums, inner_act, z_branch, decay_rate, skip_gain, moved, mine, theirs, low_rank, reach):
    tok, channels = z_branch.shape
    states = decay_rate.shape[0]
    tiles = channels // LANES
    count = tiles // ROWS
    whole = lambda a: pl.BlockSpec(a.shape, lambda i: (0,) * a.ndim)
    by_token = pl.BlockSpec((BLOCK, tiles, LANES), lambda i: (i, 0, 0))
    by_row = pl.BlockSpec((BLOCK, channels), lambda i: (i, 0))
    skip = skip_gain.reshape(1, channels)
    c_part = pl.BlockSpec((states, tok), lambda i: (low_rank // states + 1, 0))
    return pl.pallas_call(
        functools.partial(join_kernel, reach),
        grid=(tok // BLOCK,),
        in_specs=[
            c_part,
            c_part,
            by_token,
            by_token,
            by_row,
            by_row,
            whole(decay_rate),
            whole(skip),
            by_row,
            whole(mine),
            whole(theirs),
        ],
        out_specs=[by_row, by_row],
        out_shape=[jax.ShapeDtypeStruct((tok, channels), jnp.bfloat16)] * 2,
        scratch_shapes=[
            pltpu.VMEM((tok, states, LANES), jnp.float32),
            pltpu.VMEM((states * count, ROWS, LANES), jnp.float32),
            pltpu.VMEM((states * count, ROWS, LANES), jnp.float32),
            pltpu.VMEM((2, tiles * ROWS, LANES), jnp.float32),
        ],
        compiler_params=pltpu.CompilerParams(vmem_limit_bytes=VMEM_MOST),
        cost_estimate=pl.CostEstimate(
            flops=8 * tok * channels * states,
            bytes_accessed=14 * tok * channels,
            transcendentals=tok * channels * states,
        ),
        name="join_states",
    )(projected, other, y, sums, inner_act, z_branch, decay_rate, skip, moved, mine, theirs)


def attend_kernel(
    lengths_ref,
    place_ref,
    q_ref,
    keys_mine,
    keys_theirs,
    values_mine,
    values_theirs,
    out_ref,
    queries,
    scores,
    tops,
    acc,
):
    tok = q_ref.shape[0]
    heads = q_ref.shape[1] // HD
    position = lax.axis_index("seq")
    odd = lax.rem(position, 2)
    anchor = position * tok
    scale = jnp.bfloat16(LOG2E * HD**-0.5)
    starts, ends = doc_edges(lengths_ref)
    edges = list(zip(starts, ends)) + [(jnp.int32(-(2**30)), jnp.int32(0))]
    lane = lax.broadcasted_iota(jnp.int32, (1, LANES), 1)
    first = jnp.full((1, LANES), 2**30, jnp.int32)
    last = jnp.zeros((1, LANES), jnp.int32)
    for i, (start, end) in enumerate(edges):
        first = jnp.where(lane == i, start, first)
        last = jnp.where(lane == i, end, last)
    rows = lax.broadcasted_iota(jnp.int32, (tok, LANES), 0)

    def in_doc(base):
        return (rows + base >= first) & (rows + base < last)

    apart = jnp.where(in_doc(anchor) | (lane >= len(edges)), 0.0, -APART).astype(jnp.bfloat16)
    for head in range(heads):
        queries[head * tok : (head + 1) * tok, :HD] = q_ref[:, head * HD : (head + 1) * HD]
        queries[head * tok : (head + 1) * tok, HD:] = apart

    def rows_of(mine_ref, theirs_ref, back):
        if isinstance(back, int) and back == 0:
            return mine_ref[0]
        return jnp.where(lax.rem(back, 2) == 0, mine_ref[back // 2], theirs_ref[(back + 1) // 2 - odd])

    def score(back):
        marks = jnp.where(in_doc(anchor - back * tok), 1.0, 0.0).astype(jnp.bfloat16)
        keys = jnp.concatenate([rows_of(keys_mine, keys_theirs, back), marks], axis=1)
        return lax.dot_general(queries[...], keys, (((1,), (1,)), ((), ())), preferred_element_type=jnp.float32)

    causal = lax.broadcasted_iota(jnp.int32, (tok, tok), 1) <= lax.broadcasted_iota(jnp.int32, (tok, tok), 0)

    def highest(backs):
        top = None
        for back in backs:
            s = score(back)
            if isinstance(back, int) and back == 0:
                s = jnp.concatenate(
                    [jnp.where(causal, s[h * tok : (h + 1) * tok], -APART) for h in range(heads)], axis=0
                )
            scores[back] = s
            for at in range(0, tok, LANES):
                piece = s[:, at : at + LANES]
                top = piece if top is None else jnp.maximum(top, piece)
        return top

    begin = jnp.int32(0)
    for start in starts[1:]:
        begin = jnp.where(anchor >= start, start, begin)
    pairs = ((anchor - begin + tok - 1) // tok + 1) // 2

    def start_with(alone, together):
        pl.when(pairs == 0)(alone)
        pl.when(pairs > 0)(together)

    def set_tops(backs):
        tops[...] = highest(backs)

    start_with(lambda: set_tops([0]), lambda: set_tops([0, 1, 2]))

    def look(pair, carry):
        tops[...] = jnp.maximum(tops[...], highest([2 * pair - 1, 2 * pair]))
        return carry

    lax.fori_loop(2, pairs + 1, look, 0)
    tops[...] = jnp.broadcast_to(jnp.max(tops[...], axis=1, keepdims=True), tops.shape)

    def weighted(backs):
        values = jnp.concatenate([rows_of(values_mine, values_theirs, back) for back in backs], axis=0)
        values = jnp.concatenate([values, jnp.ones(values.shape, jnp.bfloat16)], axis=1)
        top = tops[...]
        weights = [
            jnp.exp2((scores[back, :, at : at + LANES] - top).astype(jnp.bfloat16) * scale)
            for back in backs
            for at in range(0, tok, LANES)
        ]
        return jnp.dot(jnp.concatenate(weights, axis=1), values, preferred_element_type=jnp.float32)

    def set_acc(backs):
        acc[...] = weighted(backs)

    start_with(lambda: set_acc([0]), lambda: set_acc([0, 1, 2]))

    def absorb(pair, carry):
        acc[...] += weighted([2 * pair - 1, 2 * pair])
        return carry

    lax.fori_loop(2, pairs + 1, absorb, 0)
    order = place_ref[pl.ds(position, 1), :]
    move = (lax.broadcasted_iota(jnp.int32, (tok, tok), 0) == order).astype(jnp.float32).astype(jnp.bfloat16)
    for head in range(heads):
        part = slice(head * tok, (head + 1) * tok)
        result = (acc[part, :HD] / acc[part, HD:]).astype(jnp.bfloat16)
        moved = jnp.dot(move, result, preferred_element_type=jnp.float32)
        out_ref[:, head * HD : (head + 1) * HD] = moved.astype(jnp.bfloat16)


def attend(lengths, send_place, query_rows, mine, theirs):
    tok, width = query_rows.shape
    kv_local = mine.shape[2] // (2 * HD)
    share = width // kv_local
    heads = share // HD
    reach = 2 * (mine.shape[0] - 1)
    by_group = pl.BlockSpec((tok, share), lambda i: (0, i))
    keys = pl.BlockSpec(mine.shape[:2] + (HD,), lambda i: (0, 0, i))
    values = pl.BlockSpec(mine.shape[:2] + (HD,), lambda i: (0, 0, i + kv_local))
    return pl.pallas_call(
        attend_kernel,
        grid=(kv_local,),
        in_specs=[
            pl.BlockSpec(memory_space=pltpu.SMEM),
            pl.BlockSpec(send_place.shape, lambda i: (0, 0)),
            by_group,
            keys,
            keys,
            values,
            values,
        ],
        out_specs=by_group,
        out_shape=jax.ShapeDtypeStruct((tok, width), jnp.bfloat16),
        scratch_shapes=[
            pltpu.VMEM((heads * tok, 2 * HD), jnp.bfloat16),
            pltpu.VMEM((reach + 1, heads * tok, tok), jnp.float32),
            pltpu.VMEM((heads * tok, LANES), jnp.float32),
            pltpu.VMEM((heads * tok, 2 * HD), jnp.float32),
        ],
        compiler_params=pltpu.CompilerParams(vmem_limit_bytes=VMEM_LIMIT // 2 + 4 * (reach + 1) * heads * tok * tok),
        cost_estimate=pl.CostEstimate(flops=tok * width, bytes_accessed=tok * width, transcendentals=0),
        name="attend",
    )(lengths, send_place, query_rows, mine, theirs, mine, theirs)


def shifted(value, steps):
    count = lax.axis_size("seq")
    return lax.ppermute(value, "seq", [(source, source + steps) for source in range(count - steps)])


def with_partner(held):
    mine = jnp.stack(held)
    count = lax.axis_size("seq")
    return mine, lax.ppermute(mine, "seq", [(source, source ^ 1) for source in range(count)])


def even_back(value, reach):
    return [value] + [shifted(value, 2 * k) for k in range(1, (reach + 1) // 2 + 1)]


def local(
    x_branch,
    z_branch,
    conv_weight,
    conv_bias,
    xproj_weight,
    dt_weight,
    dt_bias,
    decay_rate,
    skip_gain,
    query_rows,
    key_rows,
    value_rows,
    lengths,
    destination,
):
    tok = x_branch.shape[0]
    n_seq = lax.axis_size("seq")
    n_mp = lax.axis_size("mp")
    low_rank = dt_weight.shape[0]
    reach = n_seq // 2
    run_rows = tok // n_seq
    fence = lax.optimization_barrier

    halo, kv = pack(x_branch, key_rows, value_rows)
    earlier_rows = shifted(halo, 1)
    held = even_back(kv, reach)
    send_place = ((destination // tok) * run_rows + destination % run_rows).reshape(n_seq, tok)

    inner_act, partial = conv_project(lengths, x_branch, earlier_rows, conv_weight, conv_bias, xproj_weight)
    _, *held = fence((partial, *held))
    mine, theirs = with_partner(held)
    total, other = partial, jnp.zeros_like(partial)
    steps = [1 << k for k in range((n_mp - 1).bit_length())]
    for step in steps:
        if step > 1:
            total = (total.astype(jnp.float32) + other.astype(jnp.float32)).astype(jnp.bfloat16)
        if step == steps[-1]:
            total, send_place = fence((total, send_place))
        other = lax.ppermute(total, "mp", [(source, source ^ step) for source in range(n_mp)])
    attended = attend(lengths, send_place, query_rows, mine, theirs)
    total, other, attended = fence((total, other, attended))
    regrouped = lax.all_to_all(attended, "seq", split_axis=0, concat_axis=0, tiled=True)

    y, sums, state = local_scan(lengths, total, other, dt_weight, dt_bias, decay_rate, inner_act)
    states = with_partner(even_back(state, reach))
    return tuple(
        join_states(
            total,
            other,
            y,
            sums,
            inner_act,
            z_branch,
            decay_rate,
            skip_gain,
            regrouped,
            *states,
            low_rank,
            reach,
        )
    )


def solution(mesh):
    placed = (
        P("seq", "mp"),
        P("seq", "mp"),
        P(None, "mp"),
        P("mp"),
        P("mp", None),
        P(None, "mp"),
        P("mp"),
        P(None, "mp"),
        P("mp"),
        P("seq", "mp"),
        P("seq", "mp"),
        P("seq", "mp"),
        P(),
        P(),
    )
    return jax.shard_map(
        local,
        mesh=mesh,
        in_specs=placed,
        out_specs=(P("seq", "mp"), P("seq", "mp")),
        check_vma=False,
    )
```

```python
import functools

import jax
import jax.numpy as jnp
from jax import lax
from jax.experimental import pallas as pl
from jax.experimental.pallas import tpu as pltpu
from jax.sharding import PartitionSpec as P

HD = 128
LANES = 128
HALO = 16
LOG2E = 1.4426950408889634
RESET = 1e30
APART = 65536.0
VMEM_LIMIT = 32 * 1024 * 1024
VMEM_MOST = 56 * 1024 * 1024
VMEM_NEARLY = 53 * 1024 * 1024


def doc_edges(lengths_ref):
    starts, ends, total = [], [], 0
    for i in range(lengths_ref.shape[0]):
        starts.append(total)
        total = total + lengths_ref[i]
        ends.append(total)
    return starts, ends


def doc_start(places, starts):
    found = jnp.zeros_like(places)
    for start in starts[1:]:
        found = jnp.where(places >= start, start, found)
    return found


def channel_chunk(channels):
    return 1024 if channels % 1024 == 0 else channels


def pack_kernel(x_ref, k_ref, v_ref, halo_ref, kv_ref):
    width = k_ref.shape[1]
    halo_ref[...] = x_ref[...]
    kv_ref[:, :width] = k_ref[...]
    kv_ref[:, width:] = v_ref[...]


def pack(x_branch, key_rows, value_rows):
    tok, channels = x_branch.shape
    width = key_rows.shape[1]
    whole = lambda rows, columns: pl.BlockSpec((rows, columns), lambda i: (0, 0))
    return pl.pallas_call(
        pack_kernel,
        grid=(1,),
        in_specs=[
            pl.BlockSpec((HALO, channels), lambda i: (tok // HALO - 1, 0)),
            whole(tok, width),
            whole(tok, width),
        ],
        out_specs=[whole(HALO, channels), whole(tok, 2 * width)],
        out_shape=[
            jax.ShapeDtypeStruct((HALO, channels), x_branch.dtype),
            jax.ShapeDtypeStruct((tok, 2 * width), key_rows.dtype),
        ],
        compiler_params=pltpu.CompilerParams(vmem_limit_bytes=VMEM_MOST),
        cost_estimate=pl.CostEstimate(flops=0, bytes_accessed=16 * tok * width, transcendentals=0),
        name="pack",
    )(x_branch, key_rows, value_rows)


def conv_kernel(
    lengths_ref, x_ref, halo_ref, w_hbm, b_hbm, xp_ref, inner_ref, part_ref, ext, acc, w_ref, b_ref, fetched
):
    tok, chunk = x_ref.shape
    starts, _ = doc_edges(lengths_ref)
    anchor = lax.axis_index("seq") * tok
    places = anchor + lax.broadcasted_iota(jnp.int32, (tok, LANES), 0)
    depth = places - doc_start(places, starts)
    at = pl.program_id(0)
    fetches = [
        pltpu.make_async_copy(w_hbm, w_ref, fetched.at[0]),
        pltpu.make_async_copy(b_hbm, b_ref, fetched.at[1]),
    ]

    @pl.when(at == 0)
    def _():
        for fetch in fetches:
            fetch.start()

    ext[0:HALO, :] = halo_ref[...].astype(jnp.float32)
    ext[HALO:, :] = x_ref[...].astype(jnp.float32)

    @pl.when(at == 0)
    def _():
        for fetch in fetches:
            fetch.wait()

    for lane in range(0, chunk, LANES):
        cols = slice(lane, lane + LANES)
        here = pl.ds(pl.multiple_of(at * chunk + lane, LANES), LANES)
        total = b_ref[:, here] + w_ref[0:1, here] * ext[HALO:, cols]
        for lag in range(1, w_ref.shape[0]):
            window = ext[HALO - lag : HALO - lag + tok, cols]
            total += w_ref[lag : lag + 1, here] * jnp.where(depth >= lag, window, 0.0)
        act = total * (0.5 + 0.5 * jnp.tanh(0.5 * total))
        inner_ref[:, cols] = act.astype(jnp.bfloat16)
    product = lax.dot_general(
        xp_ref[...], inner_ref[...], (((1,), (1,)), ((), ())), preferred_element_type=jnp.float32
    )

    @pl.when(at == 0)
    def _():
        acc[...] = product

    @pl.when(at > 0)
    def _():
        acc[...] += product

    @pl.when(at == pl.num_programs(0) - 1)
    def _():
        part_ref[...] = acc[...].astype(jnp.bfloat16)


def conv_project(lengths, x_branch, halo, conv_weight, conv_bias, xproj_weight):
    tok, channels = x_branch.shape
    width = xproj_weight.shape[1]
    taps = conv_weight.shape[0]
    chunk = channel_chunk(channels)
    return pl.pallas_call(
        conv_kernel,
        grid=(channels // chunk,),
        in_specs=[
            pl.BlockSpec(memory_space=pltpu.SMEM),
            pl.BlockSpec((tok, chunk), lambda i: (0, i)),
            pl.BlockSpec((HALO, chunk), lambda i: (0, i)),
            pl.BlockSpec(memory_space=pltpu.HBM),
            pl.BlockSpec(memory_space=pltpu.HBM),
            pl.BlockSpec((width, chunk), lambda i: (0, i)),
        ],
        out_specs=[
            pl.BlockSpec((tok, chunk), lambda i: (0, i)),
            pl.BlockSpec((width, tok), lambda i: (0, 0)),
        ],
        out_shape=[
            jax.ShapeDtypeStruct((tok, channels), jnp.bfloat16),
            jax.ShapeDtypeStruct((width, tok), jnp.bfloat16),
        ],
        scratch_shapes=[
            pltpu.VMEM((tok + HALO, chunk), jnp.float32),
            pltpu.VMEM((width, tok), jnp.float32),
            pltpu.VMEM((taps, channels), jnp.float32),
            pltpu.VMEM((1, channels), jnp.float32),
            pltpu.SemaphoreType.DMA((2,)),
        ],
        compiler_params=pltpu.CompilerParams(vmem_limit_bytes=VMEM_NEARLY),
        cost_estimate=pl.CostEstimate(
            flops=80 * tok * channels * width, bytes_accessed=8 * tok * channels, transcendentals=tok * channels
        ),
        name="conv_project",
    )(lengths, x_branch, halo, conv_weight, conv_bias.reshape(1, channels), xproj_weight.T)


ROWS = 8
PAIR = 2 * ROWS
BLOCK = 64


def spread(columns):
    tok, k = columns.shape
    own = lax.broadcasted_iota(jnp.int32, (k, k), 0) == lax.broadcasted_iota(jnp.int32, (k, k), 1)
    picked = jnp.where(own[None], columns.astype(jnp.float32)[:, None, :], 0.0).reshape(tok * k, k)
    ones = jnp.ones((k, LANES), jnp.bfloat16)
    return jnp.dot(picked.astype(jnp.bfloat16), ones, preferred_element_type=jnp.float32).reshape(tok, k, LANES)


def lane(tile):
    return slice(tile * LANES, (tile + 1) * LANES)


def sublanes(tile):
    return slice(tile * ROWS, (tile + 1) * ROWS)


def added(one_ref, other_ref, rows):
    total = one_ref[rows, :].astype(jnp.float32) + other_ref[rows, :].astype(jnp.float32)
    return total.astype(jnp.bfloat16).astype(jnp.float32)


def by_register(rate_ref, rates):
    states = rate_ref.shape[0]
    count = rates.shape[0] // states
    for n in range(states):
        for h in range(count):
            tiles = [rate_ref[n : n + 1, lane(h * ROWS + j)] for j in range(ROWS)]
            rates[n * count + h] = jnp.concatenate(tiles, axis=0) * (-LOG2E)


def local_kernel(
    lengths_ref,
    proj_ref,
    other_ref,
    dtw_ref,
    bias_ref,
    rate_ref,
    inner_ref,
    y_ref,
    sum_ref,
    state_ref,
    low_cols,
    bc_spread,
    raw,
    rates,
    step_tiles,
    drive_tiles,
    carry,
):
    tok = proj_ref.shape[1]
    block, channels = inner_ref.shape
    states = rate_ref.shape[0]
    low_rank = dtw_ref.shape[0]
    tiles = channels // LANES
    count = tiles // ROWS
    starts, _ = doc_edges(lengths_ref)
    at = pl.program_id(0)

    @pl.when(at == 0)
    def _():
        low_cols[...] = added(proj_ref, other_ref, slice(0, low_rank)).T.astype(jnp.bfloat16)
        bc_spread[...] = spread(added(proj_ref, other_ref, slice(low_rank, None)).T)
        by_register(rate_ref, rates)
        carry[...] = jnp.zeros_like(carry)
        for first in range(0, tiles, 4):
            cols = slice(first * LANES, (first + 4) * LANES)
            part = jnp.dot(low_cols[...], dtw_ref[:, cols], preferred_element_type=jnp.float32)
            for i in range(4):
                raw[:, sublanes(first + i), :] = part[:, lane(i)].reshape(tok // ROWS, ROWS, LANES)

    def steps(pair, unused):
        rows = pl.ds(pl.multiple_of(pair * PAIR, PAIR), PAIR)
        places = lax.axis_index("seq") * tok + at * block + pair * PAIR
        places = places + lax.broadcasted_iota(jnp.int32, (PAIR, LANES), 0)
        at_start = places == doc_start(places, starts)
        for tile in range(tiles):
            inner = inner_ref[rows, lane(tile)].astype(jnp.float32)
            bias = bias_ref[:, lane(tile)]
            for k in range(2):
                biased = raw[at * (block // ROWS) + 2 * pair + k, sublanes(tile), :] + bias
                step = jnp.maximum(biased, 0.0) + jnp.log(1.0 + jnp.exp(-jnp.abs(biased)))
                drive_tiles[2 * pair + k, sublanes(tile), :] = step * inner[sublanes(k)]
                step_tiles[2 * pair + k, sublanes(tile), :] = jnp.where(at_start[sublanes(k)], RESET, step)
        return unused

    lax.fori_loop(0, block // PAIR, steps, 0)

    def scan(t8, held):
        held, total = list(held[0]), list(held[1])
        for first in range(0, ROWS, 2):
            tokens = range(first, first + 2)
            picked = [[pl.ds(r + h * ROWS * ROWS, ROWS, stride=ROWS) for h in range(count)] for r in tokens]
            step = [[step_tiles[t8, rows, :] for rows in of_token] for of_token in picked]
            drive = [[drive_tiles[t8, rows, :] for rows in of_token] for of_token in picked]
            out = [[None] * count for _ in tokens]
            for n in range(states):
                where = [at * block + t8 * ROWS + r for r in tokens]
                b_row = [bc_spread[token, n : n + 1, :] for token in where]
                c_row = [bc_spread[token, states + n : states + n + 1, :] for token in where]
                for h in range(count):
                    i = n * count + h
                    rate = rates[i]
                    decay = [jnp.exp2(rate * step[k][h]) for k in range(2)]
                    for k in range(2):
                        held[i] = decay[k] * held[i] + b_row[k] * drive[k][h]
                        term = c_row[k] * held[i]
                        out[k][h] = term if out[k][h] is None else out[k][h] + term
            for k, r in enumerate(tokens):
                for h in range(count):
                    total[h] = total[h] + step[k][h]
                    y_ref[t8 * ROWS + r, sublanes(h), :] = out[k][h]
                    sum_ref[t8 * ROWS + r, sublanes(h), :] = total[h]
        return held, total

    kept = states * count
    held = ([carry[i] for i in range(kept)], [carry[kept + h] for h in range(count)])
    held, total = lax.fori_loop(0, block // ROWS, scan, held)
    for i, value in enumerate(held + total):
        carry[i] = value

    @pl.when(at == pl.num_programs(0) - 1)
    def _():
        state_ref[: states * tiles, :] = jnp.concatenate(held, axis=0).astype(jnp.bfloat16)
        whole = jnp.concatenate(total, axis=0)
        high = whole.astype(jnp.bfloat16).astype(jnp.float32)
        state_ref[states * tiles :, :] = jnp.concatenate([high, whole - high], axis=0).astype(jnp.bfloat16)


def local_scan(lengths, projected, other, dt_weight, dt_bias, decay_rate, inner_act):
    tok, channels = inner_act.shape
    low_rank = dt_weight.shape[0]
    states = decay_rate.shape[0]
    tiles = channels // LANES
    count = tiles // ROWS
    whole = lambda a: pl.BlockSpec(a.shape, lambda i: (0,) * a.ndim)
    bias = dt_bias.reshape(1, channels)
    by_token = pl.BlockSpec((BLOCK, tiles, LANES), lambda i: (i, 0, 0))
    state_rows = (states + 2) * tiles
    return pl.pallas_call(
        local_kernel,
        grid=(tok // BLOCK,),
        in_specs=[
            pl.BlockSpec(memory_space=pltpu.SMEM),
            whole(projected),
            whole(other),
            whole(dt_weight),
            whole(bias),
            whole(decay_rate),
            pl.BlockSpec((BLOCK, channels), lambda i: (i, 0)),
        ],
        out_specs=[by_token, by_token, pl.BlockSpec((state_rows, LANES), lambda i: (0, 0))],
        out_shape=[
            jax.ShapeDtypeStruct((tok, tiles, LANES), jnp.float32),
            jax.ShapeDtypeStruct((tok, tiles, LANES), jnp.float32),
            jax.ShapeDtypeStruct((state_rows, LANES), jnp.bfloat16),
        ],
        scratch_shapes=[
            pltpu.VMEM((tok, low_rank), jnp.bfloat16),
            pltpu.VMEM((tok, 2 * states, LANES), jnp.float32),
            pltpu.VMEM((tok // ROWS, tiles * ROWS, LANES), jnp.float32),
            pltpu.VMEM((states * count, ROWS, LANES), jnp.float32),
            pltpu.VMEM((BLOCK // ROWS, tiles * ROWS, LANES), jnp.float32),
            pltpu.VMEM((BLOCK // ROWS, tiles * ROWS, LANES), jnp.float32),
            pltpu.VMEM(((states + 1) * count, ROWS, LANES), jnp.float32),
        ],
        compiler_params=pltpu.CompilerParams(vmem_limit_bytes=VMEM_MOST),
        cost_estimate=pl.CostEstimate(
            flops=12 * tok * channels * states,
            bytes_accessed=12 * tok * channels,
            transcendentals=tok * channels * states,
        ),
        name="local_scan",
    )(lengths, projected, other, dt_weight, bias, decay_rate, inner_act)


def join_kernel(
    reach,
    proj_ref,
    other_ref,
    y_ref,
    sum_ref,
    inner_ref,
    z_ref,
    rate_ref,
    skip_ref,
    moved_ref,
    mine_ref,
    theirs_ref,
    out_ref,
    regrouped_ref,
    c_spread,
    rates,
    entering,
    rows_tiles,
):
    block, channels = z_ref.shape
    states = rate_ref.shape[0]
    tiles = channels // LANES
    count = tiles // ROWS
    kept = states * count
    at = pl.program_id(0)

    @pl.when(at == 0)
    def _():
        c_spread[...] = spread(added(proj_ref, other_ref, slice(None)).T)
        by_register(rate_ref, rates)
        odd = lax.rem(lax.axis_index("seq"), 2)
        state = [jnp.zeros((ROWS, LANES), jnp.float32)] * kept
        for back in range(reach, 0, -1):
            ref, which = (mine_ref, back // 2) if back % 2 == 0 else (theirs_ref, (back + 1) // 2 - odd)
            sent = ref[which].astype(jnp.float32)
            totals = sent[states * tiles : (states + 1) * tiles] + sent[(states + 1) * tiles :]
            state = [
                jnp.exp2(rates[i] * totals[sublanes(i % count)]) * state[i] + sent[sublanes(i)] for i in range(kept)
            ]
        for i in range(kept):
            entering[i] = state[i]

    regrouped_ref[...] = moved_ref[...]

    def body(pair, unused):
        rows = pl.ds(pl.multiple_of(pair * PAIR, PAIR), PAIR)
        for k in range(2):
            first = pair * PAIR + k * ROWS
            total = [[sum_ref[first + r, sublanes(h), :] for h in range(count)] for r in range(ROWS)]
            out = [[y_ref[first + r, sublanes(h), :] for h in range(count)] for r in range(ROWS)]
            for n in range(states):
                c_row = [c_spread[at * block + first + r, n : n + 1, :] for r in range(ROWS)]
                for h in range(count):
                    rate, state = rates[n * count + h], entering[n * count + h]
                    for r in range(ROWS):
                        out[r][h] += jnp.exp2(rate * total[r][h]) * state * c_row[r]
            for r in range(ROWS):
                for h in range(count):
                    rows_tiles[k, pl.ds(r + h * ROWS * ROWS, ROWS, stride=ROWS), :] = out[r][h]
        for tile in range(tiles):
            cols = lane(tile)
            z = z_ref[rows, cols].astype(jnp.float32)
            gate = z * (0.5 + 0.5 * jnp.tanh(0.5 * z))
            scanned = jnp.concatenate([rows_tiles[k, sublanes(tile), :] for k in range(2)], axis=0)
            scanned = scanned + skip_ref[:, cols] * inner_ref[rows, cols].astype(jnp.float32)
            out_ref[rows, cols] = (scanned * gate).astype(jnp.bfloat16)
        return unused

    lax.fori_loop(0, block // PAIR, body, 0)


def join_states(projected, other, y, sums, inner_act, z_branch, decay_rate, skip_gain, moved, mine, theirs, low_rank, reach):
    tok, channels = z_branch.shape
    states = decay_rate.shape[0]
    tiles = channels // LANES
    count = tiles // ROWS
    whole = lambda a: pl.BlockSpec(a.shape, lambda i: (0,) * a.ndim)
    by_token = pl.BlockSpec((BLOCK, tiles, LANES), lambda i: (i, 0, 0))
    by_row = pl.BlockSpec((BLOCK, channels), lambda i: (i, 0))
    skip = skip_gain.reshape(1, channels)
    c_part = pl.BlockSpec((states, tok), lambda i: (low_rank // states + 1, 0))
    return pl.pallas_call(
        functools.partial(join_kernel, reach),
        grid=(tok // BLOCK,),
        in_specs=[
            c_part,
            c_part,
            by_token,
            by_token,
            by_row,
            by_row,
            whole(decay_rate),
            whole(skip),
            by_row,
            whole(mine),
            whole(theirs),
        ],
        out_specs=[by_row, by_row],
        out_shape=[jax.ShapeDtypeStruct((tok, channels), jnp.bfloat16)] * 2,
        scratch_shapes=[
            pltpu.VMEM((tok, states, LANES), jnp.float32),
            pltpu.VMEM((states * count, ROWS, LANES), jnp.float32),
            pltpu.VMEM((states * count, ROWS, LANES), jnp.float32),
            pltpu.VMEM((2, tiles * ROWS, LANES), jnp.float32),
        ],
        compiler_params=pltpu.CompilerParams(vmem_limit_bytes=VMEM_NEARLY),
        cost_estimate=pl.CostEstimate(
            flops=8 * tok * channels * states,
            bytes_accessed=14 * tok * channels,
            transcendentals=tok * channels * states,
        ),
        name="join_states",
    )(projected, other, y, sums, inner_act, z_branch, decay_rate, skip, moved, mine, theirs)


def attend_kernel(
    lengths_ref,
    place_ref,
    q_ref,
    keys_mine,
    keys_theirs,
    values_mine,
    values_theirs,
    out_ref,
    queries,
    scores,
    tops,
    acc,
):
    tok = q_ref.shape[0]
    heads = q_ref.shape[1] // HD
    position = lax.axis_index("seq")
    odd = lax.rem(position, 2)
    anchor = position * tok
    scale = jnp.bfloat16(LOG2E * HD**-0.5)
    starts, ends = doc_edges(lengths_ref)
    edges = list(zip(starts, ends)) + [(jnp.int32(-(2**30)), jnp.int32(0))]
    lane = lax.broadcasted_iota(jnp.int32, (1, LANES), 1)
    first = jnp.full((1, LANES), 2**30, jnp.int32)
    last = jnp.zeros((1, LANES), jnp.int32)
    for i, (start, end) in enumerate(edges):
        first = jnp.where(lane == i, start, first)
        last = jnp.where(lane == i, end, last)
    rows = lax.broadcasted_iota(jnp.int32, (tok, LANES), 0)

    def in_doc(base):
        return (rows + base >= first) & (rows + base < last)

    apart = jnp.where(in_doc(anchor) | (lane >= len(edges)), 0.0, -APART).astype(jnp.bfloat16)
    for head in range(heads):
        queries[head * tok : (head + 1) * tok, :HD] = q_ref[:, head * HD : (head + 1) * HD]
        queries[head * tok : (head + 1) * tok, HD:] = apart

    def rows_of(mine_ref, theirs_ref, back):
        if isinstance(back, int) and back == 0:
            return mine_ref[0]
        return jnp.where(lax.rem(back, 2) == 0, mine_ref[back // 2], theirs_ref[(back + 1) // 2 - odd])

    def score(back):
        marks = jnp.where(in_doc(anchor - back * tok), 1.0, 0.0).astype(jnp.bfloat16)
        keys = jnp.concatenate([rows_of(keys_mine, keys_theirs, back), marks], axis=1)
        return lax.dot_general(queries[...], keys, (((1,), (1,)), ((), ())), preferred_element_type=jnp.float32)

    causal = lax.broadcasted_iota(jnp.int32, (tok, tok), 1) <= lax.broadcasted_iota(jnp.int32, (tok, tok), 0)

    def highest(backs):
        top = None
        for back in backs:
            s = score(back)
            if isinstance(back, int) and back == 0:
                s = jnp.concatenate(
                    [jnp.where(causal, s[h * tok : (h + 1) * tok], -APART) for h in range(heads)], axis=0
                )
            scores[back] = s
            for at in range(0, tok, LANES):
                piece = s[:, at : at + LANES]
                top = piece if top is None else jnp.maximum(top, piece)
        return top

    begin = jnp.int32(0)
    for start in starts[1:]:
        begin = jnp.where(anchor >= start, start, begin)
    pairs = ((anchor - begin + tok - 1) // tok + 1) // 2

    def start_with(alone, together):
        pl.when(pairs == 0)(alone)
        pl.when(pairs > 0)(together)

    def set_tops(backs):
        tops[...] = highest(backs)

    start_with(lambda: set_tops([0]), lambda: set_tops([0, 1, 2]))

    def look(pair, carry):
        tops[...] = jnp.maximum(tops[...], highest([2 * pair - 1, 2 * pair]))
        return carry

    lax.fori_loop(2, pairs + 1, look, 0)
    tops[...] = jnp.broadcast_to(jnp.max(tops[...], axis=1, keepdims=True), tops.shape)

    def weighted(backs):
        values = jnp.concatenate([rows_of(values_mine, values_theirs, back) for back in backs], axis=0)
        values = jnp.concatenate([values, jnp.ones(values.shape, jnp.bfloat16)], axis=1)
        top = tops[...]
        weights = [
            jnp.exp2((scores[back, :, at : at + LANES] - top).astype(jnp.bfloat16) * scale)
            for back in backs
            for at in range(0, tok, LANES)
        ]
        return jnp.dot(jnp.concatenate(weights, axis=1), values, preferred_element_type=jnp.float32)

    def set_acc(backs):
        acc[...] = weighted(backs)

    start_with(lambda: set_acc([0]), lambda: set_acc([0, 1, 2]))

    def absorb(pair, carry):
        acc[...] += weighted([2 * pair - 1, 2 * pair])
        return carry

    lax.fori_loop(2, pairs + 1, absorb, 0)
    order = place_ref[pl.ds(position, 1), :]
    move = (lax.broadcasted_iota(jnp.int32, (tok, tok), 0) == order).astype(jnp.float32).astype(jnp.bfloat16)
    for head in range(heads):
        part = slice(head * tok, (head + 1) * tok)
        result = (acc[part, :HD] / acc[part, HD:]).astype(jnp.bfloat16)
        moved = jnp.dot(move, result, preferred_element_type=jnp.float32)
        out_ref[:, head * HD : (head + 1) * HD] = moved.astype(jnp.bfloat16)


def attend(lengths, send_place, query_rows, mine, theirs):
    tok, width = query_rows.shape
    kv_local = mine.shape[2] // (2 * HD)
    share = width // kv_local
    heads = share // HD
    reach = 2 * (mine.shape[0] - 1)
    by_group = pl.BlockSpec((tok, share), lambda i: (0, i))
    keys = pl.BlockSpec(mine.shape[:2] + (HD,), lambda i: (0, 0, i))
    values = pl.BlockSpec(mine.shape[:2] + (HD,), lambda i: (0, 0, i + kv_local))
    return pl.pallas_call(
        attend_kernel,
        grid=(kv_local,),
        in_specs=[
            pl.BlockSpec(memory_space=pltpu.SMEM),
            pl.BlockSpec(send_place.shape, lambda i: (0, 0)),
            by_group,
            keys,
            keys,
            values,
            values,
        ],
        out_specs=by_group,
        out_shape=jax.ShapeDtypeStruct((tok, width), jnp.bfloat16),
        scratch_shapes=[
            pltpu.VMEM((heads * tok, 2 * HD), jnp.bfloat16),
            pltpu.VMEM((reach + 1, heads * tok, tok), jnp.float32),
            pltpu.VMEM((heads * tok, LANES), jnp.float32),
            pltpu.VMEM((heads * tok, 2 * HD), jnp.float32),
        ],
        compiler_params=pltpu.CompilerParams(vmem_limit_bytes=VMEM_LIMIT // 2 + 4 * (reach + 1) * heads * tok * tok),
        cost_estimate=pl.CostEstimate(flops=tok * width, bytes_accessed=tok * width, transcendentals=0),
        name="attend",
    )(lengths, send_place, query_rows, mine, theirs, mine, theirs)


def shifted(value, steps):
    count = lax.axis_size("seq")
    return lax.ppermute(value, "seq", [(source, source + steps) for source in range(count - steps)])


def with_partner(held):
    mine = jnp.stack(held)
    count = lax.axis_size("seq")
    return mine, lax.ppermute(mine, "seq", [(source, source ^ 1) for source in range(count)])


def even_back(value, reach):
    return [value] + [shifted(value, 2 * k) for k in range(1, (reach + 1) // 2 + 1)]


def local(
    x_branch,
    z_branch,
    conv_weight,
    conv_bias,
    xproj_weight,
    dt_weight,
    dt_bias,
    decay_rate,
    skip_gain,
    query_rows,
    key_rows,
    value_rows,
    lengths,
    destination,
):
    tok = x_branch.shape[0]
    n_seq = lax.axis_size("seq")
    n_mp = lax.axis_size("mp")
    low_rank = dt_weight.shape[0]
    reach = n_seq // 2
    run_rows = tok // n_seq
    fence = lax.optimization_barrier

    halo, kv = pack(x_branch, key_rows, value_rows)
    earlier_rows = shifted(halo, 1)
    held = even_back(kv, reach)
    send_place = ((destination // tok) * run_rows + destination % run_rows).reshape(n_seq, tok)

    inner_act, partial = conv_project(lengths, x_branch, earlier_rows, conv_weight, conv_bias, xproj_weight)
    _, *held = fence((partial, *held))
    mine, theirs = with_partner(held)
    total, other = partial, jnp.zeros_like(partial)
    steps = [1 << k for k in range((n_mp - 1).bit_length())]
    for step in steps:
        if step > 1:
            total = (total.astype(jnp.float32) + other.astype(jnp.float32)).astype(jnp.bfloat16)
        if step == steps[-1]:
            total, send_place = fence((total, send_place))
        other = lax.ppermute(total, "mp", [(source, source ^ step) for source in range(n_mp)])
    attended = attend(lengths, send_place, query_rows, mine, theirs)
    total, other, attended = fence((total, other, attended))
    regrouped = lax.all_to_all(attended, "seq", split_axis=0, concat_axis=0, tiled=True)

    y, sums, state = local_scan(lengths, total, other, dt_weight, dt_bias, decay_rate, inner_act)
    states = with_partner(even_back(state, reach))
    return tuple(
        join_states(
            total,
            other,
            y,
            sums,
            inner_act,
            z_branch,
            decay_rate,
            skip_gain,
            regrouped,
            *states,
            low_rank,
            reach,
        )
    )


def solution(mesh):
    placed = (
        P("seq", "mp"),
        P("seq", "mp"),
        P(None, "mp"),
        P("mp"),
        P("mp", None),
        P(None, "mp"),
        P("mp"),
        P(None, "mp"),
        P("mp"),
        P("seq", "mp"),
        P("seq", "mp"),
        P("seq", "mp"),
        P(),
        P(),
    )
    return jax.shard_map(
        local,
        mesh=mesh,
        in_specs=placed,
        out_specs=(P("seq", "mp"), P("seq", "mp")),
        check_vma=False,
    )
```

```python
import functools

import jax
import jax.numpy as jnp
from jax import lax
from jax.experimental import pallas as pl
from jax.experimental.pallas import tpu as pltpu
from jax.sharding import PartitionSpec as P

HD = 128
LANES = 128
HALO = 16
LOG2E = 1.4426950408889634
RESET = 1e30
APART = 65536.0
VMEM_LIMIT = 32 * 1024 * 1024
VMEM_MOST = 56 * 1024 * 1024
VMEM_NEARLY = 52 * 1024 * 1024 + 512 * 1024
VMEM_SOME = 50 * 1024 * 1024


def doc_edges(lengths_ref):
    starts, ends, total = [], [], 0
    for i in range(lengths_ref.shape[0]):
        starts.append(total)
        total = total + lengths_ref[i]
        ends.append(total)
    return starts, ends


def doc_start(places, starts):
    found = jnp.zeros_like(places)
    for start in starts[1:]:
        found = jnp.where(places >= start, start, found)
    return found


def in_hbm(value):
    return pltpu.with_memory_space_constraint(value, pltpu.HBM)


def channel_chunk(channels):
    return 1024 if channels % 1024 == 0 else channels


def pack_kernel(x_ref, k_ref, v_ref, halo_ref, kv_ref):
    width = k_ref.shape[1]
    halo_ref[...] = x_ref[...]
    kv_ref[:, :width] = k_ref[...]
    kv_ref[:, width:] = v_ref[...]


def pack(x_branch, key_rows, value_rows):
    tok, channels = x_branch.shape
    width = key_rows.shape[1]
    whole = lambda rows, columns: pl.BlockSpec((rows, columns), lambda i: (0, 0))
    return pl.pallas_call(
        pack_kernel,
        grid=(1,),
        in_specs=[
            pl.BlockSpec((HALO, channels), lambda i: (tok // HALO - 1, 0)),
            whole(tok, width),
            whole(tok, width),
        ],
        out_specs=[whole(HALO, channels), whole(tok, 2 * width)],
        out_shape=[
            jax.ShapeDtypeStruct((HALO, channels), x_branch.dtype),
            jax.ShapeDtypeStruct((tok, 2 * width), key_rows.dtype),
        ],
        compiler_params=pltpu.CompilerParams(vmem_limit_bytes=VMEM_MOST),
        cost_estimate=pl.CostEstimate(flops=0, bytes_accessed=16 * tok * width, transcendentals=0),
        name="pack",
    )(x_branch, key_rows, value_rows)


def conv_kernel(
    lengths_ref, x_ref, halo_ref, w_hbm, b_hbm, xp_ref, inner_ref, part_ref, ext, acc, w_ref, b_ref, fetched
):
    tok, chunk = x_ref.shape
    starts, _ = doc_edges(lengths_ref)
    anchor = lax.axis_index("seq") * tok
    places = anchor + lax.broadcasted_iota(jnp.int32, (tok, LANES), 0)
    depth = places - doc_start(places, starts)
    at = pl.program_id(0)
    fetches = [
        pltpu.make_async_copy(w_hbm, w_ref, fetched.at[0]),
        pltpu.make_async_copy(b_hbm, b_ref, fetched.at[1]),
    ]

    @pl.when(at == 0)
    def _():
        for fetch in fetches:
            fetch.start()

    ext[0:HALO, :] = halo_ref[...].astype(jnp.float32)
    ext[HALO:, :] = x_ref[...].astype(jnp.float32)

    @pl.when(at == 0)
    def _():
        for fetch in fetches:
            fetch.wait()

    for lane in range(0, chunk, LANES):
        cols = slice(lane, lane + LANES)
        here = pl.ds(pl.multiple_of(at * chunk + lane, LANES), LANES)
        total = b_ref[:, here] + w_ref[0:1, here] * ext[HALO:, cols]
        for lag in range(1, w_ref.shape[0]):
            window = ext[HALO - lag : HALO - lag + tok, cols]
            total += w_ref[lag : lag + 1, here] * jnp.where(depth >= lag, window, 0.0)
        act = total * (0.5 + 0.5 * jnp.tanh(0.5 * total))
        inner_ref[:, cols] = act.astype(jnp.bfloat16)
    product = lax.dot_general(
        xp_ref[...], inner_ref[...], (((1,), (1,)), ((), ())), preferred_element_type=jnp.float32
    )

    @pl.when(at == 0)
    def _():
        acc[...] = product

    @pl.when(at > 0)
    def _():
        acc[...] += product

    @pl.when(at == pl.num_programs(0) - 1)
    def _():
        part_ref[...] = acc[...].astype(jnp.bfloat16)


def conv_project(lengths, x_branch, halo, conv_weight, conv_bias, xproj_weight):
    tok, channels = x_branch.shape
    width = xproj_weight.shape[1]
    taps = conv_weight.shape[0]
    chunk = channel_chunk(channels)
    return pl.pallas_call(
        conv_kernel,
        grid=(channels // chunk,),
        in_specs=[
            pl.BlockSpec(memory_space=pltpu.SMEM),
            pl.BlockSpec((tok, chunk), lambda i: (0, i)),
            pl.BlockSpec((HALO, chunk), lambda i: (0, i)),
            pl.BlockSpec(memory_space=pltpu.HBM),
            pl.BlockSpec(memory_space=pltpu.HBM),
            pl.BlockSpec((width, chunk), lambda i: (0, i)),
        ],
        out_specs=[
            pl.BlockSpec((tok, chunk), lambda i: (0, i)),
            pl.BlockSpec((width, tok), lambda i: (0, 0)),
        ],
        out_shape=[
            jax.ShapeDtypeStruct((tok, channels), jnp.bfloat16),
            jax.ShapeDtypeStruct((width, tok), jnp.bfloat16),
        ],
        scratch_shapes=[
            pltpu.VMEM((tok + HALO, chunk), jnp.float32),
            pltpu.VMEM((width, tok), jnp.float32),
            pltpu.VMEM((taps, channels), jnp.float32),
            pltpu.VMEM((1, channels), jnp.float32),
            pltpu.SemaphoreType.DMA((2,)),
        ],
        compiler_params=pltpu.CompilerParams(vmem_limit_bytes=VMEM_NEARLY),
        cost_estimate=pl.CostEstimate(
            flops=80 * tok * channels * width, bytes_accessed=8 * tok * channels, transcendentals=tok * channels
        ),
        name="conv_project",
    )(
        lengths,
        in_hbm(x_branch),
        halo,
        in_hbm(conv_weight),
        in_hbm(conv_bias.reshape(1, channels)),
        in_hbm(xproj_weight.T),
    )


ROWS = 8
PAIR = 2 * ROWS
BLOCK = 64


def spread(columns):
    tok, k = columns.shape
    own = lax.broadcasted_iota(jnp.int32, (k, k), 0) == lax.broadcasted_iota(jnp.int32, (k, k), 1)
    picked = jnp.where(own[None], columns.astype(jnp.float32)[:, None, :], 0.0).reshape(tok * k, k)
    ones = jnp.ones((k, LANES), jnp.bfloat16)
    return jnp.dot(picked.astype(jnp.bfloat16), ones, preferred_element_type=jnp.float32).reshape(tok, k, LANES)


def lane(tile):
    return slice(tile * LANES, (tile + 1) * LANES)


def sublanes(tile):
    return slice(tile * ROWS, (tile + 1) * ROWS)


def added(one_ref, other_ref, rows):
    total = one_ref[rows, :].astype(jnp.float32) + other_ref[rows, :].astype(jnp.float32)
    return total.astype(jnp.bfloat16).astype(jnp.float32)


def by_register(rate_ref, rates):
    states = rate_ref.shape[0]
    count = rates.shape[0] // states
    for n in range(states):
        for h in range(count):
            tiles = [rate_ref[n : n + 1, lane(h * ROWS + j)] for j in range(ROWS)]
            rates[n * count + h] = jnp.concatenate(tiles, axis=0) * (-LOG2E)


def local_kernel(
    lengths_ref,
    proj_ref,
    other_ref,
    dtw_ref,
    bias_ref,
    rate_ref,
    inner_ref,
    y_ref,
    sum_ref,
    state_ref,
    low_cols,
    bc_spread,
    raw,
    rates,
    step_tiles,
    drive_tiles,
    carry,
):
    tok = proj_ref.shape[1]
    block, channels = inner_ref.shape
    states = rate_ref.shape[0]
    low_rank = dtw_ref.shape[0]
    tiles = channels // LANES
    count = tiles // ROWS
    starts, _ = doc_edges(lengths_ref)
    at = pl.program_id(0)

    @pl.when(at == 0)
    def _():
        low_cols[...] = added(proj_ref, other_ref, slice(0, low_rank)).T.astype(jnp.bfloat16)
        bc_spread[...] = spread(added(proj_ref, other_ref, slice(low_rank, None)).T)
        by_register(rate_ref, rates)
        carry[...] = jnp.zeros_like(carry)
        for first in range(0, tiles, 4):
            cols = slice(first * LANES, (first + 4) * LANES)
            part = jnp.dot(low_cols[...], dtw_ref[:, cols], preferred_element_type=jnp.float32)
            for i in range(4):
                raw[:, sublanes(first + i), :] = part[:, lane(i)].reshape(tok // ROWS, ROWS, LANES)

    def steps(pair, unused):
        rows = pl.ds(pl.multiple_of(pair * PAIR, PAIR), PAIR)
        places = lax.axis_index("seq") * tok + at * block + pair * PAIR
        places = places + lax.broadcasted_iota(jnp.int32, (PAIR, LANES), 0)
        at_start = places == doc_start(places, starts)
        for tile in range(tiles):
            inner = inner_ref[rows, lane(tile)].astype(jnp.float32)
            bias = bias_ref[:, lane(tile)]
            for k in range(2):
                biased = raw[at * (block // ROWS) + 2 * pair + k, sublanes(tile), :] + bias
                step = jnp.maximum(biased, 0.0) + jnp.log(1.0 + jnp.exp(-jnp.abs(biased)))
                drive_tiles[2 * pair + k, sublanes(tile), :] = step * inner[sublanes(k)]
                step_tiles[2 * pair + k, sublanes(tile), :] = jnp.where(at_start[sublanes(k)], RESET, step)
        return unused

    lax.fori_loop(0, block // PAIR, steps, 0)

    def scan(t8, held):
        held, total = list(held[0]), list(held[1])
        for first in range(0, ROWS, 2):
            tokens = range(first, first + 2)
            picked = [[pl.ds(r + h * ROWS * ROWS, ROWS, stride=ROWS) for h in range(count)] for r in tokens]
            step = [[step_tiles[t8, rows, :] for rows in of_token] for of_token in picked]
            drive = [[drive_tiles[t8, rows, :] for rows in of_token] for of_token in picked]
            out = [[None] * count for _ in tokens]
            for n in range(states):
                where = [at * block + t8 * ROWS + r for r in tokens]
                b_row = [bc_spread[token, n : n + 1, :] for token in where]
                c_row = [bc_spread[token, states + n : states + n + 1, :] for token in where]
                for h in range(count):
                    i = n * count + h
                    rate = rates[i]
                    decay = [jnp.exp2(rate * step[k][h]) for k in range(2)]
                    for k in range(2):
                        held[i] = decay[k] * held[i] + b_row[k] * drive[k][h]
                        term = c_row[k] * held[i]
                        out[k][h] = term if out[k][h] is None else out[k][h] + term
            for k, r in enumerate(tokens):
                for h in range(count):
                    total[h] = total[h] + step[k][h]
                    y_ref[t8 * ROWS + r, sublanes(h), :] = out[k][h]
                    sum_ref[t8 * ROWS + r, sublanes(h), :] = total[h]
        return held, total

    kept = states * count
    held = ([carry[i] for i in range(kept)], [carry[kept + h] for h in range(count)])
    held, total = lax.fori_loop(0, block // ROWS, scan, held)
    for i, value in enumerate(held + total):
        carry[i] = value

    @pl.when(at == pl.num_programs(0) - 1)
    def _():
        state_ref[: states * tiles, :] = jnp.concatenate(held, axis=0).astype(jnp.bfloat16)
        whole = jnp.concatenate(total, axis=0)
        high = whole.astype(jnp.bfloat16).astype(jnp.float32)
        state_ref[states * tiles :, :] = jnp.concatenate([high, whole - high], axis=0).astype(jnp.bfloat16)


def local_scan(lengths, projected, other, dt_weight, dt_bias, decay_rate, inner_act):
    tok, channels = inner_act.shape
    low_rank = dt_weight.shape[0]
    states = decay_rate.shape[0]
    tiles = channels // LANES
    count = tiles // ROWS
    whole = lambda a: pl.BlockSpec(a.shape, lambda i: (0,) * a.ndim)
    bias = dt_bias.reshape(1, channels)
    by_token = pl.BlockSpec((BLOCK, tiles, LANES), lambda i: (i, 0, 0))
    state_rows = (states + 2) * tiles
    return pl.pallas_call(
        local_kernel,
        grid=(tok // BLOCK,),
        in_specs=[
            pl.BlockSpec(memory_space=pltpu.SMEM),
            whole(projected),
            whole(other),
            whole(dt_weight),
            whole(bias),
            whole(decay_rate),
            pl.BlockSpec((BLOCK, channels), lambda i: (i, 0)),
        ],
        out_specs=[by_token, by_token, pl.BlockSpec((state_rows, LANES), lambda i: (0, 0))],
        out_shape=[
            jax.ShapeDtypeStruct((tok, tiles, LANES), jnp.float32),
            jax.ShapeDtypeStruct((tok, tiles, LANES), jnp.float32),
            jax.ShapeDtypeStruct((state_rows, LANES), jnp.bfloat16),
        ],
        scratch_shapes=[
            pltpu.VMEM((tok, low_rank), jnp.bfloat16),
            pltpu.VMEM((tok, 2 * states, LANES), jnp.float32),
            pltpu.VMEM((tok // ROWS, tiles * ROWS, LANES), jnp.float32),
            pltpu.VMEM((states * count, ROWS, LANES), jnp.float32),
            pltpu.VMEM((BLOCK // ROWS, tiles * ROWS, LANES), jnp.float32),
            pltpu.VMEM((BLOCK // ROWS, tiles * ROWS, LANES), jnp.float32),
            pltpu.VMEM(((states + 1) * count, ROWS, LANES), jnp.float32),
        ],
        compiler_params=pltpu.CompilerParams(vmem_limit_bytes=VMEM_NEARLY),
        cost_estimate=pl.CostEstimate(
            flops=12 * tok * channels * states,
            bytes_accessed=12 * tok * channels,
            transcendentals=tok * channels * states,
        ),
        name="local_scan",
    )(
        lengths, projected, other, in_hbm(dt_weight), in_hbm(bias), in_hbm(decay_rate), in_hbm(inner_act)
    )


def join_kernel(
    reach,
    proj_ref,
    other_ref,
    y_ref,
    sum_ref,
    inner_ref,
    z_ref,
    rate_ref,
    skip_ref,
    moved_ref,
    mine_ref,
    theirs_ref,
    out_ref,
    regrouped_ref,
    c_spread,
    rates,
    entering,
    rows_tiles,
):
    block, channels = z_ref.shape
    states = rate_ref.shape[0]
    tiles = channels // LANES
    count = tiles // ROWS
    kept = states * count
    at = pl.program_id(0)

    @pl.when(at == 0)
    def _():
        c_spread[...] = spread(added(proj_ref, other_ref, slice(None)).T)
        by_register(rate_ref, rates)
        odd = lax.rem(lax.axis_index("seq"), 2)
        state = [jnp.zeros((ROWS, LANES), jnp.float32)] * kept
        for back in range(reach, 0, -1):
            ref, which = (mine_ref, back // 2) if back % 2 == 0 else (theirs_ref, (back + 1) // 2 - odd)
            sent = ref[which].astype(jnp.float32)
            totals = sent[states * tiles : (states + 1) * tiles] + sent[(states + 1) * tiles :]
            state = [
                jnp.exp2(rates[i] * totals[sublanes(i % count)]) * state[i] + sent[sublanes(i)] for i in range(kept)
            ]
        for i in range(kept):
            entering[i] = state[i]

    regrouped_ref[...] = moved_ref[...]

    def body(pair, unused):
        rows = pl.ds(pl.multiple_of(pair * PAIR, PAIR), PAIR)
        for k in range(2):
            first = pair * PAIR + k * ROWS
            total = [[sum_ref[first + r, sublanes(h), :] for h in range(count)] for r in range(ROWS)]
            out = [[y_ref[first + r, sublanes(h), :] for h in range(count)] for r in range(ROWS)]
            for n in range(states):
                c_row = [c_spread[at * block + first + r, n : n + 1, :] for r in range(ROWS)]
                for h in range(count):
                    rate, state = rates[n * count + h], entering[n * count + h]
                    for r in range(ROWS):
                        out[r][h] += jnp.exp2(rate * total[r][h]) * state * c_row[r]
            for r in range(ROWS):
                for h in range(count):
                    rows_tiles[k, pl.ds(r + h * ROWS * ROWS, ROWS, stride=ROWS), :] = out[r][h]
        for tile in range(tiles):
            cols = lane(tile)
            z = z_ref[rows, cols].astype(jnp.float32)
            gate = z * (0.5 + 0.5 * jnp.tanh(0.5 * z))
            scanned = jnp.concatenate([rows_tiles[k, sublanes(tile), :] for k in range(2)], axis=0)
            scanned = scanned + skip_ref[:, cols] * inner_ref[rows, cols].astype(jnp.float32)
            out_ref[rows, cols] = (scanned * gate).astype(jnp.bfloat16)
        return unused

    lax.fori_loop(0, block // PAIR, body, 0)


def join_states(projected, other, y, sums, inner_act, z_branch, decay_rate, skip_gain, moved, mine, theirs, low_rank, reach):
    tok, channels = z_branch.shape
    states = decay_rate.shape[0]
    tiles = channels // LANES
    count = tiles // ROWS
    whole = lambda a: pl.BlockSpec(a.shape, lambda i: (0,) * a.ndim)
    by_token = pl.BlockSpec((BLOCK, tiles, LANES), lambda i: (i, 0, 0))
    by_row = pl.BlockSpec((BLOCK, channels), lambda i: (i, 0))
    skip = skip_gain.reshape(1, channels)
    c_part = pl.BlockSpec((states, tok), lambda i: (low_rank // states + 1, 0))
    return pl.pallas_call(
        functools.partial(join_kernel, reach),
        grid=(tok // BLOCK,),
        in_specs=[
            c_part,
            c_part,
            by_token,
            by_token,
            by_row,
            by_row,
            whole(decay_rate),
            whole(skip),
            by_row,
            whole(mine),
            whole(theirs),
        ],
        out_specs=[by_row, by_row],
        out_shape=[jax.ShapeDtypeStruct((tok, channels), jnp.bfloat16)] * 2,
        scratch_shapes=[
            pltpu.VMEM((tok, states, LANES), jnp.float32),
            pltpu.VMEM((states * count, ROWS, LANES), jnp.float32),
            pltpu.VMEM((states * count, ROWS, LANES), jnp.float32),
            pltpu.VMEM((2, tiles * ROWS, LANES), jnp.float32),
        ],
        compiler_params=pltpu.CompilerParams(vmem_limit_bytes=VMEM_SOME),
        cost_estimate=pl.CostEstimate(
            flops=8 * tok * channels * states,
            bytes_accessed=14 * tok * channels,
            transcendentals=tok * channels * states,
        ),
        name="join_states",
    )(
        projected,
        other,
        in_hbm(y),
        in_hbm(sums),
        in_hbm(inner_act),
        in_hbm(z_branch),
        in_hbm(decay_rate),
        in_hbm(skip),
        moved,
        mine,
        theirs,
    )


def attend_kernel(
    lengths_ref,
    place_ref,
    q_ref,
    keys_mine,
    keys_theirs,
    values_mine,
    values_theirs,
    out_ref,
    queries,
    scores,
    tops,
    acc,
):
    tok = q_ref.shape[0]
    heads = q_ref.shape[1] // HD
    position = lax.axis_index("seq")
    odd = lax.rem(position, 2)
    anchor = position * tok
    scale = jnp.bfloat16(LOG2E * HD**-0.5)
    starts, ends = doc_edges(lengths_ref)
    edges = list(zip(starts, ends)) + [(jnp.int32(-(2**30)), jnp.int32(0))]
    lane = lax.broadcasted_iota(jnp.int32, (1, LANES), 1)
    first = jnp.full((1, LANES), 2**30, jnp.int32)
    last = jnp.zeros((1, LANES), jnp.int32)
    for i, (start, end) in enumerate(edges):
        first = jnp.where(lane == i, start, first)
        last = jnp.where(lane == i, end, last)
    rows = lax.broadcasted_iota(jnp.int32, (tok, LANES), 0)

    def in_doc(base):
        return (rows + base >= first) & (rows + base < last)

    apart = jnp.where(in_doc(anchor) | (lane >= len(edges)), 0.0, -APART).astype(jnp.bfloat16)
    for head in range(heads):
        queries[head * tok : (head + 1) * tok, :HD] = q_ref[:, head * HD : (head + 1) * HD]
        queries[head * tok : (head + 1) * tok, HD:] = apart

    def rows_of(mine_ref, theirs_ref, back):
        if isinstance(back, int) and back == 0:
            return mine_ref[0]
        return jnp.where(lax.rem(back, 2) == 0, mine_ref[back // 2], theirs_ref[(back + 1) // 2 - odd])

    def score(back):
        marks = jnp.where(in_doc(anchor - back * tok), 1.0, 0.0).astype(jnp.bfloat16)
        keys = jnp.concatenate([rows_of(keys_mine, keys_theirs, back), marks], axis=1)
        return lax.dot_general(queries[...], keys, (((1,), (1,)), ((), ())), preferred_element_type=jnp.float32)

    causal = lax.broadcasted_iota(jnp.int32, (tok, tok), 1) <= lax.broadcasted_iota(jnp.int32, (tok, tok), 0)

    def highest(backs):
        top = None
        for back in backs:
            s = score(back)
            if isinstance(back, int) and back == 0:
                s = jnp.concatenate(
                    [jnp.where(causal, s[h * tok : (h + 1) * tok], -APART) for h in range(heads)], axis=0
                )
            scores[back] = s
            for at in range(0, tok, LANES):
                piece = s[:, at : at + LANES]
                top = piece if top is None else jnp.maximum(top, piece)
        return top

    begin = jnp.int32(0)
    for start in starts[1:]:
        begin = jnp.where(anchor >= start, start, begin)
    pairs = ((anchor - begin + tok - 1) // tok + 1) // 2

    def start_with(alone, together):
        pl.when(pairs == 0)(alone)
        pl.when(pairs > 0)(together)

    def set_tops(backs):
        tops[...] = highest(backs)

    start_with(lambda: set_tops([0]), lambda: set_tops([0, 1, 2]))

    def look(pair, carry):
        tops[...] = jnp.maximum(tops[...], highest([2 * pair - 1, 2 * pair]))
        return carry

    lax.fori_loop(2, pairs + 1, look, 0)
    tops[...] = jnp.broadcast_to(jnp.max(tops[...], axis=1, keepdims=True), tops.shape)

    def weighted(backs):
        values = jnp.concatenate([rows_of(values_mine, values_theirs, back) for back in backs], axis=0)
        values = jnp.concatenate([values, jnp.ones(values.shape, jnp.bfloat16)], axis=1)
        top = tops[...]
        weights = [
            jnp.exp2((scores[back, :, at : at + LANES] - top).astype(jnp.bfloat16) * scale)
            for back in backs
            for at in range(0, tok, LANES)
        ]
        return jnp.dot(jnp.concatenate(weights, axis=1), values, preferred_element_type=jnp.float32)

    def set_acc(backs):
        acc[...] = weighted(backs)

    start_with(lambda: set_acc([0]), lambda: set_acc([0, 1, 2]))

    def absorb(pair, carry):
        acc[...] += weighted([2 * pair - 1, 2 * pair])
        return carry

    lax.fori_loop(2, pairs + 1, absorb, 0)
    order = place_ref[pl.ds(position, 1), :]
    move = (lax.broadcasted_iota(jnp.int32, (tok, tok), 0) == order).astype(jnp.float32).astype(jnp.bfloat16)
    for head in range(heads):
        part = slice(head * tok, (head + 1) * tok)
        result = (acc[part, :HD] / acc[part, HD:]).astype(jnp.bfloat16)
        moved = jnp.dot(move, result, preferred_element_type=jnp.float32)
        out_ref[:, head * HD : (head + 1) * HD] = moved.astype(jnp.bfloat16)


def attend(lengths, send_place, query_rows, mine, theirs):
    tok, width = query_rows.shape
    kv_local = mine.shape[2] // (2 * HD)
    share = width // kv_local
    heads = share // HD
    reach = 2 * (mine.shape[0] - 1)
    by_group = pl.BlockSpec((tok, share), lambda i: (0, i))
    keys = pl.BlockSpec(mine.shape[:2] + (HD,), lambda i: (0, 0, i))
    values = pl.BlockSpec(mine.shape[:2] + (HD,), lambda i: (0, 0, i + kv_local))
    return pl.pallas_call(
        attend_kernel,
        grid=(kv_local,),
        in_specs=[
            pl.BlockSpec(memory_space=pltpu.SMEM),
            pl.BlockSpec(send_place.shape, lambda i: (0, 0)),
            by_group,
            keys,
            keys,
            values,
            values,
        ],
        out_specs=by_group,
        out_shape=jax.ShapeDtypeStruct((tok, width), jnp.bfloat16),
        scratch_shapes=[
            pltpu.VMEM((heads * tok, 2 * HD), jnp.bfloat16),
            pltpu.VMEM((reach + 1, heads * tok, tok), jnp.float32),
            pltpu.VMEM((heads * tok, LANES), jnp.float32),
            pltpu.VMEM((heads * tok, 2 * HD), jnp.float32),
        ],
        compiler_params=pltpu.CompilerParams(vmem_limit_bytes=VMEM_LIMIT // 2 + 4 * (reach + 1) * heads * tok * tok),
        cost_estimate=pl.CostEstimate(flops=tok * width, bytes_accessed=tok * width, transcendentals=0),
        name="attend",
    )(lengths, send_place, query_rows, mine, theirs, mine, theirs)


def shifted(value, steps):
    count = lax.axis_size("seq")
    return lax.ppermute(value, "seq", [(source, source + steps) for source in range(count - steps)])


def with_partner(held):
    mine = jnp.stack(held)
    count = lax.axis_size("seq")
    return mine, lax.ppermute(mine, "seq", [(source, source ^ 1) for source in range(count)])


def even_back(value, reach):
    return [value] + [shifted(value, 2 * k) for k in range(1, (reach + 1) // 2 + 1)]


def local(
    x_branch,
    z_branch,
    conv_weight,
    conv_bias,
    xproj_weight,
    dt_weight,
    dt_bias,
    decay_rate,
    skip_gain,
    query_rows,
    key_rows,
    value_rows,
    lengths,
    destination,
):
    tok = x_branch.shape[0]
    n_seq = lax.axis_size("seq")
    n_mp = lax.axis_size("mp")
    low_rank = dt_weight.shape[0]
    reach = n_seq // 2
    run_rows = tok // n_seq
    fence = lax.optimization_barrier

    lengths = in_hbm(lengths)
    halo, kv = pack(x_branch, key_rows, value_rows)
    earlier_rows = shifted(halo, 1)
    held = even_back(kv, reach)
    send_place = ((destination // tok) * run_rows + destination % run_rows).reshape(n_seq, tok)

    inner_act, partial = conv_project(lengths, x_branch, earlier_rows, conv_weight, conv_bias, xproj_weight)
    _, *held = fence((partial, *held))
    mine, theirs = with_partner(held)
    total, other = partial, jnp.zeros_like(partial)
    steps = [1 << k for k in range((n_mp - 1).bit_length())]
    for step in steps:
        if step > 1:
            total = (total.astype(jnp.float32) + other.astype(jnp.float32)).astype(jnp.bfloat16)
        if step == steps[-1]:
            total, send_place = fence((total, send_place))
        other = lax.ppermute(total, "mp", [(source, source ^ step) for source in range(n_mp)])
    attended = attend(lengths, send_place, query_rows, mine, theirs)
    total, other, attended = fence((total, other, attended))
    regrouped = lax.all_to_all(attended, "seq", split_axis=0, concat_axis=0, tiled=True)

    y, sums, state = local_scan(lengths, total, other, dt_weight, dt_bias, decay_rate, inner_act)
    states = with_partner(even_back(state, reach))
    return tuple(
        join_states(
            total,
            other,
            y,
            sums,
            inner_act,
            z_branch,
            decay_rate,
            skip_gain,
            regrouped,
            *states,
            low_rank,
            reach,
        )
    )


def solution(mesh):
    placed = (
        P("seq", "mp"),
        P("seq", "mp"),
        P(None, "mp"),
        P("mp"),
        P("mp", None),
        P(None, "mp"),
        P("mp"),
        P(None, "mp"),
        P("mp"),
        P("seq", "mp"),
        P("seq", "mp"),
        P("seq", "mp"),
        P(),
        P(),
    )
    return jax.shard_map(
        local,
        mesh=mesh,
        in_specs=placed,
        out_specs=(P("seq", "mp"), P("seq", "mp")),
        check_vma=False,
    )
```

```python
import functools

import jax
import jax.numpy as jnp
from jax import lax
from jax.experimental import pallas as pl
from jax.experimental.pallas import tpu as pltpu
from jax.sharding import PartitionSpec as P

HD = 128
LANES = 128
HALO = 16
LOG2E = 1.4426950408889634
RESET = 1e30
APART = 65536.0
VMEM_LIMIT = 32 * 1024 * 1024
VMEM_MOST = 56 * 1024 * 1024
VMEM_NEARLY = 52 * 1024 * 1024 + 512 * 1024
VMEM_SOME = 50 * 1024 * 1024


def doc_edges(lengths_ref):
    starts, ends, total = [], [], 0
    for i in range(lengths_ref.shape[0]):
        starts.append(total)
        total = total + lengths_ref[i]
        ends.append(total)
    return starts, ends


def doc_start(places, starts):
    found = jnp.zeros_like(places)
    for start in starts[1:]:
        found = jnp.where(places >= start, start, found)
    return found


def in_hbm(value):
    return pltpu.with_memory_space_constraint(value, pltpu.HBM)


def channel_chunk(channels):
    return 1024 if channels % 1024 == 0 else channels


def pack_kernel(x_ref, k_ref, v_ref, halo_ref, kv_ref):
    width = k_ref.shape[1]
    halo_ref[...] = x_ref[...]
    kv_ref[:, :width] = k_ref[...]
    kv_ref[:, width:] = v_ref[...]


def pack(x_branch, key_rows, value_rows):
    tok, channels = x_branch.shape
    width = key_rows.shape[1]
    whole = lambda rows, columns: pl.BlockSpec((rows, columns), lambda i: (0, 0))
    return pl.pallas_call(
        pack_kernel,
        grid=(1,),
        in_specs=[
            pl.BlockSpec((HALO, channels), lambda i: (tok // HALO - 1, 0)),
            whole(tok, width),
            whole(tok, width),
        ],
        out_specs=[whole(HALO, channels), whole(tok, 2 * width)],
        out_shape=[
            jax.ShapeDtypeStruct((HALO, channels), x_branch.dtype),
            jax.ShapeDtypeStruct((tok, 2 * width), key_rows.dtype),
        ],
        compiler_params=pltpu.CompilerParams(vmem_limit_bytes=VMEM_LIMIT),
        cost_estimate=pl.CostEstimate(flops=0, bytes_accessed=16 * tok * width, transcendentals=0),
        name="pack",
    )(in_hbm(x_branch), in_hbm(key_rows), in_hbm(value_rows))


def conv_kernel(
    lengths_ref, x_ref, halo_ref, w_hbm, b_hbm, xp_ref, inner_ref, part_ref, ext, acc, w_ref, b_ref, fetched
):
    tok, chunk = x_ref.shape
    starts, _ = doc_edges(lengths_ref)
    anchor = lax.axis_index("seq") * tok
    places = anchor + lax.broadcasted_iota(jnp.int32, (tok, LANES), 0)
    depth = places - doc_start(places, starts)
    at = pl.program_id(0)
    fetches = [
        pltpu.make_async_copy(w_hbm, w_ref, fetched.at[0]),
        pltpu.make_async_copy(b_hbm, b_ref, fetched.at[1]),
    ]

    @pl.when(at == 0)
    def _():
        for fetch in fetches:
            fetch.start()

    ext[0:HALO, :] = halo_ref[...].astype(jnp.float32)
    ext[HALO:, :] = x_ref[...].astype(jnp.float32)

    @pl.when(at == 0)
    def _():
        for fetch in fetches:
            fetch.wait()

    for lane in range(0, chunk, LANES):
        cols = slice(lane, lane + LANES)
        here = pl.ds(pl.multiple_of(at * chunk + lane, LANES), LANES)
        total = b_ref[:, here] + w_ref[0:1, here] * ext[HALO:, cols]
        for lag in range(1, w_ref.shape[0]):
            window = ext[HALO - lag : HALO - lag + tok, cols]
            total += w_ref[lag : lag + 1, here] * jnp.where(depth >= lag, window, 0.0)
        act = total * (0.5 + 0.5 * jnp.tanh(0.5 * total))
        inner_ref[:, cols] = act.astype(jnp.bfloat16)
    product = lax.dot_general(
        xp_ref[...], inner_ref[...], (((1,), (1,)), ((), ())), preferred_element_type=jnp.float32
    )

    @pl.when(at == 0)
    def _():
        acc[...] = product

    @pl.when(at > 0)
    def _():
        acc[...] += product

    @pl.when(at == pl.num_programs(0) - 1)
    def _():
        part_ref[...] = acc[...].astype(jnp.bfloat16)


def conv_project(lengths, x_branch, halo, conv_weight, conv_bias, xproj_weight):
    tok, channels = x_branch.shape
    width = xproj_weight.shape[1]
    taps = conv_weight.shape[0]
    chunk = channel_chunk(channels)
    return pl.pallas_call(
        conv_kernel,
        grid=(channels // chunk,),
        in_specs=[
            pl.BlockSpec(memory_space=pltpu.SMEM),
            pl.BlockSpec((tok, chunk), lambda i: (0, i)),
            pl.BlockSpec((HALO, chunk), lambda i: (0, i)),
            pl.BlockSpec(memory_space=pltpu.HBM),
            pl.BlockSpec(memory_space=pltpu.HBM),
            pl.BlockSpec((width, chunk), lambda i: (0, i)),
        ],
        out_specs=[
            pl.BlockSpec((tok, chunk), lambda i: (0, i)),
            pl.BlockSpec((width, tok), lambda i: (0, 0)),
        ],
        out_shape=[
            jax.ShapeDtypeStruct((tok, channels), jnp.bfloat16),
            jax.ShapeDtypeStruct((width, tok), jnp.bfloat16),
        ],
        scratch_shapes=[
            pltpu.VMEM((tok + HALO, chunk), jnp.float32),
            pltpu.VMEM((width, tok), jnp.float32),
            pltpu.VMEM((taps, channels), jnp.float32),
            pltpu.VMEM((1, channels), jnp.float32),
            pltpu.SemaphoreType.DMA((2,)),
        ],
        compiler_params=pltpu.CompilerParams(vmem_limit_bytes=VMEM_NEARLY),
        cost_estimate=pl.CostEstimate(
            flops=80 * tok * channels * width, bytes_accessed=8 * tok * channels, transcendentals=tok * channels
        ),
        name="conv_project",
    )(
        lengths,
        in_hbm(x_branch),
        halo,
        in_hbm(conv_weight),
        in_hbm(conv_bias.reshape(1, channels)),
        in_hbm(xproj_weight.T),
    )


ROWS = 8
PAIR = 2 * ROWS
BLOCK = 64


def spread(columns):
    tok, k = columns.shape
    own = lax.broadcasted_iota(jnp.int32, (k, k), 0) == lax.broadcasted_iota(jnp.int32, (k, k), 1)
    picked = jnp.where(own[None], columns.astype(jnp.float32)[:, None, :], 0.0).reshape(tok * k, k)
    ones = jnp.ones((k, LANES), jnp.bfloat16)
    return jnp.dot(picked.astype(jnp.bfloat16), ones, preferred_element_type=jnp.float32).reshape(tok, k, LANES)


def lane(tile):
    return slice(tile * LANES, (tile + 1) * LANES)


def sublanes(tile):
    return slice(tile * ROWS, (tile + 1) * ROWS)


def added(one_ref, other_ref, rows):
    total = one_ref[rows, :].astype(jnp.float32) + other_ref[rows, :].astype(jnp.float32)
    return total.astype(jnp.bfloat16).astype(jnp.float32)


def by_register(rate_ref, rates):
    states = rate_ref.shape[0]
    count = rates.shape[0] // states
    for n in range(states):
        for h in range(count):
            tiles = [rate_ref[n : n + 1, lane(h * ROWS + j)] for j in range(ROWS)]
            rates[n * count + h] = jnp.concatenate(tiles, axis=0) * (-LOG2E)


def local_kernel(
    lengths_ref,
    proj_ref,
    other_ref,
    dtw_ref,
    bias_ref,
    rate_ref,
    inner_ref,
    y_ref,
    sum_ref,
    state_ref,
    low_cols,
    bc_spread,
    raw,
    rates,
    step_tiles,
    drive_tiles,
    carry,
):
    tok = proj_ref.shape[1]
    block, channels = inner_ref.shape
    states = rate_ref.shape[0]
    low_rank = dtw_ref.shape[0]
    tiles = channels // LANES
    count = tiles // ROWS
    starts, _ = doc_edges(lengths_ref)
    at = pl.program_id(0)

    @pl.when(at == 0)
    def _():
        low_cols[...] = added(proj_ref, other_ref, slice(0, low_rank)).T.astype(jnp.bfloat16)
        bc_spread[...] = spread(added(proj_ref, other_ref, slice(low_rank, None)).T)
        by_register(rate_ref, rates)
        carry[...] = jnp.zeros_like(carry)
        for first in range(0, tiles, 4):
            cols = slice(first * LANES, (first + 4) * LANES)
            part = jnp.dot(low_cols[...], dtw_ref[:, cols], preferred_element_type=jnp.float32)
            for i in range(4):
                raw[:, sublanes(first + i), :] = part[:, lane(i)].reshape(tok // ROWS, ROWS, LANES)

    def steps(pair, unused):
        rows = pl.ds(pl.multiple_of(pair * PAIR, PAIR), PAIR)
        places = lax.axis_index("seq") * tok + at * block + pair * PAIR
        places = places + lax.broadcasted_iota(jnp.int32, (PAIR, LANES), 0)
        at_start = places == doc_start(places, starts)
        for tile in range(tiles):
            inner = inner_ref[rows, lane(tile)].astype(jnp.float32)
            bias = bias_ref[:, lane(tile)]
            for k in range(2):
                biased = raw[at * (block // ROWS) + 2 * pair + k, sublanes(tile), :] + bias
                step = jnp.maximum(biased, 0.0) + jnp.log(1.0 + jnp.exp(-jnp.abs(biased)))
                drive_tiles[2 * pair + k, sublanes(tile), :] = step * inner[sublanes(k)]
                step_tiles[2 * pair + k, sublanes(tile), :] = jnp.where(at_start[sublanes(k)], RESET, step)
        return unused

    lax.fori_loop(0, block // PAIR, steps, 0)

    def scan(t8, held):
        held, total = list(held[0]), list(held[1])
        for first in range(0, ROWS, 2):
            tokens = range(first, first + 2)
            picked = [[pl.ds(r + h * ROWS * ROWS, ROWS, stride=ROWS) for h in range(count)] for r in tokens]
            step = [[step_tiles[t8, rows, :] for rows in of_token] for of_token in picked]
            drive = [[drive_tiles[t8, rows, :] for rows in of_token] for of_token in picked]
            out = [[None] * count for _ in tokens]
            for n in range(states):
                where = [at * block + t8 * ROWS + r for r in tokens]
                b_row = [bc_spread[token, n : n + 1, :] for token in where]
                c_row = [bc_spread[token, states + n : states + n + 1, :] for token in where]
                for h in range(count):
                    i = n * count + h
                    rate = rates[i]
                    decay = [jnp.exp2(rate * step[k][h]) for k in range(2)]
                    for k in range(2):
                        held[i] = decay[k] * held[i] + b_row[k] * drive[k][h]
                        term = c_row[k] * held[i]
                        out[k][h] = term if out[k][h] is None else out[k][h] + term
            for k, r in enumerate(tokens):
                for h in range(count):
                    total[h] = total[h] + step[k][h]
                    y_ref[t8 * ROWS + r, sublanes(h), :] = out[k][h]
                    sum_ref[t8 * ROWS + r, sublanes(h), :] = total[h]
        return held, total

    kept = states * count
    held = ([carry[i] for i in range(kept)], [carry[kept + h] for h in range(count)])
    held, total = lax.fori_loop(0, block // ROWS, scan, held)
    for i, value in enumerate(held + total):
        carry[i] = value

    @pl.when(at == pl.num_programs(0) - 1)
    def _():
        state_ref[: states * tiles, :] = jnp.concatenate(held, axis=0).astype(jnp.bfloat16)
        whole = jnp.concatenate(total, axis=0)
        high = whole.astype(jnp.bfloat16).astype(jnp.float32)
        state_ref[states * tiles :, :] = jnp.concatenate([high, whole - high], axis=0).astype(jnp.bfloat16)


def local_scan(lengths, projected, other, dt_weight, dt_bias, decay_rate, inner_act):
    tok, channels = inner_act.shape
    low_rank = dt_weight.shape[0]
    states = decay_rate.shape[0]
    tiles = channels // LANES
    count = tiles // ROWS
    whole = lambda a: pl.BlockSpec(a.shape, lambda i: (0,) * a.ndim)
    bias = dt_bias.reshape(1, channels)
    by_token = pl.BlockSpec((BLOCK, tiles, LANES), lambda i: (i, 0, 0))
    state_rows = (states + 2) * tiles
    return pl.pallas_call(
        local_kernel,
        grid=(tok // BLOCK,),
        in_specs=[
            pl.BlockSpec(memory_space=pltpu.SMEM),
            whole(projected),
            whole(other),
            whole(dt_weight),
            whole(bias),
            whole(decay_rate),
            pl.BlockSpec((BLOCK, channels), lambda i: (i, 0)),
        ],
        out_specs=[by_token, by_token, pl.BlockSpec((state_rows, LANES), lambda i: (0, 0))],
        out_shape=[
            jax.ShapeDtypeStruct((tok, tiles, LANES), jnp.float32),
            jax.ShapeDtypeStruct((tok, tiles, LANES), jnp.float32),
            jax.ShapeDtypeStruct((state_rows, LANES), jnp.bfloat16),
        ],
        scratch_shapes=[
            pltpu.VMEM((tok, low_rank), jnp.bfloat16),
            pltpu.VMEM((tok, 2 * states, LANES), jnp.float32),
            pltpu.VMEM((tok // ROWS, tiles * ROWS, LANES), jnp.float32),
            pltpu.VMEM((states * count, ROWS, LANES), jnp.float32),
            pltpu.VMEM((BLOCK // ROWS, tiles * ROWS, LANES), jnp.float32),
            pltpu.VMEM((BLOCK // ROWS, tiles * ROWS, LANES), jnp.float32),
            pltpu.VMEM(((states + 1) * count, ROWS, LANES), jnp.float32),
        ],
        compiler_params=pltpu.CompilerParams(vmem_limit_bytes=VMEM_NEARLY),
        cost_estimate=pl.CostEstimate(
            flops=12 * tok * channels * states,
            bytes_accessed=12 * tok * channels,
            transcendentals=tok * channels * states,
        ),
        name="local_scan",
    )(
        lengths, projected, other, in_hbm(dt_weight), in_hbm(bias), in_hbm(decay_rate), in_hbm(inner_act)
    )


def join_kernel(
    reach,
    proj_ref,
    other_ref,
    y_ref,
    sum_ref,
    inner_ref,
    z_ref,
    rate_ref,
    skip_ref,
    moved_ref,
    mine_ref,
    theirs_ref,
    out_ref,
    regrouped_ref,
    c_spread,
    rates,
    entering,
    rows_tiles,
):
    block, channels = z_ref.shape
    states = rate_ref.shape[0]
    tiles = channels // LANES
    count = tiles // ROWS
    kept = states * count
    at = pl.program_id(0)

    @pl.when(at == 0)
    def _():
        c_spread[...] = spread(added(proj_ref, other_ref, slice(None)).T)
        by_register(rate_ref, rates)
        odd = lax.rem(lax.axis_index("seq"), 2)
        state = [jnp.zeros((ROWS, LANES), jnp.float32)] * kept
        for back in range(reach, 0, -1):
            ref, which = (mine_ref, back // 2) if back % 2 == 0 else (theirs_ref, (back + 1) // 2 - odd)
            sent = ref[which].astype(jnp.float32)
            totals = sent[states * tiles : (states + 1) * tiles] + sent[(states + 1) * tiles :]
            state = [
                jnp.exp2(rates[i] * totals[sublanes(i % count)]) * state[i] + sent[sublanes(i)] for i in range(kept)
            ]
        for i in range(kept):
            entering[i] = state[i]

    regrouped_ref[...] = moved_ref[...]

    def body(pair, unused):
        rows = pl.ds(pl.multiple_of(pair * PAIR, PAIR), PAIR)
        for k in range(2):
            first = pair * PAIR + k * ROWS
            total = [[sum_ref[first + r, sublanes(h), :] for h in range(count)] for r in range(ROWS)]
            out = [[y_ref[first + r, sublanes(h), :] for h in range(count)] for r in range(ROWS)]
            for n in range(states):
                c_row = [c_spread[at * block + first + r, n : n + 1, :] for r in range(ROWS)]
                for h in range(count):
                    rate, state = rates[n * count + h], entering[n * count + h]
                    for r in range(ROWS):
                        out[r][h] += jnp.exp2(rate * total[r][h]) * state * c_row[r]
            for r in range(ROWS):
                for h in range(count):
                    rows_tiles[k, pl.ds(r + h * ROWS * ROWS, ROWS, stride=ROWS), :] = out[r][h]
        for tile in range(tiles):
            cols = lane(tile)
            z = z_ref[rows, cols].astype(jnp.float32)
            gate = z * (0.5 + 0.5 * jnp.tanh(0.5 * z))
            scanned = jnp.concatenate([rows_tiles[k, sublanes(tile), :] for k in range(2)], axis=0)
            scanned = scanned + skip_ref[:, cols] * inner_ref[rows, cols].astype(jnp.float32)
            out_ref[rows, cols] = (scanned * gate).astype(jnp.bfloat16)
        return unused

    lax.fori_loop(0, block // PAIR, body, 0)


def join_states(projected, other, y, sums, inner_act, z_branch, decay_rate, skip_gain, moved, mine, theirs, low_rank, reach):
    tok, channels = z_branch.shape
    states = decay_rate.shape[0]
    tiles = channels // LANES
    count = tiles // ROWS
    whole = lambda a: pl.BlockSpec(a.shape, lambda i: (0,) * a.ndim)
    by_token = pl.BlockSpec((BLOCK, tiles, LANES), lambda i: (i, 0, 0))
    by_row = pl.BlockSpec((BLOCK, channels), lambda i: (i, 0))
    skip = skip_gain.reshape(1, channels)
    c_part = pl.BlockSpec((states, tok), lambda i: (low_rank // states + 1, 0))
    return pl.pallas_call(
        functools.partial(join_kernel, reach),
        grid=(tok // BLOCK,),
        in_specs=[
            c_part,
            c_part,
            by_token,
            by_token,
            by_row,
            by_row,
            whole(decay_rate),
            whole(skip),
            by_row,
            whole(mine),
            whole(theirs),
        ],
        out_specs=[by_row, by_row],
        out_shape=[jax.ShapeDtypeStruct((tok, channels), jnp.bfloat16)] * 2,
        scratch_shapes=[
            pltpu.VMEM((tok, states, LANES), jnp.float32),
            pltpu.VMEM((states * count, ROWS, LANES), jnp.float32),
            pltpu.VMEM((states * count, ROWS, LANES), jnp.float32),
            pltpu.VMEM((2, tiles * ROWS, LANES), jnp.float32),
        ],
        compiler_params=pltpu.CompilerParams(vmem_limit_bytes=VMEM_SOME),
        cost_estimate=pl.CostEstimate(
            flops=8 * tok * channels * states,
            bytes_accessed=14 * tok * channels,
            transcendentals=tok * channels * states,
        ),
        name="join_states",
    )(
        projected,
        other,
        in_hbm(y),
        in_hbm(sums),
        in_hbm(inner_act),
        in_hbm(z_branch),
        in_hbm(decay_rate),
        in_hbm(skip),
        moved,
        mine,
        theirs,
    )


def attend_kernel(
    lengths_ref,
    place_ref,
    q_ref,
    keys_mine,
    keys_theirs,
    values_mine,
    values_theirs,
    out_ref,
    queries,
    scores,
    tops,
    acc,
):
    tok = q_ref.shape[0]
    heads = q_ref.shape[1] // HD
    position = lax.axis_index("seq")
    odd = lax.rem(position, 2)
    anchor = position * tok
    scale = jnp.bfloat16(LOG2E * HD**-0.5)
    starts, ends = doc_edges(lengths_ref)
    edges = list(zip(starts, ends)) + [(jnp.int32(-(2**30)), jnp.int32(0))]
    lane = lax.broadcasted_iota(jnp.int32, (1, LANES), 1)
    first = jnp.full((1, LANES), 2**30, jnp.int32)
    last = jnp.zeros((1, LANES), jnp.int32)
    for i, (start, end) in enumerate(edges):
        first = jnp.where(lane == i, start, first)
        last = jnp.where(lane == i, end, last)
    rows = lax.broadcasted_iota(jnp.int32, (tok, LANES), 0)

    def in_doc(base):
        return (rows + base >= first) & (rows + base < last)

    apart = jnp.where(in_doc(anchor) | (lane >= len(edges)), 0.0, -APART).astype(jnp.bfloat16)
    for head in range(heads):
        queries[head * tok : (head + 1) * tok, :HD] = q_ref[:, head * HD : (head + 1) * HD]
        queries[head * tok : (head + 1) * tok, HD:] = apart

    def rows_of(mine_ref, theirs_ref, back):
        if isinstance(back, int) and back == 0:
            return mine_ref[0]
        return jnp.where(lax.rem(back, 2) == 0, mine_ref[back // 2], theirs_ref[(back + 1) // 2 - odd])

    def score(back):
        marks = jnp.where(in_doc(anchor - back * tok), 1.0, 0.0).astype(jnp.bfloat16)
        keys = jnp.concatenate([rows_of(keys_mine, keys_theirs, back), marks], axis=1)
        return lax.dot_general(queries[...], keys, (((1,), (1,)), ((), ())), preferred_element_type=jnp.float32)

    causal = lax.broadcasted_iota(jnp.int32, (tok, tok), 1) <= lax.broadcasted_iota(jnp.int32, (tok, tok), 0)

    def highest(backs):
        top = None
        for back in backs:
            s = score(back)
            if isinstance(back, int) and back == 0:
                s = jnp.concatenate(
                    [jnp.where(causal, s[h * tok : (h + 1) * tok], -APART) for h in range(heads)], axis=0
                )
            scores[back] = s
            for at in range(0, tok, LANES):
                piece = s[:, at : at + LANES]
                top = piece if top is None else jnp.maximum(top, piece)
        return top

    begin = jnp.int32(0)
    for start in starts[1:]:
        begin = jnp.where(anchor >= start, start, begin)
    pairs = ((anchor - begin + tok - 1) // tok + 1) // 2

    def start_with(alone, together):
        pl.when(pairs == 0)(alone)
        pl.when(pairs > 0)(together)

    def set_tops(backs):
        tops[...] = highest(backs)

    start_with(lambda: set_tops([0]), lambda: set_tops([0, 1, 2]))

    def look(pair, carry):
        tops[...] = jnp.maximum(tops[...], highest([2 * pair - 1, 2 * pair]))
        return carry

    lax.fori_loop(2, pairs + 1, look, 0)
    tops[...] = jnp.broadcast_to(jnp.max(tops[...], axis=1, keepdims=True), tops.shape)

    def weighted(backs):
        values = jnp.concatenate([rows_of(values_mine, values_theirs, back) for back in backs], axis=0)
        values = jnp.concatenate([values, jnp.ones(values.shape, jnp.bfloat16)], axis=1)
        top = tops[...]
        weights = [
            jnp.exp2((scores[back, :, at : at + LANES] - top).astype(jnp.bfloat16) * scale)
            for back in backs
            for at in range(0, tok, LANES)
        ]
        return jnp.dot(jnp.concatenate(weights, axis=1), values, preferred_element_type=jnp.float32)

    def set_acc(backs):
        acc[...] = weighted(backs)

    start_with(lambda: set_acc([0]), lambda: set_acc([0, 1, 2]))

    def absorb(pair, carry):
        acc[...] += weighted([2 * pair - 1, 2 * pair])
        return carry

    lax.fori_loop(2, pairs + 1, absorb, 0)
    order = place_ref[pl.ds(position, 1), :]
    move = (lax.broadcasted_iota(jnp.int32, (tok, tok), 0) == order).astype(jnp.float32).astype(jnp.bfloat16)
    for head in range(heads):
        part = slice(head * tok, (head + 1) * tok)
        result = (acc[part, :HD] / acc[part, HD:]).astype(jnp.bfloat16)
        moved = jnp.dot(move, result, preferred_element_type=jnp.float32)
        out_ref[:, head * HD : (head + 1) * HD] = moved.astype(jnp.bfloat16)


def attend(lengths, send_place, query_rows, mine, theirs):
    tok, width = query_rows.shape
    kv_local = mine.shape[2] // (2 * HD)
    share = width // kv_local
    heads = share // HD
    reach = 2 * (mine.shape[0] - 1)
    by_group = pl.BlockSpec((tok, share), lambda i: (0, i))
    keys = pl.BlockSpec(mine.shape[:2] + (HD,), lambda i: (0, 0, i))
    values = pl.BlockSpec(mine.shape[:2] + (HD,), lambda i: (0, 0, i + kv_local))
    return pl.pallas_call(
        attend_kernel,
        grid=(kv_local,),
        in_specs=[
            pl.BlockSpec(memory_space=pltpu.SMEM),
            pl.BlockSpec(send_place.shape, lambda i: (0, 0)),
            by_group,
            keys,
            keys,
            values,
            values,
        ],
        out_specs=by_group,
        out_shape=jax.ShapeDtypeStruct((tok, width), jnp.bfloat16),
        scratch_shapes=[
            pltpu.VMEM((heads * tok, 2 * HD), jnp.bfloat16),
            pltpu.VMEM((reach + 1, heads * tok, tok), jnp.float32),
            pltpu.VMEM((heads * tok, LANES), jnp.float32),
            pltpu.VMEM((heads * tok, 2 * HD), jnp.float32),
        ],
        compiler_params=pltpu.CompilerParams(vmem_limit_bytes=VMEM_LIMIT // 2 + 4 * (reach + 1) * heads * tok * tok),
        cost_estimate=pl.CostEstimate(flops=tok * width, bytes_accessed=tok * width, transcendentals=0),
        name="attend",
    )(lengths, send_place, query_rows, mine, theirs, mine, theirs)


def shifted(value, steps):
    count = lax.axis_size("seq")
    return lax.ppermute(value, "seq", [(source, source + steps) for source in range(count - steps)])


def with_partner(held):
    mine = jnp.stack(held)
    count = lax.axis_size("seq")
    return mine, lax.ppermute(mine, "seq", [(source, source ^ 1) for source in range(count)])


def even_back(value, reach):
    return [value] + [shifted(value, 2 * k) for k in range(1, (reach + 1) // 2 + 1)]


def local(
    x_branch,
    z_branch,
    conv_weight,
    conv_bias,
    xproj_weight,
    dt_weight,
    dt_bias,
    decay_rate,
    skip_gain,
    query_rows,
    key_rows,
    value_rows,
    lengths,
    destination,
):
    tok = x_branch.shape[0]
    n_seq = lax.axis_size("seq")
    n_mp = lax.axis_size("mp")
    low_rank = dt_weight.shape[0]
    reach = n_seq // 2
    run_rows = tok // n_seq
    fence = lax.optimization_barrier

    lengths = in_hbm(lengths)
    halo, kv = pack(x_branch, key_rows, value_rows)
    earlier_rows = shifted(halo, 1)
    held = even_back(kv, reach)
    send_place = ((destination // tok) * run_rows + destination % run_rows).reshape(n_seq, tok)

    inner_act, partial = conv_project(lengths, x_branch, earlier_rows, conv_weight, conv_bias, xproj_weight)
    _, *held = fence((partial, *held))
    mine, theirs = with_partner(held)
    total, other = partial, jnp.zeros_like(partial)
    steps = [1 << k for k in range((n_mp - 1).bit_length())]
    for step in steps:
        if step > 1:
            total = (total.astype(jnp.float32) + other.astype(jnp.float32)).astype(jnp.bfloat16)
        if step == steps[-1]:
            total, send_place = fence((total, send_place))
        other = lax.ppermute(total, "mp", [(source, source ^ step) for source in range(n_mp)])
    attended = attend(lengths, send_place, query_rows, mine, theirs)
    regrouped = lax.all_to_all(attended, "seq", split_axis=0, concat_axis=0, tiled=True)
    total, other, _ = fence((total, other, attended))

    y, sums, state = local_scan(lengths, total, other, dt_weight, dt_bias, decay_rate, inner_act)
    states = with_partner(even_back(state, reach))
    return tuple(
        join_states(
            total,
            other,
            y,
            sums,
            inner_act,
            z_branch,
            decay_rate,
            skip_gain,
            regrouped,
            *states,
            low_rank,
            reach,
        )
    )


def solution(mesh):
    placed = (
        P("seq", "mp"),
        P("seq", "mp"),
        P(None, "mp"),
        P("mp"),
        P("mp", None),
        P(None, "mp"),
        P("mp"),
        P(None, "mp"),
        P("mp"),
        P("seq", "mp"),
        P("seq", "mp"),
        P("seq", "mp"),
        P(),
        P(),
    )
    return jax.shard_map(
        local,
        mesh=mesh,
        in_specs=placed,
        out_specs=(P("seq", "mp"), P("seq", "mp")),
        check_vma=False,
    )
```

```python
import functools

import jax
import jax.numpy as jnp
from jax import lax
from jax.experimental import pallas as pl
from jax.experimental.pallas import tpu as pltpu
from jax.sharding import PartitionSpec as P

HD = 128
LANES = 128
HALO = 16
LOG2E = 1.4426950408889634
RESET = 1e30
APART = 65536.0
VMEM_LIMIT = 32 * 1024 * 1024
VMEM_MOST = 56 * 1024 * 1024
VMEM_NEARLY = 52 * 1024 * 1024 + 512 * 1024
VMEM_SOME = 50 * 1024 * 1024


def doc_edges(lengths_ref):
    starts, ends, total = [], [], 0
    for i in range(lengths_ref.shape[0]):
        starts.append(total)
        total = total + lengths_ref[i]
        ends.append(total)
    return starts, ends


def doc_start(places, starts):
    found = jnp.zeros_like(places)
    for start in starts[1:]:
        found = jnp.where(places >= start, start, found)
    return found


def in_hbm(value):
    return pltpu.with_memory_space_constraint(value, pltpu.HBM)


def channel_chunk(channels):
    return 1024 if channels % 1024 == 0 else channels


def pack_kernel(x_ref, k_ref, v_ref, halo_ref, kv_ref):
    width = k_ref.shape[1]
    halo_ref[...] = x_ref[...]
    kv_ref[:, :width] = k_ref[...]
    kv_ref[:, width:] = v_ref[...]


def pack(x_branch, key_rows, value_rows):
    tok, channels = x_branch.shape
    width = key_rows.shape[1]
    whole = lambda rows, columns: pl.BlockSpec((rows, columns), lambda i: (0, 0))
    return pl.pallas_call(
        pack_kernel,
        grid=(1,),
        in_specs=[
            pl.BlockSpec((HALO, channels), lambda i: (tok // HALO - 1, 0)),
            whole(tok, width),
            whole(tok, width),
        ],
        out_specs=[whole(HALO, channels), whole(tok, 2 * width)],
        out_shape=[
            jax.ShapeDtypeStruct((HALO, channels), x_branch.dtype),
            jax.ShapeDtypeStruct((tok, 2 * width), key_rows.dtype),
        ],
        compiler_params=pltpu.CompilerParams(vmem_limit_bytes=VMEM_LIMIT),
        cost_estimate=pl.CostEstimate(flops=0, bytes_accessed=16 * tok * width, transcendentals=0),
        name="pack",
    )(in_hbm(x_branch), in_hbm(key_rows), in_hbm(value_rows))


def conv_kernel(
    lengths_ref, x_ref, halo_ref, w_hbm, b_hbm, xp_ref, inner_ref, part_ref, ext, acc, w_ref, b_ref, fetched
):
    tok, chunk = x_ref.shape
    starts, _ = doc_edges(lengths_ref)
    anchor = lax.axis_index("seq") * tok
    places = anchor + lax.broadcasted_iota(jnp.int32, (tok, LANES), 0)
    depth = places - doc_start(places, starts)
    at = pl.program_id(0)
    fetches = [
        pltpu.make_async_copy(w_hbm, w_ref, fetched.at[0]),
        pltpu.make_async_copy(b_hbm, b_ref, fetched.at[1]),
    ]

    @pl.when(at == 0)
    def _():
        for fetch in fetches:
            fetch.start()

    ext[0:HALO, :] = halo_ref[...].astype(jnp.float32)
    ext[HALO:, :] = x_ref[...].astype(jnp.float32)

    @pl.when(at == 0)
    def _():
        for fetch in fetches:
            fetch.wait()

    for lane in range(0, chunk, LANES):
        cols = slice(lane, lane + LANES)
        here = pl.ds(pl.multiple_of(at * chunk + lane, LANES), LANES)
        total = b_ref[:, here] + w_ref[0:1, here] * ext[HALO:, cols]
        for lag in range(1, w_ref.shape[0]):
            window = ext[HALO - lag : HALO - lag + tok, cols]
            total += w_ref[lag : lag + 1, here] * jnp.where(depth >= lag, window, 0.0)
        act = total * (0.5 + 0.5 * jnp.tanh(0.5 * total))
        inner_ref[:, cols] = act.astype(jnp.bfloat16)
    product = lax.dot_general(
        xp_ref[...], inner_ref[...], (((1,), (1,)), ((), ())), preferred_element_type=jnp.float32
    )

    @pl.when(at == 0)
    def _():
        acc[...] = product

    @pl.when(at > 0)
    def _():
        acc[...] += product

    @pl.when(at == pl.num_programs(0) - 1)
    def _():
        part_ref[...] = acc[...].astype(jnp.bfloat16)


def conv_project(lengths, x_branch, halo, conv_weight, conv_bias, xproj_weight):
    tok, channels = x_branch.shape
    width = xproj_weight.shape[1]
    taps = conv_weight.shape[0]
    chunk = channel_chunk(channels)
    return pl.pallas_call(
        conv_kernel,
        grid=(channels // chunk,),
        in_specs=[
            pl.BlockSpec(memory_space=pltpu.SMEM),
            pl.BlockSpec((tok, chunk), lambda i: (0, i)),
            pl.BlockSpec((HALO, chunk), lambda i: (0, i)),
            pl.BlockSpec(memory_space=pltpu.HBM),
            pl.BlockSpec(memory_space=pltpu.HBM),
            pl.BlockSpec((width, chunk), lambda i: (0, i)),
        ],
        out_specs=[
            pl.BlockSpec((tok, chunk), lambda i: (0, i)),
            pl.BlockSpec((width, tok), lambda i: (0, 0)),
        ],
        out_shape=[
            jax.ShapeDtypeStruct((tok, channels), jnp.bfloat16),
            jax.ShapeDtypeStruct((width, tok), jnp.bfloat16),
        ],
        scratch_shapes=[
            pltpu.VMEM((tok + HALO, chunk), jnp.float32),
            pltpu.VMEM((width, tok), jnp.float32),
            pltpu.VMEM((taps, channels), jnp.float32),
            pltpu.VMEM((1, channels), jnp.float32),
            pltpu.SemaphoreType.DMA((2,)),
        ],
        compiler_params=pltpu.CompilerParams(vmem_limit_bytes=VMEM_NEARLY),
        cost_estimate=pl.CostEstimate(
            flops=80 * tok * channels * width, bytes_accessed=8 * tok * channels, transcendentals=tok * channels
        ),
        name="conv_project",
    )(
        lengths,
        in_hbm(x_branch),
        halo,
        in_hbm(conv_weight),
        in_hbm(conv_bias.reshape(1, channels)),
        in_hbm(xproj_weight.T),
    )


ROWS = 8
PAIR = 2 * ROWS
BLOCK = 64


def spread(columns):
    tok, k = columns.shape
    own = lax.broadcasted_iota(jnp.int32, (k, k), 0) == lax.broadcasted_iota(jnp.int32, (k, k), 1)
    picked = jnp.where(own[None], columns.astype(jnp.float32)[:, None, :], 0.0).reshape(tok * k, k)
    ones = jnp.ones((k, LANES), jnp.bfloat16)
    return jnp.dot(picked.astype(jnp.bfloat16), ones, preferred_element_type=jnp.float32).reshape(tok, k, LANES)


def lane(tile):
    return slice(tile * LANES, (tile + 1) * LANES)


def sublanes(tile):
    return slice(tile * ROWS, (tile + 1) * ROWS)


def added(one_ref, other_ref, rows):
    total = one_ref[rows, :].astype(jnp.float32) + other_ref[rows, :].astype(jnp.float32)
    return total.astype(jnp.bfloat16).astype(jnp.float32)


def by_register(rate_ref, rates):
    states = rate_ref.shape[0]
    count = rates.shape[0] // states
    for n in range(states):
        for h in range(count):
            tiles = [rate_ref[n : n + 1, lane(h * ROWS + j)] for j in range(ROWS)]
            rates[n * count + h] = jnp.concatenate(tiles, axis=0) * (-LOG2E)


def local_kernel(
    lengths_ref,
    proj_ref,
    other_ref,
    dtw_ref,
    bias_ref,
    rate_ref,
    inner_ref,
    y_ref,
    sum_ref,
    state_ref,
    low_cols,
    bc_spread,
    raw,
    rates,
    step_tiles,
    drive_tiles,
    carry,
):
    tok = proj_ref.shape[1]
    block, channels = inner_ref.shape
    states = rate_ref.shape[0]
    low_rank = dtw_ref.shape[0]
    tiles = channels // LANES
    count = tiles // ROWS
    starts, _ = doc_edges(lengths_ref)
    at = pl.program_id(0)

    @pl.when(at == 0)
    def _():
        low_cols[...] = added(proj_ref, other_ref, slice(0, low_rank)).T.astype(jnp.bfloat16)
        bc_spread[...] = spread(added(proj_ref, other_ref, slice(low_rank, None)).T)
        by_register(rate_ref, rates)
        carry[...] = jnp.zeros_like(carry)
        for first in range(0, tiles, 4):
            cols = slice(first * LANES, (first + 4) * LANES)
            part = jnp.dot(low_cols[...], dtw_ref[:, cols], preferred_element_type=jnp.float32)
            for i in range(4):
                raw[:, sublanes(first + i), :] = part[:, lane(i)].reshape(tok // ROWS, ROWS, LANES)

    def steps(pair, unused):
        rows = pl.ds(pl.multiple_of(pair * PAIR, PAIR), PAIR)
        places = lax.axis_index("seq") * tok + at * block + pair * PAIR
        places = places + lax.broadcasted_iota(jnp.int32, (PAIR, LANES), 0)
        at_start = places == doc_start(places, starts)
        for tile in range(tiles):
            inner = inner_ref[rows, lane(tile)].astype(jnp.float32)
            bias = bias_ref[:, lane(tile)]
            for k in range(2):
                biased = raw[at * (block // ROWS) + 2 * pair + k, sublanes(tile), :] + bias
                step = jnp.maximum(biased, 0.0) + jnp.log(1.0 + jnp.exp(-jnp.abs(biased)))
                drive_tiles[2 * pair + k, sublanes(tile), :] = step * inner[sublanes(k)]
                step_tiles[2 * pair + k, sublanes(tile), :] = jnp.where(at_start[sublanes(k)], RESET, step)
        return unused

    lax.fori_loop(0, block // PAIR, steps, 0)

    def scan(t8, held):
        held, total = list(held[0]), list(held[1])
        for first in range(0, ROWS, 2):
            tokens = range(first, first + 2)
            picked = [[pl.ds(r + h * ROWS * ROWS, ROWS, stride=ROWS) for h in range(count)] for r in tokens]
            step = [[step_tiles[t8, rows, :] for rows in of_token] for of_token in picked]
            drive = [[drive_tiles[t8, rows, :] for rows in of_token] for of_token in picked]
            out = [[None] * count for _ in tokens]
            for n in range(states):
                where = [at * block + t8 * ROWS + r for r in tokens]
                b_row = [bc_spread[token, n : n + 1, :] for token in where]
                c_row = [bc_spread[token, states + n : states + n + 1, :] for token in where]
                for h in range(count):
                    i = n * count + h
                    rate = rates[i]
                    decay = [jnp.exp2(rate * step[k][h]) for k in range(2)]
                    for k in range(2):
                        held[i] = decay[k] * held[i] + b_row[k] * drive[k][h]
                        term = c_row[k] * held[i]
                        out[k][h] = term if out[k][h] is None else out[k][h] + term
            for k, r in enumerate(tokens):
                for h in range(count):
                    total[h] = total[h] + step[k][h]
                    y_ref[t8 * ROWS + r, sublanes(h), :] = out[k][h]
                    sum_ref[t8 * ROWS + r, sublanes(h), :] = total[h]
        return held, total

    kept = states * count
    held = ([carry[i] for i in range(kept)], [carry[kept + h] for h in range(count)])
    held, total = lax.fori_loop(0, block // ROWS, scan, held)
    for i, value in enumerate(held + total):
        carry[i] = value

    @pl.when(at == pl.num_programs(0) - 1)
    def _():
        state_ref[: states * tiles, :] = jnp.concatenate(held, axis=0).astype(jnp.bfloat16)
        whole = jnp.concatenate(total, axis=0)
        high = whole.astype(jnp.bfloat16).astype(jnp.float32)
        state_ref[states * tiles :, :] = jnp.concatenate([high, whole - high], axis=0).astype(jnp.bfloat16)


def local_scan(lengths, projected, other, dt_weight, dt_bias, decay_rate, inner_act):
    tok, channels = inner_act.shape
    low_rank = dt_weight.shape[0]
    states = decay_rate.shape[0]
    tiles = channels // LANES
    count = tiles // ROWS
    whole = lambda a: pl.BlockSpec(a.shape, lambda i: (0,) * a.ndim)
    bias = dt_bias.reshape(1, channels)
    by_token = pl.BlockSpec((BLOCK, tiles, LANES), lambda i: (i, 0, 0))
    state_rows = (states + 2) * tiles
    return pl.pallas_call(
        local_kernel,
        grid=(tok // BLOCK,),
        in_specs=[
            pl.BlockSpec(memory_space=pltpu.SMEM),
            whole(projected),
            whole(other),
            whole(dt_weight),
            whole(bias),
            whole(decay_rate),
            pl.BlockSpec((BLOCK, channels), lambda i: (i, 0)),
        ],
        out_specs=[by_token, by_token, pl.BlockSpec((state_rows, LANES), lambda i: (0, 0))],
        out_shape=[
            jax.ShapeDtypeStruct((tok, tiles, LANES), jnp.float32),
            jax.ShapeDtypeStruct((tok, tiles, LANES), jnp.float32),
            jax.ShapeDtypeStruct((state_rows, LANES), jnp.bfloat16),
        ],
        scratch_shapes=[
            pltpu.VMEM((tok, low_rank), jnp.bfloat16),
            pltpu.VMEM((tok, 2 * states, LANES), jnp.float32),
            pltpu.VMEM((tok // ROWS, tiles * ROWS, LANES), jnp.float32),
            pltpu.VMEM((states * count, ROWS, LANES), jnp.float32),
            pltpu.VMEM((BLOCK // ROWS, tiles * ROWS, LANES), jnp.float32),
            pltpu.VMEM((BLOCK // ROWS, tiles * ROWS, LANES), jnp.float32),
            pltpu.VMEM(((states + 1) * count, ROWS, LANES), jnp.float32),
        ],
        compiler_params=pltpu.CompilerParams(vmem_limit_bytes=VMEM_NEARLY),
        cost_estimate=pl.CostEstimate(
            flops=12 * tok * channels * states,
            bytes_accessed=12 * tok * channels,
            transcendentals=tok * channels * states,
        ),
        name="local_scan",
    )(
        lengths, projected, other, in_hbm(dt_weight), in_hbm(bias), in_hbm(decay_rate), in_hbm(inner_act)
    )


def join_kernel(
    reach,
    proj_ref,
    other_ref,
    y_ref,
    sum_ref,
    inner_ref,
    z_ref,
    rate_ref,
    skip_ref,
    moved_ref,
    mine_ref,
    theirs_ref,
    out_ref,
    regrouped_ref,
    c_spread,
    rates,
    entering,
    rows_tiles,
):
    block, channels = z_ref.shape
    states = rate_ref.shape[0]
    tiles = channels // LANES
    count = tiles // ROWS
    kept = states * count
    at = pl.program_id(0)

    @pl.when(at == 0)
    def _():
        c_spread[...] = spread(added(proj_ref, other_ref, slice(None)).T)
        by_register(rate_ref, rates)
        odd = lax.rem(lax.axis_index("seq"), 2)
        state = [jnp.zeros((ROWS, LANES), jnp.float32)] * kept
        for back in range(reach, 0, -1):
            ref, which = (mine_ref, back // 2) if back % 2 == 0 else (theirs_ref, (back + 1) // 2 - odd)
            sent = ref[which].astype(jnp.float32)
            totals = sent[states * tiles : (states + 1) * tiles] + sent[(states + 1) * tiles :]
            state = [
                jnp.exp2(rates[i] * totals[sublanes(i % count)]) * state[i] + sent[sublanes(i)] for i in range(kept)
            ]
        for i in range(kept):
            entering[i] = state[i]

    regrouped_ref[...] = moved_ref[...]

    def body(pair, unused):
        rows = pl.ds(pl.multiple_of(pair * PAIR, PAIR), PAIR)
        for k in range(2):
            first = pair * PAIR + k * ROWS
            total = [[sum_ref[first + r, sublanes(h), :] for h in range(count)] for r in range(ROWS)]
            out = [[y_ref[first + r, sublanes(h), :] for h in range(count)] for r in range(ROWS)]
            for n in range(states):
                c_row = [c_spread[at * block + first + r, n : n + 1, :] for r in range(ROWS)]
                for h in range(count):
                    rate, state = rates[n * count + h], entering[n * count + h]
                    for r in range(ROWS):
                        out[r][h] += jnp.exp2(rate * total[r][h]) * state * c_row[r]
            for r in range(ROWS):
                for h in range(count):
                    rows_tiles[k, pl.ds(r + h * ROWS * ROWS, ROWS, stride=ROWS), :] = out[r][h]
        for tile in range(tiles):
            cols = lane(tile)
            z = z_ref[rows, cols].astype(jnp.float32)
            gate = z * (0.5 + 0.5 * jnp.tanh(0.5 * z))
            scanned = jnp.concatenate([rows_tiles[k, sublanes(tile), :] for k in range(2)], axis=0)
            scanned = scanned + skip_ref[:, cols] * inner_ref[rows, cols].astype(jnp.float32)
            out_ref[rows, cols] = (scanned * gate).astype(jnp.bfloat16)
        return unused

    lax.fori_loop(0, block // PAIR, body, 0)


def join_states(projected, other, y, sums, inner_act, z_branch, decay_rate, skip_gain, moved, mine, theirs, low_rank, reach):
    tok, channels = z_branch.shape
    states = decay_rate.shape[0]
    tiles = channels // LANES
    count = tiles // ROWS
    whole = lambda a: pl.BlockSpec(a.shape, lambda i: (0,) * a.ndim)
    by_token = pl.BlockSpec((BLOCK, tiles, LANES), lambda i: (i, 0, 0))
    by_row = pl.BlockSpec((BLOCK, channels), lambda i: (i, 0))
    skip = skip_gain.reshape(1, channels)
    c_part = pl.BlockSpec((states, tok), lambda i: (low_rank // states + 1, 0))
    return pl.pallas_call(
        functools.partial(join_kernel, reach),
        grid=(tok // BLOCK,),
        in_specs=[
            c_part,
            c_part,
            by_token,
            by_token,
            by_row,
            by_row,
            whole(decay_rate),
            whole(skip),
            by_row,
            whole(mine),
            whole(theirs),
        ],
        out_specs=[by_row, by_row],
        out_shape=[jax.ShapeDtypeStruct((tok, channels), jnp.bfloat16)] * 2,
        scratch_shapes=[
            pltpu.VMEM((tok, states, LANES), jnp.float32),
            pltpu.VMEM((states * count, ROWS, LANES), jnp.float32),
            pltpu.VMEM((states * count, ROWS, LANES), jnp.float32),
            pltpu.VMEM((2, tiles * ROWS, LANES), jnp.float32),
        ],
        compiler_params=pltpu.CompilerParams(vmem_limit_bytes=VMEM_SOME),
        cost_estimate=pl.CostEstimate(
            flops=8 * tok * channels * states,
            bytes_accessed=14 * tok * channels,
            transcendentals=tok * channels * states,
        ),
        name="join_states",
    )(
        projected,
        other,
        in_hbm(y),
        in_hbm(sums),
        in_hbm(inner_act),
        in_hbm(z_branch),
        in_hbm(decay_rate),
        in_hbm(skip),
        moved,
        mine,
        theirs,
    )


def attend_kernel(
    lengths_ref,
    place_ref,
    q_ref,
    keys_mine,
    keys_theirs,
    values_mine,
    values_theirs,
    out_ref,
    queries,
    scores,
    tops,
    acc,
):
    tok = q_ref.shape[0]
    heads = q_ref.shape[1] // HD
    position = lax.axis_index("seq")
    odd = lax.rem(position, 2)
    anchor = position * tok
    scale = jnp.bfloat16(LOG2E * HD**-0.5)
    starts, ends = doc_edges(lengths_ref)
    edges = list(zip(starts, ends)) + [(jnp.int32(-(2**30)), jnp.int32(0))]
    lane = lax.broadcasted_iota(jnp.int32, (1, LANES), 1)
    first = jnp.full((1, LANES), 2**30, jnp.int32)
    last = jnp.zeros((1, LANES), jnp.int32)
    for i, (start, end) in enumerate(edges):
        first = jnp.where(lane == i, start, first)
        last = jnp.where(lane == i, end, last)
    rows = lax.broadcasted_iota(jnp.int32, (tok, LANES), 0)

    def in_doc(base):
        return (rows + base >= first) & (rows + base < last)

    apart = jnp.where(in_doc(anchor) | (lane >= len(edges)), 0.0, -APART).astype(jnp.bfloat16)
    for head in range(heads):
        queries[head * tok : (head + 1) * tok, :HD] = q_ref[:, head * HD : (head + 1) * HD]
        queries[head * tok : (head + 1) * tok, HD:] = apart

    def rows_of(mine_ref, theirs_ref, back):
        if isinstance(back, int) and back == 0:
            return mine_ref[0]
        return jnp.where(lax.rem(back, 2) == 0, mine_ref[back // 2], theirs_ref[(back + 1) // 2 - odd])

    def score(back):
        marks = jnp.where(in_doc(anchor - back * tok), 1.0, 0.0).astype(jnp.bfloat16)
        keys = jnp.concatenate([rows_of(keys_mine, keys_theirs, back), marks], axis=1)
        return lax.dot_general(queries[...], keys, (((1,), (1,)), ((), ())), preferred_element_type=jnp.float32)

    causal = lax.broadcasted_iota(jnp.int32, (tok, tok), 1) <= lax.broadcasted_iota(jnp.int32, (tok, tok), 0)

    def highest(backs):
        top = None
        for back in backs:
            s = score(back)
            if isinstance(back, int) and back == 0:
                s = jnp.concatenate(
                    [jnp.where(causal, s[h * tok : (h + 1) * tok], -APART) for h in range(heads)], axis=0
                )
            scores[back] = s
            for at in range(0, tok, LANES):
                piece = s[:, at : at + LANES]
                top = piece if top is None else jnp.maximum(top, piece)
        return top

    begin = jnp.int32(0)
    for start in starts[1:]:
        begin = jnp.where(anchor >= start, start, begin)
    pairs = ((anchor - begin + tok - 1) // tok + 1) // 2

    def start_with(alone, together):
        pl.when(pairs == 0)(alone)
        pl.when(pairs > 0)(together)

    def set_tops(backs):
        tops[...] = highest(backs)

    start_with(lambda: set_tops([0]), lambda: set_tops([0, 1, 2]))

    def look(pair, carry):
        tops[...] = jnp.maximum(tops[...], highest([2 * pair - 1, 2 * pair]))
        return carry

    lax.fori_loop(2, pairs + 1, look, 0)
    tops[...] = jnp.broadcast_to(jnp.max(tops[...], axis=1, keepdims=True), tops.shape)

    def weighted(backs):
        values = jnp.concatenate([rows_of(values_mine, values_theirs, back) for back in backs], axis=0)
        values = jnp.concatenate([values, jnp.ones(values.shape, jnp.bfloat16)], axis=1)
        top = tops[...]
        weights = [
            jnp.exp2((scores[back, :, at : at + LANES] - top).astype(jnp.bfloat16) * scale)
            for back in backs
            for at in range(0, tok, LANES)
        ]
        return jnp.dot(jnp.concatenate(weights, axis=1), values, preferred_element_type=jnp.float32)

    def set_acc(backs):
        acc[...] = weighted(backs)

    start_with(lambda: set_acc([0]), lambda: set_acc([0, 1, 2]))

    def absorb(pair, carry):
        acc[...] += weighted([2 * pair - 1, 2 * pair])
        return carry

    lax.fori_loop(2, pairs + 1, absorb, 0)
    order = place_ref[pl.ds(position, 1), :]
    move = (lax.broadcasted_iota(jnp.int32, (tok, tok), 0) == order).astype(jnp.float32).astype(jnp.bfloat16)
    for head in range(heads):
        part = slice(head * tok, (head + 1) * tok)
        result = (acc[part, :HD] / acc[part, HD:]).astype(jnp.bfloat16)
        moved = jnp.dot(move, result, preferred_element_type=jnp.float32)
        out_ref[:, head * HD : (head + 1) * HD] = moved.astype(jnp.bfloat16)


def attend(lengths, send_place, query_rows, mine, theirs):
    tok, width = query_rows.shape
    kv_local = mine.shape[2] // (2 * HD)
    share = width // kv_local
    heads = share // HD
    reach = 2 * (mine.shape[0] - 1)
    by_group = pl.BlockSpec((tok, share), lambda i: (0, i))
    keys = pl.BlockSpec(mine.shape[:2] + (HD,), lambda i: (0, 0, i))
    values = pl.BlockSpec(mine.shape[:2] + (HD,), lambda i: (0, 0, i + kv_local))
    return pl.pallas_call(
        attend_kernel,
        grid=(kv_local,),
        in_specs=[
            pl.BlockSpec(memory_space=pltpu.SMEM),
            pl.BlockSpec(send_place.shape, lambda i: (0, 0)),
            by_group,
            keys,
            keys,
            values,
            values,
        ],
        out_specs=by_group,
        out_shape=jax.ShapeDtypeStruct((tok, width), jnp.bfloat16),
        scratch_shapes=[
            pltpu.VMEM((heads * tok, 2 * HD), jnp.bfloat16),
            pltpu.VMEM((reach + 1, heads * tok, tok), jnp.float32),
            pltpu.VMEM((heads * tok, LANES), jnp.float32),
            pltpu.VMEM((heads * tok, 2 * HD), jnp.float32),
        ],
        compiler_params=pltpu.CompilerParams(vmem_limit_bytes=VMEM_LIMIT // 2 + 4 * (reach + 1) * heads * tok * tok),
        cost_estimate=pl.CostEstimate(flops=tok * width, bytes_accessed=tok * width, transcendentals=0),
        name="attend",
    )(lengths, send_place, query_rows, mine, theirs, mine, theirs)


def shifted(value, steps):
    count = lax.axis_size("seq")
    return lax.ppermute(value, "seq", [(source, source + steps) for source in range(count - steps)])


def with_partner(held):
    mine = jnp.stack(held)
    count = lax.axis_size("seq")
    return mine, lax.ppermute(mine, "seq", [(source, source ^ 1) for source in range(count)])


def even_back(value, reach):
    return [value] + [shifted(value, 2 * k) for k in range(1, (reach + 1) // 2 + 1)]


def local(
    x_branch,
    z_branch,
    conv_weight,
    conv_bias,
    xproj_weight,
    dt_weight,
    dt_bias,
    decay_rate,
    skip_gain,
    query_rows,
    key_rows,
    value_rows,
    lengths,
    destination,
):
    tok = x_branch.shape[0]
    n_seq = lax.axis_size("seq")
    n_mp = lax.axis_size("mp")
    low_rank = dt_weight.shape[0]
    reach = n_seq // 2
    run_rows = tok // n_seq
    fence = lax.optimization_barrier

    lengths = in_hbm(lengths)
    halo, kv = pack(x_branch, key_rows, value_rows)
    earlier_rows = shifted(halo, 1)
    held = even_back(kv, reach)
    send_place = ((destination // tok) * run_rows + destination % run_rows).reshape(n_seq, tok)

    inner_act, partial = conv_project(lengths, x_branch, earlier_rows, conv_weight, conv_bias, xproj_weight)
    _, *held = fence((partial, *held))
    mine, theirs = with_partner(held)
    total, other = partial, jnp.zeros_like(partial)
    steps = [1 << k for k in range((n_mp - 1).bit_length())]
    for step in steps:
        if step > 1:
            total = (total.astype(jnp.float32) + other.astype(jnp.float32)).astype(jnp.bfloat16)
        if step == steps[-1]:
            total, send_place = fence((total, send_place))
        other = lax.ppermute(total, "mp", [(source, source ^ step) for source in range(n_mp)])
    attended = attend(lengths, send_place, query_rows, mine, theirs)
    total, other, attended = fence((total, other, attended))
    regrouped = lax.all_to_all(attended, "seq", split_axis=0, concat_axis=0, tiled=True)

    y, sums, state = local_scan(lengths, total, other, dt_weight, dt_bias, decay_rate, inner_act)
    states = with_partner(even_back(state, reach))
    return tuple(
        join_states(
            total,
            other,
            y,
            sums,
            inner_act,
            z_branch,
            decay_rate,
            skip_gain,
            regrouped,
            *states,
            low_rank,
            reach,
        )
    )


def solution(mesh):
    placed = (
        P("seq", "mp"),
        P("seq", "mp"),
        P(None, "mp"),
        P("mp"),
        P("mp", None),
        P(None, "mp"),
        P("mp"),
        P(None, "mp"),
        P("mp"),
        P("seq", "mp"),
        P("seq", "mp"),
        P("seq", "mp"),
        P(),
        P(),
    )
    return jax.shard_map(
        local,
        mesh=mesh,
        in_specs=placed,
        out_specs=(P("seq", "mp"), P("seq", "mp")),
        check_vma=False,
    )
```

```python
import functools

import jax
import jax.numpy as jnp
from jax import lax
from jax.experimental import pallas as pl
from jax.experimental.pallas import tpu as pltpu
from jax.sharding import PartitionSpec as P

HD = 128
LANES = 128
HALO = 16
LOG2E = 1.4426950408889634
RESET = 1e30
APART = 65536.0
VMEM_LIMIT = 32 * 1024 * 1024
VMEM_MOST = 56 * 1024 * 1024
VMEM_NEARLY = 52 * 1024 * 1024 + 512 * 1024
VMEM_SOME = 50 * 1024 * 1024


def doc_edges(lengths_ref):
    starts, ends, total = [], [], 0
    for i in range(lengths_ref.shape[0]):
        starts.append(total)
        total = total + lengths_ref[i]
        ends.append(total)
    return starts, ends


def doc_start(places, starts):
    found = jnp.zeros_like(places)
    for start in starts[1:]:
        found = jnp.where(places >= start, start, found)
    return found


def in_hbm(value):
    return pltpu.with_memory_space_constraint(value, pltpu.HBM)


def channel_chunk(channels):
    return 1024 if channels % 1024 == 0 else channels


def pack_kernel(x_ref, k_ref, v_ref, halo_ref, kv_ref):
    width = k_ref.shape[1]
    halo_ref[...] = x_ref[...]
    kv_ref[:, :width] = k_ref[...]
    kv_ref[:, width:] = v_ref[...]


def pack(x_branch, key_rows, value_rows):
    tok, channels = x_branch.shape
    width = key_rows.shape[1]
    whole = lambda rows, columns: pl.BlockSpec((rows, columns), lambda i: (0, 0))
    return pl.pallas_call(
        pack_kernel,
        grid=(1,),
        in_specs=[
            pl.BlockSpec((HALO, channels), lambda i: (tok // HALO - 1, 0)),
            whole(tok, width),
            whole(tok, width),
        ],
        out_specs=[whole(HALO, channels), whole(tok, 2 * width)],
        out_shape=[
            jax.ShapeDtypeStruct((HALO, channels), x_branch.dtype),
            jax.ShapeDtypeStruct((tok, 2 * width), key_rows.dtype),
        ],
        compiler_params=pltpu.CompilerParams(vmem_limit_bytes=VMEM_LIMIT),
        cost_estimate=pl.CostEstimate(flops=0, bytes_accessed=16 * tok * width, transcendentals=0),
        name="pack",
    )(in_hbm(x_branch), in_hbm(key_rows), in_hbm(value_rows))


def conv_kernel(
    lengths_ref, x_ref, halo_ref, w_hbm, b_hbm, xp_ref, inner_ref, part_ref, ext, acc, w_ref, b_ref, fetched
):
    tok, chunk = x_ref.shape
    starts, _ = doc_edges(lengths_ref)
    anchor = lax.axis_index("seq") * tok
    places = anchor + lax.broadcasted_iota(jnp.int32, (tok, LANES), 0)
    depth = places - doc_start(places, starts)
    at = pl.program_id(0)
    fetches = [
        pltpu.make_async_copy(w_hbm, w_ref, fetched.at[0]),
        pltpu.make_async_copy(b_hbm, b_ref, fetched.at[1]),
    ]

    @pl.when(at == 0)
    def _():
        for fetch in fetches:
            fetch.start()

    ext[0:HALO, :] = halo_ref[...].astype(jnp.float32)
    ext[HALO:, :] = x_ref[...].astype(jnp.float32)

    @pl.when(at == 0)
    def _():
        for fetch in fetches:
            fetch.wait()

    for lane in range(0, chunk, LANES):
        cols = slice(lane, lane + LANES)
        here = pl.ds(pl.multiple_of(at * chunk + lane, LANES), LANES)
        total = b_ref[:, here] + w_ref[0:1, here] * ext[HALO:, cols]
        for lag in range(1, w_ref.shape[0]):
            window = ext[HALO - lag : HALO - lag + tok, cols]
            total += w_ref[lag : lag + 1, here] * jnp.where(depth >= lag, window, 0.0)
        act = total * (0.5 + 0.5 * jnp.tanh(0.5 * total))
        inner_ref[:, cols] = act.astype(jnp.bfloat16)
    product = lax.dot_general(
        xp_ref[...], inner_ref[...], (((1,), (1,)), ((), ())), preferred_element_type=jnp.float32
    )

    @pl.when(at == 0)
    def _():
        acc[...] = product

    @pl.when(at > 0)
    def _():
        acc[...] += product

    @pl.when(at == pl.num_programs(0) - 1)
    def _():
        part_ref[...] = acc[...].astype(jnp.bfloat16)


def conv_project(lengths, x_branch, halo, conv_weight, conv_bias, xproj_weight):
    tok, channels = x_branch.shape
    width = xproj_weight.shape[1]
    taps = conv_weight.shape[0]
    chunk = channel_chunk(channels)
    return pl.pallas_call(
        conv_kernel,
        grid=(channels // chunk,),
        in_specs=[
            pl.BlockSpec(memory_space=pltpu.SMEM),
            pl.BlockSpec((tok, chunk), lambda i: (0, i)),
            pl.BlockSpec((HALO, chunk), lambda i: (0, i)),
            pl.BlockSpec(memory_space=pltpu.HBM),
            pl.BlockSpec(memory_space=pltpu.HBM),
            pl.BlockSpec((width, chunk), lambda i: (0, i)),
        ],
        out_specs=[
            pl.BlockSpec((tok, chunk), lambda i: (0, i)),
            pl.BlockSpec((width, tok), lambda i: (0, 0)),
        ],
        out_shape=[
            jax.ShapeDtypeStruct((tok, channels), jnp.bfloat16),
            jax.ShapeDtypeStruct((width, tok), jnp.bfloat16),
        ],
        scratch_shapes=[
            pltpu.VMEM((tok + HALO, chunk), jnp.float32),
            pltpu.VMEM((width, tok), jnp.float32),
            pltpu.VMEM((taps, channels), jnp.float32),
            pltpu.VMEM((1, channels), jnp.float32),
            pltpu.SemaphoreType.DMA((2,)),
        ],
        compiler_params=pltpu.CompilerParams(vmem_limit_bytes=VMEM_NEARLY),
        cost_estimate=pl.CostEstimate(
            flops=80 * tok * channels * width, bytes_accessed=8 * tok * channels, transcendentals=tok * channels
        ),
        name="conv_project",
    )(
        lengths,
        in_hbm(x_branch),
        halo,
        in_hbm(conv_weight),
        in_hbm(conv_bias.reshape(1, channels)),
        in_hbm(xproj_weight.T),
    )


ROWS = 8
PAIR = 2 * ROWS
BLOCK = 128


def spread(columns):
    tok, k = columns.shape
    own = lax.broadcasted_iota(jnp.int32, (k, k), 0) == lax.broadcasted_iota(jnp.int32, (k, k), 1)
    picked = jnp.where(own[None], columns.astype(jnp.float32)[:, None, :], 0.0).reshape(tok * k, k)
    ones = jnp.ones((k, LANES), jnp.bfloat16)
    return jnp.dot(picked.astype(jnp.bfloat16), ones, preferred_element_type=jnp.float32).reshape(tok, k, LANES)


def lane(tile):
    return slice(tile * LANES, (tile + 1) * LANES)


def sublanes(tile):
    return slice(tile * ROWS, (tile + 1) * ROWS)


def added(one_ref, other_ref, rows):
    total = one_ref[rows, :].astype(jnp.float32) + other_ref[rows, :].astype(jnp.float32)
    return total.astype(jnp.bfloat16).astype(jnp.float32)


def by_register(rate_ref, rates):
    states = rate_ref.shape[0]
    count = rates.shape[0] // states
    for n in range(states):
        for h in range(count):
            tiles = [rate_ref[n : n + 1, lane(h * ROWS + j)] for j in range(ROWS)]
            rates[n * count + h] = jnp.concatenate(tiles, axis=0) * (-LOG2E)


def local_kernel(
    lengths_ref,
    proj_ref,
    other_ref,
    dtw_ref,
    bias_ref,
    rate_ref,
    inner_ref,
    y_ref,
    sum_ref,
    state_ref,
    low_cols,
    bc_spread,
    raw,
    rates,
    step_tiles,
    drive_tiles,
    carry,
):
    tok = proj_ref.shape[1]
    block, channels = inner_ref.shape
    states = rate_ref.shape[0]
    low_rank = dtw_ref.shape[0]
    tiles = channels // LANES
    count = tiles // ROWS
    starts, _ = doc_edges(lengths_ref)
    at = pl.program_id(0)

    @pl.when(at == 0)
    def _():
        low_cols[...] = added(proj_ref, other_ref, slice(0, low_rank)).T.astype(jnp.bfloat16)
        bc_spread[...] = spread(added(proj_ref, other_ref, slice(low_rank, None)).T)
        by_register(rate_ref, rates)
        carry[...] = jnp.zeros_like(carry)
        for first in range(0, tiles, 4):
            cols = slice(first * LANES, (first + 4) * LANES)
            part = jnp.dot(low_cols[...], dtw_ref[:, cols], preferred_element_type=jnp.float32)
            for i in range(4):
                raw[:, sublanes(first + i), :] = part[:, lane(i)].reshape(tok // ROWS, ROWS, LANES)

    def steps(pair, unused):
        rows = pl.ds(pl.multiple_of(pair * PAIR, PAIR), PAIR)
        places = lax.axis_index("seq") * tok + at * block + pair * PAIR
        places = places + lax.broadcasted_iota(jnp.int32, (PAIR, LANES), 0)
        at_start = places == doc_start(places, starts)
        for tile in range(tiles):
            inner = inner_ref[rows, lane(tile)].astype(jnp.float32)
            bias = bias_ref[:, lane(tile)]
            for k in range(2):
                biased = raw[at * (block // ROWS) + 2 * pair + k, sublanes(tile), :] + bias
                step = jnp.maximum(biased, 0.0) + jnp.log(1.0 + jnp.exp(-jnp.abs(biased)))
                drive_tiles[2 * pair + k, sublanes(tile), :] = step * inner[sublanes(k)]
                step_tiles[2 * pair + k, sublanes(tile), :] = jnp.where(at_start[sublanes(k)], RESET, step)
        return unused

    lax.fori_loop(0, block // PAIR, steps, 0)

    def scan(t8, held):
        held, total = list(held[0]), list(held[1])
        for first in range(0, ROWS, 2):
            tokens = range(first, first + 2)
            picked = [[pl.ds(r + h * ROWS * ROWS, ROWS, stride=ROWS) for h in range(count)] for r in tokens]
            step = [[step_tiles[t8, rows, :] for rows in of_token] for of_token in picked]
            drive = [[drive_tiles[t8, rows, :] for rows in of_token] for of_token in picked]
            out = [[None] * count for _ in tokens]
            for n in range(states):
                where = [at * block + t8 * ROWS + r for r in tokens]
                b_row = [bc_spread[token, n : n + 1, :] for token in where]
                c_row = [bc_spread[token, states + n : states + n + 1, :] for token in where]
                for h in range(count):
                    i = n * count + h
                    rate = rates[i]
                    decay = [jnp.exp2(rate * step[k][h]) for k in range(2)]
                    for k in range(2):
                        held[i] = decay[k] * held[i] + b_row[k] * drive[k][h]
                        term = c_row[k] * held[i]
                        out[k][h] = term if out[k][h] is None else out[k][h] + term
            for k, r in enumerate(tokens):
                for h in range(count):
                    total[h] = total[h] + step[k][h]
                    y_ref[t8 * ROWS + r, sublanes(h), :] = out[k][h]
                    sum_ref[t8 * ROWS + r, sublanes(h), :] = total[h]
        return held, total

    kept = states * count
    held = ([carry[i] for i in range(kept)], [carry[kept + h] for h in range(count)])
    held, total = lax.fori_loop(0, block // ROWS, scan, held)
    for i, value in enumerate(held + total):
        carry[i] = value

    @pl.when(at == pl.num_programs(0) - 1)
    def _():
        state_ref[: states * tiles, :] = jnp.concatenate(held, axis=0).astype(jnp.bfloat16)
        whole = jnp.concatenate(total, axis=0)
        high = whole.astype(jnp.bfloat16).astype(jnp.float32)
        state_ref[states * tiles :, :] = jnp.concatenate([high, whole - high], axis=0).astype(jnp.bfloat16)


def local_scan(lengths, projected, other, dt_weight, dt_bias, decay_rate, inner_act):
    tok, channels = inner_act.shape
    low_rank = dt_weight.shape[0]
    states = decay_rate.shape[0]
    tiles = channels // LANES
    count = tiles // ROWS
    whole = lambda a: pl.BlockSpec(a.shape, lambda i: (0,) * a.ndim)
    bias = dt_bias.reshape(1, channels)
    by_token = pl.BlockSpec((BLOCK, tiles, LANES), lambda i: (i, 0, 0))
    state_rows = (states + 2) * tiles
    return pl.pallas_call(
        local_kernel,
        grid=(tok // BLOCK,),
        in_specs=[
            pl.BlockSpec(memory_space=pltpu.SMEM),
            whole(projected),
            whole(other),
            whole(dt_weight),
            whole(bias),
            whole(decay_rate),
            pl.BlockSpec((BLOCK, channels), lambda i: (i, 0)),
        ],
        out_specs=[by_token, by_token, pl.BlockSpec((state_rows, LANES), lambda i: (0, 0))],
        out_shape=[
            jax.ShapeDtypeStruct((tok, tiles, LANES), jnp.float32),
            jax.ShapeDtypeStruct((tok, tiles, LANES), jnp.float32),
            jax.ShapeDtypeStruct((state_rows, LANES), jnp.bfloat16),
        ],
        scratch_shapes=[
            pltpu.VMEM((tok, low_rank), jnp.bfloat16),
            pltpu.VMEM((tok, 2 * states, LANES), jnp.float32),
            pltpu.VMEM((tok // ROWS, tiles * ROWS, LANES), jnp.float32),
            pltpu.VMEM((states * count, ROWS, LANES), jnp.float32),
            pltpu.VMEM((BLOCK // ROWS, tiles * ROWS, LANES), jnp.float32),
            pltpu.VMEM((BLOCK // ROWS, tiles * ROWS, LANES), jnp.float32),
            pltpu.VMEM(((states + 1) * count, ROWS, LANES), jnp.float32),
        ],
        compiler_params=pltpu.CompilerParams(vmem_limit_bytes=VMEM_NEARLY),
        cost_estimate=pl.CostEstimate(
            flops=12 * tok * channels * states,
            bytes_accessed=12 * tok * channels,
            transcendentals=tok * channels * states,
        ),
        name="local_scan",
    )(
        lengths, projected, other, in_hbm(dt_weight), in_hbm(bias), in_hbm(decay_rate), in_hbm(inner_act)
    )


def join_kernel(
    reach,
    proj_ref,
    other_ref,
    y_ref,
    sum_ref,
    inner_ref,
    z_ref,
    rate_ref,
    skip_ref,
    moved_ref,
    mine_ref,
    theirs_ref,
    out_ref,
    regrouped_ref,
    c_spread,
    rates,
    entering,
    rows_tiles,
):
    block, channels = z_ref.shape
    states = rate_ref.shape[0]
    tiles = channels // LANES
    count = tiles // ROWS
    kept = states * count
    at = pl.program_id(0)

    @pl.when(at == 0)
    def _():
        c_spread[...] = spread(added(proj_ref, other_ref, slice(None)).T)
        by_register(rate_ref, rates)
        odd = lax.rem(lax.axis_index("seq"), 2)
        state = [jnp.zeros((ROWS, LANES), jnp.float32)] * kept
        for back in range(reach, 0, -1):
            ref, which = (mine_ref, back // 2) if back % 2 == 0 else (theirs_ref, (back + 1) // 2 - odd)
            sent = ref[which].astype(jnp.float32)
            totals = sent[states * tiles : (states + 1) * tiles] + sent[(states + 1) * tiles :]
            state = [
                jnp.exp2(rates[i] * totals[sublanes(i % count)]) * state[i] + sent[sublanes(i)] for i in range(kept)
            ]
        for i in range(kept):
            entering[i] = state[i]

    regrouped_ref[...] = moved_ref[...]

    def body(pair, unused):
        rows = pl.ds(pl.multiple_of(pair * PAIR, PAIR), PAIR)
        for k in range(2):
            first = pair * PAIR + k * ROWS
            total = [[sum_ref[first + r, sublanes(h), :] for h in range(count)] for r in range(ROWS)]
            out = [[y_ref[first + r, sublanes(h), :] for h in range(count)] for r in range(ROWS)]
            for n in range(states):
                c_row = [c_spread[at * block + first + r, n : n + 1, :] for r in range(ROWS)]
                for h in range(count):
                    rate, state = rates[n * count + h], entering[n * count + h]
                    for r in range(ROWS):
                        out[r][h] += jnp.exp2(rate * total[r][h]) * state * c_row[r]
            for r in range(ROWS):
                for h in range(count):
                    rows_tiles[k, pl.ds(r + h * ROWS * ROWS, ROWS, stride=ROWS), :] = out[r][h]
        for tile in range(tiles):
            cols = lane(tile)
            z = z_ref[rows, cols].astype(jnp.float32)
            gate = z * (0.5 + 0.5 * jnp.tanh(0.5 * z))
            scanned = jnp.concatenate([rows_tiles[k, sublanes(tile), :] for k in range(2)], axis=0)
            scanned = scanned + skip_ref[:, cols] * inner_ref[rows, cols].astype(jnp.float32)
            out_ref[rows, cols] = (scanned * gate).astype(jnp.bfloat16)
        return unused

    lax.fori_loop(0, block // PAIR, body, 0)


def join_states(projected, other, y, sums, inner_act, z_branch, decay_rate, skip_gain, moved, mine, theirs, low_rank, reach):
    tok, channels = z_branch.shape
    states = decay_rate.shape[0]
    tiles = channels // LANES
    count = tiles // ROWS
    whole = lambda a: pl.BlockSpec(a.shape, lambda i: (0,) * a.ndim)
    by_token = pl.BlockSpec((BLOCK, tiles, LANES), lambda i: (i, 0, 0))
    by_row = pl.BlockSpec((BLOCK, channels), lambda i: (i, 0))
    skip = skip_gain.reshape(1, channels)
    c_part = pl.BlockSpec((states, tok), lambda i: (low_rank // states + 1, 0))
    return pl.pallas_call(
        functools.partial(join_kernel, reach),
        grid=(tok // BLOCK,),
        in_specs=[
            c_part,
            c_part,
            by_token,
            by_token,
            by_row,
            by_row,
            whole(decay_rate),
            whole(skip),
            by_row,
            whole(mine),
            whole(theirs),
        ],
        out_specs=[by_row, by_row],
        out_shape=[jax.ShapeDtypeStruct((tok, channels), jnp.bfloat16)] * 2,
        scratch_shapes=[
            pltpu.VMEM((tok, states, LANES), jnp.float32),
            pltpu.VMEM((states * count, ROWS, LANES), jnp.float32),
            pltpu.VMEM((states * count, ROWS, LANES), jnp.float32),
            pltpu.VMEM((2, tiles * ROWS, LANES), jnp.float32),
        ],
        compiler_params=pltpu.CompilerParams(vmem_limit_bytes=VMEM_SOME),
        cost_estimate=pl.CostEstimate(
            flops=8 * tok * channels * states,
            bytes_accessed=14 * tok * channels,
            transcendentals=tok * channels * states,
        ),
        name="join_states",
    )(
        projected,
        other,
        in_hbm(y),
        in_hbm(sums),
        in_hbm(inner_act),
        in_hbm(z_branch),
        in_hbm(decay_rate),
        in_hbm(skip),
        moved,
        mine,
        theirs,
    )


def attend_kernel(
    lengths_ref,
    place_ref,
    q_ref,
    keys_mine,
    keys_theirs,
    values_mine,
    values_theirs,
    out_ref,
    queries,
    scores,
    tops,
    acc,
):
    tok = q_ref.shape[0]
    heads = q_ref.shape[1] // HD
    position = lax.axis_index("seq")
    odd = lax.rem(position, 2)
    anchor = position * tok
    scale = jnp.bfloat16(LOG2E * HD**-0.5)
    starts, ends = doc_edges(lengths_ref)
    edges = list(zip(starts, ends)) + [(jnp.int32(-(2**30)), jnp.int32(0))]
    lane = lax.broadcasted_iota(jnp.int32, (1, LANES), 1)
    first = jnp.full((1, LANES), 2**30, jnp.int32)
    last = jnp.zeros((1, LANES), jnp.int32)
    for i, (start, end) in enumerate(edges):
        first = jnp.where(lane == i, start, first)
        last = jnp.where(lane == i, end, last)
    rows = lax.broadcasted_iota(jnp.int32, (tok, LANES), 0)

    def in_doc(base):
        return (rows + base >= first) & (rows + base < last)

    apart = jnp.where(in_doc(anchor) | (lane >= len(edges)), 0.0, -APART).astype(jnp.bfloat16)
    for head in range(heads):
        queries[head * tok : (head + 1) * tok, :HD] = q_ref[:, head * HD : (head + 1) * HD]
        queries[head * tok : (head + 1) * tok, HD:] = apart

    def rows_of(mine_ref, theirs_ref, back):
        if isinstance(back, int) and back == 0:
            return mine_ref[0]
        return jnp.where(lax.rem(back, 2) == 0, mine_ref[back // 2], theirs_ref[(back + 1) // 2 - odd])

    def score(back):
        marks = jnp.where(in_doc(anchor - back * tok), 1.0, 0.0).astype(jnp.bfloat16)
        keys = jnp.concatenate([rows_of(keys_mine, keys_theirs, back), marks], axis=1)
        return lax.dot_general(queries[...], keys, (((1,), (1,)), ((), ())), preferred_element_type=jnp.float32)

    causal = lax.broadcasted_iota(jnp.int32, (tok, tok), 1) <= lax.broadcasted_iota(jnp.int32, (tok, tok), 0)

    def highest(backs):
        top = None
        for back in backs:
            s = score(back)
            if isinstance(back, int) and back == 0:
                s = jnp.concatenate(
                    [jnp.where(causal, s[h * tok : (h + 1) * tok], -APART) for h in range(heads)], axis=0
                )
            scores[back] = s
            for at in range(0, tok, LANES):
                piece = s[:, at : at + LANES]
                top = piece if top is None else jnp.maximum(top, piece)
        return top

    begin = jnp.int32(0)
    for start in starts[1:]:
        begin = jnp.where(anchor >= start, start, begin)
    pairs = ((anchor - begin + tok - 1) // tok + 1) // 2

    def start_with(alone, together):
        pl.when(pairs == 0)(alone)
        pl.when(pairs > 0)(together)

    def set_tops(backs):
        tops[...] = highest(backs)

    start_with(lambda: set_tops([0]), lambda: set_tops([0, 1, 2]))

    def look(pair, carry):
        tops[...] = jnp.maximum(tops[...], highest([2 * pair - 1, 2 * pair]))
        return carry

    lax.fori_loop(2, pairs + 1, look, 0)
    tops[...] = jnp.broadcast_to(jnp.max(tops[...], axis=1, keepdims=True), tops.shape)

    def weighted(backs):
        values = jnp.concatenate([rows_of(values_mine, values_theirs, back) for back in backs], axis=0)
        values = jnp.concatenate([values, jnp.ones(values.shape, jnp.bfloat16)], axis=1)
        top = tops[...]
        weights = [
            jnp.exp2((scores[back, :, at : at + LANES] - top).astype(jnp.bfloat16) * scale)
            for back in backs
            for at in range(0, tok, LANES)
        ]
        return jnp.dot(jnp.concatenate(weights, axis=1), values, preferred_element_type=jnp.float32)

    def set_acc(backs):
        acc[...] = weighted(backs)

    start_with(lambda: set_acc([0]), lambda: set_acc([0, 1, 2]))

    def absorb(pair, carry):
        acc[...] += weighted([2 * pair - 1, 2 * pair])
        return carry

    lax.fori_loop(2, pairs + 1, absorb, 0)
    order = place_ref[pl.ds(position, 1), :]
    move = (lax.broadcasted_iota(jnp.int32, (tok, tok), 0) == order).astype(jnp.float32).astype(jnp.bfloat16)
    for head in range(heads):
        part = slice(head * tok, (head + 1) * tok)
        result = (acc[part, :HD] / acc[part, HD:]).astype(jnp.bfloat16)
        moved = jnp.dot(move, result, preferred_element_type=jnp.float32)
        out_ref[:, head * HD : (head + 1) * HD] = moved.astype(jnp.bfloat16)


def attend(lengths, send_place, query_rows, mine, theirs):
    tok, width = query_rows.shape
    kv_local = mine.shape[2] // (2 * HD)
    share = width // kv_local
    heads = share // HD
    reach = 2 * (mine.shape[0] - 1)
    by_group = pl.BlockSpec((tok, share), lambda i: (0, i))
    keys = pl.BlockSpec(mine.shape[:2] + (HD,), lambda i: (0, 0, i))
    values = pl.BlockSpec(mine.shape[:2] + (HD,), lambda i: (0, 0, i + kv_local))
    return pl.pallas_call(
        attend_kernel,
        grid=(kv_local,),
        in_specs=[
            pl.BlockSpec(memory_space=pltpu.SMEM),
            pl.BlockSpec(send_place.shape, lambda i: (0, 0)),
            by_group,
            keys,
            keys,
            values,
            values,
        ],
        out_specs=by_group,
        out_shape=jax.ShapeDtypeStruct((tok, width), jnp.bfloat16),
        scratch_shapes=[
            pltpu.VMEM((heads * tok, 2 * HD), jnp.bfloat16),
            pltpu.VMEM((reach + 1, heads * tok, tok), jnp.float32),
            pltpu.VMEM((heads * tok, LANES), jnp.float32),
            pltpu.VMEM((heads * tok, 2 * HD), jnp.float32),
        ],
        compiler_params=pltpu.CompilerParams(vmem_limit_bytes=VMEM_LIMIT // 2 + 4 * (reach + 1) * heads * tok * tok),
        cost_estimate=pl.CostEstimate(flops=tok * width, bytes_accessed=tok * width, transcendentals=0),
        name="attend",
    )(lengths, send_place, query_rows, mine, theirs, mine, theirs)


def shifted(value, steps):
    count = lax.axis_size("seq")
    return lax.ppermute(value, "seq", [(source, source + steps) for source in range(count - steps)])


def with_partner(held):
    mine = jnp.stack(held)
    count = lax.axis_size("seq")
    return mine, lax.ppermute(mine, "seq", [(source, source ^ 1) for source in range(count)])


def even_back(value, reach):
    return [value] + [shifted(value, 2 * k) for k in range(1, (reach + 1) // 2 + 1)]


def local(
    x_branch,
    z_branch,
    conv_weight,
    conv_bias,
    xproj_weight,
    dt_weight,
    dt_bias,
    decay_rate,
    skip_gain,
    query_rows,
    key_rows,
    value_rows,
    lengths,
    destination,
):
    tok = x_branch.shape[0]
    n_seq = lax.axis_size("seq")
    n_mp = lax.axis_size("mp")
    low_rank = dt_weight.shape[0]
    reach = n_seq // 2
    run_rows = tok // n_seq
    fence = lax.optimization_barrier

    lengths = in_hbm(lengths)
    halo, kv = pack(x_branch, key_rows, value_rows)
    earlier_rows = shifted(halo, 1)
    held = even_back(kv, reach)
    send_place = ((destination // tok) * run_rows + destination % run_rows).reshape(n_seq, tok)

    inner_act, partial = conv_project(lengths, x_branch, earlier_rows, conv_weight, conv_bias, xproj_weight)
    _, *held = fence((partial, *held))
    mine, theirs = with_partner(held)
    total, other = partial, jnp.zeros_like(partial)
    steps = [1 << k for k in range((n_mp - 1).bit_length())]
    for step in steps:
        if step > 1:
            total = (total.astype(jnp.float32) + other.astype(jnp.float32)).astype(jnp.bfloat16)
        if step == steps[-1]:
            total, send_place = fence((total, send_place))
        other = lax.ppermute(total, "mp", [(source, source ^ step) for source in range(n_mp)])
    attended = attend(lengths, send_place, query_rows, mine, theirs)
    total, other, attended = fence((total, other, attended))
    regrouped = lax.all_to_all(attended, "seq", split_axis=0, concat_axis=0, tiled=True)

    y, sums, state = local_scan(lengths, total, other, dt_weight, dt_bias, decay_rate, inner_act)
    states = with_partner(even_back(state, reach))
    return tuple(
        join_states(
            total,
            other,
            y,
            sums,
            inner_act,
            z_branch,
            decay_rate,
            skip_gain,
            regrouped,
            *states,
            low_rank,
            reach,
        )
    )


def solution(mesh):
    placed = (
        P("seq", "mp"),
        P("seq", "mp"),
        P(None, "mp"),
        P("mp"),
        P("mp", None),
        P(None, "mp"),
        P("mp"),
        P(None, "mp"),
        P("mp"),
        P("seq", "mp"),
        P("seq", "mp"),
        P("seq", "mp"),
        P(),
        P(),
    )
    return jax.shard_map(
        local,
        mesh=mesh,
        in_specs=placed,
        out_specs=(P("seq", "mp"), P("seq", "mp")),
        check_vma=False,
    )
```
